32 devices in a mesh: section: 2 (over y), tensor: 4 (over x, core), ctx: 4 (over z).
Axes of the slice: x: 2, y: 2, z: 4, core: 2. Of those that a mesh axis runs over, the one named last changes fastest.
Arguments:
- inputs: bfloat16 [4, 4, 256, 4, 2048], P(None, 'ctx', 'tensor'), may hold values from -6 to 6
- out_grads: bfloat16 [4, 4, 256, 4, 2048], P(None, 'ctx', 'tensor'), may hold values from -6 to 6
- norm1_gain: float32 [2, 2048], P('section'), may hold values from 0.5 to 1.5
- norm1_bias: float32 [2, 2048], P('section'), may hold values from -1.8 to 1.8
- norm2_gain: float32 [2, 2048], P('section'), may hold values from 0.5 to 1.5
- norm2_bias: float32 [2, 2048], P('section'), may hold values from -1.8 to 1.8
- w_qkv: bfloat16 [2, 2048, 8, 768], P('section', None, 'tensor'), may hold values from -0.125 to 0.125
- b_qkv: float32 [2, 8, 768], P('section', 'tensor'), may hold values from -3 to 3
- w_out: bfloat16 [2, 8, 256, 2048], P('section', 'tensor'), may hold values from -0.5 to 0.5
- b_out: float32 [2, 2048], P('section'), may hold values from -1.8 to 1.8
- input_projection: bfloat16 [2, 2048, 8192], P('section', None, 'tensor'), may hold values from -0.125 to 0.125
- input_bias_vector: float32 [2, 8192], P('section', 'tensor'), may hold values from -3 to 3
- down_projection: bfloat16 [2, 8192, 2048], P('section', 'tensor'), may hold values from -0.0625 to 0.0625
- b_down: float32 [2, 2048], P('section'), may hold values from -1.8 to 1.8
Outputs:
- states: bfloat16 [2, 4, 4, 256, 4, 2048], P('section', None, 'ctx', 'tensor')
- input_grads: float32 [2, 4, 4, 256, 4, 2048], P('section', None, 'ctx', 'tensor')
- grad_norm1_gain: float32 [2, 2048], P('section')
- grad_norm1_bias: float32 [2, 2048], P('section')
- grad_norm2_gain: float32 [2, 2048], P('section')
- grad_norm2_bias: float32 [2, 2048], P('section')
- grad_w_qkv: float32 [2, 2048, 8, 768], P('section', None, 'tensor')
- grad_b_qkv: float32 [2, 8, 768], P('section', 'tensor')
- grad_w_out: float32 [2, 8, 256, 2048], P('section', 'tensor')
- grad_b_out: float32 [2, 2048], P('section')
- grad_w_in: float32 [2, 2048, 8192], P('section', None, 'tensor')
- grad_b_in: float32 [2, 8192], P('section', 'tensor')
- grad_w_down: float32 [2, 8192, 2048], P('section', 'tensor')
- grad_b_down: float32 [2, 2048], P('section')
The draws below stay inside these ranges and needn't reach their ends.
All inputs are finite; a program needn't handle non-finite values.
Results may differ from the reference program's by a relative error of at most 0.013.
Values may be sent and summed in bfloat16 or wider, within the bound.
A program may use at most 768 MiB of HBM per device.

```python
import jax
import jax.numpy as jnp
from jax import lax

D = 2048
HEADS = 8
HD = 256
ROT = 64
FF = 8192
SEQS = 4
MICRO = 4
SECTIONS = 2
CTXS = 4
LENGTH = 1024
GROUP = 256


def block_levels(rng, shape, split, smallest, top_value):
    loudness, own = 1.0, jax.random.fold_in(rng, 6)
    for axis_at, shards_of in split:
        heights = jnp.exp(jax.random.uniform(jax.random.fold_in(own, axis_at), (shards_of,), jnp.float32, smallest / len(split), top_value / len(split)))
        loudness = loudness * jnp.repeat(heights, shape[axis_at] // shards_of).reshape([-1 if axis == axis_at else 1 for axis in range(len(shape))])
    return loudness


def gaussian(key, extent, scale, reach, pieces=(), kind=jnp.bfloat16):
    result = jax.random.normal(key, extent, jnp.float32) * scale
    if len(pieces) > 0:
        result = block_levels(key, extent, pieces, -0.22, 0.18) * result
    return jnp.clip(result, min=-reach, max=reach).astype(kind)


def setup_inputs(seed: int = 0) -> dict:
    key_list = jax.random.split(jax.random.key(seed), 15)
    inputs = gaussian(key_list[0], (MICRO, CTXS, GROUP, SEQS, D), 1.0, 6.0, ((1, 4), (2, 4)))
    out_grads = gaussian(key_list[1], (MICRO, CTXS, GROUP, SEQS, D), 1.0, 6.0, ((1, 4), (2, 4)))
    norm1_gain = jnp.clip(1.0 + 0.1 * jax.random.normal(key_list[2], (SECTIONS, D), jnp.float32), 0.5, 1.5)
    norm1_bias = gaussian(key_list[3], (SECTIONS, D), 0.3, 1.8, ((0, 2),), jnp.float32)
    norm2_gain = jnp.clip(1.0 + 0.1 * jax.random.normal(key_list[4], (SECTIONS, D), jnp.float32), 0.5, 1.5)
    norm2_bias = gaussian(key_list[5], (SECTIONS, D), 0.3, 1.8, ((0, 2),), jnp.float32)
    w_qkv = gaussian(key_list[6], (SECTIONS, D, HEADS, 3 * HD), D ** -0.5, 0.125, ((0, 2), (2, 4)))
    b_qkv = gaussian(key_list[7], (SECTIONS, HEADS, 3 * HD), 0.5, 3.0, ((0, 2), (1, 4)), jnp.float32)
    w_out = gaussian(key_list[8], (SECTIONS, HEADS, HD, D), (HEADS * HD // 16) ** -0.5, 0.5, ((0, 2), (1, 4)))
    b_out = gaussian(key_list[9], (SECTIONS, D), 0.3, 1.8, ((0, 2),), jnp.float32)
    input_projection = gaussian(key_list[10], (SECTIONS, D, FF), D ** -0.5, 0.125, ((0, 2), (2, 4)))
    input_bias_vector = gaussian(key_list[11], (SECTIONS, FF), 0.5, 3.0, ((0, 2), (1, 4)), jnp.float32)
    down_projection = gaussian(key_list[12], (SECTIONS, FF, D), FF ** -0.5, 0.0625, ((0, 2), (1, 4)))
    b_down = gaussian(key_list[13], (SECTIONS, D), 0.3, 1.8, ((0, 2),), jnp.float32)
    return {"inputs": inputs, "out_grads": out_grads, "norm1_gain": norm1_gain, "norm1_bias": norm1_bias, "norm2_gain": norm2_gain, "norm2_bias": norm2_bias, "w_qkv": w_qkv, "b_qkv": b_qkv, "w_out": w_out, "b_out": b_out, "input_projection": input_projection, "input_bias_vector": input_bias_vector, "down_projection": down_projection, "b_down": b_down}


@jax.custom_vjp
def low(v):
    return lax.optimization_barrier(v.astype(jnp.bfloat16)).astype(jnp.float32)

@jax.custom_vjp
def reduced_backward(v):
    return v

def low_keep(v):
    return (low(v), None)

def low_pass(kept, grad):
    return (grad,)

def back_keep(v):
    return (v, None)

def back_low(kept, grad):
    return (low(grad),)
low.defvjp(low_keep, low_pass)
reduced_backward.defvjp(back_keep, back_low)
highest_precision = lax.Precision.HIGHEST
epsilon = 1e-05

def standardize(values):
    average = lax.optimization_barrier(jnp.mean(values, axis=-1, keepdims=True))
    centred = values - average
    return centred * lax.rsqrt(lax.optimization_barrier(jnp.mean(centred * centred, axis=-1, keepdims=True)) + epsilon)

def angle_tables():
    frequency = 1.0 / 10000.0 ** (jnp.arange(0, ROT, 2, dtype=jnp.float32) / ROT)
    places = jnp.arange(LENGTH, dtype=jnp.int32).astype(jnp.float32)
    angles = places[:, None] * frequency[None, :]
    angles = jnp.concatenate([angles, angles], axis=-1)[:, None, None, :]
    return (jnp.cos(angles), jnp.sin(angles))

def rotate(values, cosine, sine_table):
    half_rot = ROT // 2
    leading = values[..., :ROT]
    turned = jnp.concatenate([-leading[..., half_rot:], leading[..., :half_rot]], axis=-1)
    return jnp.concatenate([leading * cosine + turned * sine_table, values[..., ROT:]], axis=-1)

def attend_sequence(triple):
    queries, keys_in, values = triple
    scores = jnp.einsum('qhe,khe->hqk', queries, keys_in, precision=highest_precision) * HD ** (-0.5)
    scores = reduced_backward(scores)
    places = jnp.arange(LENGTH, dtype=jnp.int32)
    allowed = places[None, :] <= places[:, None]
    scores = jnp.where(allowed[None], scores, -1e+30)
    chance = low(jax.nn.softmax(scores, axis=-1))
    return reduced_backward(low(jnp.einsum('hqk,khe->qhe', chance, values, precision=highest_precision)))

def block_layer(inbound, weights):
    gain_one, bias_one, gain_two, bias_two, w_qkv, b_qkv, w_out, b_out, input_projection, input_bias_vector, down_projection, b_down = weights
    cosine, sine_table = angle_tables()
    standard = standardize(inbound)
    normed_one = low(standard * gain_one + bias_one)
    second_normed = low(standard * gain_two + bias_two)
    projected = jnp.einsum('lsd,dhe->lshe', normed_one, w_qkv, precision=highest_precision) + b_qkv
    projected = reduced_backward(projected)
    queries = low(rotate(projected[..., :HD], cosine, sine_table))
    keys_in = low(rotate(projected[..., HD:2 * HD], cosine, sine_table))
    values = low(projected[..., 2 * HD:])
    context = lax.map(jax.checkpoint(attend_sequence), (queries.transpose(1, 0, 2, 3), keys_in.transpose(1, 0, 2, 3), values.transpose(1, 0, 2, 3)))
    context = context.transpose(1, 0, 2, 3)
    attention = jnp.einsum('lshe,hed->lsd', context, w_out, precision=highest_precision)
    hidden_state = reduced_backward(jnp.einsum('vuy,ye->vue', second_normed, input_projection, precision=highest_precision) + input_bias_vector)
    active_units = low(jax.nn.gelu(hidden_state, approximate=False))
    feed_forward = jnp.einsum('pwn,ne->pwe', active_units, down_projection, precision=highest_precision)
    return inbound + attention + feed_forward + b_out + b_down

def reference(inputs, out_grads, norm1_gain, norm1_bias, norm2_gain, norm2_bias, w_qkv, b_qkv, w_out, b_out, input_projection, input_bias_vector, down_projection, b_down):
    params = tuple((argument.astype(jnp.float32) for argument in (norm1_gain, norm1_bias, norm2_gain, norm2_bias, w_qkv, b_qkv, w_out, b_out, input_projection, input_bias_vector, down_projection, b_down)))

    def one_batch(totals, micro_batch):
        inbound, cotangent = micro_batch
        inbound = inbound.astype(jnp.float32).reshape(LENGTH, SEQS, D)
        cotangent = cotangent.astype(jnp.float32).reshape(LENGTH, SEQS, D)

        def both_layers(start_rows, offset, weights):
            first_out = block_layer(start_rows, tuple((weight[0] for weight in weights)))
            sent_state = reduced_backward(low(first_out)) + offset
            return (block_layer(sent_state, tuple((weight[1] for weight in weights))), sent_state)
        (final_out, sent_state), pullback = jax.vjp(both_layers, inbound, jnp.zeros_like(inbound), params)
        d_start, d_offset, d_weights = pullback((cotangent, jnp.zeros_like(sent_state)))
        totals = tuple((total + grad_in for total, grad_in in zip(totals, d_weights)))
        return (totals, (jnp.stack([sent_state, final_out]).astype(jnp.bfloat16), jnp.stack([d_start, d_offset])))
    totals, (states, back_list) = lax.scan(one_batch, tuple((jnp.zeros_like(argument) for argument in params)), (inputs, out_grads))
    states = states.transpose(1, 0, 2, 3, 4).reshape(SECTIONS, MICRO, CTXS, GROUP, SEQS, D)
    back_list = back_list.transpose(1, 0, 2, 3, 4).reshape(SECTIONS, MICRO, CTXS, GROUP, SEQS, D)
    return (states, back_list) + tuple(totals)
```

```python
from functools import partial

import jax
import jax.numpy as jnp
from jax import lax
from jax.experimental import pallas as pl
from jax.experimental.pallas import tpu as pltpu
from jax.sharding import PartitionSpec as P

ROT = 64
LAG = 2
LANES = 128
epsilon = 1e-05
masked_score = -1e30
f32 = jnp.float32
bf16 = jnp.bfloat16
NT = (((1,), (1,)), ((), ()))
TN = (((0,), (0,)), ((), ()))
NN = (((1,), (0,)), ((), ()))
VMEM_LIMIT = 50 * 1024 * 1024


def dot(a, b, dims=NN):
    return lax.dot_general(a, b, dims, preferred_element_type=f32)


def standardize(rows):
    values = rows.astype(f32)
    average = jnp.mean(values, axis=-1, keepdims=True)
    centred = values - average
    inverse = lax.rsqrt(jnp.mean(centred * centred, axis=-1, keepdims=True) + epsilon)
    return centred * inverse, inverse


def position_tables(section_rows, blocks, rows, tensor):
    half = ROT // 2
    frequency = 1.0 / 10000.0 ** (jnp.arange(0, ROT, 2, dtype=f32) / ROT)
    t, c, i = jnp.meshgrid(
        jnp.arange(tensor), jnp.arange(blocks), jnp.arange(rows), indexing="ij"
    )
    relative = (c * (rows * tensor) + t * rows + i).reshape(-1).astype(jnp.int32)
    tables = []
    for part in range(2):
        places = (relative + part * blocks * rows * tensor).astype(f32)
        angles = places[:, None] * frequency[None, :]
        cosine, sine = jnp.cos(angles), jnp.sin(angles)
        none = jnp.zeros_like(sine)
        rest = jnp.zeros((relative.shape[0], LANES - ROT), f32)
        tables.append(
            (
                jnp.concatenate([cosine, cosine, rest + 1.0], axis=-1),
                jnp.concatenate([-sine, none, rest], axis=-1),
                jnp.concatenate([none, sine, rest], axis=-1),
            )
        )
    return relative, tables


def turn(values, cosine, ahead, behind, sign):
    half = ROT // 2
    lead = values[:, :LANES]
    turned = pltpu.roll(lead, LANES - half, 1) * ahead + pltpu.roll(lead, half, 1) * behind
    return jnp.concatenate([lead * cosine + sign * turned, values[:, LANES:]], axis=1)


def project_kernel(heads, wide, slot, std, wq, bq, wi, bi, cosine, ahead, behind, *rest):
    qkv_out, std_out, act_out, dg_out = rest[-4:]
    step = pl.program_id(0)

    @pl.when(step == 0)
    def _():
        std_out[0] = std[...]

    @pl.when(step < heads)
    def _():
        size = wq.shape[1] // 3
        for part in range(3):
            columns = slice(part * size, (part + 1) * size)
            z = dot(std[...], wq[:, columns]) + bq[:, columns]
            if part < 2:
                z = turn(z, cosine[...], ahead[...], behind[...], 1.0)
            qkv_out[0, :, columns] = z.astype(bf16)

    @pl.when(step >= heads)
    def _():
        for at in range(0, wide, 256):
            columns = slice(at, at + 256)
            h = dot(std[...], wi[:, columns]) + bi[:, columns]
            phi = 0.5 + 0.5 * lax.erf(h * (0.5**0.5))
            density = jnp.exp(h * h * -0.5) * 0.3989422804014327
            act_out[0, :, columns] = (h * phi).astype(bf16)
            dg_out[0, :, columns] = (phi + h * density).astype(bf16)


def stacked_outputs(shapes, buffers, first_input):
    out_shape = [jax.ShapeDtypeStruct(s, d) for s, d in shapes]
    if buffers is None:
        return out_shape, [], [], {}
    aliases = {first_input + k: k for k in range(len(buffers))}
    return out_shape, list(buffers), [pl.BlockSpec(memory_space=pl.ANY)] * len(buffers), aliases


def params():
    return pltpu.CompilerParams(vmem_limit_bytes=VMEM_LIMIT)


def project(slot, std, wq, bq, wi, bi, table, slots, buffers):
    rows, width = std.shape
    heads = bq.shape[1] // 768
    head_cols = wq.shape[1] // heads
    units = wi.shape[1]
    wide = min(512, units)
    shapes = [
        ((slots, rows, wq.shape[1]), bf16),
        ((slots, rows, width), bf16),
        ((slots, rows, units), bf16),
        ((slots, rows, units), bf16),
    ]
    out_shape, extra, extra_specs, aliases = stacked_outputs(shapes, buffers, 9)
    head_of = lambda i, s: (0, jnp.minimum(i, heads - 1))
    unit_of = lambda i, s: (0, jnp.maximum(i - heads, 0))
    whole = lambda i, s: (0, 0)
    return pl.pallas_call(
        partial(project_kernel, heads, wide),
        out_shape=out_shape,
        grid_spec=pltpu.PrefetchScalarGridSpec(
            num_scalar_prefetch=1,
            grid=(heads + units // wide,),
            in_specs=[
                pl.BlockSpec((rows, width), whole),
                pl.BlockSpec((width, head_cols), head_of),
                pl.BlockSpec((1, head_cols), head_of),
                pl.BlockSpec((width, wide), unit_of),
                pl.BlockSpec((1, wide), unit_of),
                pl.BlockSpec((rows, LANES), whole),
                pl.BlockSpec((rows, LANES), whole),
                pl.BlockSpec((rows, LANES), whole),
            ]
            + extra_specs,
            out_specs=[
                pl.BlockSpec((1, rows, head_cols), lambda i, s: (s[0], 0, jnp.minimum(i, heads - 1))),
                pl.BlockSpec((1, rows, width), lambda i, s: (s[0], 0, 0)),
                pl.BlockSpec((1, rows, wide), lambda i, s: (s[0], 0, jnp.maximum(i - heads, 0))),
                pl.BlockSpec((1, rows, wide), lambda i, s: (s[0], 0, jnp.maximum(i - heads, 0))),
            ],
        ),
        input_output_aliases=aliases,
        compiler_params=params(),
        cost_estimate=pl.CostEstimate(
            flops=2 * rows * width * (wq.shape[1] + units),
            bytes_accessed=2 * width * (wq.shape[1] + units) + 8 * rows * width,
            transcendentals=2 * rows * units,
        ),
        name="project",
    )(slot, std, wq, bq, wi, bi, *table, *extra)


def attend_kernel(second, slot, *refs):
    if second:
        q, k, v, kp, vp, pq, pk = refs[:7]
    else:
        q, k, v, pq, pk = refs[:5]
    ctx_out, lse_out = refs[-2:]
    scale = q.shape[-1] ** -0.5
    s = dot(q[0], k[0], NT) * scale
    s = jnp.where(pq[...] >= pk[...], s, masked_score)
    peak = jnp.max(s, axis=-1, keepdims=True)
    if second:
        sp = dot(q[0], kp[0], NT) * scale
        peak = jnp.maximum(peak, jnp.max(sp, axis=-1, keepdims=True))
    p = jnp.exp(s - peak)
    total = jnp.sum(p, axis=-1, keepdims=True)
    if second:
        pp = jnp.exp(sp - peak)
        total = total + jnp.sum(pp, axis=-1, keepdims=True)
    share = 1.0 / total
    ctx = dot((p * share).astype(bf16), v[0])
    if second:
        ctx = ctx + dot((pp * share).astype(bf16), vp[0])
    ctx_out[0] = ctx.astype(bf16)
    lse_out[0] = jnp.broadcast_to(peak + jnp.log(total), lse_out.shape[1:])


def head_block(rows, part, back, size):
    return pl.BlockSpec((1, rows, size), lambda h, s: (s[0] - back, 0, 3 * h + part))


def attend(slot, qkv, places_q, places_k, heads, second, buffers):
    slots, rows, columns = qkv.shape
    size = columns // (3 * heads)
    shapes = [((slots, rows, heads * size), bf16), ((slots, rows, heads * LANES), f32)]
    count = 5 if second else 3
    out_shape, extra, extra_specs, aliases = stacked_outputs(shapes, buffers, count + 3)
    whole = lambda h, s: (0, 0)
    specs = [head_block(rows, part, 0, size) for part in range(3)]
    if second:
        specs += [head_block(rows, part, 1, size) for part in (1, 2)]
    keys = rows * (2 if second else 1)
    return pl.pallas_call(
        partial(attend_kernel, second),
        out_shape=out_shape,
        grid_spec=pltpu.PrefetchScalarGridSpec(
            num_scalar_prefetch=1,
            grid=(heads,),
            in_specs=specs + [pl.BlockSpec((rows, 1), whole), pl.BlockSpec((1, rows), whole)] + extra_specs,
            out_specs=[
                pl.BlockSpec((1, rows, size), lambda h, s: (s[0], 0, h)),
                pl.BlockSpec((1, rows, LANES), lambda h, s: (s[0], 0, h)),
            ],
        ),
        input_output_aliases=aliases,
        compiler_params=params(),
        cost_estimate=pl.CostEstimate(
            flops=4 * heads * rows * keys * size * 2,
            bytes_accessed=2 * rows * columns,
            transcendentals=heads * rows * keys,
        ),
        name="attend",
    )(slot, *([qkv] * count), places_q, places_k, *extra)


def combine_kernel(dims, slot, a, b, wa, wb, out):
    out[...] = (dot(a[0], wa[...], dims) + dot(b[0], wb[...], dims)).astype(bf16)


def combine(slot, a, b, wa, wb, transposed):
    rows = a.shape[1]
    width = wa.shape[0] if transposed else wa.shape[1]
    wide = min(512, width)
    if transposed:
        weight_specs = [pl.BlockSpec((wide, w.shape[1]), lambda i, s: (i, 0)) for w in (wa, wb)]
    else:
        weight_specs = [pl.BlockSpec((w.shape[0], wide), lambda i, s: (0, i)) for w in (wa, wb)]
    return pl.pallas_call(
        partial(combine_kernel, NT if transposed else NN),
        out_shape=jax.ShapeDtypeStruct((rows, width), bf16),
        grid_spec=pltpu.PrefetchScalarGridSpec(
            num_scalar_prefetch=1,
            grid=(width // wide,),
            in_specs=[
                pl.BlockSpec((1, rows, a.shape[2]), lambda i, s: (s[0], 0, 0)),
                pl.BlockSpec((1, rows, b.shape[2]), lambda i, s: (s[0], 0, 0)),
            ]
            + weight_specs,
            out_specs=pl.BlockSpec((rows, wide), lambda i, s: (0, i)),
        ),
        compiler_params=params(),
        cost_estimate=pl.CostEstimate(
            flops=2 * rows * width * (a.shape[2] + b.shape[2]),
            bytes_accessed=2 * width * (a.shape[2] + b.shape[2]) + 4 * rows * width,
            transcendentals=0,
        ),
        name="combine",
    )(slot, a, b, wa, wb)


def spread_kernel(slot, gy, wo, wd, dg, *rest):
    dctx_out, gy_out, dh_out = rest[-3:]
    step = pl.program_id(0)

    @pl.when(step == 0)
    def _():
        gy_out[0] = gy[...]
        dctx_out[...] = dot(gy[...], wo[...], NT).astype(bf16)

    @pl.when(step > 0)
    def _():
        for at in range(0, wd.shape[0], 256):
            part = slice(at, at + 256)
            dh_out[0, :, part] = (dot(gy[...], wd[part, :], NT) * dg[0, :, part].astype(f32)).astype(bf16)


def spread(slot, gy, wo, wd, dg, buffers):
    rows, width = gy.shape
    slots = dg.shape[0]
    units = wd.shape[0]
    wide = min(512, units)
    shapes = [
        ((rows, wo.shape[0]), bf16),
        ((slots, rows, width), bf16),
        ((slots, rows, units), bf16),
    ]
    out_shape = [jax.ShapeDtypeStruct(s, d) for s, d in shapes]
    extra, extra_specs, aliases = [], [], {}
    if buffers is not None:
        extra = list(buffers)
        extra_specs = [pl.BlockSpec(memory_space=pl.ANY)] * 2
        aliases = {5: 1, 6: 2}
    whole = lambda i, s: (0, 0)
    unit_of = lambda i, s: (s[0], 0, jnp.maximum(i - 1, 0))
    return pl.pallas_call(
        spread_kernel,
        out_shape=out_shape,
        grid_spec=pltpu.PrefetchScalarGridSpec(
            num_scalar_prefetch=1,
            grid=(1 + units // wide,),
            in_specs=[
                pl.BlockSpec((rows, width), whole),
                pl.BlockSpec(wo.shape, whole),
                pl.BlockSpec((wide, width), lambda i, s: (jnp.maximum(i - 1, 0), 0)),
                pl.BlockSpec((1, rows, wide), unit_of),
            ]
            + extra_specs,
            out_specs=[
                pl.BlockSpec((rows, wo.shape[0]), whole),
                pl.BlockSpec((1, rows, width), lambda i, s: (s[0], 0, 0)),
                pl.BlockSpec((1, rows, wide), unit_of),
            ],
        ),
        input_output_aliases=aliases,
        compiler_params=params(),
        cost_estimate=pl.CostEstimate(
            flops=2 * rows * width * (units + wo.shape[0]),
            bytes_accessed=2 * width * (units + wo.shape[0]) + 8 * rows * width,
            transcendentals=0,
        ),
        name="spread",
    )(slot, gy, wo, wd, dg, *extra)


def attend_back_kernel(second, slot, *refs):
    if second:
        q, k, v, dctx, ctx, lse, pq, pk, cosine, ahead, behind, kp, vp = refs[:13]
        out, dkp_out, dvp_out = refs[-3:]
    else:
        q, k, v, dctx, ctx, lse, pq, pk, cosine, ahead, behind, dk_in, dv_in = refs[:13]
        out = refs[-1]
    size = q.shape[-1]
    scale = size**-0.5
    logsum = lse[0][:, :1]
    delta = jnp.sum(dctx[...].astype(f32) * ctx[0].astype(f32), axis=-1, keepdims=True)

    def pieces(k, v, masked):
        s = dot(q[0], k[0], NT) * scale
        if masked:
            s = jnp.where(pq[...] >= pk[...], s, masked_score)
        p = jnp.exp(s - logsum)
        d_chance = dot(dctx[...], v[0], NT)
        d_scores = (p * (d_chance - delta)).astype(bf16)
        dq = dot(d_scores, k[0])
        dk = dot(d_scores, q[0], TN)
        dv = dot(p.astype(bf16), dctx[...], TN)
        return dq, dk, dv

    dq, dk, dv = pieces(k, v, True)
    if second:
        dq_more, dkp, dvp = pieces(kp, vp, False)
        dq = dq + dq_more
        dkp_out[...] = dkp
        dvp_out[...] = dvp
    else:
        dk = dk + dk_in[...]
        dv = dv + dv_in[...]
    table = (cosine[...], ahead[...], behind[...])
    out[0, :, 0:size] = turn(dq * scale, *table, -1.0).astype(bf16)
    out[0, :, size : 2 * size] = turn(dk * scale, *table, -1.0).astype(bf16)
    out[0, :, 2 * size :] = dv.astype(bf16)


def attend_back(slot, qkv, dctx, ctx, lse, places_q, places_k, table, heads, carry, buffer):
    slots, rows, columns = qkv.shape
    size = columns // (3 * heads)
    second = carry is None
    whole = lambda h, s: (0, 0)
    specs = [head_block(rows, part, 0, size) for part in range(3)]
    specs += [
        pl.BlockSpec((rows, size), lambda h, s: (0, h)),
        pl.BlockSpec((1, rows, size), lambda h, s: (s[0], 0, h)),
        pl.BlockSpec((1, rows, LANES), lambda h, s: (s[0], 0, h)),
        pl.BlockSpec((rows, 1), whole),
        pl.BlockSpec((1, rows), whole),
        pl.BlockSpec((rows, LANES), whole),
        pl.BlockSpec((rows, LANES), whole),
        pl.BlockSpec((rows, LANES), whole),
    ]
    out_shape = [jax.ShapeDtypeStruct((slots, rows, columns), bf16)]
    out_specs = [pl.BlockSpec((1, rows, 3 * size), lambda h, s: (s[0], 0, h))]
    column_spec = pl.BlockSpec((rows, size), lambda h, s: (0, h))
    if second:
        specs += [head_block(rows, part, 1, size) for part in (1, 2)]
        more = (qkv, qkv)
        out_shape += [jax.ShapeDtypeStruct((rows, heads * size), f32)] * 2
        out_specs += [column_spec] * 2
    else:
        specs += [column_spec] * 2
        more = carry
    extra, extra_specs, aliases = [], [], {}
    if buffer is not None:
        extra, extra_specs, aliases = [buffer], [pl.BlockSpec(memory_space=pl.ANY)], {14: 0}
    keys = rows * (2 if second else 1)
    return pl.pallas_call(
        partial(attend_back_kernel, second),
        out_shape=out_shape,
        grid_spec=pltpu.PrefetchScalarGridSpec(
            num_scalar_prefetch=1, grid=(heads,), in_specs=specs + extra_specs, out_specs=out_specs
        ),
        input_output_aliases=aliases,
        compiler_params=params(),
        cost_estimate=pl.CostEstimate(
            flops=10 * heads * rows * keys * size * 2,
            bytes_accessed=6 * rows * columns,
            transcendentals=heads * rows * keys,
        ),
        name="attend_back",
    )(slot, qkv, qkv, qkv, dctx, ctx, lse, places_q, places_k, *table, *more, *extra)


def exchange(blocks, axis):
    count = blocks.shape[0]
    me = lax.axis_index(axis)
    got = [lax.dynamic_index_in_dim(blocks, me, 0, keepdims=False)]
    for shift in range(1, count):
        piece = lax.dynamic_index_in_dim(blocks, (me + shift) % count, 0, keepdims=False)
        got.append(lax.ppermute(piece, axis, [(k, (k + shift) % count) for k in range(count)]))
    ring = jnp.stack(got[::-1] + got[::-1])
    return lax.dynamic_slice_in_dim(ring, (count - 1 - me) % count, count, 0)


def swap_cores(v, tensor):
    return lax.ppermute(v, "tensor", [(k, k ^ 1) for k in range(tensor)])


def shift_chips(v, tensor, shift):
    return lax.ppermute(v, "tensor", [(k, (k + 2 * shift) % tensor) for k in range(tensor)])


def gather_rows(own, tensor):
    chips = tensor // 2
    me = lax.axis_index("tensor")
    chip, core = me // 2, me % 2
    got = [own] + [shift_chips(own, tensor, shift) for shift in range(1, chips)]
    if chips == 2:
        mine = jnp.stack([jnp.where(chip == 0, got[0], got[1]), jnp.where(chip == 0, got[1], got[0])])
    else:
        ring = jnp.stack(got[::-1] + got[::-1])
        mine = lax.dynamic_slice_in_dim(ring, (chips - 1 - chip) % chips, chips, 0)
    theirs = swap_cores(mine, tensor)
    both = jnp.stack([jnp.where(core == 0, mine, theirs), jnp.where(core == 0, theirs, mine)], axis=1)
    return both.reshape(tensor * own.shape[0], own.shape[1])


def scatter_sum(partial_rows, tensor):
    chips = tensor // 2
    me = lax.axis_index("tensor")
    chip, core = me // 2, me % 2
    width = partial_rows.shape[1]
    parts = partial_rows.reshape(chips, 2, -1, width)
    mine = lax.dynamic_index_in_dim(parts, core, 1, keepdims=False)
    theirs = swap_cores(lax.dynamic_index_in_dim(parts, 1 - core, 1, keepdims=False), tensor)
    total = mine.astype(f32) + theirs.astype(f32)
    low = total.astype(bf16)
    own = lax.dynamic_index_in_dim(total, chip, 0, keepdims=False)
    for shift in range(1, chips):
        piece = lax.dynamic_index_in_dim(low, (chip + shift) % chips, 0, keepdims=False)
        own = own + shift_chips(piece, tensor, shift).astype(f32)
    return own


def body(
    inputs,
    out_grads,
    norm1_gain,
    norm1_bias,
    norm2_gain,
    norm2_bias,
    w_qkv,
    b_qkv,
    w_out,
    b_out,
    input_projection,
    input_bias_vector,
    down_projection,
    b_down,
):
    ctx_count = lax.axis_size("ctx")
    tensor = lax.axis_size("tensor")
    micro, _, rows, seqs, width = inputs.shape
    heads = w_qkv.shape[2]
    head_cols = w_qkv.shape[3]
    first = lax.axis_index("section") == 0
    per_device = micro * seqs // ctx_count
    blocks = ctx_count // 2
    own_rows = blocks * rows
    tasks = 2 * per_device
    slots = tasks + 1

    chosen = jnp.where(first, inputs[:, 0], out_grads[:, 0])
    chosen = chosen.transpose(0, 2, 1, 3).reshape(per_device, ctx_count, rows, width)
    own_chosen = []
    for j in range(per_device):
        moved = exchange(chosen[j], "ctx").reshape(2, own_rows, width)
        own_chosen += [moved[0], moved[1]]

    wq = w_qkv[0].reshape(width, heads * head_cols)
    wi = input_projection[0]
    wo = w_out[0].reshape(-1, width)
    wd = down_projection[0]
    gain_one, bias_one, gain_two, bias_two = norm1_gain[0], norm1_bias[0], norm2_gain[0], norm2_bias[0]
    wq_scaled = (wq.astype(f32) * gain_one[:, None]).astype(bf16)
    wi_scaled = (wi.astype(f32) * gain_two[:, None]).astype(bf16)
    bq = b_qkv[0].reshape(1, -1) + jnp.sum(wq.astype(f32) * bias_one[:, None], axis=0, keepdims=True)
    bi = input_bias_vector + jnp.sum(wi.astype(f32) * bias_two[:, None], axis=0, keepdims=True)
    out_bias = (b_out[0] + b_down[0])[None]

    relative, tables = position_tables(None, blocks, rows, tensor)
    places_q, places_k = relative[:, None], relative[None, :]

    arrived = {}
    kept = []
    produced = []
    forward_buffers = attend_buffers = None
    for step in range(tasks + LAG):
        x_own = own_chosen[min(step, tasks - 1)]
        if step >= LAG:
            x_own = jnp.where(first, x_own, arrived[step])
        kept.append(x_own)
        part = step % 2
        slot_first = step if step < tasks else tasks
        slot_second = step - LAG if step >= LAG else tasks
        slot = jnp.where(first, slot_first, slot_second).astype(jnp.int32).reshape(1)
        std = gather_rows(standardize(x_own)[0].astype(bf16), tensor)
        forward_buffers = project(
            slot, std, wq_scaled, bq, wi_scaled, bi, tables[part], slots, forward_buffers
        )
        attend_buffers = attend(
            slot, forward_buffers[0], places_q, places_k, heads, part == 1, attend_buffers
        )
        summed = scatter_sum(combine(slot, attend_buffers[0], forward_buffers[2], wo, wd, False), tensor)
        result = (x_own.astype(f32) + summed + out_bias).astype(bf16)
        produced.append(result)
        if step < tasks:
            arrived[step + LAG] = lax.ppermute(result, "section", [(0, 1)])
    qkv, std_all, act_all, dg_all = forward_buffers
    ctx_all, lse_all = attend_buffers

    back = {}
    back_list = []
    spread_buffers = None
    dproj_all = None
    carry = None
    bias_total = jnp.zeros((width,), f32)
    for step in range(tasks + LAG):
        part = 1 - step % 2
        task_first = max(step - LAG, 0)
        task_second = min(step, tasks - 1)
        slot_of = lambda task: (task // 2) * 2 + 1 - task % 2
        near, far = slot_of(task_first), slot_of(task_second)
        slot_first = near if step >= LAG else tasks
        slot_second = far if step < tasks else tasks
        slot = jnp.where(first, slot_first, slot_second).astype(jnp.int32).reshape(1)
        gy_own = own_chosen[far]
        if step >= LAG:
            gy_own = jnp.where(first, back[step], gy_own)
        gy = gather_rows(gy_own, tensor)
        dctx, *spread_buffers = spread(slot, gy, wo, wd, dg_all, spread_buffers)
        made = attend_back(
            slot,
            qkv,
            dctx,
            ctx_all,
            lse_all,
            places_q,
            places_k,
            tables[part],
            heads,
            None if part == 1 else carry,
            dproj_all,
        )
        dproj_all = made[0]
        carry = tuple(made[1:]) if part == 1 else None
        e = scatter_sum(combine(slot, dproj_all, spread_buffers[1], wq_scaled, wi_scaled, True), tensor)
        x_own = jnp.where(first, kept[near], kept[far + LAG])
        standard, inverse = standardize(x_own)
        gy_wide = gy_own.astype(f32)
        d_input = gy_wide + inverse * (
            e
            - jnp.mean(e, axis=-1, keepdims=True)
            - standard * jnp.mean(e * standard, axis=-1, keepdims=True)
        )
        back_list.append(d_input)
        valid = jnp.where(first, step >= LAG, step < tasks)
        bias_total = bias_total + jnp.where(valid, jnp.sum(gy_wide, axis=0), 0.0)
        if step < tasks:
            back[step + LAG] = lax.ppermute(d_input.astype(bf16), "section", [(1, 0)])
    gy_all, dh_all = spread_buffers

    def flat(v):
        return v[:tasks].reshape(-1, v.shape[-1])

    std_flat, gy_flat, dproj, dhidden = flat(std_all), flat(gy_all), flat(dproj_all), flat(dh_all)
    g_one = dot(std_flat, dproj, TN)
    g_two = dot(std_flat, dhidden, TN)
    d_b_qkv = jnp.sum(dproj, axis=0, dtype=f32)
    d_b_in = jnp.sum(dhidden, axis=0, dtype=f32)
    d_w_qkv = gain_one[:, None] * g_one + bias_one[:, None] * d_b_qkv[None]
    d_w_in = gain_two[:, None] * g_two + bias_two[:, None] * d_b_in[None]
    d_w_out = dot(flat(ctx_all), gy_flat, TN)
    d_w_down = dot(flat(act_all), gy_flat, TN)
    wq_wide, wi_wide = wq.astype(f32), wi.astype(f32)
    vectors = jnp.stack(
        [
            jnp.sum(wq_wide * g_one, axis=1),
            jnp.sum(wq_wide * d_b_qkv[None], axis=1),
            jnp.sum(wi_wide * g_two, axis=1),
            jnp.sum(wi_wide * d_b_in[None], axis=1),
            bias_total,
        ]
    )
    vectors = lax.psum(vectors, ("tensor", "ctx"))
    d_b_qkv, d_b_in = lax.psum((d_b_qkv, d_b_in), "ctx")
    big = lax.psum(tuple(v.astype(bf16) for v in (d_w_qkv, d_w_out, d_w_in, d_w_down)), "ctx")
    d_w_qkv, d_w_out, d_w_in, d_w_down = (v.astype(f32) for v in big)

    def homeward(pieces):
        stacked = jnp.stack(pieces).reshape(per_device, ctx_count, rows, width)
        moved = exchange(stacked.transpose(1, 0, 2, 3), "ctx")
        moved = moved.transpose(1, 0, 2, 3).reshape(micro, seqs, rows, width)
        return moved.transpose(0, 2, 1, 3)[None, :, None]

    states = homeward([jnp.where(first, produced[k], produced[k + LAG]) for k in range(tasks)])
    order = [(k // 2) * 2 + 1 - k % 2 for k in range(tasks)]
    input_grads = homeward(
        [jnp.where(first, back_list[k + LAG], back_list[k]).astype(bf16) for k in order]
    ).astype(f32)
    return (
        states,
        input_grads,
        vectors[0][None],
        vectors[1][None],
        vectors[2][None],
        vectors[3][None],
        d_w_qkv.reshape(w_qkv.shape),
        d_b_qkv.reshape(b_qkv.shape),
        d_w_out.reshape(w_out.shape),
        vectors[4][None],
        d_w_in[None],
        d_b_in[None],
        d_w_down[None],
        vectors[4][None],
    )


def solution(mesh):
    return jax.shard_map(
        body,
        mesh=mesh,
        in_specs=(
            P(None, "ctx", "tensor", None, None),
            P(None, "ctx", "tensor", None, None),
            P("section", None),
            P("section", None),
            P("section", None),
            P("section", None),
            P("section", None, "tensor", None),
            P("section", "tensor", None),
            P("section", "tensor", None, None),
            P("section", None),
            P("section", None, "tensor"),
            P("section", "tensor"),
            P("section", "tensor", None),
            P("section", None),
        ),
        out_specs=(
            P("section", None, "ctx", "tensor", None, None),
            P("section", None, "ctx", "tensor", None, None),
            P("section", None),
            P("section", None),
            P("section", None),
            P("section", None),
            P("section", None, "tensor", None),
            P("section", "tensor", None),
            P("section", "tensor", None, None),
            P("section", None),
            P("section", None, "tensor"),
            P("section", "tensor"),
            P("section", "tensor", None),
            P("section", None),
        ),
        check_vma=False,
    )
```

```python
from functools import partial

import jax
import jax.numpy as jnp
from jax import lax
from jax.experimental import pallas as pl
from jax.experimental.pallas import tpu as pltpu
from jax.sharding import PartitionSpec as P

ROT = 64
LAG = 2
LANES = 128
epsilon = 1e-05
masked_score = -1e30
f32 = jnp.float32
bf16 = jnp.bfloat16
NT = (((1,), (1,)), ((), ()))
TN = (((0,), (0,)), ((), ()))
NN = (((1,), (0,)), ((), ()))
VMEM_LIMIT = 50 * 1024 * 1024


def dot(a, b, dims=NN):
    return lax.dot_general(a, b, dims, preferred_element_type=f32)


def standardize(rows):
    values = rows.astype(f32)
    average = jnp.mean(values, axis=-1, keepdims=True)
    centred = values - average
    inverse = lax.rsqrt(jnp.mean(centred * centred, axis=-1, keepdims=True) + epsilon)
    return centred * inverse, inverse


def position_tables(section_rows, blocks, rows, tensor):
    half = ROT // 2
    frequency = 1.0 / 10000.0 ** (jnp.arange(0, ROT, 2, dtype=f32) / ROT)
    t, c, i = jnp.meshgrid(
        jnp.arange(tensor), jnp.arange(blocks), jnp.arange(rows), indexing="ij"
    )
    relative = (c * (rows * tensor) + t * rows + i).reshape(-1).astype(jnp.int32)
    tables = []
    for part in range(2):
        places = (relative + part * blocks * rows * tensor).astype(f32)
        angles = places[:, None] * frequency[None, :]
        cosine, sine = jnp.cos(angles), jnp.sin(angles)
        none = jnp.zeros_like(sine)
        rest = jnp.zeros((relative.shape[0], LANES - ROT), f32)
        tables.append(
            (
                jnp.concatenate([cosine, cosine, rest + 1.0], axis=-1),
                jnp.concatenate([-sine, none, rest], axis=-1),
                jnp.concatenate([none, sine, rest], axis=-1),
            )
        )
    return relative, tables


def turn(values, cosine, ahead, behind, sign):
    half = ROT // 2
    lead = values[:, :LANES]
    turned = pltpu.roll(lead, LANES - half, 1) * ahead + pltpu.roll(lead, half, 1) * behind
    return jnp.concatenate([lead * cosine + sign * turned, values[:, LANES:]], axis=1)


def project_kernel(heads, wide, slot, std, wq, bq, wi, bi, cosine, ahead, behind, *rest):
    qkv_out, std_out, act_out, dg_out = rest[-4:]
    step = pl.program_id(0)

    @pl.when(step == 0)
    def _():
        std_out[0] = std[...]

    @pl.when(step < heads)
    def _():
        size = wq.shape[1] // 3
        for part in range(3):
            columns = slice(part * size, (part + 1) * size)
            z = dot(std[...], wq[:, columns]) + bq[:, columns]
            if part < 2:
                z = turn(z, cosine[...], ahead[...], behind[...], 1.0)
            qkv_out[0, :, columns] = z.astype(bf16)

    @pl.when(step >= heads)
    def _():
        for at in range(0, wide, 256):
            columns = slice(at, at + 256)
            h = dot(std[...], wi[:, columns]) + bi[:, columns]
            phi = 0.5 + 0.5 * lax.erf(h * (0.5**0.5))
            density = jnp.exp(h * h * -0.5) * 0.3989422804014327
            act_out[0, :, columns] = (h * phi).astype(bf16)
            dg_out[0, :, columns] = (phi + h * density).astype(bf16)


def stacked_outputs(shapes, buffers, first_input):
    out_shape = [jax.ShapeDtypeStruct(s, d) for s, d in shapes]
    if buffers is None:
        return out_shape, [], [], {}
    aliases = {first_input + k: k for k in range(len(buffers))}
    return out_shape, list(buffers), [pl.BlockSpec(memory_space=pl.ANY)] * len(buffers), aliases


def params():
    return pltpu.CompilerParams(vmem_limit_bytes=VMEM_LIMIT)


def project(slot, std, wq, bq, wi, bi, table, slots, buffers):
    rows, width = std.shape
    heads = bq.shape[1] // 768
    head_cols = wq.shape[1] // heads
    units = wi.shape[1]
    wide = min(512, units)
    shapes = [
        ((slots, rows, wq.shape[1]), bf16),
        ((slots, rows, width), bf16),
        ((slots, rows, units), bf16),
        ((slots, rows, units), bf16),
    ]
    out_shape, extra, extra_specs, aliases = stacked_outputs(shapes, buffers, 9)
    head_of = lambda i, s: (0, jnp.minimum(i, heads - 1))
    unit_of = lambda i, s: (0, jnp.maximum(i - heads, 0))
    whole = lambda i, s: (0, 0)
    return pl.pallas_call(
        partial(project_kernel, heads, wide),
        out_shape=out_shape,
        grid_spec=pltpu.PrefetchScalarGridSpec(
            num_scalar_prefetch=1,
            grid=(heads + units // wide,),
            in_specs=[
                pl.BlockSpec((rows, width), whole),
                pl.BlockSpec((width, head_cols), head_of),
                pl.BlockSpec((1, head_cols), head_of),
                pl.BlockSpec((width, wide), unit_of),
                pl.BlockSpec((1, wide), unit_of),
                pl.BlockSpec((rows, LANES), whole),
                pl.BlockSpec((rows, LANES), whole),
                pl.BlockSpec((rows, LANES), whole),
            ]
            + extra_specs,
            out_specs=[
                pl.BlockSpec((1, rows, head_cols), lambda i, s: (s[0], 0, jnp.minimum(i, heads - 1))),
                pl.BlockSpec((1, rows, width), lambda i, s: (s[0], 0, 0)),
                pl.BlockSpec((1, rows, wide), lambda i, s: (s[0], 0, jnp.maximum(i - heads, 0))),
                pl.BlockSpec((1, rows, wide), lambda i, s: (s[0], 0, jnp.maximum(i - heads, 0))),
            ],
        ),
        input_output_aliases=aliases,
        compiler_params=params(),
        cost_estimate=pl.CostEstimate(
            flops=2 * rows * width * (wq.shape[1] + units),
            bytes_accessed=2 * width * (wq.shape[1] + units) + 8 * rows * width,
            transcendentals=2 * rows * units,
        ),
        name="project",
    )(slot, std, wq, bq, wi, bi, *table, *extra)


def attend_kernel(second, slot, *refs):
    if second:
        q, k, v, kp, vp, pq, pk = refs[:7]
    else:
        q, k, v, pq, pk = refs[:5]
    ctx_out, lse_out = refs[-2:]
    scale = q.shape[-1] ** -0.5
    s = dot(q[0], k[0], NT) * scale
    s = jnp.where(pq[...] >= pk[...], s, masked_score)
    peak = jnp.max(s, axis=-1, keepdims=True)
    if second:
        sp = dot(q[0], kp[0], NT) * scale
        peak = jnp.maximum(peak, jnp.max(sp, axis=-1, keepdims=True))
    p = jnp.exp(s - peak)
    total = jnp.sum(p, axis=-1, keepdims=True)
    if second:
        pp = jnp.exp(sp - peak)
        total = total + jnp.sum(pp, axis=-1, keepdims=True)
    share = 1.0 / total
    ctx = dot((p * share).astype(bf16), v[0])
    if second:
        ctx = ctx + dot((pp * share).astype(bf16), vp[0])
    ctx_out[0] = ctx.astype(bf16)
    lse_out[0] = jnp.broadcast_to(peak + jnp.log(total), lse_out.shape[1:])


def head_block(rows, part, back, size):
    return pl.BlockSpec((1, rows, size), lambda h, s: (s[0] - back, 0, 3 * h + part))


def attend(slot, qkv, places_q, places_k, heads, second, buffers):
    slots, rows, columns = qkv.shape
    size = columns // (3 * heads)
    shapes = [((slots, rows, heads * size), bf16), ((slots, rows, heads * LANES), f32)]
    count = 5 if second else 3
    out_shape, extra, extra_specs, aliases = stacked_outputs(shapes, buffers, count + 3)
    whole = lambda h, s: (0, 0)
    specs = [head_block(rows, part, 0, size) for part in range(3)]
    if second:
        specs += [head_block(rows, part, 1, size) for part in (1, 2)]
    keys = rows * (2 if second else 1)
    return pl.pallas_call(
        partial(attend_kernel, second),
        out_shape=out_shape,
        grid_spec=pltpu.PrefetchScalarGridSpec(
            num_scalar_prefetch=1,
            grid=(heads,),
            in_specs=specs + [pl.BlockSpec((rows, 1), whole), pl.BlockSpec((1, rows), whole)] + extra_specs,
            out_specs=[
                pl.BlockSpec((1, rows, size), lambda h, s: (s[0], 0, h)),
                pl.BlockSpec((1, rows, LANES), lambda h, s: (s[0], 0, h)),
            ],
        ),
        input_output_aliases=aliases,
        compiler_params=params(),
        cost_estimate=pl.CostEstimate(
            flops=4 * heads * rows * keys * size * 2,
            bytes_accessed=2 * rows * columns,
            transcendentals=heads * rows * keys,
        ),
        name="attend",
    )(slot, *([qkv] * count), places_q, places_k, *extra)


def combine_kernel(slot, a, b, wa, wb, out):
    out[...] = (dot(a[0], wa[...]) + dot(b[0], wb[...])).astype(bf16)


def combine(slot, a, b, wa, wb):
    rows = a.shape[1]
    width = wa.shape[1]
    wide = min(512, width)
    weight_specs = [pl.BlockSpec((w.shape[0], wide), lambda i, s: (0, i)) for w in (wa, wb)]
    return pl.pallas_call(
        combine_kernel,
        out_shape=jax.ShapeDtypeStruct((rows, width), bf16),
        grid_spec=pltpu.PrefetchScalarGridSpec(
            num_scalar_prefetch=1,
            grid=(width // wide,),
            in_specs=[
                pl.BlockSpec((1, rows, a.shape[2]), lambda i, s: (s[0], 0, 0)),
                pl.BlockSpec((1, rows, b.shape[2]), lambda i, s: (s[0], 0, 0)),
            ]
            + weight_specs,
            out_specs=pl.BlockSpec((rows, wide), lambda i, s: (0, i)),
        ),
        compiler_params=params(),
        cost_estimate=pl.CostEstimate(
            flops=2 * rows * width * (a.shape[2] + b.shape[2]),
            bytes_accessed=2 * width * (a.shape[2] + b.shape[2]) + 4 * rows * width,
            transcendentals=0,
        ),
        name="combine",
    )(slot, a, b, wa, wb)


def merge_kernel(slot, a, b, wa, wb, gains, std, out, vectors):
    one = dot(a[0], wa[...], NT)
    two = dot(b[0], wb[...], NT)
    out[...] = (one * gains[0] + two * gains[1]).astype(bf16)
    standard = std[0].astype(f32)
    rows = (one * standard, one, two * standard, two)
    vectors[...] = jnp.concatenate([jnp.sum(v, axis=0, keepdims=True) for v in rows])


def merge(slot, a, b, wa, wb, gains, std):
    rows, width = std.shape[1:]
    wide = min(512, width)
    return pl.pallas_call(
        merge_kernel,
        out_shape=[jax.ShapeDtypeStruct((rows, width), bf16), jax.ShapeDtypeStruct((4, width), f32)],
        grid_spec=pltpu.PrefetchScalarGridSpec(
            num_scalar_prefetch=1,
            grid=(width // wide,),
            in_specs=[
                pl.BlockSpec((1, rows, a.shape[2]), lambda i, s: (s[0], 0, 0)),
                pl.BlockSpec((1, rows, b.shape[2]), lambda i, s: (s[0], 0, 0)),
                pl.BlockSpec((wide, wa.shape[1]), lambda i, s: (i, 0)),
                pl.BlockSpec((wide, wb.shape[1]), lambda i, s: (i, 0)),
                pl.BlockSpec((2, 1, wide), lambda i, s: (0, 0, i)),
                pl.BlockSpec((1, rows, wide), lambda i, s: (s[0], 0, i)),
            ],
            out_specs=[
                pl.BlockSpec((rows, wide), lambda i, s: (0, i)),
                pl.BlockSpec((4, wide), lambda i, s: (0, i)),
            ],
        ),
        compiler_params=params(),
        cost_estimate=pl.CostEstimate(
            flops=2 * rows * width * (a.shape[2] + b.shape[2]),
            bytes_accessed=2 * width * (a.shape[2] + b.shape[2]) + 6 * rows * width,
            transcendentals=0,
        ),
        name="merge",
    )(slot, a, b, wa, wb, gains, std)


def spread_kernel(slot, gy, wo, wd, dg, *rest):
    dctx_out, gy_out, dh_out = rest[-3:]
    step = pl.program_id(0)

    @pl.when(step == 0)
    def _():
        gy_out[0] = gy[...]
        dctx_out[...] = dot(gy[...], wo[...], NT).astype(bf16)

    @pl.when(step > 0)
    def _():
        for at in range(0, wd.shape[0], 256):
            part = slice(at, at + 256)
            dh_out[0, :, part] = (dot(gy[...], wd[part, :], NT) * dg[0, :, part].astype(f32)).astype(bf16)


def spread(slot, gy, wo, wd, dg, buffers):
    rows, width = gy.shape
    slots = dg.shape[0]
    units = wd.shape[0]
    wide = min(512, units)
    shapes = [
        ((rows, wo.shape[0]), bf16),
        ((slots, rows, width), bf16),
        ((slots, rows, units), bf16),
    ]
    out_shape = [jax.ShapeDtypeStruct(s, d) for s, d in shapes]
    extra, extra_specs, aliases = [], [], {}
    if buffers is not None:
        extra = list(buffers)
        extra_specs = [pl.BlockSpec(memory_space=pl.ANY)] * 2
        aliases = {5: 1, 6: 2}
    whole = lambda i, s: (0, 0)
    unit_of = lambda i, s: (s[0], 0, jnp.maximum(i - 1, 0))
    return pl.pallas_call(
        spread_kernel,
        out_shape=out_shape,
        grid_spec=pltpu.PrefetchScalarGridSpec(
            num_scalar_prefetch=1,
            grid=(1 + units // wide,),
            in_specs=[
                pl.BlockSpec((rows, width), whole),
                pl.BlockSpec(wo.shape, whole),
                pl.BlockSpec((wide, width), lambda i, s: (jnp.maximum(i - 1, 0), 0)),
                pl.BlockSpec((1, rows, wide), unit_of),
            ]
            + extra_specs,
            out_specs=[
                pl.BlockSpec((rows, wo.shape[0]), whole),
                pl.BlockSpec((1, rows, width), lambda i, s: (s[0], 0, 0)),
                pl.BlockSpec((1, rows, wide), unit_of),
            ],
        ),
        input_output_aliases=aliases,
        compiler_params=params(),
        cost_estimate=pl.CostEstimate(
            flops=2 * rows * width * (units + wo.shape[0]),
            bytes_accessed=2 * width * (units + wo.shape[0]) + 8 * rows * width,
            transcendentals=0,
        ),
        name="spread",
    )(slot, gy, wo, wd, dg, *extra)


def attend_back_kernel(second, slot, *refs):
    if second:
        q, k, v, dctx, ctx, lse, pq, pk, cosine, ahead, behind, kp, vp = refs[:13]
        out, dkp_out, dvp_out = refs[-3:]
    else:
        q, k, v, dctx, ctx, lse, pq, pk, cosine, ahead, behind, dk_in, dv_in = refs[:13]
        out = refs[-1]
    size = q.shape[-1]
    scale = size**-0.5
    logsum = lse[0][:, :1]
    delta = jnp.sum(dctx[...].astype(f32) * ctx[0].astype(f32), axis=-1, keepdims=True)

    def pieces(k, v, masked):
        s = dot(q[0], k[0], NT) * scale
        if masked:
            s = jnp.where(pq[...] >= pk[...], s, masked_score)
        p = jnp.exp(s - logsum)
        d_chance = dot(dctx[...], v[0], NT)
        d_scores = (p * (d_chance - delta)).astype(bf16)
        dq = dot(d_scores, k[0])
        dk = dot(d_scores, q[0], TN)
        dv = dot(p.astype(bf16), dctx[...], TN)
        return dq, dk, dv

    dq, dk, dv = pieces(k, v, True)
    if second:
        dq_more, dkp, dvp = pieces(kp, vp, False)
        dq = dq + dq_more
        dkp_out[...] = dkp
        dvp_out[...] = dvp
    else:
        dk = dk + dk_in[...]
        dv = dv + dv_in[...]
    table = (cosine[...], ahead[...], behind[...])
    out[0, :, 0:size] = turn(dq * scale, *table, -1.0).astype(bf16)
    out[0, :, size : 2 * size] = turn(dk * scale, *table, -1.0).astype(bf16)
    out[0, :, 2 * size :] = dv.astype(bf16)


def attend_back(slot, qkv, dctx, ctx, lse, places_q, places_k, table, heads, carry, buffer):
    slots, rows, columns = qkv.shape
    size = columns // (3 * heads)
    second = carry is None
    whole = lambda h, s: (0, 0)
    specs = [head_block(rows, part, 0, size) for part in range(3)]
    specs += [
        pl.BlockSpec((rows, size), lambda h, s: (0, h)),
        pl.BlockSpec((1, rows, size), lambda h, s: (s[0], 0, h)),
        pl.BlockSpec((1, rows, LANES), lambda h, s: (s[0], 0, h)),
        pl.BlockSpec((rows, 1), whole),
        pl.BlockSpec((1, rows), whole),
        pl.BlockSpec((rows, LANES), whole),
        pl.BlockSpec((rows, LANES), whole),
        pl.BlockSpec((rows, LANES), whole),
    ]
    out_shape = [jax.ShapeDtypeStruct((slots, rows, columns), bf16)]
    out_specs = [pl.BlockSpec((1, rows, 3 * size), lambda h, s: (s[0], 0, h))]
    column_spec = pl.BlockSpec((rows, size), lambda h, s: (0, h))
    if second:
        specs += [head_block(rows, part, 1, size) for part in (1, 2)]
        more = (qkv, qkv)
        out_shape += [jax.ShapeDtypeStruct((rows, heads * size), f32)] * 2
        out_specs += [column_spec] * 2
    else:
        specs += [column_spec] * 2
        more = carry
    extra, extra_specs, aliases = [], [], {}
    if buffer is not None:
        extra, extra_specs, aliases = [buffer], [pl.BlockSpec(memory_space=pl.ANY)], {14: 0}
    keys = rows * (2 if second else 1)
    return pl.pallas_call(
        partial(attend_back_kernel, second),
        out_shape=out_shape,
        grid_spec=pltpu.PrefetchScalarGridSpec(
            num_scalar_prefetch=1, grid=(heads,), in_specs=specs + extra_specs, out_specs=out_specs
        ),
        input_output_aliases=aliases,
        compiler_params=params(),
        cost_estimate=pl.CostEstimate(
            flops=10 * heads * rows * keys * size * 2,
            bytes_accessed=6 * rows * columns,
            transcendentals=heads * rows * keys,
        ),
        name="attend_back",
    )(slot, qkv, qkv, qkv, dctx, ctx, lse, places_q, places_k, *table, *more, *extra)


CHUNK = 256
PIECE = 64
SKEW = 2


def reduce_kernel(
    plan, act, ctx, dproj, dhid, gy, std, gains, biases, sums, small, out, small_out, from_left, from_right,
    rhs, raw, lhs, own, inbox, outbox, stage, small_in,
    rhs_sem, raw_sem, right_sem, left_sem, final_sem, load_sem, sent, stage_left, stage_right, out_sem,
    small_sent, small_got,
):
    bounds, tasks, count, piece, skew, ring = plan
    sources = (act, ctx, dproj, dhid)
    total_chunks = bounds[-1]
    per_chunk = CHUNK // piece
    pieces = total_chunks * per_chunk
    width = gy.shape[-1]
    tile = width // per_chunk
    block = raw.shape[2]
    z = lax.axis_index("ctx")
    last = count - 1
    root = count // 2
    turn_at = max(root, last - root)
    low, high, middle = z < root, z > root, z == root

    barrier = pltpu.get_barrier_semaphore()
    for shift in range(1, count):
        pl.semaphore_signal(
            barrier,
            inc=1,
            device_id={"ctx": lax.rem(z + shift, count)},
            device_id_type=pl.DeviceIdType.MESH,
        )

    def small_copy(source, target):
        return pltpu.make_async_remote_copy(
            src_ref=small,
            dst_ref=small_in.at[source],
            send_sem=small_sent.at[target],
            recv_sem=small_got.at[source],
            device_id={"ctx": target},
            device_id_type=pl.DeviceIdType.MESH,
        )

    def rhs_copy(k):
        return pltpu.make_async_copy((gy, std)[k].at[pl.ds(0, tasks)], rhs.at[k], rhs_sem.at[k])

    def each_source(chunk, act_on):
        for g, source in enumerate(sources):

            @pl.when((chunk >= bounds[g]) & (chunk < bounds[g + 1]))
            def _(g=g, source=source):
                column = pl.multiple_of((chunk - bounds[g]) * CHUNK, CHUNK)
                act_on(
                    pltpu.make_async_copy(
                        source.at[pl.ds(0, tasks), :, pl.ds(column, CHUNK)],
                        raw.at[chunk % 2],
                        raw_sem.at[chunk % 2],
                    )
                )

    def take(chunk):
        each_source(chunk, lambda copy: copy.wait())
        for k in range(tasks):
            lhs[:, k * block : (k + 1) * block] = raw[chunk % 2, k].T
        each_source(chunk + 1, lambda copy: copy.start())

    def multiply(chunk, part):
        second = jnp.where(chunk >= bounds[2], 1, 0)
        group = second + jnp.where(chunk >= bounds[3], 1, 0)
        columns = pl.ds(pl.multiple_of(part * tile, tile), tile)
        value = dot(lhs[:, :block], rhs[second, 0, :, columns])
        for k in range(1, tasks):
            value = value + dot(lhs[:, k * block : (k + 1) * block], rhs[second, k, :, columns])
        row = pl.multiple_of(chunk * CHUNK, CHUNK)
        value = value * gains[group, :, columns] + sums[pl.ds(row, CHUNK), :] * biases[group, :, columns]
        own[chunk % ring, :, columns] = value.astype(bf16)

    def rows_of(index):
        return pl.ds(pl.multiple_of(index * piece, piece), piece)

    def own_piece(index):
        inner = pl.multiple_of((index % per_chunk) * piece, piece)
        return own[(index // per_chunk) % ring, pl.ds(inner, piece), :]

    def remote(source, target_rows, send_sem, recv_sem, target):
        return pltpu.make_async_remote_copy(
            src_ref=source,
            dst_ref=target_rows,
            send_sem=send_sem,
            recv_sem=recv_sem,
            device_id={"ctx": target},
            device_id_type=pl.DeviceIdType.MESH,
        )

    def inward(index, right):
        landing, arrived, target = (from_left, right_sem, z + 1) if right else (from_right, left_sem, z - 1)
        return remote(
            outbox.at[index % 2], landing.at[rows_of(index)], sent.at[index % 2], arrived.at[index], target
        )

    def announce(index, right):
        return remote(
            stage.at[index % 2],
            out.at[rows_of(index)],
            (stage_right if right else stage_left).at[index % 2],
            final_sem.at[index],
            z + 1 if right else z - 1,
        )

    def onward(index, right):
        return remote(
            out.at[rows_of(index)],
            out.at[rows_of(index)],
            sent.at[2 + index % 2],
            final_sem.at[index],
            z + 1 if right else z - 1,
        )

    def load(index, right):
        landing = from_left if right else from_right
        return pltpu.make_async_copy(
            landing.at[rows_of(index)], inbox.at[0 if right else 1], load_sem.at[0 if right else 1]
        )

    def valid(index):
        return (index >= 0) & (index < pieces)

    def side(step, right):
        mine = low if right else high
        hops = z if right else last - z
        inner = step - hops * skew
        comes = hops > 0

        @pl.when(mine & valid(inner) & comes)
        def _():
            inward(inner, right).wait_recv()
            load(inner, right).start()

        @pl.when(mine & valid(inner))
        def _():
            @pl.when(inner >= 2)
            def _():
                inward(inner - 2, right).wait_send()

            @pl.when(comes)
            def _():
                load(inner, right).wait()
                value = own_piece(inner).astype(f32) + inbox[0 if right else 1].astype(f32)
                outbox[inner % 2] = value.astype(bf16)

            @pl.when(jnp.logical_not(comes))
            def _():
                outbox[inner % 2] = own_piece(inner)

            inward(inner, right).start()

        away = root - z if right else z - root
        outer = step - (turn_at + away) * skew

        @pl.when(mine & valid(outer))
        def _():
            onward(outer, not right).wait_recv()

            @pl.when(comes)
            def _():
                @pl.when(outer >= 2)
                def _():
                    onward(outer - 2, not right).wait_send()

                onward(outer, not right).start()

    def out_copy(index):
        return pltpu.make_async_copy(stage.at[index % 2], out.at[rows_of(index)], out_sem.at[index % 2])

    def stage_done(index):
        out_copy(index).wait()
        announce(index, False).wait_send()
        if root < last:
            announce(index, True).wait_send()

    def centre(step):
        index = step - turn_at * skew

        @pl.when(middle & valid(index))
        def _():
            inward(index, True).wait_recv()
            load(index, True).start()
            if root < last:
                inward(index, False).wait_recv()
                load(index, False).start()

            @pl.when(index >= 2)
            def _():
                stage_done(index - 2)

            load(index, True).wait()
            value = own_piece(index).astype(f32) + inbox[0].astype(f32)
            if root < last:
                load(index, False).wait()
                value = value + inbox[1].astype(f32)
            stage[index % 2] = value.astype(bf16)
            announce(index, False).start()
            if root < last:
                announce(index, True).start()
            out_copy(index).start()

    rhs_copy(0).start()
    each_source(0, lambda copy: copy.start())
    rhs_copy(1).start()
    take(0)
    rhs_copy(0).wait()

    @pl.loop(0, per_chunk)
    def _(part):
        multiply(0, part)

    pl.semaphore_wait(barrier, count - 1)
    small_in[z] = small[...]
    for shift in range(1, count):
        small_copy(z, lax.rem(z + shift, count)).start()

    @pl.loop(0, pieces + (turn_at + max(root, last - root)) * skew)
    def _(step):
        side(step, True)
        side(step, False)
        centre(step)
        chunk, part = step // per_chunk + 1, step % per_chunk

        @pl.when(chunk < total_chunks)
        def _():
            @pl.when(part == 0)
            def _():
                take(chunk)

                @pl.when(chunk == bounds[2])
                def _():
                    rhs_copy(1).wait()

            multiply(chunk, part)

    for shift in range(1, count):
        other = lax.rem(z + shift, count)
        small_copy(z, other).wait_send()
        small_copy(other, other).wait_recv()
    value = small_in[0]
    for k in range(1, count):
        value = value + small_in[k]
    small_out[...] = value
    for back in (2, 1):
        for right in (True, False):

            @pl.when(low if right else high)
            def _(right=right, back=back):
                inward(pieces - back, right).wait_send()

                @pl.when((z > 0) & (z < last))
                def _():
                    onward(pieces - back, not right).wait_send()

        @pl.when(middle)
        def _(back=back):
            stage_done(pieces - back)


def reduce_gradients(act, ctx, dproj, dhid, gy, std, gains, biases, sums, small, tasks):
    count = lax.axis_size("ctx")
    block, width = gy.shape[1:]
    bounds = [0]
    for source in (act, ctx, dproj, dhid):
        bounds.append(bounds[-1] + source.shape[2] // CHUNK)
    total = bounds[-1] * CHUNK
    pieces = total // PIECE
    ring = count // 2 * SKEW // (CHUNK // PIECE) + 3
    plan = (tuple(bounds), tasks, count, PIECE, SKEW, ring)
    anywhere = pl.BlockSpec(memory_space=pl.ANY)
    vmem = pl.BlockSpec(memory_space=pltpu.VMEM)
    result = jax.ShapeDtypeStruct((total, width), bf16)
    out, small_out, _, _ = pl.pallas_call(
        partial(reduce_kernel, plan),
        out_shape=[result, jax.ShapeDtypeStruct(small.shape, f32), result, result],
        in_specs=[anywhere] * 6 + [vmem] * 4,
        out_specs=[anywhere, vmem, anywhere, anywhere],
        scratch_shapes=[
            pltpu.VMEM((2, tasks, block, width), bf16),
            pltpu.VMEM((2, tasks, block, CHUNK), bf16),
            pltpu.VMEM((CHUNK, tasks * block), bf16),
            pltpu.VMEM((ring, CHUNK, width), bf16),
            pltpu.VMEM((2, PIECE, width), bf16),
            pltpu.VMEM((2, PIECE, width), bf16),
            pltpu.VMEM((2, PIECE, width), bf16),
            pltpu.VMEM((count,) + small.shape, f32),
            pltpu.SemaphoreType.DMA((2,)),
            pltpu.SemaphoreType.DMA((2,)),
            pltpu.SemaphoreType.DMA((pieces,)),
            pltpu.SemaphoreType.DMA((pieces,)),
            pltpu.SemaphoreType.DMA((pieces,)),
            pltpu.SemaphoreType.DMA((2,)),
            pltpu.SemaphoreType.DMA((4,)),
            pltpu.SemaphoreType.DMA((2,)),
            pltpu.SemaphoreType.DMA((2,)),
            pltpu.SemaphoreType.DMA((2,)),
            pltpu.SemaphoreType.DMA((count,)),
            pltpu.SemaphoreType.DMA((count,)),
        ],
        compiler_params=pltpu.CompilerParams(
            collective_id=7, has_side_effects=True, vmem_limit_bytes=60 * 1024 * 1024
        ),
        cost_estimate=pl.CostEstimate(
            flops=2 * total * width * tasks * block,
            bytes_accessed=8 * total * width,
            transcendentals=0,
        ),
        name="reduce_gradients",
    )(act, ctx, dproj, dhid, gy, std, gains, biases, sums, small)
    return out, small_out


def exchange(blocks, axis):
    count = blocks.shape[0]
    me = lax.axis_index(axis)
    got = [lax.dynamic_index_in_dim(blocks, me, 0, keepdims=False)]
    for shift in range(1, count):
        piece = lax.dynamic_index_in_dim(blocks, (me + shift) % count, 0, keepdims=False)
        got.append(lax.ppermute(piece, axis, [(k, (k + shift) % count) for k in range(count)]))
    ring = jnp.stack(got[::-1] + got[::-1])
    return lax.dynamic_slice_in_dim(ring, (count - 1 - me) % count, count, 0)


def swap_cores(v, tensor):
    return lax.ppermute(v, "tensor", [(k, k ^ 1) for k in range(tensor)])


def shift_chips(v, tensor, shift):
    return lax.ppermute(v, "tensor", [(k, (k + 2 * shift) % tensor) for k in range(tensor)])


def gather_rows(own, tensor):
    chips = tensor // 2
    me = lax.axis_index("tensor")
    chip, core = me // 2, me % 2
    got = [own] + [shift_chips(own, tensor, shift) for shift in range(1, chips)]
    if chips == 2:
        mine = jnp.stack([jnp.where(chip == 0, got[0], got[1]), jnp.where(chip == 0, got[1], got[0])])
    else:
        ring = jnp.stack(got[::-1] + got[::-1])
        mine = lax.dynamic_slice_in_dim(ring, (chips - 1 - chip) % chips, chips, 0)
    theirs = swap_cores(mine, tensor)
    both = jnp.stack([jnp.where(core == 0, mine, theirs), jnp.where(core == 0, theirs, mine)], axis=1)
    return both.reshape(tensor * own.shape[0], own.shape[1])


def scatter_sum(partial_rows, tensor):
    chips = tensor // 2
    me = lax.axis_index("tensor")
    chip, core = me // 2, me % 2
    width = partial_rows.shape[1]
    parts = partial_rows.reshape(chips, 2, -1, width)
    mine = lax.dynamic_index_in_dim(parts, core, 1, keepdims=False)
    theirs = swap_cores(lax.dynamic_index_in_dim(parts, 1 - core, 1, keepdims=False), tensor)
    total = mine.astype(f32) + theirs.astype(f32)
    low = total.astype(bf16)
    own = lax.dynamic_index_in_dim(total, chip, 0, keepdims=False)
    for shift in range(1, chips):
        piece = lax.dynamic_index_in_dim(low, (chip + shift) % chips, 0, keepdims=False)
        own = own + shift_chips(piece, tensor, shift).astype(f32)
    return own


def body(
    inputs,
    out_grads,
    norm1_gain,
    norm1_bias,
    norm2_gain,
    norm2_bias,
    w_qkv,
    b_qkv,
    w_out,
    b_out,
    input_projection,
    input_bias_vector,
    down_projection,
    b_down,
):
    ctx_count = lax.axis_size("ctx")
    tensor = lax.axis_size("tensor")
    micro, _, rows, seqs, width = inputs.shape
    heads = w_qkv.shape[2]
    head_cols = w_qkv.shape[3]
    first = lax.axis_index("section") == 0
    per_device = micro * seqs // ctx_count
    blocks = ctx_count // 2
    own_rows = blocks * rows
    tasks = 2 * per_device
    slots = tasks + 1

    chosen = jnp.where(first, inputs[:, 0], out_grads[:, 0])
    chosen = chosen.transpose(0, 2, 1, 3).reshape(per_device, ctx_count, rows, width)
    own_chosen = []
    for j in range(per_device):
        moved = exchange(chosen[j], "ctx").reshape(2, own_rows, width)
        own_chosen += [moved[0], moved[1]]

    wq = w_qkv[0].reshape(width, heads * head_cols)
    wi = input_projection[0]
    wo = w_out[0].reshape(-1, width)
    wd = down_projection[0]
    gain_one, bias_one, gain_two, bias_two = norm1_gain[0], norm1_bias[0], norm2_gain[0], norm2_bias[0]
    wq_scaled = (wq.astype(f32) * gain_one[:, None]).astype(bf16)
    wi_scaled = (wi.astype(f32) * gain_two[:, None]).astype(bf16)
    bq = b_qkv[0].reshape(1, -1) + jnp.sum(wq.astype(f32) * bias_one[:, None], axis=0, keepdims=True)
    bi = input_bias_vector + jnp.sum(wi.astype(f32) * bias_two[:, None], axis=0, keepdims=True)
    out_bias = (b_out[0] + b_down[0])[None]

    relative, tables = position_tables(None, blocks, rows, tensor)
    places_q, places_k = relative[:, None], relative[None, :]

    arrived = {}
    kept = []
    produced = []
    forward_buffers = attend_buffers = None
    for step in range(tasks + LAG):
        x_own = own_chosen[min(step, tasks - 1)]
        if step >= LAG:
            x_own = jnp.where(first, x_own, arrived[step])
        kept.append(x_own)
        part = step % 2
        slot_first = step if step < tasks else tasks
        slot_second = step - LAG if step >= LAG else tasks
        slot = jnp.where(first, slot_first, slot_second).astype(jnp.int32).reshape(1)
        std = gather_rows(standardize(x_own)[0].astype(bf16), tensor)
        forward_buffers = project(
            slot, std, wq_scaled, bq, wi_scaled, bi, tables[part], slots, forward_buffers
        )
        attend_buffers = attend(
            slot, forward_buffers[0], places_q, places_k, heads, part == 1, attend_buffers
        )
        summed = scatter_sum(combine(slot, attend_buffers[0], forward_buffers[2], wo, wd), tensor)
        result = (x_own.astype(f32) + summed + out_bias).astype(bf16)
        produced.append(result)
        if step < tasks:
            arrived[step + LAG] = lax.ppermute(result, "section", [(0, 1)])
    qkv, std_all, act_all, dg_all = forward_buffers
    ctx_all, lse_all = attend_buffers

    back = {}
    back_list = []
    spread_buffers = None
    dproj_all = None
    carry = None
    vectors = jnp.zeros((5, width), f32)
    gain_pair = jnp.stack([gain_one, gain_two])[:, None]
    for step in range(tasks + LAG):
        part = 1 - step % 2
        task_first = max(step - LAG, 0)
        task_second = min(step, tasks - 1)
        slot_of = lambda task: (task // 2) * 2 + 1 - task % 2
        near, far = slot_of(task_first), slot_of(task_second)
        slot_first = near if step >= LAG else tasks
        slot_second = far if step < tasks else tasks
        slot = jnp.where(first, slot_first, slot_second).astype(jnp.int32).reshape(1)
        gy_own = own_chosen[far]
        if step >= LAG:
            gy_own = jnp.where(first, back[step], gy_own)
        gy = gather_rows(gy_own, tensor)
        dctx, *spread_buffers = spread(slot, gy, wo, wd, dg_all, spread_buffers)
        made = attend_back(
            slot,
            qkv,
            dctx,
            ctx_all,
            lse_all,
            places_q,
            places_k,
            tables[part],
            heads,
            None if part == 1 else carry,
            dproj_all,
        )
        dproj_all = made[0]
        carry = tuple(made[1:]) if part == 1 else None
        e_part, vector_part = merge(slot, dproj_all, spread_buffers[1], wq, wi, gain_pair, std_all)
        e = scatter_sum(e_part, tensor)
        x_own = jnp.where(first, kept[near], kept[far + LAG])
        standard, inverse = standardize(x_own)
        gy_wide = gy_own.astype(f32)
        d_input = gy_wide + inverse * (
            e
            - jnp.mean(e, axis=-1, keepdims=True)
            - standard * jnp.mean(e * standard, axis=-1, keepdims=True)
        )
        back_list.append(d_input)
        valid = jnp.where(first, step >= LAG, step < tasks)
        vector_part = jnp.concatenate([vector_part, jnp.sum(gy_wide, axis=0, keepdims=True)])
        vectors = vectors + jnp.where(valid, vector_part, 0.0)
        if step < tasks:
            back[step + LAG] = lax.ppermute(d_input.astype(bf16), "section", [(1, 0)])
    gy_all, dh_all = spread_buffers

    d_b_qkv = jnp.sum(dproj_all[:tasks], axis=(0, 1), dtype=f32)
    d_b_in = jnp.sum(dh_all[:tasks], axis=(0, 1), dtype=f32)
    units, inner = wd.shape[0], wo.shape[0]
    sums = jnp.concatenate([jnp.zeros((units + inner,), f32), d_b_qkv, d_b_in])[:, None]
    gains = jnp.stack([jnp.ones_like(gain_one), gain_one, gain_two])[:, None]
    biases = jnp.stack([jnp.zeros_like(bias_one), bias_one, bias_two])[:, None]
    mask = 1
    while mask < tensor:
        vectors = vectors + lax.ppermute(vectors, "tensor", [(k, k ^ mask) for k in range(tensor)])
        mask *= 2
    sides = jnp.concatenate([d_b_qkv, d_b_in])
    side_rows = -(-sides.shape[0] // width)
    small = jnp.zeros((-(-(5 + side_rows) // 8) * 8, width), f32)
    small = small.at[:5].set(vectors)
    small = small.at[5 : 5 + side_rows].set(
        jnp.pad(sides, (0, side_rows * width - sides.shape[0])).reshape(side_rows, width)
    )
    summed, small = reduce_gradients(
        act_all, ctx_all, dproj_all, dh_all, gy_all, std_all, gains, biases, sums, small, tasks
    )
    vectors = small[:5]
    sides = small[5 : 5 + side_rows].reshape(-1)
    d_b_qkv, d_b_in = sides[: d_b_qkv.shape[0]], sides[d_b_qkv.shape[0] : sides.shape[0]]
    d_b_in = d_b_in[: wi.shape[1]]
    d_w_down = summed[:units].astype(f32)
    d_w_out = summed[units : units + inner].astype(f32)
    summed = summed[units + inner :]
    d_w_qkv = summed[: wq.shape[1]].T.astype(f32)
    d_w_in = summed[wq.shape[1] :].T.astype(f32)

    def homeward(pieces):
        stacked = jnp.stack(pieces).reshape(per_device, ctx_count, rows, width)
        moved = exchange(stacked.transpose(1, 0, 2, 3), "ctx")
        moved = moved.transpose(1, 0, 2, 3).reshape(micro, seqs, rows, width)
        return moved.transpose(0, 2, 1, 3)[None, :, None]

    states = homeward([jnp.where(first, produced[k], produced[k + LAG]) for k in range(tasks)])
    order = [(k // 2) * 2 + 1 - k % 2 for k in range(tasks)]
    input_grads = homeward(
        [jnp.where(first, back_list[k + LAG], back_list[k]).astype(bf16) for k in order]
    ).astype(f32)
    return (
        states,
        input_grads,
        vectors[0][None],
        vectors[1][None],
        vectors[2][None],
        vectors[3][None],
        d_w_qkv.reshape(w_qkv.shape),
        d_b_qkv.reshape(b_qkv.shape),
        d_w_out.reshape(w_out.shape),
        vectors[4][None],
        d_w_in[None],
        d_b_in[None],
        d_w_down[None],
        vectors[4][None],
    )


def solution(mesh):
    return jax.shard_map(
        body,
        mesh=mesh,
        in_specs=(
            P(None, "ctx", "tensor", None, None),
            P(None, "ctx", "tensor", None, None),
            P("section", None),
            P("section", None),
            P("section", None),
            P("section", None),
            P("section", None, "tensor", None),
            P("section", "tensor", None),
            P("section", "tensor", None, None),
            P("section", None),
            P("section", None, "tensor"),
            P("section", "tensor"),
            P("section", "tensor", None),
            P("section", None),
        ),
        out_specs=(
            P("section", None, "ctx", "tensor", None, None),
            P("section", None, "ctx", "tensor", None, None),
            P("section", None),
            P("section", None),
            P("section", None),
            P("section", None),
            P("section", None, "tensor", None),
            P("section", "tensor", None),
            P("section", "tensor", None, None),
            P("section", None),
            P("section", None, "tensor"),
            P("section", "tensor"),
            P("section", "tensor", None),
            P("section", None),
        ),
        check_vma=False,
    )
```

```python
from functools import partial

import jax
import jax.numpy as jnp
from jax import lax
from jax.experimental import pallas as pl
from jax.experimental.pallas import tpu as pltpu
from jax.sharding import PartitionSpec as P

ROT = 64
LAG = 3
LANES = 128
epsilon = 1e-05
masked_score = -1e30
f32 = jnp.float32
bf16 = jnp.bfloat16
NT = (((1,), (1,)), ((), ()))
TN = (((0,), (0,)), ((), ()))
NN = (((1,), (0,)), ((), ()))
PASS_VMEM = 62 * 1024 * 1024


def dot(a, b, dims=NN):
    return lax.dot_general(a, b, dims, preferred_element_type=f32)


def standardize(rows):
    values = rows.astype(f32)
    average = jnp.mean(values, axis=-1, keepdims=True)
    centred = values - average
    inverse = lax.rsqrt(jnp.mean(centred * centred, axis=-1, keepdims=True) + epsilon)
    return centred * inverse, inverse


def position_tables(section_rows, blocks, rows, tensor):
    half = ROT // 2
    frequency = 1.0 / 10000.0 ** (jnp.arange(0, ROT, 2, dtype=f32) / ROT)
    t, c, i = jnp.meshgrid(
        jnp.arange(tensor), jnp.arange(blocks), jnp.arange(rows), indexing="ij"
    )
    relative = (c * (rows * tensor) + t * rows + i).reshape(-1).astype(jnp.int32)
    tables = []
    for part in range(2):
        places = (relative + part * blocks * rows * tensor).astype(f32)
        angles = places[:, None] * frequency[None, :]
        cosine, sine = jnp.cos(angles), jnp.sin(angles)
        none = jnp.zeros_like(sine)
        rest = jnp.zeros((relative.shape[0], LANES - ROT), f32)
        tables.append(
            (
                jnp.concatenate([cosine, cosine, rest + 1.0], axis=-1),
                jnp.concatenate([-sine, none, rest], axis=-1),
                jnp.concatenate([none, sine, rest], axis=-1),
            )
        )
    return relative, tables


def turn(values, cosine, ahead, behind, sign):
    half = ROT // 2
    lead = values[:, :LANES]
    turned = pltpu.roll(lead, LANES - half, 1) * ahead + pltpu.roll(lead, half, 1) * behind
    return jnp.concatenate([lead * cosine + sign * turned, values[:, LANES:]], axis=1)


class Moves:
    def __init__(self, plan, place, land, arrive, core_land, chip_land, own, theirs, low, handed, sems):
        self.tasks, self.chips, self.rows = plan
        self.place = place
        self.land, self.arrive, self.core_land, self.chip_land = land, arrive, core_land, chip_land
        self.own, self.theirs, self.low, self.handed = own, theirs, low, handed
        (
            self.got_chip, self.got_core, self.got_theirs, self.got_low, self.got_hand,
            self.put_chip, self.put_core, self.put_theirs, self.put_low, self.put_hand,
        ) = sems
        self.section = lax.axis_index("section")
        self.index = lax.axis_index("tensor")
        self.total = 2 * self.chips
        self.chip, self.core = self.index // 2, self.index % 2
        self.mate = self.chip * 2 + 1 - self.core

    def mate_on(self, shift):
        return lax.rem(self.index + 2 * shift, self.total)

    def part(self, member):
        return pl.ds(pl.multiple_of(member * self.rows, self.rows), self.rows)

    def remote(self, source, target, sent, arrived, **device):
        return pltpu.make_async_remote_copy(
            src_ref=source,
            dst_ref=target,
            send_sem=sent,
            recv_sem=arrived,
            device_id=device,
            device_id_type=pl.DeviceIdType.MESH,
        )

    def greet(self):
        barrier = pltpu.get_barrier_semaphore()
        peers = [{"section": 1 - self.section}, {"tensor": self.mate}]
        peers += [{"tensor": self.mate_on(shift)} for shift in range(1, self.chips)]
        for peer in peers:
            pl.semaphore_signal(barrier, inc=1, device_id=peer, device_id_type=pl.DeviceIdType.MESH)
        pl.semaphore_wait(barrier, len(peers))

    def gather_chip(self, task, shift, member=None):
        member = self.index if member is None else member
        return self.remote(
            self.own,
            self.land.at[self.place(task), self.part(member)],
            self.put_chip.at[shift - 1],
            self.got_chip.at[task, shift - 1],
            tensor=self.mate_on(shift),
        )

    def gather_chip_in(self, task, shift):
        return self.gather_chip(task, shift, lax.rem(self.index + self.total - 2 * shift, self.total))

    def gather_core(self, task, shift, member=None):
        if member is None:
            member = lax.rem(self.index + self.total - 2 * shift, self.total)
        target = self.land.at[self.place(task), self.part(member)]
        return self.remote(
            self.own if shift == 0 else target,
            target,
            self.put_core.at[shift],
            self.got_core.at[task, shift],
            tensor=self.mate,
        )

    def gather_core_in(self, task, shift):
        return self.gather_core(task, shift, lax.rem(self.mate + self.total - 2 * shift, self.total))

    def give_theirs(self, task):
        return self.remote(
            self.theirs, self.core_land.at[task], self.put_theirs, self.got_theirs.at[task], tensor=self.mate
        )

    def give_low(self, task, shift):
        return self.remote(
            self.low.at[lax.rem(self.chip + shift, self.chips)],
            self.chip_land.at[task, shift - 1],
            self.put_low.at[shift - 1],
            self.got_low.at[task, shift - 1],
            tensor=self.mate_on(shift),
        )

    def hand(self, task):
        return self.remote(
            self.handed, self.arrive.at[task], self.put_hand, self.got_hand.at[task], section=1 - self.section
        )


def reduce_first(moves, task, mine, core_in, load_sem):
    moves.give_theirs(task).wait_recv()
    load = pltpu.make_async_copy(moves.core_land.at[task], core_in, load_sem)
    load.start()

    @pl.when(task >= 1)
    def _():
        for shift in range(1, moves.chips):
            moves.give_low(task - 1, shift).wait_send()

    load.wait()
    for j in range(moves.chips):
        value = mine[j] + core_in[j].astype(f32)
        mine[j] = value
        moves.low[j] = value.astype(bf16)
    for shift in range(1, moves.chips):
        moves.give_low(task, shift).start()


def reduce_second(moves, task, mine, chip_in, load_sem):
    for shift in range(1, moves.chips):
        moves.give_low(task, shift).wait_recv()
    load = pltpu.make_async_copy(moves.chip_land.at[task], chip_in, load_sem)
    load.start()
    load.wait()
    value = mine[moves.chip]
    for shift in range(1, moves.chips):
        value = value + chip_in[shift - 1].astype(f32)
    return value


def gather_start(moves, task, keep_sem):
    pltpu.make_async_copy(
        moves.own, moves.land.at[moves.place(task), moves.part(moves.index)], keep_sem
    ).start()
    for shift in range(1, moves.chips):
        moves.gather_chip(task, shift).start()
    moves.gather_core(task, 0).start()


def gather_free(moves, task):
    for shift in range(1, moves.chips):
        moves.gather_chip(task, shift).wait_send()
    moves.gather_core(task, 0).wait_send()


def gather_pass(moves, task, keep_sem):
    pltpu.make_async_copy(
        moves.own, moves.land.at[moves.place(task), moves.part(moves.index)], keep_sem
    ).wait()
    for shift in range(1, moves.chips):
        moves.gather_chip_in(task, shift).wait_recv()

        @pl.when(task >= 1)
        def _():
            moves.gather_core(task - 1, shift).wait_send()

        moves.gather_core(task, shift).start()


def gather_wait(moves, task):
    for shift in range(moves.chips):
        moves.gather_core_in(task, shift).wait_recv()


def drain(moves, task):
    gather_free(moves, task)
    for shift in range(1, moves.chips):
        moves.gather_core(task, shift).wait_send()
        moves.give_low(task, shift).wait_send()
    moves.give_theirs(task).wait_send()


def when(condition):
    return pl.when(condition)


def forward_kernel(
    plan, xin, wq_all, wi_all, wo_all, wd_all, bq, bi, out_bias, cosine, ahead, behind, pq, pk,
    land, qkv_all, act_all, dg_all, ctx_all, lse_all, states, arrive, core_land, chip_land,
    wq, wi, wo, wd, std, qkv, act, dg, ctx, lse, kept, own, theirs, mine, core_in, low, chip_in, handed,
    weight_sem, load_sem, store_sem, keep_sem, state_sem, *sems,
):
    tasks, chips, rows, heads = plan
    size = wq.shape[1] // (3 * heads)
    moves = Moves(
        (tasks, chips, rows), lambda task: task, land, arrive, core_land, chip_land, own, theirs, low, handed, sems
    )
    first = moves.section == 0
    base = jnp.where(first, 0, LAG)

    weights = [
        pltpu.make_async_copy(a, b, weight_sem.at[k])
        for k, (a, b) in enumerate(((wq_all, wq), (wi_all, wi), (wo_all, wo), (wd_all, wd)))
    ]
    for copy in weights:
        copy.start()
    moves.greet()

    def valid(task):
        return (task >= 0) & (task < tasks)

    def store(k, task):
        return pltpu.make_async_copy(
            (qkv.at[task % 2], act, dg, ctx, lse)[k],
            (qkv_all, act_all, dg_all, ctx_all, lse_all)[k].at[task],
            store_sem.at[k],
        )

    def project(task):
        half = task % 2
        table = (cosine[half], ahead[half], behind[half])
        for h in range(heads):
            for k in range(3):
                columns = slice((3 * h + k) * size, (3 * h + k + 1) * size)
                z = dot(std[...], wq[:, columns]) + bq[:, columns]
                if k < 2:
                    z = turn(z, *table, 1.0)
                qkv[half, :, columns] = z.astype(bf16)

    def attend(task, second):
        half = 1 if second else 0
        scale = size**-0.5
        for h in range(heads):
            at = [slice((3 * h + k) * size, (3 * h + k + 1) * size) for k in range(3)]
            q = qkv[half, :, at[0]]
            s = dot(q, qkv[half, :, at[1]], NT) * scale
            s = jnp.where(pq[...] >= pk[...], s, masked_score)
            peak = jnp.max(s, axis=-1, keepdims=True)
            if second:
                sp = dot(q, qkv[0, :, at[1]], NT) * scale
                peak = jnp.maximum(peak, jnp.max(sp, axis=-1, keepdims=True))
            p = jnp.exp(s - peak)
            total = jnp.sum(p, axis=-1, keepdims=True)
            if second:
                pp = jnp.exp(sp - peak)
                total = total + jnp.sum(pp, axis=-1, keepdims=True)
            share = 1.0 / total
            value = dot((p * share).astype(bf16), qkv[half, :, at[2]])
            if second:
                value = value + dot((pp * share).astype(bf16), qkv[0, :, at[2]])
            ctx[:, h * size : (h + 1) * size] = value.astype(bf16)
            lse[:, h * LANES : (h + 1) * LANES] = jnp.broadcast_to(
                peak + jnp.log(total), (q.shape[0], LANES)
            )

    def expand():
        for at in range(0, wi.shape[1], 256):
            columns = slice(at, at + 256)
            h = dot(std[...], wi[:, columns]) + bi[:, columns]
            phi = 0.5 + 0.5 * lax.erf(h * (0.5**0.5))
            density = jnp.exp(h * h * -0.5) * 0.3989422804014327
            act[:, columns] = (h * phi).astype(bf16)
            dg[:, columns] = (phi + h * density).astype(bf16)

    def branch_rows(member):
        at = moves.part(member)
        return dot(ctx[at, :], wo[...]) + dot(act[at, :], wd[...])

    @pl.loop(0, tasks + LAG + 2)
    def _(step):
        g = step - base
        c = g - 1
        r = g - 2

        def load_rows(task, held):
            return pltpu.make_async_copy(held.at[task], kept.at[task % 4], load_sem.at[0])

        @when(valid(g) & first)
        def _():
            load_rows(g, xin).start()

        @when(valid(r))
        def _():
            reduce_first(moves, r, mine, core_in, load_sem.at[1])

        @when(valid(c))
        def _():
            gather_wait(moves, c)
            load = pltpu.make_async_copy(land.at[c], std, load_sem.at[2])
            load.start()

            @when(c == 0)
            def _():
                weights[0].wait()

            @when(c >= 1)
            def _():
                for k in range(5):
                    store(k, c - 1).wait()

            load.wait()
            project(c)
            store(0, c).start()

            @when(c % 2 == 0)
            def _():
                attend(c, False)

            @when(c % 2 == 1)
            def _():
                attend(c, True)

            store(3, c).start()
            store(4, c).start()

        @when(valid(g))
        def _():
            @when(jnp.logical_not(first))
            def _():
                moves.hand(g).wait_recv()
                load_rows(g, arrive).start()

            load_rows(g, xin).wait()

            @when(g >= 1)
            def _():
                gather_free(moves, g - 1)

            own[...] = standardize(kept[g % 4])[0].astype(bf16)
            gather_start(moves, g, keep_sem)

        @when(valid(c))
        def _():
            @when(c == 0)
            def _():
                weights[1].wait()

            expand()
            store(1, c).start()
            store(2, c).start()

        @when(valid(r))
        def _():
            value = reduce_second(moves, r, mine, chip_in, load_sem.at[1])

            @when(r >= 1)
            def _():
                pltpu.make_async_copy(handed, states.at[r - 1], state_sem).wait()

                @when(first)
                def _():
                    moves.hand(r - 1).wait_send()

            handed[...] = (kept[r % 4].astype(f32) + value + out_bias[...]).astype(bf16)
            pltpu.make_async_copy(handed, states.at[r], state_sem).start()

            @when(first)
            def _():
                moves.hand(r).start()

        @when(valid(c))
        def _():
            @when(c == 0)
            def _():
                weights[2].wait()
                weights[3].wait()

            @when(c >= 1)
            def _():
                moves.give_theirs(c - 1).wait_send()

            for j in range(chips):
                theirs[j] = branch_rows(2 * j + 1 - moves.core).astype(bf16)
            moves.give_theirs(c).start()
            for j in range(chips):
                mine[j] = branch_rows(2 * j + moves.core)

        @when(valid(g))
        def _():
            gather_pass(moves, g, keep_sem)

    drain(moves, tasks - 1)
    for k in range(5):
        store(k, tasks - 1).wait()
    pltpu.make_async_copy(handed, states.at[tasks - 1], state_sem).wait()

    @when(first)
    def _():
        moves.hand(tasks - 1).wait_send()


def move_semaphores(tasks, chips):
    dma = pltpu.SemaphoreType.DMA
    return [
        dma((tasks, chips - 1)),
        dma((tasks, chips)),
        dma((tasks,)),
        dma((tasks, chips - 1)),
        dma((tasks,)),
        dma((chips - 1,)),
        dma((chips,)),
        dma,
        dma((chips - 1,)),
        dma,
    ]


def forward_pass(xin, wq, wi, wo, wd, bq, bi, out_bias, tables, pq, pk, chips, heads):
    tasks, rows, width = xin.shape
    block = pq.shape[0]
    units, inner = wd.shape[0], wo.shape[0]
    anywhere = pl.BlockSpec(memory_space=pl.ANY)
    vmem = pl.BlockSpec(memory_space=pltpu.VMEM)
    shape = jax.ShapeDtypeStruct
    return pl.pallas_call(
        partial(forward_kernel, (tasks, chips, rows, heads)),
        out_shape=[
            shape((tasks, block, width), bf16),
            shape((tasks, block, 3 * inner), bf16),
            shape((tasks, block, units), bf16),
            shape((tasks, block, units), bf16),
            shape((tasks, block, inner), bf16),
            shape((tasks, block, heads * LANES), f32),
            shape((tasks, rows, width), bf16),
            shape((tasks, rows, width), bf16),
            shape((tasks, chips, rows, width), bf16),
            shape((tasks, chips - 1, rows, width), bf16),
        ],
        in_specs=[anywhere] * 5 + [vmem] * 8,
        out_specs=[anywhere] * 10,
        scratch_shapes=[
            pltpu.VMEM(wq.shape, bf16),
            pltpu.VMEM(wi.shape, bf16),
            pltpu.VMEM(wo.shape, bf16),
            pltpu.VMEM(wd.shape, bf16),
            pltpu.VMEM((block, width), bf16),
            pltpu.VMEM((2, block, 3 * inner), bf16),
            pltpu.VMEM((block, units), bf16),
            pltpu.VMEM((block, units), bf16),
            pltpu.VMEM((block, inner), bf16),
            pltpu.VMEM((block, heads * LANES), f32),
            pltpu.VMEM((4, rows, width), bf16),
            pltpu.VMEM((rows, width), bf16),
            pltpu.VMEM((chips, rows, width), bf16),
            pltpu.VMEM((chips, rows, width), f32),
            pltpu.VMEM((chips, rows, width), bf16),
            pltpu.VMEM((chips, rows, width), bf16),
            pltpu.VMEM((chips - 1, rows, width), bf16),
            pltpu.VMEM((rows, width), bf16),
            pltpu.SemaphoreType.DMA((4,)),
            pltpu.SemaphoreType.DMA((3,)),
            pltpu.SemaphoreType.DMA((5,)),
            pltpu.SemaphoreType.DMA,
            pltpu.SemaphoreType.DMA,
        ]
        + move_semaphores(tasks, chips),
        compiler_params=pltpu.CompilerParams(
            collective_id=3, has_side_effects=True, vmem_limit_bytes=PASS_VMEM
        ),
        cost_estimate=pl.CostEstimate(
            flops=2 * tasks * block * width * (3 * inner + 2 * units + inner),
            bytes_accessed=tasks * block * width * 16,
            transcendentals=0,
        ),
        name="forward_pass",
    )(xin, wq, wi, wo, wd, bq, bi, out_bias, *tables, pq, pk)


def backward_kernel(
    plan, gin, xin, xarrive, qkv_all, dg_all, ctx_all, lse_all, std_all, wq_all, wi_all, wo_all, wd_all,
    gains, cosine, ahead, behind, pq, pk,
    land, dproj_all, dh_all, dx_all, arrive, core_land, chip_land, vectors,
    wq, wi, wo, wd, gy, dg, dh, qkv, before, ctx, lse, std, dctx, dproj, dk_held, dv_held,
    kept, xrows, own, theirs, mine, core_in, low, chip_in, handed,
    weight_sem, load_sem, store_sem, keep_sem, state_sem, *sems,
):
    tasks, chips, rows, heads = plan
    size = wq.shape[1] // (3 * heads)
    scale = size**-0.5

    def place(task):
        return task + 1 - 2 * (task % 2)

    moves = Moves(
        (tasks, chips, rows), place, land, arrive, core_land, chip_land, own, theirs, low, handed, sems
    )
    first = moves.section == 0
    source = moves.section == 1
    base = jnp.where(source, 0, LAG)

    weights = [
        pltpu.make_async_copy(a, b, weight_sem.at[k])
        for k, (a, b) in enumerate(((wo_all, wo), (wd_all, wd), (wq_all, wq), (wi_all, wi)))
    ]
    for copy in weights:
        copy.start()
    vectors[...] = jnp.zeros_like(vectors)
    moves.greet()

    def valid(task):
        return (task >= 0) & (task < tasks)

    def store(k, task):
        return pltpu.make_async_copy(
            (dproj, dh)[k], (dproj_all, dh_all)[k].at[place(task)], store_sem.at[k]
        )

    def load(k, task):
        return pltpu.make_async_copy(
            (land, dg_all, qkv_all, ctx_all, lse_all, std_all)[k].at[place(task)],
            (gy, dg, qkv, ctx, lse, std)[k],
            load_sem.at[k],
        )

    def load_before(task):
        return pltpu.make_async_copy(qkv_all.at[place(task) - 1], before, load_sem.at[6])

    def spread():
        dctx[...] = dot(gy[...], wo[...], NT).astype(bf16)
        for at in range(0, wd.shape[0], 256):
            part = slice(at, at + 256)
            dh[:, part] = (dot(gy[...], wd[part, :], NT) * dg[:, part].astype(f32)).astype(bf16)

    def attend_back(second):
        half = 1 if second else 0
        table = (cosine[half], ahead[half], behind[half])
        for h in range(heads):
            at = [slice((3 * h + k) * size, (3 * h + k + 1) * size) for k in range(3)]
            mid = slice(h * size, (h + 1) * size)
            q = qkv[:, at[0]]
            d_ctx = dctx[:, mid]
            logsum = lse[:, h * LANES : h * LANES + 1]
            delta = jnp.sum(d_ctx.astype(f32) * ctx[:, mid].astype(f32), axis=-1, keepdims=True)

            def pieces(held, masked):
                k, v = held[:, at[1]], held[:, at[2]]
                s = dot(q, k, NT) * scale
                if masked:
                    s = jnp.where(pq[...] >= pk[...], s, masked_score)
                p = jnp.exp(s - logsum)
                d_chance = dot(d_ctx, v, NT)
                d_scores = (p * (d_chance - delta)).astype(bf16)
                return dot(d_scores, k), dot(d_scores, q, TN), dot(p.astype(bf16), d_ctx, TN)

            dq, dk, dv = pieces(qkv, True)
            if second:
                dq_more, dk_more, dv_more = pieces(before, False)
                dq = dq + dq_more
                dk_held[:, mid] = dk_more
                dv_held[:, mid] = dv_more
            else:
                dk = dk + dk_held[:, mid]
                dv = dv + dv_held[:, mid]
            dproj[:, at[0]] = turn(dq * scale, *table, -1.0).astype(bf16)
            dproj[:, at[1]] = turn(dk * scale, *table, -1.0).astype(bf16)
            dproj[:, at[2]] = dv.astype(bf16)

    def merge_rows(member):
        at = moves.part(member)
        one = dot(dproj[at, :], wq[...], NT)
        two = dot(dh[at, :], wi[...], NT)
        standard = std[at, :].astype(f32)
        for k, term in enumerate((one * standard, one, two * standard, two)):
            vectors[k : k + 1, :] += jnp.sum(term, axis=0, keepdims=True)
        return one * gains[0] + two * gains[1]

    @pl.loop(0, tasks + LAG + 2)
    def _(step):
        g = step - base
        c = g - 1
        r = g - 2

        def load_rows(task, held, number):
            return pltpu.make_async_copy(held.at[number], kept.at[task % 4], load_sem.at[7])

        def load_x(task, held):
            return pltpu.make_async_copy(held.at[place(task)], xrows, load_sem.at[8])

        @when(valid(g) & source)
        def _():
            load_rows(g, gin, place(g)).start()

        @when(valid(r))
        def _():
            @when(first)
            def _():
                load_x(r, xin).start()

            @when(jnp.logical_not(first))
            def _():
                load_x(r, xarrive).start()

            reduce_first(moves, r, mine, core_in, load_sem.at[9])

        @when(valid(c))
        def _():
            gather_wait(moves, c)
            for k in range(6):
                load(k, c).start()

            @when(c % 2 == 0)
            def _():
                load_before(c).start()

            @when(c == 0)
            def _():
                weights[0].wait()
                weights[1].wait()

            @when(c >= 1)
            def _():
                for k in range(2):
                    store(k, c - 1).wait()

            load(0, c).wait()
            load(1, c).wait()
            spread()
            store(1, c).start()
            for k in range(2, 6):
                load(k, c).wait()

        @when(valid(g))
        def _():
            @when(first)
            def _():
                moves.hand(g).wait_recv()
                load_rows(g, arrive, g).start()

            load_rows(g, gin, g).wait()

            @when(g >= 1)
            def _():
                gather_free(moves, g - 1)

            own[...] = kept[g % 4]
            gather_start(moves, g, keep_sem)
            vectors[4:5, :] += jnp.sum(kept[g % 4].astype(f32), axis=0, keepdims=True)

        @when(valid(c))
        def _():
            @when(c % 2 == 0)
            def _():
                load_before(c).wait()
                attend_back(True)

            @when(c % 2 == 1)
            def _():
                attend_back(False)

            store(0, c).start()

        @when(valid(r))
        def _():
            e = reduce_second(moves, r, mine, chip_in, load_sem.at[9])
            load_x(r, xin).wait()

            @when(r >= 1)
            def _():
                pltpu.make_async_copy(handed, dx_all.at[place(r - 1)], state_sem).wait()

                @when(source)
                def _():
                    moves.hand(r - 1).wait_send()

            standard, inverse = standardize(xrows[...])
            d_input = kept[r % 4].astype(f32) + inverse * (
                e
                - jnp.mean(e, axis=-1, keepdims=True)
                - standard * jnp.mean(e * standard, axis=-1, keepdims=True)
            )
            handed[...] = d_input.astype(bf16)
            pltpu.make_async_copy(handed, dx_all.at[place(r)], state_sem).start()

            @when(source)
            def _():
                moves.hand(r).start()

        @when(valid(c))
        def _():
            @when(c == 0)
            def _():
                weights[2].wait()
                weights[3].wait()

            @when(c >= 1)
            def _():
                moves.give_theirs(c - 1).wait_send()

            for j in range(chips):
                theirs[j] = merge_rows(2 * j + 1 - moves.core).astype(bf16)
            moves.give_theirs(c).start()
            for j in range(chips):
                mine[j] = merge_rows(2 * j + moves.core)

        @when(valid(g))
        def _():
            gather_pass(moves, g, keep_sem)

    drain(moves, tasks - 1)
    for k in range(2):
        store(k, tasks - 1).wait()
    pltpu.make_async_copy(handed, dx_all.at[place(tasks - 1)], state_sem).wait()

    @when(source)
    def _():
        moves.hand(tasks - 1).wait_send()


def backward_pass(gin, xin, xarrive, qkv, dg, ctx, lse, std, wq, wi, wo, wd, gains, tables, pq, pk, chips, heads):
    tasks, rows, width = xin.shape
    block = pq.shape[0]
    units, inner = wd.shape[0], wo.shape[0]
    anywhere = pl.BlockSpec(memory_space=pl.ANY)
    vmem = pl.BlockSpec(memory_space=pltpu.VMEM)
    shape = jax.ShapeDtypeStruct
    return pl.pallas_call(
        partial(backward_kernel, (tasks, chips, rows, heads)),
        out_shape=[
            shape((tasks, block, width), bf16),
            shape((tasks, block, 3 * inner), bf16),
            shape((tasks, block, units), bf16),
            shape((tasks, rows, width), bf16),
            shape((tasks, rows, width), bf16),
            shape((tasks, chips, rows, width), bf16),
            shape((tasks, chips - 1, rows, width), bf16),
            shape((8, width), f32),
        ],
        in_specs=[anywhere] * 12 + [vmem] * 6,
        out_specs=[anywhere] * 7 + [vmem],
        scratch_shapes=[
            pltpu.VMEM(wq.shape, bf16),
            pltpu.VMEM(wi.shape, bf16),
            pltpu.VMEM(wo.shape, bf16),
            pltpu.VMEM(wd.shape, bf16),
            pltpu.VMEM((block, width), bf16),
            pltpu.VMEM((block, units), bf16),
            pltpu.VMEM((block, units), bf16),
            pltpu.VMEM((block, 3 * inner), bf16),
            pltpu.VMEM((block, 3 * inner), bf16),
            pltpu.VMEM((block, inner), bf16),
            pltpu.VMEM((block, heads * LANES), f32),
            pltpu.VMEM((block, width), bf16),
            pltpu.VMEM((block, inner), bf16),
            pltpu.VMEM((block, 3 * inner), bf16),
            pltpu.VMEM((block, inner), f32),
            pltpu.VMEM((block, inner), f32),
            pltpu.VMEM((4, rows, width), bf16),
            pltpu.VMEM((rows, width), bf16),
            pltpu.VMEM((rows, width), bf16),
            pltpu.VMEM((chips, rows, width), bf16),
            pltpu.VMEM((chips, rows, width), f32),
            pltpu.VMEM((chips, rows, width), bf16),
            pltpu.VMEM((chips, rows, width), bf16),
            pltpu.VMEM((chips - 1, rows, width), bf16),
            pltpu.VMEM((rows, width), bf16),
            pltpu.SemaphoreType.DMA((4,)),
            pltpu.SemaphoreType.DMA((10,)),
            pltpu.SemaphoreType.DMA((2,)),
            pltpu.SemaphoreType.DMA,
            pltpu.SemaphoreType.DMA,
        ]
        + move_semaphores(tasks, chips),
        compiler_params=pltpu.CompilerParams(
            collective_id=5, has_side_effects=True, vmem_limit_bytes=PASS_VMEM
        ),
        cost_estimate=pl.CostEstimate(
            flops=2 * tasks * block * width * (3 * inner + 2 * units + inner),
            bytes_accessed=tasks * block * width * 20,
            transcendentals=0,
        ),
        name="backward_pass",
    )(gin, xin, xarrive, qkv, dg, ctx, lse, std, wq, wi, wo, wd, gains, *tables, pq, pk)


CHUNK = 256
PIECE = 64
SKEW = 2


def reduce_kernel(
    plan, act, ctx, dproj, dhid, gy, std, gains, biases, sums, small, out, small_out, from_left, from_right,
    rhs, raw, lhs, own, inbox, outbox, stage, small_in,
    rhs_sem, raw_sem, right_sem, left_sem, final_sem, load_sem, sent, stage_left, stage_right, out_sem,
    small_sent, small_got,
):
    bounds, tasks, count, piece, skew, ring = plan
    sources = (act, ctx, dproj, dhid)
    total_chunks = bounds[-1]
    per_chunk = CHUNK // piece
    pieces = total_chunks * per_chunk
    width = gy.shape[-1]
    tile = width // per_chunk
    block = raw.shape[2]
    z = lax.axis_index("ctx")
    last = count - 1
    root = count // 2
    turn_at = max(root, last - root)
    low, high, middle = z < root, z > root, z == root

    barrier = pltpu.get_barrier_semaphore()
    for shift in range(1, count):
        pl.semaphore_signal(
            barrier,
            inc=1,
            device_id={"ctx": lax.rem(z + shift, count)},
            device_id_type=pl.DeviceIdType.MESH,
        )

    def small_copy(source, target):
        return pltpu.make_async_remote_copy(
            src_ref=small,
            dst_ref=small_in.at[source],
            send_sem=small_sent.at[target],
            recv_sem=small_got.at[source],
            device_id={"ctx": target},
            device_id_type=pl.DeviceIdType.MESH,
        )

    def rhs_copy(k):
        return pltpu.make_async_copy((gy, std)[k].at[pl.ds(0, tasks)], rhs.at[k], rhs_sem.at[k])

    def each_source(chunk, act_on):
        for g, source in enumerate(sources):

            @pl.when((chunk >= bounds[g]) & (chunk < bounds[g + 1]))
            def _(g=g, source=source):
                column = pl.multiple_of((chunk - bounds[g]) * CHUNK, CHUNK)
                act_on(
                    pltpu.make_async_copy(
                        source.at[pl.ds(0, tasks), :, pl.ds(column, CHUNK)],
                        raw.at[chunk % 2],
                        raw_sem.at[chunk % 2],
                    )
                )

    def take(chunk):
        each_source(chunk, lambda copy: copy.wait())
        for k in range(tasks):
            lhs[:, k * block : (k + 1) * block] = raw[chunk % 2, k].T
        each_source(chunk + 1, lambda copy: copy.start())

    def multiply(chunk, part):
        second = jnp.where(chunk >= bounds[2], 1, 0)
        group = second + jnp.where(chunk >= bounds[3], 1, 0)
        columns = pl.ds(pl.multiple_of(part * tile, tile), tile)
        value = dot(lhs[:, :block], rhs[second, 0, :, columns])
        for k in range(1, tasks):
            value = value + dot(lhs[:, k * block : (k + 1) * block], rhs[second, k, :, columns])
        row = pl.multiple_of(chunk * CHUNK, CHUNK)
        value = value * gains[group, :, columns] + sums[pl.ds(row, CHUNK), :] * biases[group, :, columns]
        own[chunk % ring, :, columns] = value.astype(bf16)

    def rows_of(index):
        return pl.ds(pl.multiple_of(index * piece, piece), piece)

    def own_piece(index):
        inner = pl.multiple_of((index % per_chunk) * piece, piece)
        return own[(index // per_chunk) % ring, pl.ds(inner, piece), :]

    def remote(source, target_rows, send_sem, recv_sem, target):
        return pltpu.make_async_remote_copy(
            src_ref=source,
            dst_ref=target_rows,
            send_sem=send_sem,
            recv_sem=recv_sem,
            device_id={"ctx": target},
            device_id_type=pl.DeviceIdType.MESH,
        )

    def inward(index, right):
        landing, arrived, target = (from_left, right_sem, z + 1) if right else (from_right, left_sem, z - 1)
        return remote(
            outbox.at[index % 2], landing.at[rows_of(index)], sent.at[index % 2], arrived.at[index], target
        )

    def announce(index, right):
        return remote(
            stage.at[index % 2],
            out.at[rows_of(index)],
            (stage_right if right else stage_left).at[index % 2],
            final_sem.at[index],
            z + 1 if right else z - 1,
        )

    def onward(index, right):
        return remote(
            out.at[rows_of(index)],
            out.at[rows_of(index)],
            sent.at[2 + index % 2],
            final_sem.at[index],
            z + 1 if right else z - 1,
        )

    def load(index, right):
        landing = from_left if right else from_right
        return pltpu.make_async_copy(
            landing.at[rows_of(index)], inbox.at[0 if right else 1], load_sem.at[0 if right else 1]
        )

    def valid(index):
        return (index >= 0) & (index < pieces)

    def side(step, right):
        mine = low if right else high
        hops = z if right else last - z
        inner = step - hops * skew
        comes = hops > 0

        @pl.when(mine & valid(inner) & comes)
        def _():
            inward(inner, right).wait_recv()
            load(inner, right).start()

        @pl.when(mine & valid(inner))
        def _():
            @pl.when(inner >= 2)
            def _():
                inward(inner - 2, right).wait_send()

            @pl.when(comes)
            def _():
                load(inner, right).wait()
                value = own_piece(inner).astype(f32) + inbox[0 if right else 1].astype(f32)
                outbox[inner % 2] = value.astype(bf16)

            @pl.when(jnp.logical_not(comes))
            def _():
                outbox[inner % 2] = own_piece(inner)

            inward(inner, right).start()

        away = root - z if right else z - root
        outer = step - (turn_at + away) * skew

        @pl.when(mine & valid(outer))
        def _():
            onward(outer, not right).wait_recv()

            @pl.when(comes)
            def _():
                @pl.when(outer >= 2)
                def _():
                    onward(outer - 2, not right).wait_send()

                onward(outer, not right).start()

    def out_copy(index):
        return pltpu.make_async_copy(stage.at[index % 2], out.at[rows_of(index)], out_sem.at[index % 2])

    def stage_done(index):
        out_copy(index).wait()
        announce(index, False).wait_send()
        if root < last:
            announce(index, True).wait_send()

    def centre(step):
        index = step - turn_at * skew

        @pl.when(middle & valid(index))
        def _():
            inward(index, True).wait_recv()
            load(index, True).start()
            if root < last:
                inward(index, False).wait_recv()
                load(index, False).start()

            @pl.when(index >= 2)
            def _():
                stage_done(index - 2)

            load(index, True).wait()
            value = own_piece(index).astype(f32) + inbox[0].astype(f32)
            if root < last:
                load(index, False).wait()
                value = value + inbox[1].astype(f32)
            stage[index % 2] = value.astype(bf16)
            announce(index, False).start()
            if root < last:
                announce(index, True).start()
            out_copy(index).start()

    rhs_copy(0).start()
    each_source(0, lambda copy: copy.start())
    rhs_copy(1).start()
    take(0)
    rhs_copy(0).wait()

    @pl.loop(0, per_chunk)
    def _(part):
        multiply(0, part)

    pl.semaphore_wait(barrier, count - 1)
    small_in[z] = small[...]
    for shift in range(1, count):
        small_copy(z, lax.rem(z + shift, count)).start()

    @pl.loop(0, pieces + (turn_at + max(root, last - root)) * skew)
    def _(step):
        side(step, True)
        side(step, False)
        centre(step)
        chunk, part = step // per_chunk + 1, step % per_chunk

        @pl.when(chunk < total_chunks)
        def _():
            @pl.when(part == 0)
            def _():
                take(chunk)

                @pl.when(chunk == bounds[2])
                def _():
                    rhs_copy(1).wait()

            multiply(chunk, part)

    for shift in range(1, count):
        other = lax.rem(z + shift, count)
        small_copy(z, other).wait_send()
        small_copy(other, other).wait_recv()
    value = small_in[0]
    for k in range(1, count):
        value = value + small_in[k]
    small_out[...] = value
    for back in (2, 1):
        for right in (True, False):

            @pl.when(low if right else high)
            def _(right=right, back=back):
                inward(pieces - back, right).wait_send()

                @pl.when((z > 0) & (z < last))
                def _():
                    onward(pieces - back, not right).wait_send()

        @pl.when(middle)
        def _(back=back):
            stage_done(pieces - back)


def reduce_gradients(act, ctx, dproj, dhid, gy, std, gains, biases, sums, small, tasks):
    count = lax.axis_size("ctx")
    block, width = gy.shape[1:]
    bounds = [0]
    for source in (act, ctx, dproj, dhid):
        bounds.append(bounds[-1] + source.shape[2] // CHUNK)
    total = bounds[-1] * CHUNK
    pieces = total // PIECE
    ring = count // 2 * SKEW // (CHUNK // PIECE) + 3
    plan = (tuple(bounds), tasks, count, PIECE, SKEW, ring)
    anywhere = pl.BlockSpec(memory_space=pl.ANY)
    vmem = pl.BlockSpec(memory_space=pltpu.VMEM)
    result = jax.ShapeDtypeStruct((total, width), bf16)
    out, small_out, _, _ = pl.pallas_call(
        partial(reduce_kernel, plan),
        out_shape=[result, jax.ShapeDtypeStruct(small.shape, f32), result, result],
        in_specs=[anywhere] * 6 + [vmem] * 4,
        out_specs=[anywhere, vmem, anywhere, anywhere],
        scratch_shapes=[
            pltpu.VMEM((2, tasks, block, width), bf16),
            pltpu.VMEM((2, tasks, block, CHUNK), bf16),
            pltpu.VMEM((CHUNK, tasks * block), bf16),
            pltpu.VMEM((ring, CHUNK, width), bf16),
            pltpu.VMEM((2, PIECE, width), bf16),
            pltpu.VMEM((2, PIECE, width), bf16),
            pltpu.VMEM((2, PIECE, width), bf16),
            pltpu.VMEM((count,) + small.shape, f32),
            pltpu.SemaphoreType.DMA((2,)),
            pltpu.SemaphoreType.DMA((2,)),
            pltpu.SemaphoreType.DMA((pieces,)),
            pltpu.SemaphoreType.DMA((pieces,)),
            pltpu.SemaphoreType.DMA((pieces,)),
            pltpu.SemaphoreType.DMA((2,)),
            pltpu.SemaphoreType.DMA((4,)),
            pltpu.SemaphoreType.DMA((2,)),
            pltpu.SemaphoreType.DMA((2,)),
            pltpu.SemaphoreType.DMA((2,)),
            pltpu.SemaphoreType.DMA((count,)),
            pltpu.SemaphoreType.DMA((count,)),
        ],
        compiler_params=pltpu.CompilerParams(
            collective_id=7, has_side_effects=True, vmem_limit_bytes=60 * 1024 * 1024
        ),
        cost_estimate=pl.CostEstimate(
            flops=2 * total * width * tasks * block,
            bytes_accessed=8 * total * width,
            transcendentals=0,
        ),
        name="reduce_gradients",
    )(act, ctx, dproj, dhid, gy, std, gains, biases, sums, small)
    return out, small_out


def exchange(blocks, axis):
    count = blocks.shape[0]
    me = lax.axis_index(axis)
    got = [lax.dynamic_index_in_dim(blocks, me, 0, keepdims=False)]
    for shift in range(1, count):
        piece = lax.dynamic_index_in_dim(blocks, (me + shift) % count, 0, keepdims=False)
        got.append(lax.ppermute(piece, axis, [(k, (k + shift) % count) for k in range(count)]))
    ring = jnp.stack(got[::-1] + got[::-1])
    return lax.dynamic_slice_in_dim(ring, (count - 1 - me) % count, count, 0)


def body(
    inputs,
    out_grads,
    norm1_gain,
    norm1_bias,
    norm2_gain,
    norm2_bias,
    w_qkv,
    b_qkv,
    w_out,
    b_out,
    input_projection,
    input_bias_vector,
    down_projection,
    b_down,
):
    ctx_count = lax.axis_size("ctx")
    tensor = lax.axis_size("tensor")
    micro, _, rows, seqs, width = inputs.shape
    heads = w_qkv.shape[2]
    head_cols = w_qkv.shape[3]
    first = lax.axis_index("section") == 0
    per_device = micro * seqs // ctx_count
    blocks = ctx_count // 2
    own_rows = blocks * rows
    tasks = 2 * per_device

    chosen = jnp.where(first, inputs[:, 0], out_grads[:, 0])
    chosen = chosen.transpose(0, 2, 1, 3).reshape(per_device, ctx_count, rows, width)
    own_chosen = []
    for j in range(per_device):
        moved = exchange(chosen[j], "ctx").reshape(2, own_rows, width)
        own_chosen += [moved[0], moved[1]]

    wq = w_qkv[0].reshape(width, heads * head_cols)
    wi = input_projection[0]
    wo = w_out[0].reshape(-1, width)
    wd = down_projection[0]
    gain_one, bias_one, gain_two, bias_two = norm1_gain[0], norm1_bias[0], norm2_gain[0], norm2_bias[0]
    wq_scaled = (wq.astype(f32) * gain_one[:, None]).astype(bf16)
    wi_scaled = (wi.astype(f32) * gain_two[:, None]).astype(bf16)
    bq = b_qkv[0].reshape(1, -1) + jnp.sum(wq.astype(f32) * bias_one[:, None], axis=0, keepdims=True)
    bi = input_bias_vector + jnp.sum(wi.astype(f32) * bias_two[:, None], axis=0, keepdims=True)
    out_bias = (b_out[0] + b_down[0])[None]

    relative, tables = position_tables(None, blocks, rows, tensor)
    places_q, places_k = relative[:, None], relative[None, :]

    chips = tensor // 2
    chosen_rows = jnp.stack(own_chosen)
    stacked_tables = [jnp.stack(pair) for pair in zip(*tables)]
    std_all, qkv, act_all, dg_all, ctx_all, lse_all, states, arrive, _, _ = forward_pass(
        chosen_rows,
        wq_scaled,
        wi_scaled,
        wo,
        wd,
        bq,
        bi,
        out_bias,
        stacked_tables,
        places_q,
        places_k,
        chips,
        heads,
    )
    gains = jnp.stack([gain_one, gain_two])[:, None]
    gy_all, dproj_all, dh_all, dx_all, _, _, _, vectors = backward_pass(
        chosen_rows,
        chosen_rows,
        arrive,
        qkv,
        dg_all,
        ctx_all,
        lse_all,
        std_all,
        wq,
        wi,
        wo,
        wd,
        gains,
        stacked_tables,
        places_q,
        places_k,
        chips,
        heads,
    )
    vectors = vectors[:5]

    d_b_qkv = jnp.sum(dproj_all[:tasks], axis=(0, 1), dtype=f32)
    d_b_in = jnp.sum(dh_all[:tasks], axis=(0, 1), dtype=f32)
    units, inner = wd.shape[0], wo.shape[0]
    sums = jnp.concatenate([jnp.zeros((units + inner,), f32), d_b_qkv, d_b_in])[:, None]
    gains = jnp.stack([jnp.ones_like(gain_one), gain_one, gain_two])[:, None]
    biases = jnp.stack([jnp.zeros_like(bias_one), bias_one, bias_two])[:, None]
    mask = 1
    while mask < tensor:
        vectors = vectors + lax.ppermute(vectors, "tensor", [(k, k ^ mask) for k in range(tensor)])
        mask *= 2
    sides = jnp.concatenate([d_b_qkv, d_b_in])
    side_rows = -(-sides.shape[0] // width)
    small = jnp.zeros((-(-(5 + side_rows) // 8) * 8, width), f32)
    small = small.at[:5].set(vectors)
    small = small.at[5 : 5 + side_rows].set(
        jnp.pad(sides, (0, side_rows * width - sides.shape[0])).reshape(side_rows, width)
    )
    summed, small = reduce_gradients(
        act_all, ctx_all, dproj_all, dh_all, gy_all, std_all, gains, biases, sums, small, tasks
    )
    vectors = small[:5]
    sides = small[5 : 5 + side_rows].reshape(-1)
    d_b_qkv, d_b_in = sides[: d_b_qkv.shape[0]], sides[d_b_qkv.shape[0] : sides.shape[0]]
    d_b_in = d_b_in[: wi.shape[1]]
    d_w_down = summed[:units].astype(f32)
    d_w_out = summed[units : units + inner].astype(f32)
    summed = summed[units + inner :]
    d_w_qkv = summed[: wq.shape[1]].T.astype(f32)
    d_w_in = summed[wq.shape[1] :].T.astype(f32)

    def homeward(rows_of_tasks):
        stacked = rows_of_tasks.reshape(per_device, ctx_count, rows, width)
        moved = exchange(stacked.transpose(1, 0, 2, 3), "ctx")
        moved = moved.transpose(1, 0, 2, 3).reshape(micro, seqs, rows, width)
        return moved.transpose(0, 2, 1, 3)[None, :, None]

    states = homeward(states)
    input_grads = homeward(dx_all).astype(f32)
    return (
        states,
        input_grads,
        vectors[0][None],
        vectors[1][None],
        vectors[2][None],
        vectors[3][None],
        d_w_qkv.reshape(w_qkv.shape),
        d_b_qkv.reshape(b_qkv.shape),
        d_w_out.reshape(w_out.shape),
        vectors[4][None],
        d_w_in[None],
        d_b_in[None],
        d_w_down[None],
        vectors[4][None],
    )


def solution(mesh):
    return jax.shard_map(
        body,
        mesh=mesh,
        in_specs=(
            P(None, "ctx", "tensor", None, None),
            P(None, "ctx", "tensor", None, None),
            P("section", None),
            P("section", None),
            P("section", None),
            P("section", None),
            P("section", None, "tensor", None),
            P("section", "tensor", None),
            P("section", "tensor", None, None),
            P("section", None),
            P("section", None, "tensor"),
            P("section", "tensor"),
            P("section", "tensor", None),
            P("section", None),
        ),
        out_specs=(
            P("section", None, "ctx", "tensor", None, None),
            P("section", None, "ctx", "tensor", None, None),
            P("section", None),
            P("section", None),
            P("section", None),
            P("section", None),
            P("section", None, "tensor", None),
            P("section", "tensor", None),
            P("section", "tensor", None, None),
            P("section", None),
            P("section", None, "tensor"),
            P("section", "tensor"),
            P("section", "tensor", None),
            P("section", None),
        ),
        check_vma=False,
    )
```

```python
from functools import partial

import jax
import jax.numpy as jnp
from jax import lax
from jax.experimental import pallas as pl
from jax.experimental.pallas import tpu as pltpu
from jax.sharding import PartitionSpec as P

ROT = 64
LAG = 3
LANES = 128
epsilon = 1e-05
masked_score = -1e30
f32 = jnp.float32
bf16 = jnp.bfloat16
NT = (((1,), (1,)), ((), ()))
TN = (((0,), (0,)), ((), ()))
NN = (((1,), (0,)), ((), ()))
PASS_VMEM = 62 * 1024 * 1024


def dot(a, b, dims=NN):
    return lax.dot_general(a, b, dims, preferred_element_type=f32)


def standardize(rows):
    values = rows.astype(f32)
    average = jnp.mean(values, axis=-1, keepdims=True)
    centred = values - average
    inverse = lax.rsqrt(jnp.mean(centred * centred, axis=-1, keepdims=True) + epsilon)
    return centred * inverse, inverse


def position_tables(section_rows, blocks, rows, tensor):
    half = ROT // 2
    frequency = 1.0 / 10000.0 ** (jnp.arange(0, ROT, 2, dtype=f32) / ROT)
    core, chip, c, i = jnp.meshgrid(
        jnp.arange(2), jnp.arange(tensor // 2), jnp.arange(blocks), jnp.arange(rows), indexing="ij"
    )
    relative = (c * (rows * tensor) + (chip * 2 + core) * rows + i).reshape(-1).astype(jnp.int32)
    tables = []
    for part in range(2):
        places = (relative + part * blocks * rows * tensor).astype(f32)
        angles = places[:, None] * frequency[None, :]
        cosine, sine = jnp.cos(angles), jnp.sin(angles)
        none = jnp.zeros_like(sine)
        rest = jnp.zeros((relative.shape[0], LANES - ROT), f32)
        tables.append(
            (
                jnp.concatenate([cosine, cosine, rest + 1.0], axis=-1),
                jnp.concatenate([-sine, none, rest], axis=-1),
                jnp.concatenate([none, sine, rest], axis=-1),
            )
        )
    return relative, tables


def turn(values, cosine, ahead, behind, sign):
    half = ROT // 2
    lead = values[:, :LANES]
    turned = pltpu.roll(lead, LANES - half, 1) * ahead + pltpu.roll(lead, half, 1) * behind
    return jnp.concatenate([lead * cosine + sign * turned, values[:, LANES:]], axis=1)


class Moves:
    def __init__(self, plan, place, land, arrive, core_land, chip_land, own, theirs, low, handed, sems):
        self.tasks, self.chips, self.rows = plan
        self.place = place
        self.land, self.arrive, self.core_land, self.chip_land = land, arrive, core_land, chip_land
        self.own, self.theirs, self.low, self.handed = own, theirs, low, handed
        (
            self.got_chip, self.got_core, self.got_theirs, self.got_low, self.got_hand,
            self.put_chip, self.put_core, self.put_theirs, self.put_low, self.put_hand,
        ) = sems
        self.section = lax.axis_index("section")
        self.index = lax.axis_index("tensor")
        self.total = 2 * self.chips
        self.chip, self.core = self.index // 2, self.index % 2
        self.mate = self.chip * 2 + 1 - self.core

    def mate_on(self, shift):
        return lax.rem(self.index + 2 * shift, self.total)

    def part(self, member):
        at = (member % 2) * self.chips + member // 2
        return pl.ds(pl.multiple_of(at * self.rows, self.rows), self.rows)

    def share(self, core):
        size = self.chips * self.rows
        return pl.ds(pl.multiple_of(core * size, size), size)

    def of_chip(self, chip):
        return pl.ds(pl.multiple_of(chip * self.rows, self.rows), self.rows)

    def remote(self, source, target, sent, arrived, **device):
        return pltpu.make_async_remote_copy(
            src_ref=source,
            dst_ref=target,
            send_sem=sent,
            recv_sem=arrived,
            device_id=device,
            device_id_type=pl.DeviceIdType.MESH,
        )

    def greet(self, line):
        barrier = pltpu.get_barrier_semaphore()
        peers = [{"section": 1 - self.section}, {"tensor": self.mate}]
        peers += [{"ctx": other} for other in line.others()]
        peers += [{"tensor": self.mate_on(shift)} for shift in range(1, self.chips)]
        for peer in peers:
            pl.semaphore_signal(barrier, inc=1, device_id=peer, device_id_type=pl.DeviceIdType.MESH)
        pl.semaphore_wait(barrier, len(peers))

    def gather_chip(self, task, shift, member=None):
        member = self.index if member is None else member
        return self.remote(
            self.own,
            self.land.at[self.place(task), self.part(member)],
            self.put_chip.at[shift - 1],
            self.got_chip.at[task, shift - 1],
            tensor=self.mate_on(shift),
        )

    def gather_chip_in(self, task, shift):
        return self.gather_chip(task, shift, lax.rem(self.index + self.total - 2 * shift, self.total))

    def gather_core(self, task, shift, member=None):
        if member is None:
            member = lax.rem(self.index + self.total - 2 * shift, self.total)
        target = self.land.at[self.place(task), self.part(member)]
        return self.remote(
            self.own if shift == 0 else target,
            target,
            self.put_core.at[shift],
            self.got_core.at[task, shift],
            tensor=self.mate,
        )

    def gather_core_in(self, task, shift):
        return self.gather_core(task, shift, lax.rem(self.mate + self.total - 2 * shift, self.total))

    def give_theirs(self, task):
        return self.remote(
            self.theirs, self.core_land.at[task], self.put_theirs, self.got_theirs.at[task], tensor=self.mate
        )

    def give_low(self, task, shift):
        return self.remote(
            self.low.at[self.of_chip(lax.rem(self.chip + shift, self.chips))],
            self.chip_land.at[task, shift - 1],
            self.put_low.at[shift - 1],
            self.got_low.at[task, shift - 1],
            tensor=self.mate_on(shift),
        )

    def hand(self, task):
        return self.remote(
            self.handed, self.arrive.at[task], self.put_hand, self.got_hand.at[task], section=1 - self.section
        )


class Line:
    def __init__(self, rows):
        self.rows = rows
        self.count = lax.axis_size("ctx")
        self.blocks = self.count // 2
        self.z = lax.axis_index("ctx")

    def others(self):
        return [lax.rem(self.z + shift, self.count) for shift in range(1, self.count)]

    def remote(self, source, target, sent, arrived, device):
        return pltpu.make_async_remote_copy(
            src_ref=source,
            dst_ref=target,
            send_sem=sent,
            recv_sem=arrived,
            device_id={"ctx": device},
            device_id_type=pl.DeviceIdType.MESH,
        )

    def block(self, at):
        return pl.ds(pl.multiple_of(at * self.rows, self.rows), self.rows)

    def set_in(self, chosen, landed, put, got, kept):
        self.chosen, self.landed, self.put_in, self.got_in, self.kept_in = chosen, landed, put, got, kept

    def bring(self, j, shift, source=None):
        source = self.z if source is None else source
        half = source // self.blocks
        return self.remote(
            self.chosen.at[j, lax.rem(self.z + shift, self.count)],
            self.landed.at[2 * j + half, self.block(source - half * self.blocks)],
            self.put_in.at[j, shift - 1],
            self.got_in.at[j, source],
            lax.rem(self.z + shift, self.count),
        )

    def bring_own(self, j):
        half = self.z // self.blocks
        return pltpu.make_async_copy(
            self.chosen.at[j, self.z],
            self.landed.at[2 * j + half, self.block(self.z - half * self.blocks)],
            self.kept_in.at[j],
        )

    def bring_start(self, j):
        for shift in range(1, self.count):
            self.bring(j, shift).start()
        self.bring_own(j).start()

    def bring_wait(self, task):
        j, half = task // 2, task % 2
        for k in range(self.blocks):
            source = half * self.blocks + k

            @pl.when(source != self.z)
            def _():
                self.bring(j, 1, source).wait_recv()

            @pl.when(source == self.z)
            def _():
                self.bring_own(j).wait()

    def bring_done(self, count):
        for j in range(count):
            for shift in range(1, self.count):
                self.bring(j, shift).wait_send()

    def set_home(self, handed, home, put, got, kept):
        self.handed, self.home, self.put_home, self.got_home, self.kept_home = handed, home, put, got, kept

    def take_home(self, task, k, source=None):
        j, half = task // 2, task % 2
        source = self.z if source is None else source
        return self.remote(
            self.handed.at[pl.ds(k * self.rows, self.rows)],
            self.home.at[j * self.count + source],
            self.put_home.at[k],
            self.got_home.at[j, source],
            half * self.blocks + k,
        )

    def keep_home(self, task, k):
        return pltpu.make_async_copy(
            self.handed.at[pl.ds(k * self.rows, self.rows)],
            self.home.at[(task // 2) * self.count + self.z],
            self.kept_home,
        )

    def home_each(self, task, begin):
        half = task % 2
        for k in range(self.blocks):
            there = half * self.blocks + k

            @pl.when(there != self.z)
            def _():
                copy = self.take_home(task, k)
                copy.start() if begin else copy.wait_send()

            @pl.when(there == self.z)
            def _():
                copy = self.keep_home(task, k)
                copy.start() if begin else copy.wait()

    def home_wait(self, tasks):
        for j in range(tasks // 2):
            for other in self.others():
                self.take_home(2 * j, 0, other).wait_recv()


def line_semaphores(tasks, count):
    dma = pltpu.SemaphoreType.DMA
    half = tasks // 2
    return [dma((half, count - 1)), dma((half, count)), dma((half,))], [
        dma((count // 2,)),
        dma((half, count)),
        dma,
    ]


def reduce_first(moves, task, mine, core_in, load_sem):
    moves.give_theirs(task).wait_recv()
    load = pltpu.make_async_copy(moves.core_land.at[task], core_in, load_sem)
    load.start()

    @pl.when(task >= 1)
    def _():
        for shift in range(1, moves.chips):
            moves.give_low(task - 1, shift).wait_send()

    load.wait()
    value = mine[...] + core_in[...].astype(f32)
    mine[...] = value
    moves.low[...] = value.astype(bf16)
    for shift in range(1, moves.chips):
        moves.give_low(task, shift).start()


def reduce_second(moves, task, mine, chip_in, load_sem):
    for shift in range(1, moves.chips):
        moves.give_low(task, shift).wait_recv()
    load = pltpu.make_async_copy(moves.chip_land.at[task], chip_in, load_sem)
    load.start()
    load.wait()
    value = mine[moves.of_chip(moves.chip), :]
    for shift in range(1, moves.chips):
        value = value + chip_in[shift - 1].astype(f32)
    return value


def gather_start(moves, task, keep_sem):
    pltpu.make_async_copy(
        moves.own, moves.land.at[moves.place(task), moves.part(moves.index)], keep_sem
    ).start()
    for shift in range(1, moves.chips):
        moves.gather_chip(task, shift).start()
    moves.gather_core(task, 0).start()


def gather_free(moves, task):
    for shift in range(1, moves.chips):
        moves.gather_chip(task, shift).wait_send()
    moves.gather_core(task, 0).wait_send()


def gather_pass(moves, task, keep_sem):
    pltpu.make_async_copy(
        moves.own, moves.land.at[moves.place(task), moves.part(moves.index)], keep_sem
    ).wait()
    for shift in range(1, moves.chips):
        moves.gather_chip_in(task, shift).wait_recv()

        @pl.when(task >= 1)
        def _():
            moves.gather_core(task - 1, shift).wait_send()

        moves.gather_core(task, shift).start()


def gather_wait(moves, task):
    for shift in range(moves.chips):
        moves.gather_core_in(task, shift).wait_recv()


def drain(moves, task):
    gather_free(moves, task)
    for shift in range(1, moves.chips):
        moves.gather_core(task, shift).wait_send()
        moves.give_low(task, shift).wait_send()
    moves.give_theirs(task).wait_send()


def when(condition):
    return pl.when(condition)


def forward_kernel(
    plan, chosen, wq_all, wi_all, wo_all, wd_all, bq_in, bi_in, norms, out_bias, cosine, ahead, behind, pq, pk,
    land, qkv_all, act_all, dg_all, ctx_all, lse_all, xin, home, arrive, core_land, chip_land,
    wq, wi, wo, wd, bq, bi, std, qkv, act, dg, ctx, lse, kept, own, theirs, mine, core_in, low, chip_in, handed,
    weight_sem, load_sem, store_sem, keep_sem,
    put_in, got_in, kept_in, put_home, got_home, kept_home, *sems,
):
    tasks, chips, rows, heads = plan
    line = Line(chosen.shape[2])
    line.set_in(chosen, xin, put_in, got_in, kept_in)
    line.set_home(handed, home, put_home, got_home, kept_home)
    size = wq.shape[1] // (3 * heads)
    moves = Moves(
        (tasks, chips, rows), lambda task: task, land, arrive, core_land, chip_land, own, theirs, low, handed, sems
    )
    first = moves.section == 0
    base = jnp.where(first, 0, LAG)

    weights = [
        pltpu.make_async_copy(a, b, weight_sem.at[k])
        for k, (a, b) in enumerate(((wq_all, wq), (wi_all, wi), (wo_all, wo), (wd_all, wd)))
    ]
    moves.greet(line)
    line.bring_start(0)
    for copy in weights:
        copy.start()

    def valid(task):
        return (task >= 0) & (task < tasks)

    def fold(weight, bias_in, bias, gain_column):
        bias[...] = bias_in[...]
        step = 256

        @pl.loop(0, weight.shape[0] // step)
        def _(k):
            at = pl.ds(pl.multiple_of(k * step, step), step)
            value = weight[at, :].astype(f32)
            gain = norms[at, gain_column : gain_column + 1]
            shift = norms[at, gain_column + 1 : gain_column + 2]
            bias[...] += jnp.sum(value * shift, axis=0, keepdims=True)
            weight[at, :] = (value * gain).astype(bf16)

    def store(k, task):
        return pltpu.make_async_copy(
            (qkv.at[task % 2], act, dg, ctx, lse)[k],
            (qkv_all, act_all, dg_all, ctx_all, lse_all)[k].at[task],
            store_sem.at[k],
        )

    def project(task):
        half = task % 2
        table = (cosine[half], ahead[half], behind[half])
        for h in range(heads):
            for k in range(3):
                columns = slice((3 * h + k) * size, (3 * h + k + 1) * size)
                z = dot(std[...], wq[:, columns]) + bq[:, columns]
                if k < 2:
                    z = turn(z, *table, 1.0)
                qkv[half, :, columns] = z.astype(bf16)

    def attend(task, second):
        half = 1 if second else 0
        scale = size**-0.5
        for h in range(heads):
            at = [slice((3 * h + k) * size, (3 * h + k + 1) * size) for k in range(3)]
            q = qkv[half, :, at[0]]
            s = dot(q, qkv[half, :, at[1]], NT) * scale
            s = jnp.where(pq[...] >= pk[...], s, masked_score)
            peak = jnp.max(s, axis=-1, keepdims=True)
            if second:
                sp = dot(q, qkv[0, :, at[1]], NT) * scale
                peak = jnp.maximum(peak, jnp.max(sp, axis=-1, keepdims=True))
            p = jnp.exp(s - peak)
            total = jnp.sum(p, axis=-1, keepdims=True)
            if second:
                pp = jnp.exp(sp - peak)
                total = total + jnp.sum(pp, axis=-1, keepdims=True)
            share = 1.0 / total
            value = dot((p * share).astype(bf16), qkv[half, :, at[2]])
            if second:
                value = value + dot((pp * share).astype(bf16), qkv[0, :, at[2]])
            ctx[:, h * size : (h + 1) * size] = value.astype(bf16)
            lse[:, h * LANES : (h + 1) * LANES] = jnp.broadcast_to(
                peak + jnp.log(total), (q.shape[0], LANES)
            )

    def expand():
        for at in range(0, wi.shape[1], 256):
            columns = slice(at, at + 256)
            h = dot(std[...], wi[:, columns]) + bi[:, columns]
            phi = 0.5 + 0.5 * lax.erf(h * (0.5**0.5))
            density = jnp.exp(h * h * -0.5) * 0.3989422804014327
            act[:, columns] = (h * phi).astype(bf16)
            dg[:, columns] = (phi + h * density).astype(bf16)

    def branch_rows(core, result):
        at = moves.share(core)
        for column in range(0, wo.shape[1], 512):
            columns = slice(column, column + 512)
            value = dot(ctx[at, :], wo[:, columns]) + dot(act[at, :], wd[:, columns])
            result[:, columns] = value.astype(result.dtype)

    @pl.loop(0, tasks + LAG + 2)
    def _(step):
        g = step - base
        c = g - 1
        r = g - 2

        def load_rows(task, held):
            return pltpu.make_async_copy(held.at[task], kept.at[task % 4], load_sem.at[0])

        @when((step % 2 == 0) & (step // 2 + 1 < tasks // 2))
        def _():
            line.bring_start(step // 2 + 1)

        @when(valid(r))
        def _():
            reduce_first(moves, r, mine, core_in, load_sem.at[1])

        @when(valid(c))
        def _():
            gather_wait(moves, c)
            load = pltpu.make_async_copy(land.at[c], std, load_sem.at[2])
            load.start()

            @when(c >= 1)
            def _():
                for k in range(5):
                    store(k, c - 1).wait()

            load.wait()
            project(c)
            store(0, c).start()

            @when(c % 2 == 0)
            def _():
                attend(c, False)

            @when(c % 2 == 1)
            def _():
                attend(c, True)

            store(3, c).start()
            store(4, c).start()

        @when(step < tasks)
        def _():
            line.bring_wait(step)

        @when(valid(g))
        def _():
            @when(first)
            def _():
                load_rows(g, xin).start()

            @when(jnp.logical_not(first))
            def _():
                moves.hand(g).wait_recv()
                load_rows(g, arrive).start()

            load_rows(g, xin).wait()

            @when(g >= 1)
            def _():
                gather_free(moves, g - 1)

            own[...] = standardize(kept[g % 4])[0].astype(bf16)
            gather_start(moves, g, keep_sem)

        @when(step == 0)
        def _():
            weights[0].wait()
            fold(wq, bq_in, bq, 0)
            weights[1].wait()
            fold(wi, bi_in, bi, 2)
            weights[2].wait()
            weights[3].wait()

        @when(valid(c))
        def _():
            expand()
            store(1, c).start()
            store(2, c).start()

        @when(valid(r))
        def _():
            value = reduce_second(moves, r, mine, chip_in, load_sem.at[1])

            @when(r >= 1)
            def _():
                line.home_each(r - 1, False)

                @when(first)
                def _():
                    moves.hand(r - 1).wait_send()

            handed[...] = (kept[r % 4].astype(f32) + value + out_bias[...]).astype(bf16)

            @when(first)
            def _():
                moves.hand(r).start()

            line.home_each(r, True)

        @when(valid(c))
        def _():
            @when(c >= 1)
            def _():
                moves.give_theirs(c - 1).wait_send()

            branch_rows(1 - moves.core, theirs)
            moves.give_theirs(c).start()
            branch_rows(moves.core, mine)

        @when(valid(g))
        def _():
            gather_pass(moves, g, keep_sem)

    drain(moves, tasks - 1)
    for k in range(5):
        store(k, tasks - 1).wait()
    line.home_each(tasks - 1, False)
    line.home_wait(tasks)
    line.bring_done(tasks // 2)

    @when(first)
    def _():
        moves.hand(tasks - 1).wait_send()


def move_semaphores(tasks, chips):
    dma = pltpu.SemaphoreType.DMA
    return [
        dma((tasks, chips - 1)),
        dma((tasks, chips)),
        dma((tasks,)),
        dma((tasks, chips - 1)),
        dma((tasks,)),
        dma((chips - 1,)),
        dma((chips,)),
        dma,
        dma((chips - 1,)),
        dma,
    ]


def forward_pass(chosen, wq, wi, wo, wd, bq, bi, norms, out_bias, tables, pq, pk, chips, heads):
    per_device, count, part_rows, width = chosen.shape
    tasks, rows = 2 * per_device, count // 2 * part_rows
    in_sems, home_sems = line_semaphores(tasks, count)
    block = pq.shape[0]
    units, inner = wd.shape[0], wo.shape[0]
    anywhere = pl.BlockSpec(memory_space=pl.ANY)
    vmem = pl.BlockSpec(memory_space=pltpu.VMEM)
    shape = jax.ShapeDtypeStruct
    return pl.pallas_call(
        partial(forward_kernel, (tasks, chips, rows, heads)),
        out_shape=[
            shape((tasks, block, width), bf16),
            shape((tasks, block, 3 * inner), bf16),
            shape((tasks, block, units), bf16),
            shape((tasks, block, units), bf16),
            shape((tasks, block, inner), bf16),
            shape((tasks, block, heads * LANES), f32),
            shape((tasks, rows, width), bf16),
            shape((per_device * count, part_rows, width), bf16),
            shape((tasks, rows, width), bf16),
            shape((tasks, chips * rows, width), bf16),
            shape((tasks, chips - 1, rows, width), bf16),
        ],
        in_specs=[anywhere] * 5 + [vmem] * 9,
        out_specs=[anywhere] * 11,
        scratch_shapes=[
            pltpu.VMEM(wq.shape, bf16),
            pltpu.VMEM(wi.shape, bf16),
            pltpu.VMEM(wo.shape, bf16),
            pltpu.VMEM(wd.shape, bf16),
            pltpu.VMEM(bq.shape, f32),
            pltpu.VMEM(bi.shape, f32),
            pltpu.VMEM((block, width), bf16),
            pltpu.VMEM((2, block, 3 * inner), bf16),
            pltpu.VMEM((block, units), bf16),
            pltpu.VMEM((block, units), bf16),
            pltpu.VMEM((block, inner), bf16),
            pltpu.VMEM((block, heads * LANES), f32),
            pltpu.VMEM((4, rows, width), bf16),
            pltpu.VMEM((rows, width), bf16),
            pltpu.VMEM((chips * rows, width), bf16),
            pltpu.VMEM((chips * rows, width), f32),
            pltpu.VMEM((chips * rows, width), bf16),
            pltpu.VMEM((chips * rows, width), bf16),
            pltpu.VMEM((chips - 1, rows, width), bf16),
            pltpu.VMEM((rows, width), bf16),
            pltpu.SemaphoreType.DMA((4,)),
            pltpu.SemaphoreType.DMA((3,)),
            pltpu.SemaphoreType.DMA((5,)),
            pltpu.SemaphoreType.DMA,
        ]
        + in_sems
        + home_sems
        + move_semaphores(tasks, chips),
        compiler_params=pltpu.CompilerParams(
            collective_id=3, has_side_effects=True, vmem_limit_bytes=PASS_VMEM
        ),
        cost_estimate=pl.CostEstimate(
            flops=2 * tasks * block * width * (3 * inner + 2 * units + inner),
            bytes_accessed=tasks * block * width * 16,
            transcendentals=0,
        ),
        name="forward_pass",
    )(chosen, wq, wi, wo, wd, bq, bi, norms, out_bias, *tables, pq, pk)


def backward_kernel(
    plan, gin, xin, xarrive, qkv_all, dg_all, ctx_all, lse_all, std_all, wq_all, wi_all, wo_all, wd_all,
    gains, cosine, ahead, behind, pq, pk,
    land, dproj_all, dh_all, home, arrive, core_land, chip_land, vectors, side_q, side_h,
    wq, wi, wo, wd, gy, dg, dh, qkv, before, ctx, lse, std, dctx, dproj, dk_held, dv_held,
    kept, xrows, own, theirs, mine, core_in, low, chip_in, handed,
    weight_sem, load_sem, store_sem, keep_sem, put_home, got_home, kept_home, *sems,
):
    tasks, chips, rows, heads = plan
    line = Line(home.shape[1])
    line.set_home(handed, home, put_home, got_home, kept_home)
    size = wq.shape[1] // (3 * heads)
    scale = size**-0.5

    def place(task):
        return task + 1 - 2 * (task % 2)

    moves = Moves(
        (tasks, chips, rows), place, land, arrive, core_land, chip_land, own, theirs, low, handed, sems
    )
    first = moves.section == 0
    source = moves.section == 1
    base = jnp.where(source, 0, LAG)

    weights = [
        pltpu.make_async_copy(a, b, weight_sem.at[k])
        for k, (a, b) in enumerate(((wo_all, wo), (wd_all, wd), (wq_all, wq), (wi_all, wi)))
    ]
    for copy in weights:
        copy.start()
    for total in (vectors, side_q, side_h):
        total[...] = jnp.zeros_like(total)
    moves.greet(line)

    def valid(task):
        return (task >= 0) & (task < tasks)

    def store(k, task):
        return pltpu.make_async_copy(
            (dproj, dh)[k], (dproj_all, dh_all)[k].at[place(task)], store_sem.at[k]
        )

    def load(k, task):
        return pltpu.make_async_copy(
            (land, dg_all, qkv_all, ctx_all, lse_all, std_all)[k].at[place(task)],
            (gy, dg, qkv, ctx, lse, std)[k],
            load_sem.at[k],
        )

    def load_before(task):
        return pltpu.make_async_copy(qkv_all.at[place(task) - 1], before, load_sem.at[6])

    def spread():
        dctx[...] = dot(gy[...], wo[...], NT).astype(bf16)
        for at in range(0, wd.shape[0], 256):
            part = slice(at, at + 256)
            value = (dot(gy[...], wd[part, :], NT) * dg[:, part].astype(f32)).astype(bf16)
            dh[:, part] = value
            side_h[:, part] += jnp.sum(value.astype(f32), axis=0, keepdims=True)

    def attend_back(second):
        half = 1 if second else 0
        table = (cosine[half], ahead[half], behind[half])
        for h in range(heads):
            at = [slice((3 * h + k) * size, (3 * h + k + 1) * size) for k in range(3)]
            mid = slice(h * size, (h + 1) * size)
            q = qkv[:, at[0]]
            d_ctx = dctx[:, mid]
            logsum = lse[:, h * LANES : h * LANES + 1]
            delta = jnp.sum(d_ctx.astype(f32) * ctx[:, mid].astype(f32), axis=-1, keepdims=True)

            def pieces(held, masked):
                k, v = held[:, at[1]], held[:, at[2]]
                s = dot(q, k, NT) * scale
                if masked:
                    s = jnp.where(pq[...] >= pk[...], s, masked_score)
                p = jnp.exp(s - logsum)
                d_chance = dot(d_ctx, v, NT)
                d_scores = (p * (d_chance - delta)).astype(bf16)
                return dot(d_scores, k), dot(d_scores, q, TN), dot(p.astype(bf16), d_ctx, TN)

            dq, dk, dv = pieces(qkv, True)
            if second:
                dq_more, dk_more, dv_more = pieces(before, False)
                dq = dq + dq_more
                dk_held[:, mid] = dk_more
                dv_held[:, mid] = dv_more
            else:
                dk = dk + dk_held[:, mid]
                dv = dv + dv_held[:, mid]
            made = (turn(dq * scale, *table, -1.0), turn(dk * scale, *table, -1.0), dv)
            for k in range(3):
                value = made[k].astype(bf16)
                dproj[:, at[k]] = value
                side_q[:, at[k]] += jnp.sum(value.astype(f32), axis=0, keepdims=True)

    def merge_rows(core, result):
        at = moves.share(core)
        for column in range(0, wq.shape[0], 512):
            columns = slice(column, column + 512)
            one = dot(dproj[at, :], wq[columns, :], NT)
            two = dot(dh[at, :], wi[columns, :], NT)
            standard = std[at, columns].astype(f32)
            vectors[0:1, columns] += jnp.sum(one * standard, axis=0, keepdims=True)
            vectors[2:3, columns] += jnp.sum(two * standard, axis=0, keepdims=True)
            value = one * gains[0, :, columns] + two * gains[1, :, columns]
            result[:, columns] = value.astype(result.dtype)

    @pl.loop(0, tasks + LAG + 2)
    def _(step):
        g = step - base
        c = g - 1
        r = g - 2

        def load_rows(task, held, number):
            return pltpu.make_async_copy(held.at[number], kept.at[task % 4], load_sem.at[7])

        def load_x(task, held):
            return pltpu.make_async_copy(held.at[place(task)], xrows, load_sem.at[8])

        @when(valid(g) & source)
        def _():
            load_rows(g, gin, place(g)).start()

        @when(valid(r))
        def _():
            @when(first)
            def _():
                load_x(r, xin).start()

            @when(jnp.logical_not(first))
            def _():
                load_x(r, xarrive).start()

            reduce_first(moves, r, mine, core_in, load_sem.at[9])

        @when(valid(c))
        def _():
            gather_wait(moves, c)
            for k in range(6):
                load(k, c).start()

            @when(c % 2 == 0)
            def _():
                load_before(c).start()

            @when(c == 0)
            def _():
                weights[0].wait()
                weights[1].wait()

            @when(c >= 1)
            def _():
                for k in range(2):
                    store(k, c - 1).wait()

            load(0, c).wait()
            load(1, c).wait()
            spread()
            store(1, c).start()
            for k in range(2, 6):
                load(k, c).wait()

        @when(valid(g))
        def _():
            @when(first)
            def _():
                moves.hand(g).wait_recv()
                load_rows(g, arrive, g).start()

            load_rows(g, gin, g).wait()

            @when(g >= 1)
            def _():
                gather_free(moves, g - 1)

            own[...] = kept[g % 4]
            gather_start(moves, g, keep_sem)
            vectors[4:5, :] += jnp.sum(kept[g % 4].astype(f32), axis=0, keepdims=True)

        @when(valid(c))
        def _():
            @when(c % 2 == 0)
            def _():
                load_before(c).wait()
                attend_back(True)

            @when(c % 2 == 1)
            def _():
                attend_back(False)

            store(0, c).start()

        @when(valid(r))
        def _():
            e = reduce_second(moves, r, mine, chip_in, load_sem.at[9])
            load_x(r, xin).wait()

            @when(r >= 1)
            def _():
                line.home_each(place(r - 1), False)

                @when(source)
                def _():
                    moves.hand(r - 1).wait_send()

            standard, inverse = standardize(xrows[...])
            d_input = kept[r % 4].astype(f32) + inverse * (
                e
                - jnp.mean(e, axis=-1, keepdims=True)
                - standard * jnp.mean(e * standard, axis=-1, keepdims=True)
            )
            handed[...] = d_input.astype(bf16)

            @when(source)
            def _():
                moves.hand(r).start()

            line.home_each(place(r), True)

        @when(valid(c))
        def _():
            @when(c == 0)
            def _():
                weights[2].wait()
                weights[3].wait()

            @when(c >= 1)
            def _():
                moves.give_theirs(c - 1).wait_send()

            merge_rows(1 - moves.core, theirs)
            moves.give_theirs(c).start()
            merge_rows(moves.core, mine)

        @when(valid(g))
        def _():
            gather_pass(moves, g, keep_sem)

    drain(moves, tasks - 1)
    for k in range(2):
        store(k, tasks - 1).wait()
    for k, (side, weight) in enumerate(((side_q, wq), (side_h, wi))):
        value = side[...]
        high = value.astype(bf16)
        rest = (value - high.astype(f32)).astype(bf16)
        pair = jnp.concatenate([high, rest, jnp.zeros((14, value.shape[1]), bf16)])
        vectors[2 * k + 1 : 2 * k + 2, :] = jnp.sum(dot(pair, weight[...], NT), axis=0, keepdims=True)
    line.home_each(place(tasks - 1), False)
    line.home_wait(tasks)

    @when(source)
    def _():
        moves.hand(tasks - 1).wait_send()


def backward_pass(gin, xin, xarrive, qkv, dg, ctx, lse, std, wq, wi, wo, wd, gains, tables, pq, pk, chips, heads):
    tasks, rows, width = xin.shape
    count = lax.axis_size("ctx")
    home_sems = line_semaphores(tasks, count)[1]
    block = pq.shape[0]
    units, inner = wd.shape[0], wo.shape[0]
    anywhere = pl.BlockSpec(memory_space=pl.ANY)
    vmem = pl.BlockSpec(memory_space=pltpu.VMEM)
    shape = jax.ShapeDtypeStruct
    return pl.pallas_call(
        partial(backward_kernel, (tasks, chips, rows, heads)),
        out_shape=[
            shape((tasks, block, width), bf16),
            shape((tasks, block, 3 * inner), bf16),
            shape((tasks, block, units), bf16),
            shape((tasks // 2 * count, 2 * rows // count, width), bf16),
            shape((tasks, rows, width), bf16),
            shape((tasks, chips * rows, width), bf16),
            shape((tasks, chips - 1, rows, width), bf16),
            shape((8, width), f32),
            shape((1, 3 * inner), f32),
            shape((1, units), f32),
        ],
        in_specs=[anywhere] * 12 + [vmem] * 6,
        out_specs=[anywhere] * 7 + [vmem] * 3,
        scratch_shapes=[
            pltpu.VMEM(wq.shape, bf16),
            pltpu.VMEM(wi.shape, bf16),
            pltpu.VMEM(wo.shape, bf16),
            pltpu.VMEM(wd.shape, bf16),
            pltpu.VMEM((block, width), bf16),
            pltpu.VMEM((block, units), bf16),
            pltpu.VMEM((block, units), bf16),
            pltpu.VMEM((block, 3 * inner), bf16),
            pltpu.VMEM((block, 3 * inner), bf16),
            pltpu.VMEM((block, inner), bf16),
            pltpu.VMEM((block, heads * LANES), f32),
            pltpu.VMEM((block, width), bf16),
            pltpu.VMEM((block, inner), bf16),
            pltpu.VMEM((block, 3 * inner), bf16),
            pltpu.VMEM((block, inner), f32),
            pltpu.VMEM((block, inner), f32),
            pltpu.VMEM((4, rows, width), bf16),
            pltpu.VMEM((rows, width), bf16),
            pltpu.VMEM((rows, width), bf16),
            pltpu.VMEM((chips * rows, width), bf16),
            pltpu.VMEM((chips * rows, width), f32),
            pltpu.VMEM((chips * rows, width), bf16),
            pltpu.VMEM((chips * rows, width), bf16),
            pltpu.VMEM((chips - 1, rows, width), bf16),
            pltpu.VMEM((rows, width), bf16),
            pltpu.SemaphoreType.DMA((4,)),
            pltpu.SemaphoreType.DMA((10,)),
            pltpu.SemaphoreType.DMA((2,)),
            pltpu.SemaphoreType.DMA,
        ]
        + home_sems
        + move_semaphores(tasks, chips),
        compiler_params=pltpu.CompilerParams(
            collective_id=5, has_side_effects=True, vmem_limit_bytes=PASS_VMEM
        ),
        cost_estimate=pl.CostEstimate(
            flops=2 * tasks * block * width * (3 * inner + 2 * units + inner),
            bytes_accessed=tasks * block * width * 20,
            transcendentals=0,
        ),
        name="backward_pass",
    )(gin, xin, xarrive, qkv, dg, ctx, lse, std, wq, wi, wo, wd, gains, *tables, pq, pk)


CHUNK = 256
PIECE = 32
SKEW = 2


def reduce_kernel(
    plan, act, ctx, dproj, dhid, gy, std, gains, biases, sums, small, out, small_out, from_left, from_right,
    rhs, raw, lhs, own, inbox, outbox, stage, small_in,
    rhs_sem, raw_sem, right_sem, left_sem, final_sem, load_sem, sent, stage_left, stage_right, out_sem,
    small_sent, small_got,
):
    bounds, tasks, count, piece, skew, ring = plan
    sources = (dproj, dhid, act, ctx)
    total_chunks = bounds[-1]
    per_chunk = CHUNK // piece
    pieces = total_chunks * per_chunk
    width = gy.shape[-1]
    tile = width // per_chunk
    block = raw.shape[2]
    z = lax.axis_index("ctx")
    last = count - 1
    root = count // 2
    turn_at = max(root, last - root)
    low, high, middle = z < root, z > root, z == root

    barrier = pltpu.get_barrier_semaphore()
    for shift in range(1, count):
        pl.semaphore_signal(
            barrier,
            inc=1,
            device_id={"ctx": lax.rem(z + shift, count)},
            device_id_type=pl.DeviceIdType.MESH,
        )

    def small_copy(source, target):
        return pltpu.make_async_remote_copy(
            src_ref=small,
            dst_ref=small_in.at[source],
            send_sem=small_sent.at[target],
            recv_sem=small_got.at[source],
            device_id={"ctx": target},
            device_id_type=pl.DeviceIdType.MESH,
        )

    def rhs_copy(k):
        return pltpu.make_async_copy((std, gy)[k].at[pl.ds(0, tasks)], rhs.at[k], rhs_sem.at[k])

    def each_source(chunk, act_on):
        for g, source in enumerate(sources):

            @pl.when((chunk >= bounds[g]) & (chunk < bounds[g + 1]))
            def _(g=g, source=source):
                column = pl.multiple_of((chunk - bounds[g]) * CHUNK, CHUNK)
                act_on(
                    pltpu.make_async_copy(
                        source.at[pl.ds(0, tasks), :, pl.ds(column, CHUNK)],
                        raw.at[chunk % 2],
                        raw_sem.at[chunk % 2],
                    )
                )

    def take(chunk):
        each_source(chunk, lambda copy: copy.wait())
        for k in range(tasks):
            lhs[:, k * block : (k + 1) * block] = raw[chunk % 2, k].T
        each_source(chunk + 1, lambda copy: copy.start())

    def multiply(chunk, part):
        second = jnp.where(chunk >= bounds[2], 1, 0)
        group = second + jnp.where(chunk >= bounds[1], 1, 0)
        columns = pl.ds(pl.multiple_of(part * tile, tile), tile)
        value = dot(lhs[:, :block], rhs[second, 0, :, columns])
        for k in range(1, tasks):
            value = value + dot(lhs[:, k * block : (k + 1) * block], rhs[second, k, :, columns])
        row = pl.multiple_of(chunk * CHUNK, CHUNK)
        value = value * gains[group, :, columns] + sums[pl.ds(row, CHUNK), :] * biases[group, :, columns]
        own[chunk % ring, :, columns] = value.astype(bf16)

    def rows_of(index):
        return pl.ds(pl.multiple_of(index * piece, piece), piece)

    def own_piece(index):
        inner = pl.multiple_of((index % per_chunk) * piece, piece)
        return own[(index // per_chunk) % ring, pl.ds(inner, piece), :]

    def remote(source, target_rows, send_sem, recv_sem, target):
        return pltpu.make_async_remote_copy(
            src_ref=source,
            dst_ref=target_rows,
            send_sem=send_sem,
            recv_sem=recv_sem,
            device_id={"ctx": target},
            device_id_type=pl.DeviceIdType.MESH,
        )

    def inward(index, right):
        landing, arrived, target = (from_left, right_sem, z + 1) if right else (from_right, left_sem, z - 1)
        return remote(
            outbox.at[index % 2], landing.at[rows_of(index)], sent.at[index % 2], arrived.at[index], target
        )

    def announce(index, right):
        return remote(
            stage.at[index % 2],
            out.at[rows_of(index)],
            (stage_right if right else stage_left).at[index % 2],
            final_sem.at[index],
            z + 1 if right else z - 1,
        )

    def onward(index, right):
        return remote(
            out.at[rows_of(index)],
            out.at[rows_of(index)],
            sent.at[2 + index % 2],
            final_sem.at[index],
            z + 1 if right else z - 1,
        )

    def load(index, right):
        landing = from_left if right else from_right
        return pltpu.make_async_copy(
            landing.at[rows_of(index)], inbox.at[0 if right else 1], load_sem.at[0 if right else 1]
        )

    def valid(index):
        return (index >= 0) & (index < pieces)

    def side(step, right):
        mine = low if right else high
        hops = z if right else last - z
        inner = step - hops * skew
        comes = hops > 0

        @pl.when(mine & valid(inner) & comes)
        def _():
            inward(inner, right).wait_recv()
            load(inner, right).start()

        @pl.when(mine & valid(inner))
        def _():
            @pl.when(inner >= 2)
            def _():
                inward(inner - 2, right).wait_send()

            @pl.when(comes)
            def _():
                load(inner, right).wait()
                value = own_piece(inner).astype(f32) + inbox[0 if right else 1].astype(f32)
                outbox[inner % 2] = value.astype(bf16)

            @pl.when(jnp.logical_not(comes))
            def _():
                outbox[inner % 2] = own_piece(inner)

            inward(inner, right).start()

        away = root - z if right else z - root
        outer = step - (turn_at + away) * skew

        @pl.when(mine & valid(outer))
        def _():
            onward(outer, not right).wait_recv()

            @pl.when(comes)
            def _():
                @pl.when(outer >= 2)
                def _():
                    onward(outer - 2, not right).wait_send()

                onward(outer, not right).start()

    def out_copy(index):
        return pltpu.make_async_copy(stage.at[index % 2], out.at[rows_of(index)], out_sem.at[index % 2])

    def stage_done(index):
        out_copy(index).wait()
        announce(index, False).wait_send()
        if root < last:
            announce(index, True).wait_send()

    def centre(step):
        index = step - turn_at * skew

        @pl.when(middle & valid(index))
        def _():
            inward(index, True).wait_recv()
            load(index, True).start()
            if root < last:
                inward(index, False).wait_recv()
                load(index, False).start()

            @pl.when(index >= 2)
            def _():
                stage_done(index - 2)

            load(index, True).wait()
            value = own_piece(index).astype(f32) + inbox[0].astype(f32)
            if root < last:
                load(index, False).wait()
                value = value + inbox[1].astype(f32)
            stage[index % 2] = value.astype(bf16)
            announce(index, False).start()
            if root < last:
                announce(index, True).start()
            out_copy(index).start()

    rhs_copy(0).start()
    each_source(0, lambda copy: copy.start())
    rhs_copy(1).start()
    take(0)
    rhs_copy(0).wait()

    @pl.loop(0, per_chunk)
    def _(part):
        multiply(0, part)

    pl.semaphore_wait(barrier, count - 1)
    small_in[z] = small[...]
    for shift in range(1, count):
        small_copy(z, lax.rem(z + shift, count)).start()

    @pl.loop(0, pieces + (turn_at + max(root, last - root)) * skew)
    def _(step):
        side(step, True)
        side(step, False)
        centre(step)
        chunk, part = step // per_chunk + 1, step % per_chunk

        @pl.when(chunk < total_chunks)
        def _():
            @pl.when(part == 0)
            def _():
                take(chunk)

                @pl.when(chunk == bounds[2])
                def _():
                    rhs_copy(1).wait()

            multiply(chunk, part)

    for shift in range(1, count):
        other = lax.rem(z + shift, count)
        small_copy(z, other).wait_send()
        small_copy(other, other).wait_recv()
    value = small_in[0]
    for k in range(1, count):
        value = value + small_in[k]
    small_out[...] = value
    for back in (2, 1):
        for right in (True, False):

            @pl.when(low if right else high)
            def _(right=right, back=back):
                inward(pieces - back, right).wait_send()

                @pl.when((z > 0) & (z < last))
                def _():
                    onward(pieces - back, not right).wait_send()

        @pl.when(middle)
        def _(back=back):
            stage_done(pieces - back)


def reduce_gradients(act, ctx, dproj, dhid, gy, std, gains, biases, sums, small, tasks):
    count = lax.axis_size("ctx")
    block, width = gy.shape[1:]
    bounds = [0]
    for source in (dproj, dhid, act, ctx):
        bounds.append(bounds[-1] + source.shape[2] // CHUNK)
    total = bounds[-1] * CHUNK
    pieces = total // PIECE
    ring = count // 2 * SKEW // (CHUNK // PIECE) + 3
    plan = (tuple(bounds), tasks, count, PIECE, SKEW, ring)
    anywhere = pl.BlockSpec(memory_space=pl.ANY)
    vmem = pl.BlockSpec(memory_space=pltpu.VMEM)
    result = jax.ShapeDtypeStruct((total, width), bf16)
    out, small_out, _, _ = pl.pallas_call(
        partial(reduce_kernel, plan),
        out_shape=[result, jax.ShapeDtypeStruct(small.shape, f32), result, result],
        in_specs=[anywhere] * 6 + [vmem] * 4,
        out_specs=[anywhere, vmem, anywhere, anywhere],
        scratch_shapes=[
            pltpu.VMEM((2, tasks, block, width), bf16),
            pltpu.VMEM((2, tasks, block, CHUNK), bf16),
            pltpu.VMEM((CHUNK, tasks * block), bf16),
            pltpu.VMEM((ring, CHUNK, width), bf16),
            pltpu.VMEM((2, PIECE, width), bf16),
            pltpu.VMEM((2, PIECE, width), bf16),
            pltpu.VMEM((2, PIECE, width), bf16),
            pltpu.VMEM((count,) + small.shape, f32),
            pltpu.SemaphoreType.DMA((2,)),
            pltpu.SemaphoreType.DMA((2,)),
            pltpu.SemaphoreType.DMA((pieces,)),
            pltpu.SemaphoreType.DMA((pieces,)),
            pltpu.SemaphoreType.DMA((pieces,)),
            pltpu.SemaphoreType.DMA((2,)),
            pltpu.SemaphoreType.DMA((4,)),
            pltpu.SemaphoreType.DMA((2,)),
            pltpu.SemaphoreType.DMA((2,)),
            pltpu.SemaphoreType.DMA((2,)),
            pltpu.SemaphoreType.DMA((count,)),
            pltpu.SemaphoreType.DMA((count,)),
        ],
        compiler_params=pltpu.CompilerParams(
            collective_id=7, has_side_effects=True, vmem_limit_bytes=60 * 1024 * 1024
        ),
        cost_estimate=pl.CostEstimate(
            flops=2 * total * width * tasks * block,
            bytes_accessed=8 * total * width,
            transcendentals=0,
        ),
        name="reduce_gradients",
    )(act, ctx, dproj, dhid, gy, std, gains, biases, sums, small)
    return out, small_out


def turned_kernel(part, out):
    out[...] = part[...].astype(f32).T


def turned(total, start, count):
    width = total.shape[1]
    return pl.pallas_call(
        turned_kernel,
        out_shape=jax.ShapeDtypeStruct((width, count), f32),
        grid=(count // CHUNK,),
        in_specs=[pl.BlockSpec((CHUNK, width), lambda i: (start // CHUNK + i, 0))],
        out_specs=pl.BlockSpec((width, CHUNK), lambda i: (0, i)),
        compiler_params=pltpu.CompilerParams(vmem_limit_bytes=32 * 1024 * 1024),
        name="turned",
    )(total)


def turned_heads_kernel(heads, part, out):
    size = part.shape[0] // heads
    for h in range(heads):
        out[:, h, :] = part[h * size : (h + 1) * size, :].astype(f32).T


def turned_heads(total, start, count, heads):
    width = total.shape[1]
    return pl.pallas_call(
        partial(turned_heads_kernel, heads),
        out_shape=jax.ShapeDtypeStruct((width, heads, count // heads), f32),
        grid=(width // CHUNK,),
        in_specs=[pl.BlockSpec((count, CHUNK), lambda i: (start // count, i))],
        out_specs=pl.BlockSpec((CHUNK, heads, count // heads), lambda i: (i, 0, 0)),
        compiler_params=pltpu.CompilerParams(vmem_limit_bytes=32 * 1024 * 1024),
        name="turned_heads",
    )(total)


def body(
    inputs,
    out_grads,
    norm1_gain,
    norm1_bias,
    norm2_gain,
    norm2_bias,
    w_qkv,
    b_qkv,
    w_out,
    b_out,
    input_projection,
    input_bias_vector,
    down_projection,
    b_down,
):
    ctx_count = lax.axis_size("ctx")
    tensor = lax.axis_size("tensor")
    micro, _, rows, seqs, width = inputs.shape
    heads = w_qkv.shape[2]
    head_cols = w_qkv.shape[3]
    first = lax.axis_index("section") == 0
    per_device = micro * seqs // ctx_count
    blocks = ctx_count // 2
    tasks = 2 * per_device

    chosen = jnp.where(first, inputs[:, 0], out_grads[:, 0])
    chosen = chosen.transpose(0, 2, 1, 3).reshape(per_device, ctx_count, rows, width)

    wq = w_qkv[0].reshape(width, heads * head_cols)
    wi = input_projection[0]
    wo = w_out[0].reshape(-1, width)
    wd = down_projection[0]
    gain_one, bias_one, gain_two, bias_two = norm1_gain[0], norm1_bias[0], norm2_gain[0], norm2_bias[0]
    norms = jnp.stack([gain_one, bias_one, gain_two, bias_two], axis=1)
    out_bias = (b_out[0] + b_down[0])[None]

    relative, tables = position_tables(None, blocks, rows, tensor)
    places_q, places_k = relative[:, None], relative[None, :]

    chips = tensor // 2
    stacked_tables = [jnp.stack(pair) for pair in zip(*tables)]
    std_all, qkv, act_all, dg_all, ctx_all, lse_all, chosen_rows, states, arrive, _, _ = forward_pass(
        chosen,
        wq,
        wi,
        wo,
        wd,
        b_qkv[0].reshape(1, -1),
        input_bias_vector,
        norms,
        out_bias,
        stacked_tables,
        places_q,
        places_k,
        chips,
        heads,
    )
    gains = jnp.stack([gain_one, gain_two])[:, None]
    gy_all, dproj_all, dh_all, dx_home, _, _, _, vectors, side_q, side_h = backward_pass(
        chosen_rows,
        chosen_rows,
        arrive,
        qkv,
        dg_all,
        ctx_all,
        lse_all,
        std_all,
        wq,
        wi,
        wo,
        wd,
        gains,
        stacked_tables,
        places_q,
        places_k,
        chips,
        heads,
    )
    vectors = vectors[:5]

    d_b_qkv, d_b_in = side_q[0], side_h[0]
    units, inner = wd.shape[0], wo.shape[0]
    sums = jnp.concatenate([d_b_qkv, d_b_in, jnp.zeros((units + inner,), f32)])[:, None]
    gains = jnp.stack([gain_one, gain_two, jnp.ones_like(gain_one)])[:, None]
    biases = jnp.stack([bias_one, bias_two, jnp.zeros_like(bias_one)])[:, None]
    mask = 1
    while mask < tensor:
        vectors = vectors + lax.ppermute(vectors, "tensor", [(k, k ^ mask) for k in range(tensor)])
        mask *= 2
    sides = jnp.concatenate([d_b_qkv, d_b_in])
    side_rows = -(-sides.shape[0] // width)
    small = jnp.zeros((-(-(5 + side_rows) // 8) * 8, width), f32)
    small = small.at[:5].set(vectors)
    small = small.at[5 : 5 + side_rows].set(
        jnp.pad(sides, (0, side_rows * width - sides.shape[0])).reshape(side_rows, width)
    )
    summed, small = reduce_gradients(
        act_all, ctx_all, dproj_all, dh_all, gy_all, std_all, gains, biases, sums, small, tasks
    )
    columns = wq.shape[1]
    vectors = small[:5]
    sides = small[5 : 5 + side_rows].reshape(-1)
    d_b_qkv, d_b_in = sides[: d_b_qkv.shape[0]], sides[d_b_qkv.shape[0] : sides.shape[0]]
    d_b_in = d_b_in[: wi.shape[1]]
    d_w_qkv = turned_heads(summed, 0, columns, heads)
    d_w_in = turned(summed, columns, units)
    d_w_down = summed[columns + units : columns + 2 * units].astype(f32)
    d_w_out = summed[columns + 2 * units :].astype(f32)

    def homeward(pieces):
        return pieces.reshape(micro, seqs, rows, width).transpose(0, 2, 1, 3)[None, :, None]

    states = homeward(states)
    input_grads = homeward(dx_home).astype(f32)
    return (
        states,
        input_grads,
        vectors[0][None],
        vectors[1][None],
        vectors[2][None],
        vectors[3][None],
        d_w_qkv.reshape(w_qkv.shape),
        d_b_qkv.reshape(b_qkv.shape),
        d_w_out.reshape(w_out.shape),
        vectors[4][None],
        d_w_in[None],
        d_b_in[None],
        d_w_down[None],
        vectors[4][None],
    )


def solution(mesh):
    return jax.shard_map(
        body,
        mesh=mesh,
        in_specs=(
            P(None, "ctx", "tensor", None, None),
            P(None, "ctx", "tensor", None, None),
            P("section", None),
            P("section", None),
            P("section", None),
            P("section", None),
            P("section", None, "tensor", None),
            P("section", "tensor", None),
            P("section", "tensor", None, None),
            P("section", None),
            P("section", None, "tensor"),
            P("section", "tensor"),
            P("section", "tensor", None),
            P("section", None),
        ),
        out_specs=(
            P("section", None, "ctx", "tensor", None, None),
            P("section", None, "ctx", "tensor", None, None),
            P("section", None),
            P("section", None),
            P("section", None),
            P("section", None),
            P("section", None, "tensor", None),
            P("section", "tensor", None),
            P("section", "tensor", None, None),
            P("section", None),
            P("section", None, "tensor"),
            P("section", "tensor"),
            P("section", "tensor", None),
            P("section", None),
        ),
        check_vma=False,
    )
```

```python
from functools import partial

import jax
import jax.numpy as jnp
from jax import lax
from jax.experimental import pallas as pl
from jax.experimental.pallas import tpu as pltpu
from jax.sharding import PartitionSpec as P

ROT = 64
LAG = 3
LANES = 128
epsilon = 1e-05
masked_score = -1e30
f32 = jnp.float32
bf16 = jnp.bfloat16
NT = (((1,), (1,)), ((), ()))
TN = (((0,), (0,)), ((), ()))
NN = (((1,), (0,)), ((), ()))
PASS_VMEM = 62 * 1024 * 1024


def dot(a, b, dims=NN):
    return lax.dot_general(a, b, dims, preferred_element_type=f32)


def standardize(rows):
    values = rows.astype(f32)
    average = jnp.mean(values, axis=-1, keepdims=True)
    centred = values - average
    inverse = lax.rsqrt(jnp.mean(centred * centred, axis=-1, keepdims=True) + epsilon)
    return centred * inverse, inverse


def position_tables(section_rows, blocks, rows, tensor):
    half = ROT // 2
    frequency = 1.0 / 10000.0 ** (jnp.arange(0, ROT, 2, dtype=f32) / ROT)
    core, chip, c, i = jnp.meshgrid(
        jnp.arange(2), jnp.arange(tensor // 2), jnp.arange(blocks), jnp.arange(rows), indexing="ij"
    )
    relative = (c * (rows * tensor) + (chip * 2 + core) * rows + i).reshape(-1).astype(jnp.int32)
    tables = []
    for part in range(2):
        places = (relative + part * blocks * rows * tensor).astype(f32)
        angles = places[:, None] * frequency[None, :]
        cosine, sine = jnp.cos(angles), jnp.sin(angles)
        none = jnp.zeros_like(sine)
        rest = jnp.zeros((relative.shape[0], LANES - ROT), f32)
        tables.append(
            (
                jnp.concatenate([cosine, cosine, rest + 1.0], axis=-1),
                jnp.concatenate([-sine, none, rest], axis=-1),
                jnp.concatenate([none, sine, rest], axis=-1),
            )
        )
    return relative, tables


def turn(values, cosine, ahead, behind, sign):
    half = ROT // 2
    lead = values[:, :LANES]
    turned = pltpu.roll(lead, LANES - half, 1) * ahead + pltpu.roll(lead, half, 1) * behind
    return jnp.concatenate([lead * cosine + sign * turned, values[:, LANES:]], axis=1)


class Moves:
    def __init__(self, plan, land, arrive, core_land, chip_land, theirs, low, handed, sems):
        self.tasks, self.chips, self.rows = plan
        self.land, self.arrive, self.core_land, self.chip_land = land, arrive, core_land, chip_land
        self.theirs, self.low, self.handed = theirs, low, handed
        self.slots = land.shape[0]
        (
            self.got_chip, self.got_core, self.got_theirs, self.got_low, self.got_hand,
            self.put_chip, self.put_core, self.put_theirs, self.put_low, self.put_hand,
        ) = sems
        self.section = lax.axis_index("section")
        self.index = lax.axis_index("tensor")
        self.total = 2 * self.chips
        self.chip, self.core = self.index // 2, self.index % 2
        self.mate = self.chip * 2 + 1 - self.core

    def mate_on(self, shift):
        return lax.rem(self.index + 2 * shift, self.total)

    def part(self, member):
        at = (member % 2) * self.chips + member // 2
        return pl.ds(pl.multiple_of(at * self.rows, self.rows), self.rows)

    def share(self, core):
        size = self.chips * self.rows
        return pl.ds(pl.multiple_of(core * size, size), size)

    def of_chip(self, chip):
        return pl.ds(pl.multiple_of(chip * self.rows, self.rows), self.rows)

    def remote(self, source, target, sent, arrived, **device):
        return pltpu.make_async_remote_copy(
            src_ref=source,
            dst_ref=target,
            send_sem=sent,
            recv_sem=arrived,
            device_id=device,
            device_id_type=pl.DeviceIdType.MESH,
        )

    def greet(self, line):
        barrier = pltpu.get_barrier_semaphore()
        peers = [{"section": 1 - self.section}, {"tensor": self.mate}]
        peers += [{"ctx": other} for other in line.others()]
        peers += [{"tensor": self.mate_on(shift)} for shift in range(1, self.chips)]
        for peer in peers:
            pl.semaphore_signal(barrier, inc=1, device_id=peer, device_id_type=pl.DeviceIdType.MESH)
        pl.semaphore_wait(barrier, len(peers))

    def gather_chip(self, task, shift, member=None):
        rows = self.land.at[task % self.slots, self.part(self.index if member is None else member)]
        return self.remote(
            rows,
            rows,
            self.put_chip.at[shift - 1],
            self.got_chip.at[task, shift - 1],
            tensor=self.mate_on(shift),
        )

    def gather_chip_in(self, task, shift):
        return self.gather_chip(task, shift, lax.rem(self.index + self.total - 2 * shift, self.total))

    def gather_core(self, task, shift, member=None):
        if member is None:
            member = lax.rem(self.index + self.total - 2 * shift, self.total)
        rows = self.land.at[task % self.slots, self.part(member)]
        return self.remote(
            rows,
            rows,
            self.put_core.at[shift],
            self.got_core.at[task, shift],
            tensor=self.mate,
        )

    def gather_core_in(self, task, shift):
        return self.gather_core(task, shift, lax.rem(self.mate + self.total - 2 * shift, self.total))

    def give_theirs(self, task):
        return self.remote(
            self.theirs, self.core_land.at[task % 2], self.put_theirs, self.got_theirs.at[task], tensor=self.mate
        )

    def give_low(self, task, shift):
        return self.remote(
            self.low.at[self.of_chip(lax.rem(self.chip + shift, self.chips))],
            self.chip_land.at[task % 2, shift - 1],
            self.put_low.at[shift - 1],
            self.got_low.at[task, shift - 1],
            tensor=self.mate_on(shift),
        )

    def hand(self, task):
        return self.remote(
            self.handed.at[task % 2],
            self.arrive.at[task],
            self.put_hand.at[task % 2],
            self.got_hand.at[task],
            section=1 - self.section,
        )


class Line:
    def __init__(self, rows):
        self.rows = rows
        self.count = lax.axis_size("ctx")
        self.blocks = self.count // 2
        self.z = lax.axis_index("ctx")

    def others(self):
        return [lax.rem(self.z + shift, self.count) for shift in range(1, self.count)]

    def remote(self, source, target, sent, arrived, device):
        return pltpu.make_async_remote_copy(
            src_ref=source,
            dst_ref=target,
            send_sem=sent,
            recv_sem=arrived,
            device_id={"ctx": device},
            device_id_type=pl.DeviceIdType.MESH,
        )

    def block(self, at):
        return pl.ds(pl.multiple_of(at * self.rows, self.rows), self.rows)

    def set_in(self, chosen, landed, put, got, kept):
        self.chosen, self.landed, self.put_in, self.got_in, self.kept_in = chosen, landed, put, got, kept

    def bring(self, j, shift, source=None):
        source = self.z if source is None else source
        half = source // self.blocks
        return self.remote(
            self.chosen.at[j, lax.rem(self.z + shift, self.count)],
            self.landed.at[2 * j + half, self.block(source - half * self.blocks)],
            self.put_in.at[j, shift - 1],
            self.got_in.at[j, source],
            lax.rem(self.z + shift, self.count),
        )

    def bring_own(self, j):
        half = self.z // self.blocks
        return pltpu.make_async_copy(
            self.chosen.at[j, self.z],
            self.landed.at[2 * j + half, self.block(self.z - half * self.blocks)],
            self.kept_in.at[j],
        )

    def bring_start(self, j):
        for shift in range(1, self.count):
            self.bring(j, shift).start()
        self.bring_own(j).start()

    def bring_wait(self, task):
        j, half = task // 2, task % 2
        for k in range(self.blocks):
            source = half * self.blocks + k

            @pl.when(source != self.z)
            def _():
                self.bring(j, 1, source).wait_recv()

            @pl.when(source == self.z)
            def _():
                self.bring_own(j).wait()

    def bring_done(self, count):
        for j in range(count):
            for shift in range(1, self.count):
                self.bring(j, shift).wait_send()


class Home:
    def __init__(self, line, source, home, put, got, kept):
        self.line, self.source, self.home = line, source, home
        self.put, self.got, self.kept = put, got, kept

    def take(self, task, k, sender=None):
        line = self.line
        sender = line.z if sender is None else sender
        return line.remote(
            self.source(task).at[pl.ds(k * line.rows, line.rows)],
            self.home.at[(task // 2) * line.count + sender],
            self.put.at[task, k],
            self.got.at[task // 2, sender],
            (task % 2) * line.blocks + k,
        )

    def keep(self, task, k):
        line = self.line
        return pltpu.make_async_copy(
            self.source(task).at[pl.ds(k * line.rows, line.rows)],
            self.home.at[(task // 2) * line.count + line.z],
            self.kept.at[task],
        )

    def each(self, task, begin):
        line = self.line
        for k in range(line.blocks):
            there = (task % 2) * line.blocks + k

            @pl.when(there != line.z)
            def _():
                copy = self.take(task, k)
                copy.start() if begin else copy.wait_send()

            @pl.when(there == line.z)
            def _():
                copy = self.keep(task, k)
                copy.start() if begin else copy.wait()

    def wait(self, tasks):
        for j in range(tasks // 2):
            for other in self.line.others():
                self.take(2 * j, 0, other).wait_recv()


def line_semaphores(tasks, count):
    dma = pltpu.SemaphoreType.DMA
    half = tasks // 2
    return [dma((half, count - 1)), dma((half, count)), dma((half,))], [
        dma((tasks, count // 2)),
        dma((half, count)),
        dma((tasks,)),
    ]


class Early:
    def __init__(self, moves, source, gathered, got_chip, got_core, put_chip, put_core, kept):
        self.moves, self.source, self.gathered = moves, source, gathered
        self.got_chip, self.got_core, self.put_chip, self.put_core = got_chip, got_core, put_chip, put_core
        self.kept = kept

    def at(self, task, member):
        return self.gathered.at[task, self.moves.part(member)]

    def behind(self, start, shift):
        return lax.rem(start + self.moves.total - 2 * shift, self.moves.total)

    def chip(self, task, shift, member=None):
        member = self.moves.index if member is None else member
        return self.moves.remote(
            self.source.at[task],
            self.at(task, member),
            self.put_chip.at[task, shift - 1],
            self.got_chip.at[task, shift - 1],
            tensor=self.moves.mate_on(shift),
        )

    def core(self, task, shift, member=None):
        member = self.behind(self.moves.index, shift) if member is None else member
        rows = self.at(task, member)
        return self.moves.remote(
            self.source.at[task] if shift == 0 else rows,
            rows,
            self.put_core.at[task, shift],
            self.got_core.at[task, shift],
            tensor=self.moves.mate,
        )

    def keep(self, task):
        return pltpu.make_async_copy(
            self.source.at[task], self.at(task, self.moves.index), self.kept.at[task]
        )

    def start(self, task):
        for shift in range(1, self.moves.chips):
            self.chip(task, shift).start()
        self.core(task, 0).start()
        self.keep(task).start()

    def hand_on(self, task):
        for shift in range(1, self.moves.chips):
            self.chip(task, shift, self.behind(self.moves.index, shift)).wait_recv()
            self.core(task, shift).start()

    def finish(self, task):
        self.keep(task).wait()
        for shift in range(1, self.moves.chips):
            self.chip(task, shift).wait_send()
        for shift in range(self.moves.chips):
            self.core(task, shift).wait_send()
            self.core(task, shift, self.behind(self.moves.mate, shift)).wait_recv()


def early_semaphores(tasks, chips):
    dma = pltpu.SemaphoreType.DMA
    return [dma((tasks, chips - 1)), dma((tasks, chips)), dma((tasks, chips - 1)), dma((tasks, chips)), dma((tasks,))]


def opposite(task):
    return task + 1 - 2 * (task % 2)


def reduce_first(moves, task, mine):
    moves.give_theirs(task).wait_recv()

    @pl.when(task >= 1)
    def _():
        for shift in range(1, moves.chips):
            moves.give_low(task - 1, shift).wait_send()

    value = mine[...] + moves.core_land[task % 2].astype(f32)
    mine[...] = value
    moves.low[...] = value.astype(bf16)
    for shift in range(1, moves.chips):
        moves.give_low(task, shift).start()


def reduce_second(moves, task, mine):
    value = mine[moves.of_chip(moves.chip), :]
    for shift in range(1, moves.chips):
        moves.give_low(task, shift).wait_recv()
        value = value + moves.chip_land[task % 2, shift - 1].astype(f32)
    return value


def gather_start(moves, task, value):
    moves.land[task % moves.slots, moves.part(moves.index), :] = value
    for shift in range(1, moves.chips):
        moves.gather_chip(task, shift).start()
    moves.gather_core(task, 0).start()


def gather_free(moves, task):
    for shift in range(1, moves.chips):
        moves.gather_chip(task, shift).wait_send()
    for shift in range(moves.chips):
        moves.gather_core(task, shift).wait_send()


def gather_pass(moves, task):
    for shift in range(1, moves.chips):
        moves.gather_chip_in(task, shift).wait_recv()
        moves.gather_core(task, shift).start()


def gather_wait(moves, task):
    for shift in range(moves.chips):
        moves.gather_core_in(task, shift).wait_recv()


def drain(moves, task):
    for shift in range(1, moves.chips):
        moves.give_low(task, shift).wait_send()
    moves.give_theirs(task).wait_send()


def when(condition):
    return pl.when(condition)


def forward_kernel(
    plan, chosen, wq_all, wi_all, wo_all, wd_all, bq_in, bi_in, norms, out_bias, cosine, ahead, behind, pq, pk,
    std_all, qkv_all, act_all, dg_all, ctx_all, lse_all, xin, states, arrive, early_all,
    wq, wi, wo, wd, bq, bi, land, qkv, act, dg, ctx, lse, kept, theirs, mine, core_land, low, chip_land, handed,
    weight_sem, load_sem, store_sem, state_sem, put_in, got_in, kept_in,
    early_a, early_b, early_c, early_d, early_e, *sems,
):
    tasks, chips, rows, heads = plan
    line = Line(chosen.shape[2])
    line.set_in(chosen, xin, put_in, got_in, kept_in)
    size = wq.shape[1] // (3 * heads)
    moves = Moves((tasks, chips, rows), land, arrive, core_land, chip_land, theirs, low, handed, sems)
    first = moves.section == 0
    base = jnp.where(first, 0, LAG)
    early = Early(moves, xin, early_all, early_a, early_b, early_c, early_d, early_e)
    early_count = min(tasks, 2 * (LAG - 1))

    weights = [
        pltpu.make_async_copy(a, b, weight_sem.at[k])
        for k, (a, b) in enumerate(((wq_all, wq), (wi_all, wi), (wo_all, wo), (wd_all, wd)))
    ]
    moves.greet(line)
    line.bring_start(0)
    for copy in weights:
        copy.start()

    @when(jnp.logical_not(first))
    def _():
        for j in range(1, tasks // 2):
            line.bring_start(j)

    def valid(task):
        return (task >= 0) & (task < tasks)

    def keep_state(task):
        return pltpu.make_async_copy(handed.at[task % 2], states.at[task], state_sem.at[task % 2])

    def fold(weight, bias_in, bias, gain_column):
        bias[...] = bias_in[...]
        step = 256

        @pl.loop(0, weight.shape[0] // step)
        def _(k):
            at = pl.ds(pl.multiple_of(k * step, step), step)
            value = weight[at, :].astype(f32)
            gain = norms[at, gain_column : gain_column + 1]
            shift = norms[at, gain_column + 1 : gain_column + 2]
            bias[...] += jnp.sum(value * shift, axis=0, keepdims=True)
            weight[at, :] = (value * gain).astype(bf16)

    def store(k, task):
        return pltpu.make_async_copy(
            (qkv.at[task % 2], act, dg, ctx, lse, land.at[task % 3])[k],
            (qkv_all, act_all, dg_all, ctx_all, lse_all, std_all)[k].at[task],
            store_sem.at[k],
        )

    def project(task):
        half = task % 2
        table = (cosine[half], ahead[half], behind[half])
        for h in range(heads):
            for k in range(3):
                columns = slice((3 * h + k) * size, (3 * h + k + 1) * size)
                z = dot(land[task % 3], wq[:, columns]) + bq[:, columns]
                if k < 2:
                    z = turn(z, *table, 1.0)
                qkv[half, :, columns] = z.astype(bf16)

    def attend(task, second):
        half = 1 if second else 0
        scale = size**-0.5
        for h in range(heads):
            at = [slice((3 * h + k) * size, (3 * h + k + 1) * size) for k in range(3)]
            q = qkv[half, :, at[0]]
            s = dot(q, qkv[half, :, at[1]], NT) * scale
            s = jnp.where(pq[...] >= pk[...], s, masked_score)
            peak = jnp.max(s, axis=-1, keepdims=True)
            if second:
                sp = dot(q, qkv[0, :, at[1]], NT) * scale
                peak = jnp.maximum(peak, jnp.max(sp, axis=-1, keepdims=True))
            p = jnp.exp(s - peak)
            total = jnp.sum(p, axis=-1, keepdims=True)
            if second:
                pp = jnp.exp(sp - peak)
                total = total + jnp.sum(pp, axis=-1, keepdims=True)
            share = 1.0 / total
            value = dot((p * share).astype(bf16), qkv[half, :, at[2]])
            if second:
                value = value + dot((pp * share).astype(bf16), qkv[0, :, at[2]])
            ctx[:, h * size : (h + 1) * size] = value.astype(bf16)
            lse[:, h * LANES : (h + 1) * LANES] = jnp.broadcast_to(
                peak + jnp.log(total), (q.shape[0], LANES)
            )

    def expand(task):
        for at in range(0, wi.shape[1], 256):
            columns = slice(at, at + 256)
            h = dot(land[task % 3], wi[:, columns]) + bi[:, columns]
            phi = 0.5 + 0.5 * lax.erf(h * (0.5**0.5))
            density = jnp.exp(h * h * -0.5) * 0.3989422804014327
            act[:, columns] = (h * phi).astype(bf16)
            dg[:, columns] = (phi + h * density).astype(bf16)

    def branch_rows(core, result):
        at = moves.share(core)
        for column in range(0, wo.shape[1], 512):
            columns = slice(column, column + 512)
            value = dot(ctx[at, :], wo[:, columns]) + dot(act[at, :], wd[:, columns])
            result[:, columns] = value.astype(result.dtype)

    @pl.loop(0, tasks + LAG + 2)
    def _(step):
        g = step - base
        c = g - 1
        r = g - 2

        def load_rows(task, held):
            return pltpu.make_async_copy(held.at[task], kept.at[task % 3], load_sem)

        @when(first & (step % 2 == 0) & (step // 2 + 1 < tasks // 2))
        def _():
            line.bring_start(step // 2 + 1)

        @when(first & (step < tasks))
        def _():
            line.bring_wait(step)

        for k in range(2):
            late = 2 * (step - 1) + k

            @when(jnp.logical_not(first) & (late >= 0) & (late < early_count))
            def _(late=late):
                early.hand_on(opposite(late))

        for k in range(2):
            fresh = 2 * step + k

            @when(jnp.logical_not(first) & (fresh < early_count))
            def _(fresh=fresh):
                line.bring_wait(opposite(fresh))
                early.start(opposite(fresh))

        @when(valid(g) & first)
        def _():
            load_rows(g, xin).start()

        @when(valid(c))
        def _():
            gather_wait(moves, c)

            @when(c >= 1)
            def _():
                for k in range(6):
                    store(k, c - 1).wait()

            store(5, c).start()
            project(c)
            store(0, c).start()

        @when(valid(g) & jnp.logical_not(first))
        def _():
            moves.hand(g).wait_recv()
            load_rows(g, arrive).start()

        @when(valid(c))
        def _():
            @when(c % 2 == 0)
            def _():
                attend(c, False)

            @when(c % 2 == 1)
            def _():
                attend(c, True)

            store(3, c).start()
            store(4, c).start()

        @when(valid(g))
        def _():
            load_rows(g, xin).wait()

            @when(g >= 1)
            def _():
                gather_free(moves, g - 1)

            gather_start(moves, g, standardize(kept[g % 3])[0].astype(bf16))

        @when(step == 0)
        def _():
            weights[0].wait()
            fold(wq, bq_in, bq, 0)
            weights[1].wait()
            fold(wi, bi_in, bi, 2)
            weights[2].wait()
            weights[3].wait()

        @when(valid(c))
        def _():
            expand(c)
            store(1, c).start()
            store(2, c).start()

        @when(valid(r))
        def _():
            value = reduce_second(moves, r, mine)

            @when(r >= 2)
            def _():
                keep_state(r - 2).wait()

                @when(first)
                def _():
                    moves.hand(r - 2).wait_send()

            handed[r % 2] = (kept[r % 3].astype(f32) + value + out_bias[...]).astype(bf16)

            @when(first)
            def _():
                moves.hand(r).start()

            keep_state(r).start()

        @when(valid(c))
        def _():
            @when(c >= 1)
            def _():
                moves.give_theirs(c - 1).wait_send()

            branch_rows(1 - moves.core, theirs)
            moves.give_theirs(c).start()

        @when(valid(g))
        def _():
            gather_pass(moves, g)

        @when(valid(c))
        def _():
            branch_rows(moves.core, mine)
            reduce_first(moves, c, mine)

    gather_free(moves, tasks - 1)
    drain(moves, tasks - 1)
    for k in range(6):
        store(k, tasks - 1).wait()

    @when(jnp.logical_not(first))
    def _():
        for task in range(early_count):
            early.finish(opposite(task))
        for task in range(early_count, tasks):
            line.bring_wait(opposite(task))

    line.bring_done(tasks // 2)
    for task in range(tasks - 2, tasks):
        keep_state(task).wait()

        @when(first)
        def _(task=task):
            moves.hand(task).wait_send()


def move_semaphores(tasks, chips):
    dma = pltpu.SemaphoreType.DMA
    return [
        dma((tasks, chips - 1)),
        dma((tasks, chips)),
        dma((tasks,)),
        dma((tasks, chips - 1)),
        dma((tasks,)),
        dma((chips - 1,)),
        dma((chips,)),
        dma,
        dma((chips - 1,)),
        dma((2,)),
    ]


def forward_pass(chosen, wq, wi, wo, wd, bq, bi, norms, out_bias, tables, pq, pk, chips, heads):
    per_device, count, part_rows, width = chosen.shape
    tasks, rows = 2 * per_device, count // 2 * part_rows
    in_sems = line_semaphores(tasks, count)[0]
    block = pq.shape[0]
    units, inner = wd.shape[0], wo.shape[0]
    anywhere = pl.BlockSpec(memory_space=pl.ANY)
    vmem = pl.BlockSpec(memory_space=pltpu.VMEM)
    shape = jax.ShapeDtypeStruct
    return pl.pallas_call(
        partial(forward_kernel, (tasks, chips, rows, heads)),
        out_shape=[
            shape((tasks, block, width), bf16),
            shape((tasks, block, 3 * inner), bf16),
            shape((tasks, block, units), bf16),
            shape((tasks, block, units), bf16),
            shape((tasks, block, inner), bf16),
            shape((tasks, block, heads * LANES), f32),
            shape((tasks, rows, width), bf16),
            shape((tasks, rows, width), bf16),
            shape((tasks, rows, width), bf16),
            shape((tasks, block, width), bf16),
        ],
        in_specs=[anywhere] * 5 + [vmem] * 9,
        out_specs=[anywhere] * 10,
        scratch_shapes=[
            pltpu.VMEM(wq.shape, bf16),
            pltpu.VMEM(wi.shape, bf16),
            pltpu.VMEM(wo.shape, bf16),
            pltpu.VMEM(wd.shape, bf16),
            pltpu.VMEM(bq.shape, f32),
            pltpu.VMEM(bi.shape, f32),
            pltpu.VMEM((3, block, width), bf16),
            pltpu.VMEM((2, block, 3 * inner), bf16),
            pltpu.VMEM((block, units), bf16),
            pltpu.VMEM((block, units), bf16),
            pltpu.VMEM((block, inner), bf16),
            pltpu.VMEM((block, heads * LANES), f32),
            pltpu.VMEM((3, rows, width), bf16),
            pltpu.VMEM((chips * rows, width), bf16),
            pltpu.VMEM((chips * rows, width), f32),
            pltpu.VMEM((2, chips * rows, width), bf16),
            pltpu.VMEM((chips * rows, width), bf16),
            pltpu.VMEM((2, chips - 1, rows, width), bf16),
            pltpu.VMEM((2, rows, width), bf16),
            pltpu.SemaphoreType.DMA((4,)),
            pltpu.SemaphoreType.DMA,
            pltpu.SemaphoreType.DMA((6,)),
            pltpu.SemaphoreType.DMA((2,)),
        ]
        + in_sems
        + early_semaphores(tasks, chips)
        + move_semaphores(tasks, chips),
        compiler_params=pltpu.CompilerParams(
            collective_id=3, has_side_effects=True, vmem_limit_bytes=PASS_VMEM
        ),
        cost_estimate=pl.CostEstimate(
            flops=2 * tasks * block * width * (3 * inner + 2 * units + inner),
            bytes_accessed=tasks * block * width * 16,
            transcendentals=0,
        ),
        name="forward_pass",
    )(chosen, wq, wi, wo, wd, bq, bi, norms, out_bias, *tables, pq, pk)


def backward_kernel(
    plan, gin, xin, xarrive, states, early_all, qkv_all, dg_all, ctx_all, lse_all, std_all, wq_all, wi_all, wo_all, wd_all,
    gains, cosine, ahead, behind, pq, pk,
    gy_all, dproj_all, dh_all, home, state_home, arrive, vectors, side_q, side_h,
    wq, wi, wo, wd, land, dg, dh, qkv, before, ctx, lse, std, dctx, dproj, dk_held, dv_held,
    kept, theirs, mine, core_land, low, chip_land, handed, xrows,
    weight_sem, load_sem, store_sem,
    put_home, got_home, kept_home, put_state, got_state, kept_state, *sems,
):
    tasks, chips, rows, heads = plan
    line = Line(home.shape[1])
    grads_home = Home(line, lambda task: handed.at[place(task) % 2], home, put_home, got_home, kept_home)
    states_home = Home(line, lambda task: states.at[task], state_home, put_state, got_state, kept_state)
    size = wq.shape[1] // (3 * heads)
    scale = size**-0.5

    place = opposite
    moves = Moves((tasks, chips, rows), land, arrive, core_land, chip_land, theirs, low, handed, sems)
    first = moves.section == 0
    source = moves.section == 1
    base = jnp.where(source, 0, LAG)
    early_count = min(tasks, 2 * (LAG - 1))

    def gathers(task):
        return first | (task >= early_count)

    def load_early(task):
        return pltpu.make_async_copy(early_all.at[place(task)], land.at[task % 3], load_sem.at[8])

    weights = [
        pltpu.make_async_copy(a, b, weight_sem.at[k])
        for k, (a, b) in enumerate(((wo_all, wo), (wd_all, wd), (wq_all, wq), (wi_all, wi)))
    ]
    for copy in weights:
        copy.start()
    for total in (vectors, side_q, side_h):
        total[...] = jnp.zeros_like(total)
    moves.greet(line)

    def valid(task):
        return (task >= 0) & (task < tasks)

    def store(k, task):
        return pltpu.make_async_copy(
            (dproj, dh, land.at[task % 3])[k],
            (dproj_all, dh_all, gy_all)[k].at[place(task)],
            store_sem.at[k],
        )

    def load(k, task):
        return pltpu.make_async_copy(
            (dg_all, qkv_all, ctx_all, lse_all, std_all)[k].at[place(task)],
            (dg, qkv, ctx, lse, std)[k],
            load_sem.at[k],
        )

    def load_before(task):
        return pltpu.make_async_copy(qkv_all.at[place(task) - 1], before, load_sem.at[5])

    def spread(task):
        dctx[...] = dot(land[task % 3], wo[...], NT).astype(bf16)
        for at in range(0, wd.shape[0], 256):
            part = slice(at, at + 256)
            value = (dot(land[task % 3], wd[part, :], NT) * dg[:, part].astype(f32)).astype(bf16)
            dh[:, part] = value
            side_h[:, part] += jnp.sum(value.astype(f32), axis=0, keepdims=True)

    def attend_back(second):
        half = 1 if second else 0
        table = (cosine[half], ahead[half], behind[half])
        for h in range(heads):
            at = [slice((3 * h + k) * size, (3 * h + k + 1) * size) for k in range(3)]
            mid = slice(h * size, (h + 1) * size)
            q = qkv[:, at[0]]
            d_ctx = dctx[:, mid]
            logsum = lse[:, h * LANES : h * LANES + 1]
            delta = jnp.sum(d_ctx.astype(f32) * ctx[:, mid].astype(f32), axis=-1, keepdims=True)

            def pieces(held, masked):
                k, v = held[:, at[1]], held[:, at[2]]
                s = dot(q, k, NT) * scale
                if masked:
                    s = jnp.where(pq[...] >= pk[...], s, masked_score)
                p = jnp.exp(s - logsum)
                d_chance = dot(d_ctx, v, NT)
                d_scores = (p * (d_chance - delta)).astype(bf16)
                return dot(d_scores, k), dot(d_scores, q, TN), dot(p.astype(bf16), d_ctx, TN)

            dq, dk, dv = pieces(qkv, True)
            if second:
                dq_more, dk_more, dv_more = pieces(before, False)
                dq = dq + dq_more
                dk_held[:, mid] = dk_more
                dv_held[:, mid] = dv_more
            else:
                dk = dk + dk_held[:, mid]
                dv = dv + dv_held[:, mid]
            made = (turn(dq * scale, *table, -1.0), turn(dk * scale, *table, -1.0), dv)
            for k in range(3):
                value = made[k].astype(bf16)
                dproj[:, at[k]] = value
                side_q[:, at[k]] += jnp.sum(value.astype(f32), axis=0, keepdims=True)

    def merge_rows(core, result):
        at = moves.share(core)
        for column in range(0, wq.shape[0], 512):
            columns = slice(column, column + 512)
            one = dot(dproj[at, :], wq[columns, :], NT)
            two = dot(dh[at, :], wi[columns, :], NT)
            standard = std[at, columns].astype(f32)
            vectors[0:1, columns] += jnp.sum(one * standard, axis=0, keepdims=True)
            vectors[2:3, columns] += jnp.sum(two * standard, axis=0, keepdims=True)
            value = one * gains[0, :, columns] + two * gains[1, :, columns]
            result[:, columns] = value.astype(result.dtype)

    @pl.loop(0, tasks + LAG + 2)
    def _(step):
        g = step - base
        c = g - 1
        r = g - 2

        def load_rows(task, held, number):
            return pltpu.make_async_copy(held.at[number], kept.at[task % 3], load_sem.at[6])

        def load_x(task, held):
            return pltpu.make_async_copy(held.at[place(task)], xrows, load_sem.at[7])

        @when(step < tasks)
        def _():
            states_home.each(step, True)

        @when(valid(g) & source)
        def _():
            load_rows(g, gin, place(g)).start()

        @when(valid(r))
        def _():
            @when(first)
            def _():
                load_x(r, xin).start()

            @when(jnp.logical_not(first))
            def _():
                load_x(r, xarrive).start()


        @when(valid(c))
        def _():
            @when(gathers(c))
            def _():
                gather_wait(moves, c)

            @when(jnp.logical_not(gathers(c)))
            def _():
                load_early(c).wait()

            store(2, c).start()

            @when(c == 0)
            def _():
                weights[0].wait()
                weights[1].wait()

            @when(c >= 1)
            def _():
                for k in range(2):
                    store(k, c - 1).wait()

            load(0, c).wait()
            spread(c)
            store(1, c).start()
            for k in range(1, 5):
                load(k, c).wait()
            store(2, c).wait()

        @when(valid(g))
        def _():
            @when(first)
            def _():
                moves.hand(g).wait_recv()
                load_rows(g, arrive, g).start()

            load_rows(g, gin, g).wait()

            @when((g >= 1) & gathers(g - 1))
            def _():
                gather_free(moves, g - 1)

            @when(gathers(g))
            def _():
                gather_start(moves, g, kept[g % 3])

            @when(jnp.logical_not(gathers(g)))
            def _():
                load_early(g).start()

            vectors[4:5, :] += jnp.sum(kept[g % 3].astype(f32), axis=0, keepdims=True)

        @when(valid(c))
        def _():
            @when(c % 2 == 0)
            def _():
                load_before(c).wait()
                attend_back(True)

            @when(c % 2 == 1)
            def _():
                attend_back(False)

            store(0, c).start()

        @when(valid(r))
        def _():
            e = reduce_second(moves, r, mine)
            load_x(r, xin).wait()

            @when(r >= 2)
            def _():
                grads_home.each(place(r - 2), False)

                @when(source)
                def _():
                    moves.hand(r - 2).wait_send()

            standard, inverse = standardize(xrows[...])
            d_input = kept[r % 3].astype(f32) + inverse * (
                e
                - jnp.mean(e, axis=-1, keepdims=True)
                - standard * jnp.mean(e * standard, axis=-1, keepdims=True)
            )
            handed[r % 2] = d_input.astype(bf16)

            @when(source)
            def _():
                moves.hand(r).start()

            grads_home.each(place(r), True)

        @when(valid(c))
        def _():
            @when(c == 0)
            def _():
                weights[2].wait()
                weights[3].wait()

            @when(c >= 1)
            def _():
                moves.give_theirs(c - 1).wait_send()

            merge_rows(1 - moves.core, theirs)
            moves.give_theirs(c).start()

        @when(valid(g) & gathers(g))
        def _():
            gather_pass(moves, g)

        @when(valid(c))
        def _():
            merge_rows(moves.core, mine)
            reduce_first(moves, c, mine)

        @when(valid(c + 1))
        def _():
            for k in range(5):
                load(k, c + 1).start()

            @when((c + 1) % 2 == 0)
            def _():
                load_before(c + 1).start()

    @when(gathers(tasks - 1))
    def _():
        gather_free(moves, tasks - 1)

    drain(moves, tasks - 1)
    for k in range(2):
        store(k, tasks - 1).wait()
    for k, (side, weight) in enumerate(((side_q, wq), (side_h, wi))):
        value = side[...]
        high = value.astype(bf16)
        rest = (value - high.astype(f32)).astype(bf16)
        pair = jnp.concatenate([high, rest, jnp.zeros((14, value.shape[1]), bf16)])
        vectors[2 * k + 1 : 2 * k + 2, :] = jnp.sum(dot(pair, weight[...], NT), axis=0, keepdims=True)
    for task in range(tasks - 2, tasks):
        grads_home.each(place(task), False)

        @when(source)
        def _(task=task):
            moves.hand(task).wait_send()

    grads_home.wait(tasks)
    for task in range(tasks):
        states_home.each(task, False)
    states_home.wait(tasks)


def backward_pass(gin, xin, xarrive, states, early, qkv, dg, ctx, lse, std, wq, wi, wo, wd, gains, tables, pq, pk, chips, heads):
    tasks, rows, width = xin.shape
    count = lax.axis_size("ctx")
    home_sems = line_semaphores(tasks, count)[1]
    block = pq.shape[0]
    units, inner = wd.shape[0], wo.shape[0]
    anywhere = pl.BlockSpec(memory_space=pl.ANY)
    vmem = pl.BlockSpec(memory_space=pltpu.VMEM)
    shape = jax.ShapeDtypeStruct
    return pl.pallas_call(
        partial(backward_kernel, (tasks, chips, rows, heads)),
        out_shape=[
            shape((tasks, block, width), bf16),
            shape((tasks, block, 3 * inner), bf16),
            shape((tasks, block, units), bf16),
            shape((tasks // 2 * count, 2 * rows // count, width), bf16),
            shape((tasks // 2 * count, 2 * rows // count, width), bf16),
            shape((tasks, rows, width), bf16),
            shape((8, width), f32),
            shape((1, 3 * inner), f32),
            shape((1, units), f32),
        ],
        in_specs=[anywhere] * 14 + [vmem] * 6,
        out_specs=[anywhere] * 6 + [vmem] * 3,
        scratch_shapes=[
            pltpu.VMEM(wq.shape, bf16),
            pltpu.VMEM(wi.shape, bf16),
            pltpu.VMEM(wo.shape, bf16),
            pltpu.VMEM(wd.shape, bf16),
            pltpu.VMEM((3, block, width), bf16),
            pltpu.VMEM((block, units), bf16),
            pltpu.VMEM((block, units), bf16),
            pltpu.VMEM((block, 3 * inner), bf16),
            pltpu.VMEM((block, 3 * inner), bf16),
            pltpu.VMEM((block, inner), bf16),
            pltpu.VMEM((block, heads * LANES), f32),
            pltpu.VMEM((block, width), bf16),
            pltpu.VMEM((block, inner), bf16),
            pltpu.VMEM((block, 3 * inner), bf16),
            pltpu.VMEM((block, inner), f32),
            pltpu.VMEM((block, inner), f32),
            pltpu.VMEM((3, rows, width), bf16),
            pltpu.VMEM((chips * rows, width), bf16),
            pltpu.VMEM((chips * rows, width), f32),
            pltpu.VMEM((2, chips * rows, width), bf16),
            pltpu.VMEM((chips * rows, width), bf16),
            pltpu.VMEM((2, chips - 1, rows, width), bf16),
            pltpu.VMEM((2, rows, width), bf16),
            pltpu.VMEM((rows, width), bf16),
            pltpu.SemaphoreType.DMA((4,)),
            pltpu.SemaphoreType.DMA((9,)),
            pltpu.SemaphoreType.DMA((3,)),
        ]
        + home_sems
        + home_sems
        + move_semaphores(tasks, chips),
        compiler_params=pltpu.CompilerParams(
            collective_id=5, has_side_effects=True, vmem_limit_bytes=PASS_VMEM
        ),
        cost_estimate=pl.CostEstimate(
            flops=2 * tasks * block * width * (3 * inner + 2 * units + inner),
            bytes_accessed=tasks * block * width * 20,
            transcendentals=0,
        ),
        name="backward_pass",
    )(gin, xin, xarrive, states, early, qkv, dg, ctx, lse, std, wq, wi, wo, wd, gains, *tables, pq, pk)


CHUNK = 256
PIECE = 32
SKEW = 2


def reduce_kernel(
    plan, act, ctx, dproj, dhid, gy, std, gains, biases, sums, small, out, small_out, from_left, from_right,
    rhs, raw, lhs, own, inbox, outbox, stage, small_in,
    rhs_sem, raw_sem, right_sem, left_sem, final_sem, load_sem, sent, stage_left, stage_right, out_sem,
    small_sent, small_got,
):
    bounds, tasks, count, piece, skew, ring = plan
    sources = (dproj, dhid, act, ctx)
    total_chunks = bounds[-1]
    per_chunk = CHUNK // piece
    pieces = total_chunks * per_chunk
    width = gy.shape[-1]
    tile = width // per_chunk
    block = raw.shape[2]
    z = lax.axis_index("ctx")
    last = count - 1
    root = count // 2
    turn_at = max(root, last - root)
    low, high, middle = z < root, z > root, z == root

    barrier = pltpu.get_barrier_semaphore()
    for shift in range(1, count):
        pl.semaphore_signal(
            barrier,
            inc=1,
            device_id={"ctx": lax.rem(z + shift, count)},
            device_id_type=pl.DeviceIdType.MESH,
        )

    def small_copy(source, target):
        return pltpu.make_async_remote_copy(
            src_ref=small,
            dst_ref=small_in.at[source],
            send_sem=small_sent.at[target],
            recv_sem=small_got.at[source],
            device_id={"ctx": target},
            device_id_type=pl.DeviceIdType.MESH,
        )

    def rhs_copy(k):
        return pltpu.make_async_copy((std, gy)[k].at[pl.ds(0, tasks)], rhs.at[k], rhs_sem.at[k])

    def each_source(chunk, act_on):
        for g, source in enumerate(sources):

            @pl.when((chunk >= bounds[g]) & (chunk < bounds[g + 1]))
            def _(g=g, source=source):
                column = pl.multiple_of((chunk - bounds[g]) * CHUNK, CHUNK)
                act_on(
                    pltpu.make_async_copy(
                        source.at[pl.ds(0, tasks), :, pl.ds(column, CHUNK)],
                        raw.at[chunk % 2],
                        raw_sem.at[chunk % 2],
                    )
                )

    def take(chunk):
        each_source(chunk, lambda copy: copy.wait())
        for k in range(tasks):
            lhs[:, k * block : (k + 1) * block] = raw[chunk % 2, k].T
        each_source(chunk + 1, lambda copy: copy.start())

    def multiply(chunk, part):
        second = jnp.where(chunk >= bounds[2], 1, 0)
        group = second + jnp.where(chunk >= bounds[1], 1, 0)
        columns = pl.ds(pl.multiple_of(part * tile, tile), tile)
        value = dot(lhs[:, :block], rhs[second, 0, :, columns])
        for k in range(1, tasks):
            value = value + dot(lhs[:, k * block : (k + 1) * block], rhs[second, k, :, columns])
        row = pl.multiple_of(chunk * CHUNK, CHUNK)
        value = value * gains[group, :, columns] + sums[pl.ds(row, CHUNK), :] * biases[group, :, columns]
        own[chunk % ring, :, columns] = value.astype(bf16)

    def rows_of(index):
        return pl.ds(pl.multiple_of(index * piece, piece), piece)

    def own_piece(index):
        inner = pl.multiple_of((index % per_chunk) * piece, piece)
        return own[(index // per_chunk) % ring, pl.ds(inner, piece), :]

    def remote(source, target_rows, send_sem, recv_sem, target):
        return pltpu.make_async_remote_copy(
            src_ref=source,
            dst_ref=target_rows,
            send_sem=send_sem,
            recv_sem=recv_sem,
            device_id={"ctx": target},
            device_id_type=pl.DeviceIdType.MESH,
        )

    def inward(index, right):
        landing, arrived, target = (from_left, right_sem, z + 1) if right else (from_right, left_sem, z - 1)
        return remote(
            outbox.at[index % 2], landing.at[rows_of(index)], sent.at[index % 2], arrived.at[index], target
        )

    def announce(index, right):
        return remote(
            stage.at[index % 2],
            out.at[rows_of(index)],
            (stage_right if right else stage_left).at[index % 2],
            final_sem.at[index],
            z + 1 if right else z - 1,
        )

    def onward(index, right):
        return remote(
            out.at[rows_of(index)],
            out.at[rows_of(index)],
            sent.at[2 + index % 2],
            final_sem.at[index],
            z + 1 if right else z - 1,
        )

    def load(index, right):
        landing = from_left if right else from_right
        return pltpu.make_async_copy(
            landing.at[rows_of(index)], inbox.at[0 if right else 1], load_sem.at[0 if right else 1]
        )

    def valid(index):
        return (index >= 0) & (index < pieces)

    def side(step, right):
        mine = low if right else high
        hops = z if right else last - z
        inner = step - hops * skew
        comes = hops > 0

        @pl.when(mine & valid(inner) & comes)
        def _():
            inward(inner, right).wait_recv()
            load(inner, right).start()

        @pl.when(mine & valid(inner))
        def _():
            @pl.when(inner >= 2)
            def _():
                inward(inner - 2, right).wait_send()

            @pl.when(comes)
            def _():
                load(inner, right).wait()
                value = own_piece(inner).astype(f32) + inbox[0 if right else 1].astype(f32)
                outbox[inner % 2] = value.astype(bf16)

            @pl.when(jnp.logical_not(comes))
            def _():
                outbox[inner % 2] = own_piece(inner)

            inward(inner, right).start()

        away = root - z if right else z - root
        outer = step - (turn_at + away) * skew

        @pl.when(mine & valid(outer))
        def _():
            onward(outer, not right).wait_recv()

            @pl.when(comes)
            def _():
                @pl.when(outer >= 2)
                def _():
                    onward(outer - 2, not right).wait_send()

                onward(outer, not right).start()

    def out_copy(index):
        return pltpu.make_async_copy(stage.at[index % 2], out.at[rows_of(index)], out_sem.at[index % 2])

    def stage_done(index):
        out_copy(index).wait()
        announce(index, False).wait_send()
        if root < last:
            announce(index, True).wait_send()

    def centre(step):
        index = step - turn_at * skew

        @pl.when(middle & valid(index))
        def _():
            inward(index, True).wait_recv()
            load(index, True).start()
            if root < last:
                inward(index, False).wait_recv()
                load(index, False).start()

            @pl.when(index >= 2)
            def _():
                stage_done(index - 2)

            load(index, True).wait()
            value = own_piece(index).astype(f32) + inbox[0].astype(f32)
            if root < last:
                load(index, False).wait()
                value = value + inbox[1].astype(f32)
            stage[index % 2] = value.astype(bf16)
            announce(index, False).start()
            if root < last:
                announce(index, True).start()
            out_copy(index).start()

    rhs_copy(0).start()
    each_source(0, lambda copy: copy.start())
    rhs_copy(1).start()
    take(0)
    rhs_copy(0).wait()

    @pl.loop(0, per_chunk)
    def _(part):
        multiply(0, part)

    pl.semaphore_wait(barrier, count - 1)
    small_in[z] = small[...]
    for shift in range(1, count):
        small_copy(z, lax.rem(z + shift, count)).start()

    @pl.loop(0, pieces + (turn_at + max(root, last - root)) * skew)
    def _(step):
        side(step, True)
        side(step, False)
        centre(step)
        chunk, part = step // per_chunk + 1, step % per_chunk

        @pl.when(chunk < total_chunks)
        def _():
            @pl.when(part == 0)
            def _():
                take(chunk)

                @pl.when(chunk == bounds[2])
                def _():
                    rhs_copy(1).wait()

            multiply(chunk, part)

    for shift in range(1, count):
        other = lax.rem(z + shift, count)
        small_copy(z, other).wait_send()
        small_copy(other, other).wait_recv()
    value = small_in[0]
    for k in range(1, count):
        value = value + small_in[k]
    small_out[...] = value
    for back in (2, 1):
        for right in (True, False):

            @pl.when(low if right else high)
            def _(right=right, back=back):
                inward(pieces - back, right).wait_send()

                @pl.when((z > 0) & (z < last))
                def _():
                    onward(pieces - back, not right).wait_send()

        @pl.when(middle)
        def _(back=back):
            stage_done(pieces - back)


def reduce_gradients(act, ctx, dproj, dhid, gy, std, gains, biases, sums, small, tasks):
    count = lax.axis_size("ctx")
    block, width = gy.shape[1:]
    bounds = [0]
    for source in (dproj, dhid, act, ctx):
        bounds.append(bounds[-1] + source.shape[2] // CHUNK)
    total = bounds[-1] * CHUNK
    pieces = total // PIECE
    ring = count // 2 * SKEW // (CHUNK // PIECE) + 3
    plan = (tuple(bounds), tasks, count, PIECE, SKEW, ring)
    anywhere = pl.BlockSpec(memory_space=pl.ANY)
    vmem = pl.BlockSpec(memory_space=pltpu.VMEM)
    result = jax.ShapeDtypeStruct((total, width), bf16)
    out, small_out, _, _ = pl.pallas_call(
        partial(reduce_kernel, plan),
        out_shape=[result, jax.ShapeDtypeStruct(small.shape, f32), result, result],
        in_specs=[anywhere] * 6 + [vmem] * 4,
        out_specs=[anywhere, vmem, anywhere, anywhere],
        scratch_shapes=[
            pltpu.VMEM((2, tasks, block, width), bf16),
            pltpu.VMEM((2, tasks, block, CHUNK), bf16),
            pltpu.VMEM((CHUNK, tasks * block), bf16),
            pltpu.VMEM((ring, CHUNK, width), bf16),
            pltpu.VMEM((2, PIECE, width), bf16),
            pltpu.VMEM((2, PIECE, width), bf16),
            pltpu.VMEM((2, PIECE, width), bf16),
            pltpu.VMEM((count,) + small.shape, f32),
            pltpu.SemaphoreType.DMA((2,)),
            pltpu.SemaphoreType.DMA((2,)),
            pltpu.SemaphoreType.DMA((pieces,)),
            pltpu.SemaphoreType.DMA((pieces,)),
            pltpu.SemaphoreType.DMA((pieces,)),
            pltpu.SemaphoreType.DMA((2,)),
            pltpu.SemaphoreType.DMA((4,)),
            pltpu.SemaphoreType.DMA((2,)),
            pltpu.SemaphoreType.DMA((2,)),
            pltpu.SemaphoreType.DMA((2,)),
            pltpu.SemaphoreType.DMA((count,)),
            pltpu.SemaphoreType.DMA((count,)),
        ],
        compiler_params=pltpu.CompilerParams(
            collective_id=7, has_side_effects=True, vmem_limit_bytes=60 * 1024 * 1024
        ),
        cost_estimate=pl.CostEstimate(
            flops=2 * total * width * tasks * block,
            bytes_accessed=8 * total * width,
            transcendentals=0,
        ),
        name="reduce_gradients",
    )(act, ctx, dproj, dhid, gy, std, gains, biases, sums, small)
    return out, small_out


def turned_kernel(part, out):
    out[...] = part[...].astype(f32).T


def turned(total, start, count):
    width = total.shape[1]
    return pl.pallas_call(
        turned_kernel,
        out_shape=jax.ShapeDtypeStruct((width, count), f32),
        grid=(count // CHUNK,),
        in_specs=[pl.BlockSpec((CHUNK, width), lambda i: (start // CHUNK + i, 0))],
        out_specs=pl.BlockSpec((width, CHUNK), lambda i: (0, i)),
        compiler_params=pltpu.CompilerParams(vmem_limit_bytes=32 * 1024 * 1024),
        name="turned",
    )(total)


def turned_heads_kernel(heads, part, out):
    size = part.shape[0] // heads
    for h in range(heads):
        out[:, h, :] = part[h * size : (h + 1) * size, :].astype(f32).T


def turned_heads(total, start, count, heads):
    width = total.shape[1]
    return pl.pallas_call(
        partial(turned_heads_kernel, heads),
        out_shape=jax.ShapeDtypeStruct((width, heads, count // heads), f32),
        grid=(width // CHUNK,),
        in_specs=[pl.BlockSpec((count, CHUNK), lambda i: (start // count, i))],
        out_specs=pl.BlockSpec((CHUNK, heads, count // heads), lambda i: (i, 0, 0)),
        compiler_params=pltpu.CompilerParams(vmem_limit_bytes=32 * 1024 * 1024),
        name="turned_heads",
    )(total)


def body(
    inputs,
    out_grads,
    norm1_gain,
    norm1_bias,
    norm2_gain,
    norm2_bias,
    w_qkv,
    b_qkv,
    w_out,
    b_out,
    input_projection,
    input_bias_vector,
    down_projection,
    b_down,
):
    ctx_count = lax.axis_size("ctx")
    tensor = lax.axis_size("tensor")
    micro, _, rows, seqs, width = inputs.shape
    heads = w_qkv.shape[2]
    head_cols = w_qkv.shape[3]
    first = lax.axis_index("section") == 0
    per_device = micro * seqs // ctx_count
    blocks = ctx_count // 2
    tasks = 2 * per_device

    chosen = jnp.where(first, inputs[:, 0], out_grads[:, 0])
    chosen = chosen.transpose(0, 2, 1, 3).reshape(per_device, ctx_count, rows, width)

    wq = w_qkv[0].reshape(width, heads * head_cols)
    wi = input_projection[0]
    wo = w_out[0].reshape(-1, width)
    wd = down_projection[0]
    gain_one, bias_one, gain_two, bias_two = norm1_gain[0], norm1_bias[0], norm2_gain[0], norm2_bias[0]
    norms = jnp.stack([gain_one, bias_one, gain_two, bias_two], axis=1)
    out_bias = (b_out[0] + b_down[0])[None]

    relative, tables = position_tables(None, blocks, rows, tensor)
    places_q, places_k = relative[:, None], relative[None, :]

    chips = tensor // 2
    stacked_tables = [jnp.stack(pair) for pair in zip(*tables)]
    std_all, qkv, act_all, dg_all, ctx_all, lse_all, chosen_rows, states, arrive, early = forward_pass(
        chosen,
        wq,
        wi,
        wo,
        wd,
        b_qkv[0].reshape(1, -1),
        input_bias_vector,
        norms,
        out_bias,
        stacked_tables,
        places_q,
        places_k,
        chips,
        heads,
    )
    gains = jnp.stack([gain_one, gain_two])[:, None]
    gy_all, dproj_all, dh_all, dx_home, states_home, _, vectors, side_q, side_h = backward_pass(
        chosen_rows,
        chosen_rows,
        arrive,
        states,
        early,
        qkv,
        dg_all,
        ctx_all,
        lse_all,
        std_all,
        wq,
        wi,
        wo,
        wd,
        gains,
        stacked_tables,
        places_q,
        places_k,
        chips,
        heads,
    )
    vectors = vectors[:5]

    d_b_qkv, d_b_in = side_q[0], side_h[0]
    units, inner = wd.shape[0], wo.shape[0]
    sums = jnp.concatenate([d_b_qkv, d_b_in, jnp.zeros((units + inner,), f32)])[:, None]
    gains = jnp.stack([gain_one, gain_two, jnp.ones_like(gain_one)])[:, None]
    biases = jnp.stack([bias_one, bias_two, jnp.zeros_like(bias_one)])[:, None]
    mask = 1
    while mask < tensor:
        vectors = vectors + lax.ppermute(vectors, "tensor", [(k, k ^ mask) for k in range(tensor)])
        mask *= 2
    sides = jnp.concatenate([d_b_qkv, d_b_in])
    side_rows = -(-sides.shape[0] // width)
    small = jnp.zeros((-(-(5 + side_rows) // 8) * 8, width), f32)
    small = small.at[:5].set(vectors)
    small = small.at[5 : 5 + side_rows].set(
        jnp.pad(sides, (0, side_rows * width - sides.shape[0])).reshape(side_rows, width)
    )
    summed, small = reduce_gradients(
        act_all, ctx_all, dproj_all, dh_all, gy_all, std_all, gains, biases, sums, small, tasks
    )
    columns = wq.shape[1]
    vectors = small[:5]
    sides = small[5 : 5 + side_rows].reshape(-1)
    d_b_qkv, d_b_in = sides[: d_b_qkv.shape[0]], sides[d_b_qkv.shape[0] : sides.shape[0]]
    d_b_in = d_b_in[: wi.shape[1]]
    d_w_qkv = turned_heads(summed, 0, columns, heads)
    d_w_in = turned(summed, columns, units)
    d_w_down = summed[columns + units : columns + 2 * units].astype(f32)
    d_w_out = summed[columns + 2 * units :].astype(f32)

    def homeward(pieces):
        return pieces.reshape(micro, seqs, rows, width).transpose(0, 2, 1, 3)[None, :, None]

    states = homeward(states_home)
    input_grads = homeward(dx_home).astype(f32)
    return (
        states,
        input_grads,
        vectors[0][None],
        vectors[1][None],
        vectors[2][None],
        vectors[3][None],
        d_w_qkv.reshape(w_qkv.shape),
        d_b_qkv.reshape(b_qkv.shape),
        d_w_out.reshape(w_out.shape),
        vectors[4][None],
        d_w_in[None],
        d_b_in[None],
        d_w_down[None],
        vectors[4][None],
    )


def solution(mesh):
    return jax.shard_map(
        body,
        mesh=mesh,
        in_specs=(
            P(None, "ctx", "tensor", None, None),
            P(None, "ctx", "tensor", None, None),
            P("section", None),
            P("section", None),
            P("section", None),
            P("section", None),
            P("section", None, "tensor", None),
            P("section", "tensor", None),
            P("section", "tensor", None, None),
            P("section", None),
            P("section", None, "tensor"),
            P("section", "tensor"),
            P("section", "tensor", None),
            P("section", None),
        ),
        out_specs=(
            P("section", None, "ctx", "tensor", None, None),
            P("section", None, "ctx", "tensor", None, None),
            P("section", None),
            P("section", None),
            P("section", None),
            P("section", None),
            P("section", None, "tensor", None),
            P("section", "tensor", None),
            P("section", "tensor", None, None),
            P("section", None),
            P("section", None, "tensor"),
            P("section", "tensor"),
            P("section", "tensor", None),
            P("section", None),
        ),
        check_vma=False,
    )
```

```python
from functools import partial

import jax
import jax.numpy as jnp
from jax import lax
from jax.experimental import pallas as pl
from jax.experimental.pallas import tpu as pltpu
from jax.sharding import PartitionSpec as P

ROT = 64
LAG = 3
LANES = 128
epsilon = 1e-05
masked_score = -1e30
f32 = jnp.float32
bf16 = jnp.bfloat16
NT = (((1,), (1,)), ((), ()))
TN = (((0,), (0,)), ((), ()))
NN = (((1,), (0,)), ((), ()))
PASS_VMEM = 62 * 1024 * 1024


def dot(a, b, dims=NN):
    return lax.dot_general(a, b, dims, preferred_element_type=f32)


def standardize(rows):
    values = rows.astype(f32)
    average = jnp.mean(values, axis=-1, keepdims=True)
    centred = values - average
    inverse = lax.rsqrt(jnp.mean(centred * centred, axis=-1, keepdims=True) + epsilon)
    return centred * inverse, inverse


def position_tables(section_rows, blocks, rows, tensor):
    half = ROT // 2
    frequency = 1.0 / 10000.0 ** (jnp.arange(0, ROT, 2, dtype=f32) / ROT)
    core, chip, c, i = jnp.meshgrid(
        jnp.arange(2), jnp.arange(tensor // 2), jnp.arange(blocks), jnp.arange(rows), indexing="ij"
    )
    relative = (c * (rows * tensor) + (chip * 2 + core) * rows + i).reshape(-1).astype(jnp.int32)
    tables = []
    for part in range(2):
        places = (relative + part * blocks * rows * tensor).astype(f32)
        angles = places[:, None] * frequency[None, :]
        cosine, sine = jnp.cos(angles), jnp.sin(angles)
        none = jnp.zeros_like(sine)
        rest = jnp.zeros((relative.shape[0], LANES - ROT), f32)
        tables.append(
            (
                jnp.concatenate([cosine, cosine, rest + 1.0], axis=-1),
                jnp.concatenate([-sine, none, rest], axis=-1),
                jnp.concatenate([none, sine, rest], axis=-1),
            )
        )
    return relative, tables


def turn(values, cosine, ahead, behind, sign):
    half = ROT // 2
    lead = values[:, :LANES]
    turned = pltpu.roll(lead, LANES - half, 1) * ahead + pltpu.roll(lead, half, 1) * behind
    return jnp.concatenate([lead * cosine + sign * turned, values[:, LANES:]], axis=1)


class Moves:
    def __init__(self, plan, land, arrive, core_land, chip_land, theirs, low, handed, sems):
        self.tasks, self.chips, self.rows = plan
        self.land, self.arrive, self.core_land, self.chip_land = land, arrive, core_land, chip_land
        self.theirs, self.low, self.handed = theirs, low, handed
        self.slots = land.shape[0]
        (
            self.got_chip, self.got_core, self.got_theirs, self.got_low, self.got_hand,
            self.put_chip, self.put_core, self.put_theirs, self.put_low, self.put_hand,
        ) = sems
        self.section = lax.axis_index("section")
        self.index = lax.axis_index("tensor")
        self.total = 2 * self.chips
        self.chip, self.core = self.index // 2, self.index % 2
        self.mate = self.chip * 2 + 1 - self.core

    def mate_on(self, shift):
        return lax.rem(self.index + 2 * shift, self.total)

    def part(self, member):
        at = (member % 2) * self.chips + member // 2
        return pl.ds(pl.multiple_of(at * self.rows, self.rows), self.rows)

    def share(self, core):
        size = self.chips * self.rows
        return pl.ds(pl.multiple_of(core * size, size), size)

    def of_chip(self, chip):
        return pl.ds(pl.multiple_of(chip * self.rows, self.rows), self.rows)

    def remote(self, source, target, sent, arrived, **device):
        return pltpu.make_async_remote_copy(
            src_ref=source,
            dst_ref=target,
            send_sem=sent,
            recv_sem=arrived,
            device_id=device,
            device_id_type=pl.DeviceIdType.MESH,
        )

    def greet(self, line):
        barrier = pltpu.get_barrier_semaphore()
        peers = [{"section": 1 - self.section}, {"tensor": self.mate}]
        peers += [{"ctx": other} for other in line.others()]
        peers += [{"tensor": self.mate_on(shift)} for shift in range(1, self.chips)]
        for peer in peers:
            pl.semaphore_signal(barrier, inc=1, device_id=peer, device_id_type=pl.DeviceIdType.MESH)
        pl.semaphore_wait(barrier, len(peers))

    def gather_chip(self, task, shift, member=None):
        rows = self.land.at[task % self.slots, self.part(self.index if member is None else member)]
        return self.remote(
            rows,
            rows,
            self.put_chip.at[shift - 1],
            self.got_chip.at[task, shift - 1],
            tensor=self.mate_on(shift),
        )

    def gather_chip_in(self, task, shift):
        return self.gather_chip(task, shift, lax.rem(self.index + self.total - 2 * shift, self.total))

    def gather_core(self, task, shift, member=None):
        if member is None:
            member = lax.rem(self.index + self.total - 2 * shift, self.total)
        rows = self.land.at[task % self.slots, self.part(member)]
        return self.remote(
            rows,
            rows,
            self.put_core.at[shift],
            self.got_core.at[task, shift],
            tensor=self.mate,
        )

    def gather_core_in(self, task, shift):
        return self.gather_core(task, shift, lax.rem(self.mate + self.total - 2 * shift, self.total))

    def give_theirs(self, task):
        return self.remote(
            self.theirs, self.core_land.at[task % 2], self.put_theirs, self.got_theirs.at[task], tensor=self.mate
        )

    def give_low(self, task, shift):
        return self.remote(
            self.low.at[self.of_chip(lax.rem(self.chip + shift, self.chips))],
            self.chip_land.at[task % 2, shift - 1],
            self.put_low.at[shift - 1],
            self.got_low.at[task, shift - 1],
            tensor=self.mate_on(shift),
        )

    def hand(self, task):
        return self.remote(
            self.handed.at[task % 2],
            self.arrive.at[task],
            self.put_hand.at[task % 2],
            self.got_hand.at[task],
            section=1 - self.section,
        )


class Line:
    def __init__(self, rows):
        self.rows = rows
        self.count = lax.axis_size("ctx")
        self.blocks = self.count // 2
        self.z = lax.axis_index("ctx")

    def others(self):
        return [lax.rem(self.z + shift, self.count) for shift in range(1, self.count)]

    def remote(self, source, target, sent, arrived, device):
        return pltpu.make_async_remote_copy(
            src_ref=source,
            dst_ref=target,
            send_sem=sent,
            recv_sem=arrived,
            device_id={"ctx": device},
            device_id_type=pl.DeviceIdType.MESH,
        )

    def block(self, at):
        return pl.ds(pl.multiple_of(at * self.rows, self.rows), self.rows)

    def set_in(self, chosen, landed, put, got, kept):
        self.chosen, self.landed, self.put_in, self.got_in, self.kept_in = chosen, landed, put, got, kept

    def bring(self, j, shift, source=None):
        source = self.z if source is None else source
        half = source // self.blocks
        return self.remote(
            self.chosen.at[j, lax.rem(self.z + shift, self.count)],
            self.landed.at[2 * j + half, self.block(source - half * self.blocks)],
            self.put_in.at[j, shift - 1],
            self.got_in.at[j, source],
            lax.rem(self.z + shift, self.count),
        )

    def bring_own(self, j):
        half = self.z // self.blocks
        return pltpu.make_async_copy(
            self.chosen.at[j, self.z],
            self.landed.at[2 * j + half, self.block(self.z - half * self.blocks)],
            self.kept_in.at[j],
        )

    def bring_start(self, j):
        for shift in range(1, self.count):
            self.bring(j, shift).start()
        self.bring_own(j).start()

    def bring_wait(self, task):
        j, half = task // 2, task % 2
        for k in range(self.blocks):
            source = half * self.blocks + k

            @pl.when(source != self.z)
            def _():
                self.bring(j, 1, source).wait_recv()

            @pl.when(source == self.z)
            def _():
                self.bring_own(j).wait()

    def bring_done(self, count):
        for j in range(count):
            for shift in range(1, self.count):
                self.bring(j, shift).wait_send()


class Home:
    def __init__(self, line, source, home, put, got, kept):
        self.line, self.source, self.home = line, source, home
        self.put, self.got, self.kept = put, got, kept

    def take(self, task, k, sender=None):
        line = self.line
        sender = line.z if sender is None else sender
        return line.remote(
            self.source(task).at[pl.ds(k * line.rows, line.rows)],
            self.home.at[(task // 2) * line.count + sender],
            self.put.at[task, k],
            self.got.at[task // 2, sender],
            (task % 2) * line.blocks + k,
        )

    def keep(self, task, k):
        line = self.line
        return pltpu.make_async_copy(
            self.source(task).at[pl.ds(k * line.rows, line.rows)],
            self.home.at[(task // 2) * line.count + line.z],
            self.kept.at[task],
        )

    def each(self, task, begin):
        line = self.line
        for k in range(line.blocks):
            there = (task % 2) * line.blocks + k

            @pl.when(there != line.z)
            def _():
                copy = self.take(task, k)
                copy.start() if begin else copy.wait_send()

            @pl.when(there == line.z)
            def _():
                copy = self.keep(task, k)
                copy.start() if begin else copy.wait()

    def wait(self, tasks):
        for j in range(tasks // 2):
            for other in self.line.others():
                self.take(2 * j, 0, other).wait_recv()


def line_semaphores(tasks, count):
    dma = pltpu.SemaphoreType.DMA
    half = tasks // 2
    return [dma((half, count - 1)), dma((half, count)), dma((half,))], [
        dma((tasks, count // 2)),
        dma((half, count)),
        dma((tasks,)),
    ]


class Early:
    def __init__(self, moves, source, gathered, got_chip, got_core, put_chip, put_core, kept):
        self.moves, self.source, self.gathered = moves, source, gathered
        self.got_chip, self.got_core, self.put_chip, self.put_core = got_chip, got_core, put_chip, put_core
        self.kept = kept

    def at(self, task, member):
        return self.gathered.at[task, self.moves.part(member)]

    def behind(self, start, shift):
        return lax.rem(start + self.moves.total - 2 * shift, self.moves.total)

    def chip(self, task, shift, member=None):
        member = self.moves.index if member is None else member
        return self.moves.remote(
            self.source.at[task],
            self.at(task, member),
            self.put_chip.at[task, shift - 1],
            self.got_chip.at[task, shift - 1],
            tensor=self.moves.mate_on(shift),
        )

    def core(self, task, shift, member=None):
        member = self.behind(self.moves.index, shift) if member is None else member
        rows = self.at(task, member)
        return self.moves.remote(
            self.source.at[task] if shift == 0 else rows,
            rows,
            self.put_core.at[task, shift],
            self.got_core.at[task, shift],
            tensor=self.moves.mate,
        )

    def keep(self, task):
        return pltpu.make_async_copy(
            self.source.at[task], self.at(task, self.moves.index), self.kept.at[task]
        )

    def start(self, task):
        for shift in range(1, self.moves.chips):
            self.chip(task, shift).start()
        self.core(task, 0).start()
        self.keep(task).start()

    def hand_on(self, task):
        for shift in range(1, self.moves.chips):
            self.chip(task, shift, self.behind(self.moves.index, shift)).wait_recv()
            self.core(task, shift).start()

    def finish(self, task):
        self.keep(task).wait()
        for shift in range(1, self.moves.chips):
            self.chip(task, shift).wait_send()
        for shift in range(self.moves.chips):
            self.core(task, shift).wait_send()
            self.core(task, shift, self.behind(self.moves.mate, shift)).wait_recv()


def early_semaphores(tasks, chips):
    dma = pltpu.SemaphoreType.DMA
    return [dma((tasks, chips - 1)), dma((tasks, chips)), dma((tasks, chips - 1)), dma((tasks, chips)), dma((tasks,))]


def opposite(task):
    return task + 1 - 2 * (task % 2)


def reduce_first(moves, task, mine):
    moves.give_theirs(task).wait_recv()

    @pl.when(task >= 1)
    def _():
        for shift in range(1, moves.chips):
            moves.give_low(task - 1, shift).wait_send()

    value = mine[...] + moves.core_land[task % 2].astype(f32)
    mine[...] = value
    moves.low[...] = value.astype(bf16)
    for shift in range(1, moves.chips):
        moves.give_low(task, shift).start()


def reduce_second(moves, task, mine):
    value = mine[moves.of_chip(moves.chip), :]
    for shift in range(1, moves.chips):
        moves.give_low(task, shift).wait_recv()
        value = value + moves.chip_land[task % 2, shift - 1].astype(f32)
    return value


def gather_start(moves, task, value):
    moves.land[task % moves.slots, moves.part(moves.index), :] = value
    for shift in range(1, moves.chips):
        moves.gather_chip(task, shift).start()
    moves.gather_core(task, 0).start()


def gather_free(moves, task):
    for shift in range(1, moves.chips):
        moves.gather_chip(task, shift).wait_send()
    for shift in range(moves.chips):
        moves.gather_core(task, shift).wait_send()


def gather_pass(moves, task):
    for shift in range(1, moves.chips):
        moves.gather_chip_in(task, shift).wait_recv()
        moves.gather_core(task, shift).start()


def gather_wait(moves, task):
    for shift in range(moves.chips):
        moves.gather_core_in(task, shift).wait_recv()


def drain(moves, task):
    for shift in range(1, moves.chips):
        moves.give_low(task, shift).wait_send()
    moves.give_theirs(task).wait_send()


def when(condition):
    return pl.when(condition)


def forward_kernel(
    plan, chosen, wq_all, wi_all, wo_all, wd_all, bq_in, bi_in, norms, out_bias, cosine, ahead, behind, pq, pk,
    std_all, qkv_all, act_all, dg_all, ctx_all, lse_all, xin, states, arrive, early_all,
    wq, wi, wo, wd, bq, bi, land, qkv, act, dg, ctx, lse, kept, theirs, mine, core_land, low, chip_land, handed,
    weight_sem, load_sem, store_sem, state_sem, put_in, got_in, kept_in,
    early_a, early_b, early_c, early_d, early_e, *sems,
):
    tasks, chips, rows, heads = plan
    line = Line(chosen.shape[2])
    line.set_in(chosen, xin, put_in, got_in, kept_in)
    size = wq.shape[1] // (3 * heads)
    moves = Moves((tasks, chips, rows), land, arrive, core_land, chip_land, theirs, low, handed, sems)
    first = moves.section == 0
    base = jnp.where(first, 0, LAG)
    early = Early(moves, xin, early_all, early_a, early_b, early_c, early_d, early_e)
    early_count = min(tasks, 2 * (LAG - 1))

    weights = [
        pltpu.make_async_copy(a, b, weight_sem.at[k])
        for k, (a, b) in enumerate(((wq_all, wq), (wi_all, wi), (wo_all, wo), (wd_all, wd)))
    ]
    moves.greet(line)
    line.bring_start(0)
    for copy in weights:
        copy.start()

    @when(jnp.logical_not(first))
    def _():
        for j in range(1, tasks // 2):
            line.bring_start(j)

    def valid(task):
        return (task >= 0) & (task < tasks)

    def keep_state(task):
        return pltpu.make_async_copy(handed.at[task % 2], states.at[task], state_sem.at[task % 2])

    def fold(weight, bias_in, bias, gain_column):
        bias[...] = bias_in[...]
        step = 256

        @pl.loop(0, weight.shape[0] // step)
        def _(k):
            at = pl.ds(pl.multiple_of(k * step, step), step)
            value = weight[at, :].astype(f32)
            gain = norms[at, gain_column : gain_column + 1]
            shift = norms[at, gain_column + 1 : gain_column + 2]
            bias[...] += jnp.sum(value * shift, axis=0, keepdims=True)
            weight[at, :] = (value * gain).astype(bf16)

    def store(k, task):
        return pltpu.make_async_copy(
            (qkv.at[task % 2], act, dg, ctx, lse, land.at[task % 3])[k],
            (qkv_all, act_all, dg_all, ctx_all, lse_all, std_all)[k].at[task],
            store_sem.at[k],
        )

    def project(task):
        half = task % 2
        table = (cosine[half], ahead[half], behind[half])
        for h in range(heads):
            for k in range(3):
                columns = slice((3 * h + k) * size, (3 * h + k + 1) * size)
                z = dot(land[task % 3], wq[:, columns]) + bq[:, columns]
                if k < 2:
                    z = turn(z, *table, 1.0)
                qkv[half, :, columns] = z.astype(bf16)

    def attend(task, second):
        half = 1 if second else 0
        scale = size**-0.5
        for h in range(heads):
            at = [slice((3 * h + k) * size, (3 * h + k + 1) * size) for k in range(3)]
            q = qkv[half, :, at[0]]
            s = dot(q, qkv[half, :, at[1]], NT) * scale
            s = jnp.where(pq[...] >= pk[...], s, masked_score)
            peak = jnp.max(s, axis=-1, keepdims=True)
            if second:
                sp = dot(q, qkv[0, :, at[1]], NT) * scale
                peak = jnp.maximum(peak, jnp.max(sp, axis=-1, keepdims=True))
            p = jnp.exp(s - peak)
            total = jnp.sum(p, axis=-1, keepdims=True)
            if second:
                pp = jnp.exp(sp - peak)
                total = total + jnp.sum(pp, axis=-1, keepdims=True)
            share = 1.0 / total
            value = dot((p * share).astype(bf16), qkv[half, :, at[2]])
            if second:
                value = value + dot((pp * share).astype(bf16), qkv[0, :, at[2]])
            ctx[:, h * size : (h + 1) * size] = value.astype(bf16)
            lse[:, h * LANES : (h + 1) * LANES] = jnp.broadcast_to(
                peak + jnp.log(total), (q.shape[0], LANES)
            )

    def expand(task):
        for at in range(0, wi.shape[1], 256):
            columns = slice(at, at + 256)
            h = dot(land[task % 3], wi[:, columns]) + bi[:, columns]
            phi = 0.5 + 0.5 * lax.erf(h * (0.5**0.5))
            density = jnp.exp(h * h * -0.5) * 0.3989422804014327
            act[:, columns] = (h * phi).astype(bf16)
            dg[:, columns] = (phi + h * density).astype(bf16)

    def branch_rows(core, result):
        at = moves.share(core)
        for column in range(0, wo.shape[1], 512):
            columns = slice(column, column + 512)
            value = dot(ctx[at, :], wo[:, columns]) + dot(act[at, :], wd[:, columns])
            result[:, columns] = value.astype(result.dtype)

    weights[0].wait()
    fold(wq, bq_in, bq, 0)
    weights[1].wait()
    fold(wi, bi_in, bi, 2)
    weights[2].wait()
    weights[3].wait()

    @pl.loop(0, tasks + LAG + 2)
    def _(step):
        g = step - base
        c = g - 1
        r = g - 2

        def load_rows(task, held):
            return pltpu.make_async_copy(held.at[task], kept.at[task % 3], load_sem)

        @when(first & (step % 2 == 0) & (step // 2 + 1 < tasks // 2))
        def _():
            line.bring_start(step // 2 + 1)

        @when(first & (step < tasks))
        def _():
            line.bring_wait(step)

        for k in range(2):
            late = 2 * (step - 1) + k

            @when(jnp.logical_not(first) & (late >= 0) & (late < early_count))
            def _(late=late):
                early.hand_on(opposite(late))

        for k in range(2):
            fresh = 2 * step + k

            @when(jnp.logical_not(first) & (fresh < early_count))
            def _(fresh=fresh):
                line.bring_wait(opposite(fresh))
                early.start(opposite(fresh))

        @when(valid(g) & first)
        def _():
            load_rows(g, xin).start()

        @when(valid(c))
        def _():
            gather_wait(moves, c)

            @when(c >= 1)
            def _():
                for k in range(6):
                    store(k, c - 1).wait()

            store(5, c).start()
            project(c)
            store(0, c).start()

        @when(valid(g) & jnp.logical_not(first))
        def _():
            moves.hand(g).wait_recv()
            load_rows(g, arrive).start()

        @when(valid(c))
        def _():
            @when(c % 2 == 0)
            def _():
                attend(c, False)

            @when(c % 2 == 1)
            def _():
                attend(c, True)

            store(3, c).start()
            store(4, c).start()

        @when(valid(g))
        def _():
            load_rows(g, xin).wait()

            @when(g >= 1)
            def _():
                gather_free(moves, g - 1)

            gather_start(moves, g, standardize(kept[g % 3])[0].astype(bf16))

        @when(valid(c))
        def _():
            expand(c)
            store(1, c).start()
            store(2, c).start()

        @when(valid(r))
        def _():
            value = reduce_second(moves, r, mine)

            @when(r >= 2)
            def _():
                keep_state(r - 2).wait()

                @when(first)
                def _():
                    moves.hand(r - 2).wait_send()

            handed[r % 2] = (kept[r % 3].astype(f32) + value + out_bias[...]).astype(bf16)

            @when(first)
            def _():
                moves.hand(r).start()

            keep_state(r).start()

        @when(valid(c))
        def _():
            @when(c >= 1)
            def _():
                moves.give_theirs(c - 1).wait_send()

            branch_rows(1 - moves.core, theirs)
            moves.give_theirs(c).start()

            branch_rows(moves.core, mine)
            reduce_first(moves, c, mine)

        @when(valid(g))
        def _():
            gather_pass(moves, g)

    gather_free(moves, tasks - 1)
    drain(moves, tasks - 1)
    for k in range(6):
        store(k, tasks - 1).wait()

    @when(jnp.logical_not(first))
    def _():
        for task in range(early_count):
            early.finish(opposite(task))
        for task in range(early_count, tasks):
            line.bring_wait(opposite(task))

    line.bring_done(tasks // 2)
    for task in range(tasks - 2, tasks):
        keep_state(task).wait()

        @when(first)
        def _(task=task):
            moves.hand(task).wait_send()


def move_semaphores(tasks, chips):
    dma = pltpu.SemaphoreType.DMA
    return [
        dma((tasks, chips - 1)),
        dma((tasks, chips)),
        dma((tasks,)),
        dma((tasks, chips - 1)),
        dma((tasks,)),
        dma((chips - 1,)),
        dma((chips,)),
        dma,
        dma((chips - 1,)),
        dma((2,)),
    ]


def forward_pass(chosen, wq, wi, wo, wd, bq, bi, norms, out_bias, tables, pq, pk, chips, heads):
    per_device, count, part_rows, width = chosen.shape
    tasks, rows = 2 * per_device, count // 2 * part_rows
    in_sems = line_semaphores(tasks, count)[0]
    block = pq.shape[0]
    units, inner = wd.shape[0], wo.shape[0]
    anywhere = pl.BlockSpec(memory_space=pl.ANY)
    vmem = pl.BlockSpec(memory_space=pltpu.VMEM)
    shape = jax.ShapeDtypeStruct
    return pl.pallas_call(
        partial(forward_kernel, (tasks, chips, rows, heads)),
        out_shape=[
            shape((tasks, block, width), bf16),
            shape((tasks, block, 3 * inner), bf16),
            shape((tasks, block, units), bf16),
            shape((tasks, block, units), bf16),
            shape((tasks, block, inner), bf16),
            shape((tasks, block, heads * LANES), f32),
            shape((tasks, rows, width), bf16),
            shape((tasks, rows, width), bf16),
            shape((tasks, rows, width), bf16),
            shape((tasks, block, width), bf16),
        ],
        in_specs=[anywhere] * 5 + [vmem] * 9,
        out_specs=[anywhere] * 10,
        scratch_shapes=[
            pltpu.VMEM(wq.shape, bf16),
            pltpu.VMEM(wi.shape, bf16),
            pltpu.VMEM(wo.shape, bf16),
            pltpu.VMEM(wd.shape, bf16),
            pltpu.VMEM(bq.shape, f32),
            pltpu.VMEM(bi.shape, f32),
            pltpu.VMEM((3, block, width), bf16),
            pltpu.VMEM((2, block, 3 * inner), bf16),
            pltpu.VMEM((block, units), bf16),
            pltpu.VMEM((block, units), bf16),
            pltpu.VMEM((block, inner), bf16),
            pltpu.VMEM((block, heads * LANES), f32),
            pltpu.VMEM((3, rows, width), bf16),
            pltpu.VMEM((chips * rows, width), bf16),
            pltpu.VMEM((chips * rows, width), f32),
            pltpu.VMEM((2, chips * rows, width), bf16),
            pltpu.VMEM((chips * rows, width), bf16),
            pltpu.VMEM((2, chips - 1, rows, width), bf16),
            pltpu.VMEM((2, rows, width), bf16),
            pltpu.SemaphoreType.DMA((4,)),
            pltpu.SemaphoreType.DMA,
            pltpu.SemaphoreType.DMA((6,)),
            pltpu.SemaphoreType.DMA((2,)),
        ]
        + in_sems
        + early_semaphores(tasks, chips)
        + move_semaphores(tasks, chips),
        compiler_params=pltpu.CompilerParams(
            collective_id=3, has_side_effects=True, vmem_limit_bytes=PASS_VMEM
        ),
        cost_estimate=pl.CostEstimate(
            flops=2 * tasks * block * width * (3 * inner + 2 * units + inner),
            bytes_accessed=tasks * block * width * 16,
            transcendentals=0,
        ),
        name="forward_pass",
    )(chosen, wq, wi, wo, wd, bq, bi, norms, out_bias, *tables, pq, pk)


def backward_kernel(
    plan, gin, xin, xarrive, states, early_all, qkv_all, dg_all, ctx_all, lse_all, std_all, wq_all, wi_all, wo_all, wd_all,
    gains, cosine, ahead, behind, pq, pk,
    gy_all, dproj_all, dh_all, home, state_home, last_rows, arrive, vectors, side_q, side_h,
    wq, wi, wo, wd, land, dg, dh, qkv, before, ctx, lse, std, dctx, dproj, dk_held, dv_held,
    kept, theirs, mine, core_land, low, chip_land, handed, xrows,
    weight_sem, load_sem, store_sem, last_sem,
    put_home, got_home, kept_home, put_state, got_state, kept_state, *sems,
):
    tasks, chips, rows, heads = plan
    line = Line(home.shape[1])
    grads_home = Home(line, lambda task: handed.at[place(task) % 2], home, put_home, got_home, kept_home)
    states_home = Home(line, lambda task: states.at[task], state_home, put_state, got_state, kept_state)
    size = wq.shape[1] // (3 * heads)
    scale = size**-0.5

    place = opposite
    moves = Moves((tasks, chips, rows), land, arrive, core_land, chip_land, theirs, low, handed, sems)
    first = moves.section == 0
    source = moves.section == 1
    base = jnp.where(source, 0, LAG)
    early_count = min(tasks, 2 * (LAG - 1))

    def gathers(task):
        return first | (task >= early_count)

    def load_early(task):
        return pltpu.make_async_copy(early_all.at[place(task)], land.at[task % 3], load_sem.at[8])

    weights = [
        pltpu.make_async_copy(a, b, weight_sem.at[k])
        for k, (a, b) in enumerate(((wo_all, wo), (wd_all, wd), (wq_all, wq), (wi_all, wi)))
    ]
    for copy in weights:
        copy.start()
    for total in (vectors, side_q, side_h):
        total[...] = jnp.zeros_like(total)
    moves.greet(line)

    def valid(task):
        return (task >= 0) & (task < tasks)

    def store(k, task):
        return pltpu.make_async_copy(
            (dproj, dh, land.at[task % 3])[k],
            (dproj_all, dh_all, gy_all)[k].at[place(task)],
            store_sem.at[k],
        )

    def load(k, task):
        return pltpu.make_async_copy(
            (dg_all, qkv_all, ctx_all, lse_all, std_all)[k].at[place(task)],
            (dg, qkv, ctx, lse, std)[k],
            load_sem.at[k],
        )

    def load_before(task):
        return pltpu.make_async_copy(qkv_all.at[place(task) - 1], before, load_sem.at[5])

    def spread(task):
        dctx[...] = dot(land[task % 3], wo[...], NT).astype(bf16)
        for at in range(0, wd.shape[0], 256):
            part = slice(at, at + 256)
            value = (dot(land[task % 3], wd[part, :], NT) * dg[:, part].astype(f32)).astype(bf16)
            dh[:, part] = value
            side_h[:, part] += jnp.sum(value.astype(f32), axis=0, keepdims=True)

    def attend_back(second):
        half = 1 if second else 0
        table = (cosine[half], ahead[half], behind[half])
        for h in range(heads):
            at = [slice((3 * h + k) * size, (3 * h + k + 1) * size) for k in range(3)]
            mid = slice(h * size, (h + 1) * size)
            q = qkv[:, at[0]]
            d_ctx = dctx[:, mid]
            logsum = lse[:, h * LANES : h * LANES + 1]
            delta = jnp.sum(d_ctx.astype(f32) * ctx[:, mid].astype(f32), axis=-1, keepdims=True)

            def pieces(held, masked):
                k, v = held[:, at[1]], held[:, at[2]]
                s = dot(q, k, NT) * scale
                if masked:
                    s = jnp.where(pq[...] >= pk[...], s, masked_score)
                p = jnp.exp(s - logsum)
                d_chance = dot(d_ctx, v, NT)
                d_scores = (p * (d_chance - delta)).astype(bf16)
                return dot(d_scores, k), dot(d_scores, q, TN), dot(p.astype(bf16), d_ctx, TN)

            dq, dk, dv = pieces(qkv, True)
            if second:
                dq_more, dk_more, dv_more = pieces(before, False)
                dq = dq + dq_more
                dk_held[:, mid] = dk_more
                dv_held[:, mid] = dv_more
            else:
                dk = dk + dk_held[:, mid]
                dv = dv + dv_held[:, mid]
            made = (turn(dq * scale, *table, -1.0), turn(dk * scale, *table, -1.0), dv)
            for k in range(3):
                value = made[k].astype(bf16)
                dproj[:, at[k]] = value
                side_q[:, at[k]] += jnp.sum(value.astype(f32), axis=0, keepdims=True)

    def merge_rows(core, result):
        at = moves.share(core)
        for column in range(0, wq.shape[0], 512):
            columns = slice(column, column + 512)
            one = dot(dproj[at, :], wq[columns, :], NT)
            two = dot(dh[at, :], wi[columns, :], NT)
            standard = std[at, columns].astype(f32)
            vectors[0:1, columns] += jnp.sum(one * standard, axis=0, keepdims=True)
            vectors[2:3, columns] += jnp.sum(two * standard, axis=0, keepdims=True)
            value = one * gains[0, :, columns] + two * gains[1, :, columns]
            result[:, columns] = value.astype(result.dtype)

    def keep_last():
        return pltpu.make_async_copy(handed.at[(tasks - 1) % 2], last_rows, last_sem)

    def side_products():
        for k, (side, weight) in enumerate(((side_q, wq), (side_h, wi))):
            value = side[...]
            high = value.astype(bf16)
            rest = (value - high.astype(f32)).astype(bf16)
            pair = jnp.concatenate([high, rest, jnp.zeros((14, value.shape[1]), bf16)])
            vectors[2 * k + 1 : 2 * k + 2, :] = jnp.sum(dot(pair, weight[...], NT), axis=0, keepdims=True)

    @pl.loop(0, tasks + LAG + 2)
    def _(step):
        g = step - base
        c = g - 1
        r = g - 2

        def load_rows(task, held, number):
            return pltpu.make_async_copy(held.at[number], kept.at[task % 3], load_sem.at[6])

        def load_x(task, held):
            return pltpu.make_async_copy(held.at[place(task)], xrows, load_sem.at[7])

        @when(step < tasks)
        def _():
            states_home.each(step, True)

        @when(valid(g) & source)
        def _():
            load_rows(g, gin, place(g)).start()

        @when(valid(r))
        def _():
            @when(first)
            def _():
                load_x(r, xin).start()

            @when(jnp.logical_not(first))
            def _():
                load_x(r, xarrive).start()


        @when(valid(c))
        def _():
            @when(gathers(c))
            def _():
                gather_wait(moves, c)

            @when(jnp.logical_not(gathers(c)))
            def _():
                load_early(c).wait()

            store(2, c).start()

            @when(c == 0)
            def _():
                weights[0].wait()
                weights[1].wait()

            @when(c >= 1)
            def _():
                for k in range(2):
                    store(k, c - 1).wait()

            load(0, c).wait()
            spread(c)
            store(1, c).start()
            for k in range(1, 5):
                load(k, c).wait()
            store(2, c).wait()

        @when(valid(g))
        def _():
            @when(first)
            def _():
                moves.hand(g).wait_recv()
                load_rows(g, arrive, g).start()

            load_rows(g, gin, g).wait()

            @when((g >= 1) & gathers(g - 1))
            def _():
                gather_free(moves, g - 1)

            @when(gathers(g))
            def _():
                gather_start(moves, g, kept[g % 3])

            @when(jnp.logical_not(gathers(g)))
            def _():
                load_early(g).start()

            vectors[4:5, :] += jnp.sum(kept[g % 3].astype(f32), axis=0, keepdims=True)

        @when(valid(c))
        def _():
            @when(c % 2 == 0)
            def _():
                load_before(c).wait()
                attend_back(True)

            @when(c % 2 == 1)
            def _():
                attend_back(False)

            store(0, c).start()

        @when(valid(r))
        def _():
            @when(r == tasks - 1)
            def _():
                side_products()

            e = reduce_second(moves, r, mine)
            load_x(r, xin).wait()

            @when(r >= 2)
            def _():
                grads_home.each(place(r - 2), False)

                @when(source)
                def _():
                    moves.hand(r - 2).wait_send()

            standard, inverse = standardize(xrows[...])
            d_input = kept[r % 3].astype(f32) + inverse * (
                e
                - jnp.mean(e, axis=-1, keepdims=True)
                - standard * jnp.mean(e * standard, axis=-1, keepdims=True)
            )
            handed[r % 2] = d_input.astype(bf16)

            @when(source)
            def _():
                moves.hand(r).start()

            @when(r < tasks - 1)
            def _():
                grads_home.each(place(r), True)

            @when(r == tasks - 1)
            def _():
                keep_last().start()

        @when(valid(c))
        def _():
            @when(c == 0)
            def _():
                weights[2].wait()
                weights[3].wait()

            @when(c >= 1)
            def _():
                moves.give_theirs(c - 1).wait_send()

            merge_rows(1 - moves.core, theirs)
            moves.give_theirs(c).start()

            merge_rows(moves.core, mine)
            reduce_first(moves, c, mine)

        @when(valid(g) & gathers(g))
        def _():
            gather_pass(moves, g)

        @when(valid(c + 1))
        def _():
            for k in range(5):
                load(k, c + 1).start()

            @when((c + 1) % 2 == 0)
            def _():
                load_before(c + 1).start()

    @when(gathers(tasks - 1))
    def _():
        gather_free(moves, tasks - 1)

    drain(moves, tasks - 1)
    for k in range(2):
        store(k, tasks - 1).wait()
    grads_home.each(place(tasks - 2), False)
    keep_last().wait()
    for task in range(tasks - 2, tasks):

        @when(source)
        def _(task=task):
            moves.hand(task).wait_send()

    grads_home.wait(tasks - 2)

    @when(line.z >= line.blocks)
    def _():
        for other in line.others():
            grads_home.take(tasks - 1, 0, other).wait_recv()

    for task in range(tasks):
        states_home.each(task, False)
    states_home.wait(tasks)


def backward_pass(gin, xin, xarrive, states, early, qkv, dg, ctx, lse, std, wq, wi, wo, wd, gains, tables, pq, pk, chips, heads):
    tasks, rows, width = xin.shape
    count = lax.axis_size("ctx")
    home_sems = line_semaphores(tasks, count)[1]
    block = pq.shape[0]
    units, inner = wd.shape[0], wo.shape[0]
    anywhere = pl.BlockSpec(memory_space=pl.ANY)
    vmem = pl.BlockSpec(memory_space=pltpu.VMEM)
    shape = jax.ShapeDtypeStruct
    return pl.pallas_call(
        partial(backward_kernel, (tasks, chips, rows, heads)),
        out_shape=[
            shape((tasks, block, width), bf16),
            shape((tasks, block, 3 * inner), bf16),
            shape((tasks, block, units), bf16),
            shape((tasks // 2 * count, 2 * rows // count, width), bf16),
            shape((tasks // 2 * count, 2 * rows // count, width), bf16),
            shape((rows, width), bf16),
            shape((tasks, rows, width), bf16),
            shape((8, width), f32),
            shape((1, 3 * inner), f32),
            shape((1, units), f32),
        ],
        in_specs=[anywhere] * 14 + [vmem] * 6,
        out_specs=[anywhere] * 7 + [vmem] * 3,
        scratch_shapes=[
            pltpu.VMEM(wq.shape, bf16),
            pltpu.VMEM(wi.shape, bf16),
            pltpu.VMEM(wo.shape, bf16),
            pltpu.VMEM(wd.shape, bf16),
            pltpu.VMEM((3, block, width), bf16),
            pltpu.VMEM((block, units), bf16),
            pltpu.VMEM((block, units), bf16),
            pltpu.VMEM((block, 3 * inner), bf16),
            pltpu.VMEM((block, 3 * inner), bf16),
            pltpu.VMEM((block, inner), bf16),
            pltpu.VMEM((block, heads * LANES), f32),
            pltpu.VMEM((block, width), bf16),
            pltpu.VMEM((block, inner), bf16),
            pltpu.VMEM((block, 3 * inner), bf16),
            pltpu.VMEM((block, inner), f32),
            pltpu.VMEM((block, inner), f32),
            pltpu.VMEM((3, rows, width), bf16),
            pltpu.VMEM((chips * rows, width), bf16),
            pltpu.VMEM((chips * rows, width), f32),
            pltpu.VMEM((2, chips * rows, width), bf16),
            pltpu.VMEM((chips * rows, width), bf16),
            pltpu.VMEM((2, chips - 1, rows, width), bf16),
            pltpu.VMEM((2, rows, width), bf16),
            pltpu.VMEM((rows, width), bf16),
            pltpu.SemaphoreType.DMA((4,)),
            pltpu.SemaphoreType.DMA((9,)),
            pltpu.SemaphoreType.DMA((3,)),
            pltpu.SemaphoreType.DMA,
        ]
        + home_sems
        + home_sems
        + move_semaphores(tasks, chips),
        compiler_params=pltpu.CompilerParams(
            collective_id=5, has_side_effects=True, vmem_limit_bytes=PASS_VMEM
        ),
        cost_estimate=pl.CostEstimate(
            flops=2 * tasks * block * width * (3 * inner + 2 * units + inner),
            bytes_accessed=tasks * block * width * 20,
            transcendentals=0,
        ),
        name="backward_pass",
    )(gin, xin, xarrive, states, early, qkv, dg, ctx, lse, std, wq, wi, wo, wd, gains, *tables, pq, pk)


CHUNK = 256
PIECE = 32
SKEW = 2


def reduce_kernel(
    plan, act, ctx, dproj, dhid, gy, std, late, gains, biases, sums, small,
    out, small_out, late_home, from_left, from_right,
    rhs, raw, lhs, own, inbox, outbox, stage, small_in,
    rhs_sem, raw_sem, right_sem, left_sem, final_sem, load_sem, sent, stage_left, stage_right, out_sem,
    small_sent, small_got, late_sent, late_got, late_kept,
):
    bounds, tasks, count, piece, skew, ring = plan
    sources = (dproj, dhid, act, ctx)
    total_chunks = bounds[-1]
    per_chunk = CHUNK // piece
    pieces = total_chunks * per_chunk
    width = gy.shape[-1]
    tile = width // per_chunk
    block = raw.shape[2]
    z = lax.axis_index("ctx")
    last = count - 1
    root = count // 2
    turn_at = max(root, last - root)
    low, high, middle = z < root, z > root, z == root

    barrier = pltpu.get_barrier_semaphore()
    for shift in range(1, count):
        pl.semaphore_signal(
            barrier,
            inc=1,
            device_id={"ctx": lax.rem(z + shift, count)},
            device_id_type=pl.DeviceIdType.MESH,
        )

    def small_copy(source, target):
        return pltpu.make_async_remote_copy(
            src_ref=small,
            dst_ref=small_in.at[source],
            send_sem=small_sent.at[target],
            recv_sem=small_got.at[source],
            device_id={"ctx": target},
            device_id_type=pl.DeviceIdType.MESH,
        )

    late_blocks = count // 2
    late_rows = late.shape[0] // late_blocks

    def late_copy(k, source):
        return pltpu.make_async_remote_copy(
            src_ref=late.at[pl.ds(k * late_rows, late_rows)],
            dst_ref=late_home.at[source],
            send_sem=late_sent.at[k],
            recv_sem=late_got.at[source],
            device_id={"ctx": k},
            device_id_type=pl.DeviceIdType.MESH,
        )

    def late_keep(k):
        return pltpu.make_async_copy(
            late.at[pl.ds(k * late_rows, late_rows)], late_home.at[z], late_kept
        )

    def rhs_copy(k):
        return pltpu.make_async_copy((std, gy)[k].at[pl.ds(0, tasks)], rhs.at[k], rhs_sem.at[k])

    def each_source(chunk, act_on):
        for g, source in enumerate(sources):

            @pl.when((chunk >= bounds[g]) & (chunk < bounds[g + 1]))
            def _(g=g, source=source):
                column = pl.multiple_of((chunk - bounds[g]) * CHUNK, CHUNK)
                act_on(
                    pltpu.make_async_copy(
                        source.at[pl.ds(0, tasks), :, pl.ds(column, CHUNK)],
                        raw.at[chunk % 2],
                        raw_sem.at[chunk % 2],
                    )
                )

    def take(chunk):
        each_source(chunk, lambda copy: copy.wait())
        for k in range(tasks):
            lhs[:, k * block : (k + 1) * block] = raw[chunk % 2, k].T
        each_source(chunk + 1, lambda copy: copy.start())

    def multiply(chunk, part):
        second = jnp.where(chunk >= bounds[2], 1, 0)
        group = second + jnp.where(chunk >= bounds[1], 1, 0)
        columns = pl.ds(pl.multiple_of(part * tile, tile), tile)
        value = dot(lhs[:, :block], rhs[second, 0, :, columns])
        for k in range(1, tasks):
            value = value + dot(lhs[:, k * block : (k + 1) * block], rhs[second, k, :, columns])
        row = pl.multiple_of(chunk * CHUNK, CHUNK)
        value = value * gains[group, :, columns] + sums[pl.ds(row, CHUNK), :] * biases[group, :, columns]
        own[chunk % ring, :, columns] = value.astype(bf16)

    def rows_of(index):
        return pl.ds(pl.multiple_of(index * piece, piece), piece)

    def own_piece(index):
        inner = pl.multiple_of((index % per_chunk) * piece, piece)
        return own[(index // per_chunk) % ring, pl.ds(inner, piece), :]

    def remote(source, target_rows, send_sem, recv_sem, target):
        return pltpu.make_async_remote_copy(
            src_ref=source,
            dst_ref=target_rows,
            send_sem=send_sem,
            recv_sem=recv_sem,
            device_id={"ctx": target},
            device_id_type=pl.DeviceIdType.MESH,
        )

    def inward(index, right):
        landing, arrived, target = (from_left, right_sem, z + 1) if right else (from_right, left_sem, z - 1)
        return remote(
            outbox.at[index % 2], landing.at[rows_of(index)], sent.at[index % 2], arrived.at[index], target
        )

    def announce(index, right):
        return remote(
            stage.at[index % 2],
            out.at[rows_of(index)],
            (stage_right if right else stage_left).at[index % 2],
            final_sem.at[index],
            z + 1 if right else z - 1,
        )

    def onward(index, right):
        return remote(
            out.at[rows_of(index)],
            out.at[rows_of(index)],
            sent.at[2 + index % 2],
            final_sem.at[index],
            z + 1 if right else z - 1,
        )

    def load(index, right):
        landing = from_left if right else from_right
        return pltpu.make_async_copy(
            landing.at[rows_of(index)], inbox.at[0 if right else 1], load_sem.at[0 if right else 1]
        )

    def valid(index):
        return (index >= 0) & (index < pieces)

    def side(step, right):
        mine = low if right else high
        hops = z if right else last - z
        inner = step - hops * skew
        comes = hops > 0

        @pl.when(mine & valid(inner) & comes)
        def _():
            inward(inner, right).wait_recv()
            load(inner, right).start()

        @pl.when(mine & valid(inner))
        def _():
            @pl.when(inner >= 2)
            def _():
                inward(inner - 2, right).wait_send()

            @pl.when(comes)
            def _():
                load(inner, right).wait()
                value = own_piece(inner).astype(f32) + inbox[0 if right else 1].astype(f32)
                outbox[inner % 2] = value.astype(bf16)

            @pl.when(jnp.logical_not(comes))
            def _():
                outbox[inner % 2] = own_piece(inner)

            inward(inner, right).start()

        away = root - z if right else z - root
        outer = step - (turn_at + away) * skew

        @pl.when(mine & valid(outer))
        def _():
            onward(outer, not right).wait_recv()

            @pl.when(comes)
            def _():
                @pl.when(outer >= 2)
                def _():
                    onward(outer - 2, not right).wait_send()

                onward(outer, not right).start()

    def out_copy(index):
        return pltpu.make_async_copy(stage.at[index % 2], out.at[rows_of(index)], out_sem.at[index % 2])

    def stage_done(index):
        out_copy(index).wait()
        announce(index, False).wait_send()
        if root < last:
            announce(index, True).wait_send()

    def centre(step):
        index = step - turn_at * skew

        @pl.when(middle & valid(index))
        def _():
            inward(index, True).wait_recv()
            load(index, True).start()
            if root < last:
                inward(index, False).wait_recv()
                load(index, False).start()

            @pl.when(index >= 2)
            def _():
                stage_done(index - 2)

            load(index, True).wait()
            value = own_piece(index).astype(f32) + inbox[0].astype(f32)
            if root < last:
                load(index, False).wait()
                value = value + inbox[1].astype(f32)
            stage[index % 2] = value.astype(bf16)
            announce(index, False).start()
            if root < last:
                announce(index, True).start()
            out_copy(index).start()

    rhs_copy(0).start()
    each_source(0, lambda copy: copy.start())
    rhs_copy(1).start()
    take(0)
    rhs_copy(0).wait()

    @pl.loop(0, per_chunk)
    def _(part):
        multiply(0, part)

    pl.semaphore_wait(barrier, count - 1)
    small_in[z] = small[...]
    for shift in range(1, count):
        small_copy(z, lax.rem(z + shift, count)).start()
    for k in range(late_blocks):

        @pl.when(z != k)
        def _(k=k):
            late_copy(k, z).start()

        @pl.when(z == k)
        def _(k=k):
            late_keep(k).start()

    @pl.loop(0, pieces + (turn_at + max(root, last - root)) * skew)
    def _(step):
        side(step, True)
        side(step, False)
        centre(step)
        chunk, part = step // per_chunk + 1, step % per_chunk

        @pl.when(chunk < total_chunks)
        def _():
            @pl.when(part == 0)
            def _():
                take(chunk)

                @pl.when(chunk == bounds[2])
                def _():
                    rhs_copy(1).wait()

            multiply(chunk, part)

    for shift in range(1, count):
        other = lax.rem(z + shift, count)
        small_copy(z, other).wait_send()
        small_copy(other, other).wait_recv()
    for k in range(late_blocks):

        @pl.when(z != k)
        def _(k=k):
            late_copy(k, z).wait_send()

        @pl.when(z == k)
        def _(k=k):
            late_keep(k).wait()
            for shift in range(1, count):
                late_copy(k, lax.rem(z + shift, count)).wait_recv()

    value = small_in[0]
    for k in range(1, count):
        value = value + small_in[k]
    small_out[...] = value
    for back in (2, 1):
        for right in (True, False):

            @pl.when(low if right else high)
            def _(right=right, back=back):
                inward(pieces - back, right).wait_send()

                @pl.when((z > 0) & (z < last))
                def _():
                    onward(pieces - back, not right).wait_send()

        @pl.when(middle)
        def _(back=back):
            stage_done(pieces - back)


def reduce_gradients(act, ctx, dproj, dhid, gy, std, late, gains, biases, sums, small, tasks):
    count = lax.axis_size("ctx")
    block, width = gy.shape[1:]
    bounds = [0]
    for source in (dproj, dhid, act, ctx):
        bounds.append(bounds[-1] + source.shape[2] // CHUNK)
    total = bounds[-1] * CHUNK
    pieces = total // PIECE
    ring = count // 2 * SKEW // (CHUNK // PIECE) + 3
    plan = (tuple(bounds), tasks, count, PIECE, SKEW, ring)
    anywhere = pl.BlockSpec(memory_space=pl.ANY)
    vmem = pl.BlockSpec(memory_space=pltpu.VMEM)
    result = jax.ShapeDtypeStruct((total, width), bf16)
    late_shape = jax.ShapeDtypeStruct((count, 2 * late.shape[0] // count, width), bf16)
    out, small_out, late_home, _, _ = pl.pallas_call(
        partial(reduce_kernel, plan),
        out_shape=[result, jax.ShapeDtypeStruct(small.shape, f32), late_shape, result, result],
        in_specs=[anywhere] * 7 + [vmem] * 4,
        out_specs=[anywhere, vmem, anywhere, anywhere, anywhere],
        scratch_shapes=[
            pltpu.VMEM((2, tasks, block, width), bf16),
            pltpu.VMEM((2, tasks, block, CHUNK), bf16),
            pltpu.VMEM((CHUNK, tasks * block), bf16),
            pltpu.VMEM((ring, CHUNK, width), bf16),
            pltpu.VMEM((2, PIECE, width), bf16),
            pltpu.VMEM((2, PIECE, width), bf16),
            pltpu.VMEM((2, PIECE, width), bf16),
            pltpu.VMEM((count,) + small.shape, f32),
            pltpu.SemaphoreType.DMA((2,)),
            pltpu.SemaphoreType.DMA((2,)),
            pltpu.SemaphoreType.DMA((pieces,)),
            pltpu.SemaphoreType.DMA((pieces,)),
            pltpu.SemaphoreType.DMA((pieces,)),
            pltpu.SemaphoreType.DMA((2,)),
            pltpu.SemaphoreType.DMA((4,)),
            pltpu.SemaphoreType.DMA((2,)),
            pltpu.SemaphoreType.DMA((2,)),
            pltpu.SemaphoreType.DMA((2,)),
            pltpu.SemaphoreType.DMA((count,)),
            pltpu.SemaphoreType.DMA((count,)),
            pltpu.SemaphoreType.DMA((count // 2,)),
            pltpu.SemaphoreType.DMA((count,)),
            pltpu.SemaphoreType.DMA,
        ],
        compiler_params=pltpu.CompilerParams(
            collective_id=7, has_side_effects=True, vmem_limit_bytes=60 * 1024 * 1024
        ),
        cost_estimate=pl.CostEstimate(
            flops=2 * total * width * tasks * block,
            bytes_accessed=8 * total * width,
            transcendentals=0,
        ),
        name="reduce_gradients",
    )(act, ctx, dproj, dhid, gy, std, late, gains, biases, sums, small)
    return out, small_out, late_home


def turned_kernel(part, out):
    out[...] = part[...].astype(f32).T


def turned(total, start, count):
    width = total.shape[1]
    wide = 2 * CHUNK if start % (2 * CHUNK) == 0 and count % (2 * CHUNK) == 0 else CHUNK
    return pl.pallas_call(
        turned_kernel,
        out_shape=jax.ShapeDtypeStruct((width, count), f32),
        grid=(count // wide,),
        in_specs=[pl.BlockSpec((wide, width), lambda i: (start // wide + i, 0))],
        out_specs=pl.BlockSpec((width, wide), lambda i: (0, i)),
        compiler_params=pltpu.CompilerParams(vmem_limit_bytes=32 * 1024 * 1024),
        name="turned",
    )(total)


def turned_heads_kernel(heads, part, out):
    size = part.shape[0] // heads
    for h in range(heads):
        out[:, h, :] = part[h * size : (h + 1) * size, :].astype(f32).T


def turned_heads(total, start, count, heads):
    width = total.shape[1]
    return pl.pallas_call(
        partial(turned_heads_kernel, heads),
        out_shape=jax.ShapeDtypeStruct((width, heads, count // heads), f32),
        grid=(width // CHUNK,),
        in_specs=[pl.BlockSpec((count, CHUNK), lambda i: (start // count, i))],
        out_specs=pl.BlockSpec((CHUNK, heads, count // heads), lambda i: (i, 0, 0)),
        compiler_params=pltpu.CompilerParams(vmem_limit_bytes=32 * 1024 * 1024),
        name="turned_heads",
    )(total)


def body(
    inputs,
    out_grads,
    norm1_gain,
    norm1_bias,
    norm2_gain,
    norm2_bias,
    w_qkv,
    b_qkv,
    w_out,
    b_out,
    input_projection,
    input_bias_vector,
    down_projection,
    b_down,
):
    ctx_count = lax.axis_size("ctx")
    tensor = lax.axis_size("tensor")
    micro, _, rows, seqs, width = inputs.shape
    heads = w_qkv.shape[2]
    head_cols = w_qkv.shape[3]
    first = lax.axis_index("section") == 0
    per_device = micro * seqs // ctx_count
    blocks = ctx_count // 2
    tasks = 2 * per_device

    chosen = jnp.where(first, inputs[:, 0], out_grads[:, 0])
    chosen = chosen.transpose(0, 2, 1, 3).reshape(per_device, ctx_count, rows, width)

    wq = w_qkv[0].reshape(width, heads * head_cols)
    wi = input_projection[0]
    wo = w_out[0].reshape(-1, width)
    wd = down_projection[0]
    gain_one, bias_one, gain_two, bias_two = norm1_gain[0], norm1_bias[0], norm2_gain[0], norm2_bias[0]
    norms = jnp.stack([gain_one, bias_one, gain_two, bias_two], axis=1)
    out_bias = (b_out[0] + b_down[0])[None]

    relative, tables = position_tables(None, blocks, rows, tensor)
    places_q, places_k = relative[:, None], relative[None, :]

    chips = tensor // 2
    stacked_tables = [jnp.stack(pair) for pair in zip(*tables)]
    std_all, qkv, act_all, dg_all, ctx_all, lse_all, chosen_rows, states, arrive, early = forward_pass(
        chosen,
        wq,
        wi,
        wo,
        wd,
        b_qkv[0].reshape(1, -1),
        input_bias_vector,
        norms,
        out_bias,
        stacked_tables,
        places_q,
        places_k,
        chips,
        heads,
    )
    gains = jnp.stack([gain_one, gain_two])[:, None]
    gy_all, dproj_all, dh_all, dx_home, states_home, last_rows, _, vectors, side_q, side_h = backward_pass(
        chosen_rows,
        chosen_rows,
        arrive,
        states,
        early,
        qkv,
        dg_all,
        ctx_all,
        lse_all,
        std_all,
        wq,
        wi,
        wo,
        wd,
        gains,
        stacked_tables,
        places_q,
        places_k,
        chips,
        heads,
    )
    vectors = vectors[:5]

    d_b_qkv, d_b_in = side_q[0], side_h[0]
    units, inner = wd.shape[0], wo.shape[0]
    sums = jnp.concatenate([d_b_qkv, d_b_in, jnp.zeros((units + inner,), f32)])[:, None]
    gains = jnp.stack([gain_one, gain_two, jnp.ones_like(gain_one)])[:, None]
    biases = jnp.stack([bias_one, bias_two, jnp.zeros_like(bias_one)])[:, None]
    mask = 1
    while mask < tensor:
        vectors = vectors + lax.ppermute(vectors, "tensor", [(k, k ^ mask) for k in range(tensor)])
        mask *= 2
    sides = jnp.concatenate([d_b_qkv, d_b_in])
    side_rows = -(-sides.shape[0] // width)
    small = jnp.zeros((-(-(5 + side_rows) // 8) * 8, width), f32)
    small = small.at[:5].set(vectors)
    small = small.at[5 : 5 + side_rows].set(
        jnp.pad(sides, (0, side_rows * width - sides.shape[0])).reshape(side_rows, width)
    )
    summed, small, late_home = reduce_gradients(
        act_all, ctx_all, dproj_all, dh_all, gy_all, std_all, last_rows, gains, biases, sums, small, tasks
    )
    columns = wq.shape[1]
    vectors = small[:5]
    sides = small[5 : 5 + side_rows].reshape(-1)
    d_b_qkv, d_b_in = sides[: d_b_qkv.shape[0]], sides[d_b_qkv.shape[0] : sides.shape[0]]
    d_b_in = d_b_in[: wi.shape[1]]
    d_w_qkv = turned_heads(summed, 0, columns, heads)
    d_w_in = turned(summed, columns, units)
    d_w_down = summed[columns + units : columns + 2 * units].astype(f32)
    d_w_out = summed[columns + 2 * units :].astype(f32)

    def homeward(pieces):
        return pieces.reshape(micro, seqs, rows, width).transpose(0, 2, 1, 3)[None, :, None]

    states = homeward(states_home)
    late_home = jnp.where(lax.axis_index("ctx") < blocks, late_home, dx_home[-ctx_count:])
    input_grads = homeward(jnp.concatenate([dx_home[:-ctx_count], late_home])).astype(f32)
    return (
        states,
        input_grads,
        vectors[0][None],
        vectors[1][None],
        vectors[2][None],
        vectors[3][None],
        d_w_qkv.reshape(w_qkv.shape),
        d_b_qkv.reshape(b_qkv.shape),
        d_w_out.reshape(w_out.shape),
        vectors[4][None],
        d_w_in[None],
        d_b_in[None],
        d_w_down[None],
        vectors[4][None],
    )


def solution(mesh):
    return jax.shard_map(
        body,
        mesh=mesh,
        in_specs=(
            P(None, "ctx", "tensor", None, None),
            P(None, "ctx", "tensor", None, None),
            P("section", None),
            P("section", None),
            P("section", None),
            P("section", None),
            P("section", None, "tensor", None),
            P("section", "tensor", None),
            P("section", "tensor", None, None),
            P("section", None),
            P("section", None, "tensor"),
            P("section", "tensor"),
            P("section", "tensor", None),
            P("section", None),
        ),
        out_specs=(
            P("section", None, "ctx", "tensor", None, None),
            P("section", None, "ctx", "tensor", None, None),
            P("section", None),
            P("section", None),
            P("section", None),
            P("section", None),
            P("section", None, "tensor", None),
            P("section", "tensor", None),
            P("section", "tensor", None, None),
            P("section", None),
            P("section", None, "tensor"),
            P("section", "tensor"),
            P("section", "tensor", None),
            P("section", None),
        ),
        check_vma=False,
    )
```

```python
from functools import partial

import jax
import jax.numpy as jnp
import numpy as np
from jax import lax
from jax.experimental import pallas as pl
from jax.experimental.pallas import tpu as pltpu
from jax.sharding import PartitionSpec as P

ROT = 64
LAG = 3
LANES = 128
epsilon = 1e-05
masked_score = -1e30
f32 = jnp.float32
bf16 = jnp.bfloat16
NT = (((1,), (1,)), ((), ()))
TN = (((0,), (0,)), ((), ()))
NN = (((1,), (0,)), ((), ()))
PASS_VMEM = 62 * 1024 * 1024


def dot(a, b, dims=NN):
    return lax.dot_general(a, b, dims, preferred_element_type=f32)


def standardize(rows):
    values = rows.astype(f32)
    average = jnp.mean(values, axis=-1, keepdims=True)
    centred = values - average
    inverse = lax.rsqrt(jnp.mean(centred * centred, axis=-1, keepdims=True) + epsilon)
    return centred * inverse, inverse


def position_tables(blocks, rows, tensor):
    frequency = (1.0 / 10000.0 ** (np.arange(0, ROT, 2) / ROT)).astype(np.float32)
    core, chip, c, i = np.meshgrid(
        np.arange(2), np.arange(tensor // 2), np.arange(blocks), np.arange(rows), indexing="ij"
    )
    relative = (c * (rows * tensor) + (chip * 2 + core) * rows + i).reshape(-1).astype(np.int32)
    tables = []
    for part in range(2):
        places = (relative + part * blocks * rows * tensor).astype(np.float32)
        angles = (places[:, None] * frequency[None, :]).astype(np.float64)
        cosine, sine = np.cos(angles), np.sin(angles)
        none = np.zeros_like(sine)
        rest = np.zeros((relative.shape[0], LANES - ROT))
        tables.append(
            (
                np.concatenate([cosine, cosine, rest + 1.0], axis=-1),
                np.concatenate([-sine, none, rest], axis=-1),
                np.concatenate([none, sine, rest], axis=-1),
            )
        )
    return relative, [jnp.asarray(np.stack(pair).astype(np.float32)) for pair in zip(*tables)]


def turn(values, cosine, ahead, behind, sign):
    half = ROT // 2
    lead = values[:, :LANES]
    turned = pltpu.roll(lead, LANES - half, 1) * ahead + pltpu.roll(lead, half, 1) * behind
    return jnp.concatenate([lead * cosine + sign * turned, values[:, LANES:]], axis=1)


class Moves:
    def __init__(self, plan, land, arrive, core_land, chip_land, theirs, low, handed, sems):
        self.tasks, self.chips, self.rows = plan
        self.land, self.arrive, self.core_land, self.chip_land = land, arrive, core_land, chip_land
        self.theirs, self.low, self.handed = theirs, low, handed
        self.slots = land.shape[0]
        (
            self.got_chip, self.got_core, self.got_theirs, self.got_low, self.got_hand,
            self.put_chip, self.put_core, self.put_theirs, self.put_low, self.put_hand,
        ) = sems
        self.section = lax.axis_index("section")
        self.index = lax.axis_index("tensor")
        self.total = 2 * self.chips
        self.chip, self.core = self.index // 2, self.index % 2
        self.mate = self.chip * 2 + 1 - self.core

    def mate_on(self, shift):
        return lax.rem(self.index + 2 * shift, self.total)

    def part(self, member):
        at = (member % 2) * self.chips + member // 2
        return pl.ds(pl.multiple_of(at * self.rows, self.rows), self.rows)

    def share(self, core):
        size = self.chips * self.rows
        return pl.ds(pl.multiple_of(core * size, size), size)

    def of_chip(self, chip):
        return pl.ds(pl.multiple_of(chip * self.rows, self.rows), self.rows)

    def remote(self, source, target, sent, arrived, **device):
        return pltpu.make_async_remote_copy(
            src_ref=source,
            dst_ref=target,
            send_sem=sent,
            recv_sem=arrived,
            device_id=device,
            device_id_type=pl.DeviceIdType.MESH,
        )

    def greet(self, line):
        barrier = pltpu.get_barrier_semaphore()
        peers = [{"section": 1 - self.section}, {"tensor": self.mate}]
        peers += [{"ctx": other} for other in line.others()]
        peers += [{"tensor": self.mate_on(shift)} for shift in range(1, self.chips)]
        for peer in peers:
            pl.semaphore_signal(barrier, inc=1, device_id=peer, device_id_type=pl.DeviceIdType.MESH)
        pl.semaphore_wait(barrier, len(peers))

    def gather_chip(self, task, shift, member=None):
        rows = self.land.at[task % self.slots, self.part(self.index if member is None else member)]
        return self.remote(
            rows,
            rows,
            self.put_chip.at[shift - 1],
            self.got_chip.at[task, shift - 1],
            tensor=self.mate_on(shift),
        )

    def gather_chip_in(self, task, shift):
        return self.gather_chip(task, shift, lax.rem(self.index + self.total - 2 * shift, self.total))

    def gather_core(self, task, shift, member=None):
        if member is None:
            member = lax.rem(self.index + self.total - 2 * shift, self.total)
        rows = self.land.at[task % self.slots, self.part(member)]
        return self.remote(
            rows,
            rows,
            self.put_core.at[shift],
            self.got_core.at[task, shift],
            tensor=self.mate,
        )

    def gather_core_in(self, task, shift):
        return self.gather_core(task, shift, lax.rem(self.mate + self.total - 2 * shift, self.total))

    def give_theirs(self, task):
        return self.remote(
            self.theirs, self.core_land.at[task % 2], self.put_theirs, self.got_theirs.at[task], tensor=self.mate
        )

    def give_low(self, task, shift):
        return self.remote(
            self.low.at[self.of_chip(lax.rem(self.chip + shift, self.chips))],
            self.chip_land.at[task % 2, shift - 1],
            self.put_low.at[shift - 1],
            self.got_low.at[task, shift - 1],
            tensor=self.mate_on(shift),
        )

    def hand(self, task):
        return self.remote(
            self.handed.at[task % 2],
            self.arrive.at[task],
            self.put_hand.at[task % 2],
            self.got_hand.at[task],
            section=1 - self.section,
        )


class Line:
    def __init__(self, rows):
        self.rows = rows
        self.count = lax.axis_size("ctx")
        self.blocks = self.count // 2
        self.z = lax.axis_index("ctx")

    def others(self):
        return [lax.rem(self.z + shift, self.count) for shift in range(1, self.count)]

    def remote(self, source, target, sent, arrived, device):
        return pltpu.make_async_remote_copy(
            src_ref=source,
            dst_ref=target,
            send_sem=sent,
            recv_sem=arrived,
            device_id={"ctx": device},
            device_id_type=pl.DeviceIdType.MESH,
        )

    def block(self, at):
        return pl.ds(pl.multiple_of(at * self.rows, self.rows), self.rows)

    def set_in(self, chosen, landed, put, got, kept):
        self.chosen, self.landed, self.put_in, self.got_in, self.kept_in = chosen, landed, put, got, kept

    def bring(self, j, shift, source=None):
        source = self.z if source is None else source
        half = source // self.blocks
        return self.remote(
            self.chosen.at[j, lax.rem(self.z + shift, self.count)],
            self.landed.at[2 * j + half, self.block(source - half * self.blocks)],
            self.put_in.at[j, shift - 1],
            self.got_in.at[j, source],
            lax.rem(self.z + shift, self.count),
        )

    def bring_own(self, j):
        half = self.z // self.blocks
        return pltpu.make_async_copy(
            self.chosen.at[j, self.z],
            self.landed.at[2 * j + half, self.block(self.z - half * self.blocks)],
            self.kept_in.at[j],
        )

    def bring_start(self, j):
        for shift in range(1, self.count):
            self.bring(j, shift).start()
        self.bring_own(j).start()

    def bring_wait(self, task):
        j, half = task // 2, task % 2
        for k in range(self.blocks):
            source = half * self.blocks + k

            @pl.when(source != self.z)
            def _():
                self.bring(j, 1, source).wait_recv()

            @pl.when(source == self.z)
            def _():
                self.bring_own(j).wait()

    def bring_done(self, count):
        for j in range(count):
            for shift in range(1, self.count):
                self.bring(j, shift).wait_send()


class Home:
    def __init__(self, line, source, home, put, got, kept):
        self.line, self.source, self.home = line, source, home
        self.put, self.got, self.kept = put, got, kept

    def take(self, task, k, sender=None):
        line = self.line
        sender = line.z if sender is None else sender
        return line.remote(
            self.source(task).at[pl.ds(k * line.rows, line.rows)],
            self.home.at[(task // 2) * line.count + sender],
            self.put.at[task, k],
            self.got.at[task // 2, sender],
            (task % 2) * line.blocks + k,
        )

    def keep(self, task, k):
        line = self.line
        return pltpu.make_async_copy(
            self.source(task).at[pl.ds(k * line.rows, line.rows)],
            self.home.at[(task // 2) * line.count + line.z],
            self.kept.at[task],
        )

    def each(self, task, begin):
        line = self.line
        for k in range(line.blocks):
            there = (task % 2) * line.blocks + k

            @pl.when(there != line.z)
            def _():
                copy = self.take(task, k)
                copy.start() if begin else copy.wait_send()

            @pl.when(there == line.z)
            def _():
                copy = self.keep(task, k)
                copy.start() if begin else copy.wait()

    def wait(self, tasks):
        for j in range(tasks // 2):
            for other in self.line.others():
                self.take(2 * j, 0, other).wait_recv()


def line_semaphores(tasks, count):
    dma = pltpu.SemaphoreType.DMA
    half = tasks // 2
    return [dma((half, count - 1)), dma((half, count)), dma((half,))], [
        dma((tasks, count // 2)),
        dma((half, count)),
        dma((tasks,)),
    ]


class Early:
    def __init__(self, moves, source, gathered, got_chip, got_core, put_chip, put_core, kept):
        self.moves, self.source, self.gathered = moves, source, gathered
        self.got_chip, self.got_core, self.put_chip, self.put_core = got_chip, got_core, put_chip, put_core
        self.kept = kept

    def at(self, task, member):
        return self.gathered.at[task, self.moves.part(member)]

    def behind(self, start, shift):
        return lax.rem(start + self.moves.total - 2 * shift, self.moves.total)

    def chip(self, task, shift, member=None):
        member = self.moves.index if member is None else member
        return self.moves.remote(
            self.source.at[task],
            self.at(task, member),
            self.put_chip.at[task, shift - 1],
            self.got_chip.at[task, shift - 1],
            tensor=self.moves.mate_on(shift),
        )

    def core(self, task, shift, member=None):
        member = self.behind(self.moves.index, shift) if member is None else member
        rows = self.at(task, member)
        return self.moves.remote(
            self.source.at[task] if shift == 0 else rows,
            rows,
            self.put_core.at[task, shift],
            self.got_core.at[task, shift],
            tensor=self.moves.mate,
        )

    def keep(self, task):
        return pltpu.make_async_copy(
            self.source.at[task], self.at(task, self.moves.index), self.kept.at[task]
        )

    def start(self, task):
        for shift in range(1, self.moves.chips):
            self.chip(task, shift).start()
        self.core(task, 0).start()
        self.keep(task).start()

    def hand_on(self, task):
        for shift in range(1, self.moves.chips):
            self.chip(task, shift, self.behind(self.moves.index, shift)).wait_recv()
            self.core(task, shift).start()

    def finish(self, task):
        self.keep(task).wait()
        for shift in range(1, self.moves.chips):
            self.chip(task, shift).wait_send()
        for shift in range(self.moves.chips):
            self.core(task, shift).wait_send()
            self.core(task, shift, self.behind(self.moves.mate, shift)).wait_recv()


def early_semaphores(tasks, chips):
    dma = pltpu.SemaphoreType.DMA
    return [dma((tasks, chips - 1)), dma((tasks, chips)), dma((tasks, chips - 1)), dma((tasks, chips)), dma((tasks,))]


def opposite(task):
    return task + 1 - 2 * (task % 2)


def reduce_first(moves, task, mine):
    moves.give_theirs(task).wait_recv()

    @pl.when(task >= 1)
    def _():
        for shift in range(1, moves.chips):
            moves.give_low(task - 1, shift).wait_send()

    value = mine[...] + moves.core_land[task % 2].astype(f32)
    mine[...] = value
    moves.low[...] = value.astype(bf16)
    for shift in range(1, moves.chips):
        moves.give_low(task, shift).start()


def reduce_second(moves, task, mine):
    value = mine[moves.of_chip(moves.chip), :]
    for shift in range(1, moves.chips):
        moves.give_low(task, shift).wait_recv()
        value = value + moves.chip_land[task % 2, shift - 1].astype(f32)
    return value


def gather_start(moves, task, value):
    moves.land[task % moves.slots, moves.part(moves.index), :] = value
    for shift in range(1, moves.chips):
        moves.gather_chip(task, shift).start()
    moves.gather_core(task, 0).start()


def gather_free(moves, task):
    for shift in range(1, moves.chips):
        moves.gather_chip(task, shift).wait_send()
    for shift in range(moves.chips):
        moves.gather_core(task, shift).wait_send()


def gather_pass(moves, task):
    for shift in range(1, moves.chips):
        moves.gather_chip_in(task, shift).wait_recv()
        moves.gather_core(task, shift).start()


def gather_wait(moves, task):
    for shift in range(moves.chips):
        moves.gather_core_in(task, shift).wait_recv()


def drain(moves, task):
    for shift in range(1, moves.chips):
        moves.give_low(task, shift).wait_send()
    moves.give_theirs(task).wait_send()


def when(condition):
    return pl.when(condition)


def forward_kernel(
    plan, chosen, wq_all, wi_all, wo_all, wd_all, bq_in, bi_in, norms, out_bias, cosine, ahead, behind, pq, pk,
    std_all, qkv_all, act_all, dg_all, ctx_all, lse_all, xin, states, arrive, early_all,
    wq, wi, wo, wd, bq, bi, land, qkv, act, dg, ctx, lse, kept, theirs, mine, core_land, low, chip_land, handed,
    weight_sem, load_sem, store_sem, state_sem, put_in, got_in, kept_in,
    early_a, early_b, early_c, early_d, early_e, *sems,
):
    tasks, chips, rows, heads = plan
    line = Line(chosen.shape[2])
    line.set_in(chosen, xin, put_in, got_in, kept_in)
    size = wq.shape[1] // (3 * heads)
    moves = Moves((tasks, chips, rows), land, arrive, core_land, chip_land, theirs, low, handed, sems)
    first = moves.section == 0
    base = jnp.where(first, 0, LAG)
    early = Early(moves, xin, early_all, early_a, early_b, early_c, early_d, early_e)
    early_count = min(tasks, 2 * (LAG - 1))

    weights = [
        pltpu.make_async_copy(a, b, weight_sem.at[k])
        for k, (a, b) in enumerate(((wq_all, wq), (wi_all, wi), (wo_all, wo), (wd_all, wd)))
    ]
    moves.greet(line)
    line.bring_start(0)
    for copy in weights:
        copy.start()

    @when(jnp.logical_not(first))
    def _():
        for j in range(1, tasks // 2):
            line.bring_start(j)

    def valid(task):
        return (task >= 0) & (task < tasks)

    def keep_state(task):
        return pltpu.make_async_copy(handed.at[task % 2], states.at[task], state_sem.at[task % 2])

    def fold(weight, bias_in, bias, gain_column):
        bias[...] = bias_in[...]
        step = 256

        @pl.loop(0, weight.shape[0] // step)
        def _(k):
            at = pl.ds(pl.multiple_of(k * step, step), step)
            value = weight[at, :].astype(f32)
            gain = norms[at, gain_column : gain_column + 1]
            shift = norms[at, gain_column + 1 : gain_column + 2]
            bias[...] += jnp.sum(value * shift, axis=0, keepdims=True)
            weight[at, :] = (value * gain).astype(bf16)

    def store(k, task):
        return pltpu.make_async_copy(
            (qkv.at[task % 2], act, dg, ctx, lse, land.at[task % 3])[k],
            (qkv_all, act_all, dg_all, ctx_all, lse_all, std_all)[k].at[task],
            store_sem.at[k],
        )

    def project(task):
        half = task % 2
        table = (cosine[half], ahead[half], behind[half])
        for h in range(heads):
            for k in range(3):
                columns = slice((3 * h + k) * size, (3 * h + k + 1) * size)
                z = dot(land[task % 3], wq[:, columns]) + bq[:, columns]
                if k < 2:
                    z = turn(z, *table, 1.0)
                qkv[half, :, columns] = z.astype(bf16)

    def attend(task, second):
        half = 1 if second else 0
        scale = size**-0.5
        for h in range(heads):
            at = [slice((3 * h + k) * size, (3 * h + k + 1) * size) for k in range(3)]
            q = qkv[half, :, at[0]]
            s = dot(q, qkv[half, :, at[1]], NT) * scale
            s = jnp.where(pq[...] >= pk[...], s, masked_score)
            peak = jnp.max(s, axis=-1, keepdims=True)
            if second:
                sp = dot(q, qkv[0, :, at[1]], NT) * scale
                peak = jnp.maximum(peak, jnp.max(sp, axis=-1, keepdims=True))
            p = jnp.exp(s - peak)
            total = jnp.sum(p, axis=-1, keepdims=True)
            if second:
                pp = jnp.exp(sp - peak)
                total = total + jnp.sum(pp, axis=-1, keepdims=True)
            share = 1.0 / total
            value = dot((p * share).astype(bf16), qkv[half, :, at[2]])
            if second:
                value = value + dot((pp * share).astype(bf16), qkv[0, :, at[2]])
            ctx[:, h * size : (h + 1) * size] = value.astype(bf16)
            lse[:, h * LANES : (h + 1) * LANES] = jnp.broadcast_to(
                peak + jnp.log(total), (q.shape[0], LANES)
            )

    def expand(task):
        for at in range(0, wi.shape[1], 256):
            columns = slice(at, at + 256)
            h = dot(land[task % 3], wi[:, columns]) + bi[:, columns]
            phi = 0.5 + 0.5 * lax.erf(h * (0.5**0.5))
            density = jnp.exp(h * h * -0.5) * 0.3989422804014327
            act[:, columns] = (h * phi).astype(bf16)
            dg[:, columns] = (phi + h * density).astype(bf16)

    def branch_rows(core, result):
        at = moves.share(core)
        for column in range(0, wo.shape[1], 512):
            columns = slice(column, column + 512)
            value = dot(ctx[at, :], wo[:, columns]) + dot(act[at, :], wd[:, columns])
            result[:, columns] = value.astype(result.dtype)

    weights[0].wait()
    fold(wq, bq_in, bq, 0)
    weights[1].wait()
    fold(wi, bi_in, bi, 2)
    weights[2].wait()
    weights[3].wait()

    @pl.loop(0, tasks + LAG + 2)
    def _(step):
        g = step - base
        c = g - 1
        r = g - 2

        def load_rows(task, held):
            return pltpu.make_async_copy(held.at[task], kept.at[task % 3], load_sem)

        @when(first & (step % 2 == 0) & (step // 2 + 1 < tasks // 2))
        def _():
            line.bring_start(step // 2 + 1)

        @when(first & (step < tasks))
        def _():
            line.bring_wait(step)

        for k in range(2):
            late = 2 * (step - 1) + k

            @when(jnp.logical_not(first) & (late >= 0) & (late < early_count))
            def _(late=late):
                early.hand_on(opposite(late))

        for k in range(2):
            fresh = 2 * step + k

            @when(jnp.logical_not(first) & (fresh < early_count))
            def _(fresh=fresh):
                line.bring_wait(opposite(fresh))
                early.start(opposite(fresh))

        @when(valid(g) & first)
        def _():
            load_rows(g, xin).start()

        @when(valid(c))
        def _():
            gather_wait(moves, c)

            @when(c >= 1)
            def _():
                for k in range(6):
                    store(k, c - 1).wait()

            store(5, c).start()
            project(c)
            store(0, c).start()

        @when(valid(g) & jnp.logical_not(first))
        def _():
            moves.hand(g).wait_recv()
            load_rows(g, arrive).start()

        @when(valid(c))
        def _():
            @when(c % 2 == 0)
            def _():
                attend(c, False)

            @when(c % 2 == 1)
            def _():
                attend(c, True)

            store(3, c).start()
            store(4, c).start()

        @when(valid(g))
        def _():
            load_rows(g, xin).wait()

            @when(g >= 1)
            def _():
                gather_free(moves, g - 1)

            gather_start(moves, g, standardize(kept[g % 3])[0].astype(bf16))

        @when(valid(c))
        def _():
            expand(c)
            store(1, c).start()
            store(2, c).start()

        @when(valid(r))
        def _():
            value = reduce_second(moves, r, mine)

            @when(r >= 2)
            def _():
                keep_state(r - 2).wait()

                @when(first)
                def _():
                    moves.hand(r - 2).wait_send()

            handed[r % 2] = (kept[r % 3].astype(f32) + value + out_bias[...]).astype(bf16)

            @when(first)
            def _():
                moves.hand(r).start()

            keep_state(r).start()

        @when(valid(c))
        def _():
            @when(c >= 1)
            def _():
                moves.give_theirs(c - 1).wait_send()

            branch_rows(1 - moves.core, theirs)
            moves.give_theirs(c).start()

            branch_rows(moves.core, mine)
            reduce_first(moves, c, mine)

        @when(valid(g))
        def _():
            gather_pass(moves, g)

    gather_free(moves, tasks - 1)
    drain(moves, tasks - 1)
    for k in range(6):
        store(k, tasks - 1).wait()

    @when(jnp.logical_not(first))
    def _():
        for task in range(early_count):
            early.finish(opposite(task))
        for task in range(early_count, tasks):
            line.bring_wait(opposite(task))

    line.bring_done(tasks // 2)
    for task in range(tasks - 2, tasks):
        keep_state(task).wait()

        @when(first)
        def _(task=task):
            moves.hand(task).wait_send()


def move_semaphores(tasks, chips):
    dma = pltpu.SemaphoreType.DMA
    return [
        dma((tasks, chips - 1)),
        dma((tasks, chips)),
        dma((tasks,)),
        dma((tasks, chips - 1)),
        dma((tasks,)),
        dma((chips - 1,)),
        dma((chips,)),
        dma,
        dma((chips - 1,)),
        dma((2,)),
    ]


def forward_pass(chosen, wq, wi, wo, wd, bq, bi, norms, out_bias, tables, pq, pk, chips, heads):
    per_device, count, part_rows, width = chosen.shape
    tasks, rows = 2 * per_device, count // 2 * part_rows
    in_sems = line_semaphores(tasks, count)[0]
    block = pq.shape[0]
    units, inner = wd.shape[0], wo.shape[0]
    anywhere = pl.BlockSpec(memory_space=pl.ANY)
    vmem = pl.BlockSpec(memory_space=pltpu.VMEM)
    shape = jax.ShapeDtypeStruct
    return pl.pallas_call(
        partial(forward_kernel, (tasks, chips, rows, heads)),
        out_shape=[
            shape((tasks, block, width), bf16),
            shape((tasks, block, 3 * inner), bf16),
            shape((tasks, block, units), bf16),
            shape((tasks, block, units), bf16),
            shape((tasks, block, inner), bf16),
            shape((tasks, block, heads * LANES), f32),
            shape((tasks, rows, width), bf16),
            shape((tasks, rows, width), bf16),
            shape((tasks, rows, width), bf16),
            shape((tasks, block, width), bf16),
        ],
        in_specs=[anywhere] * 5 + [vmem] * 9,
        out_specs=[anywhere] * 10,
        scratch_shapes=[
            pltpu.VMEM(wq.shape, bf16),
            pltpu.VMEM(wi.shape, bf16),
            pltpu.VMEM(wo.shape, bf16),
            pltpu.VMEM(wd.shape, bf16),
            pltpu.VMEM(bq.shape, f32),
            pltpu.VMEM(bi.shape, f32),
            pltpu.VMEM((3, block, width), bf16),
            pltpu.VMEM((2, block, 3 * inner), bf16),
            pltpu.VMEM((block, units), bf16),
            pltpu.VMEM((block, units), bf16),
            pltpu.VMEM((block, inner), bf16),
            pltpu.VMEM((block, heads * LANES), f32),
            pltpu.VMEM((3, rows, width), bf16),
            pltpu.VMEM((chips * rows, width), bf16),
            pltpu.VMEM((chips * rows, width), f32),
            pltpu.VMEM((2, chips * rows, width), bf16),
            pltpu.VMEM((chips * rows, width), bf16),
            pltpu.VMEM((2, chips - 1, rows, width), bf16),
            pltpu.VMEM((2, rows, width), bf16),
            pltpu.SemaphoreType.DMA((4,)),
            pltpu.SemaphoreType.DMA,
            pltpu.SemaphoreType.DMA((6,)),
            pltpu.SemaphoreType.DMA((2,)),
        ]
        + in_sems
        + early_semaphores(tasks, chips)
        + move_semaphores(tasks, chips),
        compiler_params=pltpu.CompilerParams(
            collective_id=3, has_side_effects=True, vmem_limit_bytes=PASS_VMEM
        ),
        cost_estimate=pl.CostEstimate(
            flops=2 * tasks * block * width * (3 * inner + 2 * units + inner),
            bytes_accessed=tasks * block * width * 16,
            transcendentals=0,
        ),
        name="forward_pass",
    )(chosen, wq, wi, wo, wd, bq, bi, norms, out_bias, *tables, pq, pk)


def backward_kernel(
    plan, gin, xin, xarrive, states, early_all, qkv_all, dg_all, ctx_all, lse_all, std_all, wq_all, wi_all, wo_all, wd_all,
    gains, cosine, ahead, behind, pq, pk,
    gy_all, dproj_all, dh_all, home, state_home, last_rows, arrive, vectors, side_q, side_h,
    wq, wi, wo, wd, land, dg, dh, qkv, before, ctx, lse, std, dctx, dproj, dk_held, dv_held,
    kept, theirs, mine, core_land, low, chip_land, handed, xrows,
    weight_sem, load_sem, store_sem, last_sem,
    put_home, got_home, kept_home, put_state, got_state, kept_state, *sems,
):
    tasks, chips, rows, heads = plan
    line = Line(home.shape[1])
    grads_home = Home(line, lambda task: handed.at[place(task) % 2], home, put_home, got_home, kept_home)
    states_home = Home(line, lambda task: states.at[task], state_home, put_state, got_state, kept_state)
    size = wq.shape[1] // (3 * heads)
    scale = size**-0.5

    place = opposite
    moves = Moves((tasks, chips, rows), land, arrive, core_land, chip_land, theirs, low, handed, sems)
    first = moves.section == 0
    source = moves.section == 1
    base = jnp.where(source, 0, LAG)
    early_count = min(tasks, 2 * (LAG - 1))

    def gathers(task):
        return first | (task >= early_count)

    def load_early(task):
        return pltpu.make_async_copy(early_all.at[place(task)], land.at[task % 3], load_sem.at[8])

    weights = [
        pltpu.make_async_copy(a, b, weight_sem.at[k])
        for k, (a, b) in enumerate(((wo_all, wo), (wd_all, wd), (wq_all, wq), (wi_all, wi)))
    ]
    for copy in weights[:2]:
        copy.start()
    for total in (vectors, side_q, side_h):
        total[...] = jnp.zeros_like(total)
    moves.greet(line)

    def valid(task):
        return (task >= 0) & (task < tasks)

    def store(k, task):
        return pltpu.make_async_copy(
            (dproj, dh, land.at[task % 3])[k],
            (dproj_all, dh_all, gy_all)[k].at[place(task)],
            store_sem.at[k],
        )

    def load(k, task):
        return pltpu.make_async_copy(
            (dg_all, qkv_all, ctx_all, lse_all, std_all)[k].at[place(task)],
            (dg, qkv, ctx, lse, std)[k],
            load_sem.at[k],
        )

    def load_before(task):
        return pltpu.make_async_copy(qkv_all.at[place(task) - 1], before, load_sem.at[5])

    def spread(task):
        dctx[...] = dot(land[task % 3], wo[...], NT).astype(bf16)
        for at in range(0, wd.shape[0], 256):
            part = slice(at, at + 256)
            value = (dot(land[task % 3], wd[part, :], NT) * dg[:, part].astype(f32)).astype(bf16)
            dh[:, part] = value
            side_h[:, part] += jnp.sum(value.astype(f32), axis=0, keepdims=True)

    def attend_back(second):
        half = 1 if second else 0
        table = (cosine[half], ahead[half], behind[half])
        for h in range(heads):
            at = [slice((3 * h + k) * size, (3 * h + k + 1) * size) for k in range(3)]
            mid = slice(h * size, (h + 1) * size)
            q = qkv[:, at[0]]
            d_ctx = dctx[:, mid]
            logsum = lse[:, h * LANES : h * LANES + 1]
            delta = jnp.sum(d_ctx.astype(f32) * ctx[:, mid].astype(f32), axis=-1, keepdims=True)

            def pieces(held, masked):
                k, v = held[:, at[1]], held[:, at[2]]
                s = dot(q, k, NT) * scale
                if masked:
                    s = jnp.where(pq[...] >= pk[...], s, masked_score)
                p = jnp.exp(s - logsum)
                d_chance = dot(d_ctx, v, NT)
                d_scores = (p * (d_chance - delta)).astype(bf16)
                return dot(d_scores, k), dot(d_scores, q, TN), dot(p.astype(bf16), d_ctx, TN)

            dq, dk, dv = pieces(qkv, True)
            if second:
                dq_more, dk_more, dv_more = pieces(before, False)
                dq = dq + dq_more
                dk_held[:, mid] = dk_more
                dv_held[:, mid] = dv_more
            else:
                dk = dk + dk_held[:, mid]
                dv = dv + dv_held[:, mid]
            made = (turn(dq * scale, *table, -1.0), turn(dk * scale, *table, -1.0), dv)
            for k in range(3):
                value = made[k].astype(bf16)
                dproj[:, at[k]] = value
                side_q[:, at[k]] += jnp.sum(value.astype(f32), axis=0, keepdims=True)

    def merge_rows(core, result):
        at = moves.share(core)
        for column in range(0, wq.shape[0], 512):
            columns = slice(column, column + 512)
            one = dot(dproj[at, :], wq[columns, :], NT)
            two = dot(dh[at, :], wi[columns, :], NT)
            standard = std[at, columns].astype(f32)
            vectors[0:1, columns] += jnp.sum(one * standard, axis=0, keepdims=True)
            vectors[2:3, columns] += jnp.sum(two * standard, axis=0, keepdims=True)
            value = one * gains[0, :, columns] + two * gains[1, :, columns]
            result[:, columns] = value.astype(result.dtype)

    def keep_last():
        return pltpu.make_async_copy(handed.at[(tasks - 1) % 2], last_rows, last_sem)

    def side_products():
        for k, (side, weight) in enumerate(((side_q, wq), (side_h, wi))):
            value = side[...]
            high = value.astype(bf16)
            rest = (value - high.astype(f32)).astype(bf16)
            pair = jnp.concatenate([high, rest, jnp.zeros((14, value.shape[1]), bf16)])
            vectors[2 * k + 1 : 2 * k + 2, :] = jnp.sum(dot(pair, weight[...], NT), axis=0, keepdims=True)

    @pl.loop(0, tasks + LAG + 2)
    def _(step):
        g = step - base
        c = g - 1
        r = g - 2

        def load_rows(task, held, number):
            return pltpu.make_async_copy(held.at[number], kept.at[task % 3], load_sem.at[6])

        def load_x(task, held):
            return pltpu.make_async_copy(held.at[place(task)], xrows, load_sem.at[7])

        @when(step < tasks)
        def _():
            states_home.each(step, True)

        @when(valid(g) & source)
        def _():
            load_rows(g, gin, place(g)).start()

        @when(valid(r))
        def _():
            @when(first)
            def _():
                load_x(r, xin).start()

            @when(jnp.logical_not(first))
            def _():
                load_x(r, xarrive).start()


        @when(valid(c))
        def _():
            @when(gathers(c))
            def _():
                gather_wait(moves, c)

            @when(jnp.logical_not(gathers(c)))
            def _():
                load_early(c).wait()

            store(2, c).start()

            @when(c == 0)
            def _():
                weights[0].wait()
                weights[1].wait()

            @when(c >= 1)
            def _():
                for k in range(2):
                    store(k, c - 1).wait()

            load(0, c).wait()
            spread(c)
            store(1, c).start()
            for k in range(1, 5):
                load(k, c).wait()
            store(2, c).wait()

        @when(valid(g))
        def _():
            @when(first)
            def _():
                moves.hand(g).wait_recv()
                load_rows(g, arrive, g).start()

            load_rows(g, gin, g).wait()

            @when((g >= 1) & gathers(g - 1))
            def _():
                gather_free(moves, g - 1)

            @when(gathers(g))
            def _():
                gather_start(moves, g, kept[g % 3])

            @when(jnp.logical_not(gathers(g)))
            def _():
                load_early(g).start()

            vectors[4:5, :] += jnp.sum(kept[g % 3].astype(f32), axis=0, keepdims=True)

        @when(valid(c))
        def _():
            @when(c % 2 == 0)
            def _():
                load_before(c).wait()
                attend_back(True)

            @when(c % 2 == 1)
            def _():
                attend_back(False)

            store(0, c).start()

        @when(valid(r))
        def _():
            @when(r == tasks - 1)
            def _():
                side_products()

            e = reduce_second(moves, r, mine)
            load_x(r, xin).wait()

            @when(r >= 2)
            def _():
                grads_home.each(place(r - 2), False)

                @when(source)
                def _():
                    moves.hand(r - 2).wait_send()

            standard, inverse = standardize(xrows[...])
            d_input = kept[r % 3].astype(f32) + inverse * (
                e
                - jnp.mean(e, axis=-1, keepdims=True)
                - standard * jnp.mean(e * standard, axis=-1, keepdims=True)
            )
            handed[r % 2] = d_input.astype(bf16)

            @when(source)
            def _():
                moves.hand(r).start()

            @when((r < tasks - 1) | (line.z != line.blocks))
            def _():
                grads_home.each(place(r), True)

            @when((r == tasks - 1) & (line.z == line.blocks))
            def _():
                keep_last().start()

        @when(valid(c))
        def _():
            @when(c == 0)
            def _():
                weights[2].wait()
                weights[3].wait()

            @when(c >= 1)
            def _():
                moves.give_theirs(c - 1).wait_send()

            merge_rows(1 - moves.core, theirs)
            moves.give_theirs(c).start()

            merge_rows(moves.core, mine)
            reduce_first(moves, c, mine)

        @when(valid(g) & gathers(g))
        def _():
            gather_pass(moves, g)

        @when(valid(c + 1))
        def _():
            for k in range(5):
                load(k, c + 1).start()

            @when((c + 1) % 2 == 0)
            def _():
                load_before(c + 1).start()

            @when(c + 1 == 0)
            def _():
                for copy in weights[2:]:
                    copy.start()

    @when(gathers(tasks - 1))
    def _():
        gather_free(moves, tasks - 1)

    drain(moves, tasks - 1)
    for k in range(2):
        store(k, tasks - 1).wait()
    grads_home.each(place(tasks - 2), False)

    @when(line.z != line.blocks)
    def _():
        grads_home.each(place(tasks - 1), False)

    @when(line.z == line.blocks)
    def _():
        keep_last().wait()

    for task in range(tasks - 2, tasks):

        @when(source)
        def _(task=task):
            moves.hand(task).wait_send()

    grads_home.wait(tasks - 2)

    for other in line.others():

        @when((line.z >= line.blocks) | (other != line.blocks))
        def _(other=other):
            grads_home.take(tasks - 1, 0, other).wait_recv()

    for task in range(tasks):
        states_home.each(task, False)
    states_home.wait(tasks)


def backward_pass(gin, xin, xarrive, states, early, qkv, dg, ctx, lse, std, wq, wi, wo, wd, gains, tables, pq, pk, chips, heads):
    tasks, rows, width = xin.shape
    count = lax.axis_size("ctx")
    home_sems = line_semaphores(tasks, count)[1]
    block = pq.shape[0]
    units, inner = wd.shape[0], wo.shape[0]
    anywhere = pl.BlockSpec(memory_space=pl.ANY)
    vmem = pl.BlockSpec(memory_space=pltpu.VMEM)
    shape = jax.ShapeDtypeStruct
    return pl.pallas_call(
        partial(backward_kernel, (tasks, chips, rows, heads)),
        out_shape=[
            shape((tasks, block, width), bf16),
            shape((tasks, block, 3 * inner), bf16),
            shape((tasks, block, units), bf16),
            shape((tasks // 2 * count, 2 * rows // count, width), bf16),
            shape((tasks // 2 * count, 2 * rows // count, width), bf16),
            shape((rows, width), bf16),
            shape((tasks, rows, width), bf16),
            shape((8, width), f32),
            shape((1, 3 * inner), f32),
            shape((1, units), f32),
        ],
        in_specs=[anywhere] * 14 + [vmem] * 6,
        out_specs=[anywhere] * 7 + [vmem] * 3,
        scratch_shapes=[
            pltpu.VMEM(wq.shape, bf16),
            pltpu.VMEM(wi.shape, bf16),
            pltpu.VMEM(wo.shape, bf16),
            pltpu.VMEM(wd.shape, bf16),
            pltpu.VMEM((3, block, width), bf16),
            pltpu.VMEM((block, units), bf16),
            pltpu.VMEM((block, units), bf16),
            pltpu.VMEM((block, 3 * inner), bf16),
            pltpu.VMEM((block, 3 * inner), bf16),
            pltpu.VMEM((block, inner), bf16),
            pltpu.VMEM((block, heads * LANES), f32),
            pltpu.VMEM((block, width), bf16),
            pltpu.VMEM((block, inner), bf16),
            pltpu.VMEM((block, 3 * inner), bf16),
            pltpu.VMEM((block, inner), f32),
            pltpu.VMEM((block, inner), f32),
            pltpu.VMEM((3, rows, width), bf16),
            pltpu.VMEM((chips * rows, width), bf16),
            pltpu.VMEM((chips * rows, width), f32),
            pltpu.VMEM((2, chips * rows, width), bf16),
            pltpu.VMEM((chips * rows, width), bf16),
            pltpu.VMEM((2, chips - 1, rows, width), bf16),
            pltpu.VMEM((2, rows, width), bf16),
            pltpu.VMEM((rows, width), bf16),
            pltpu.SemaphoreType.DMA((4,)),
            pltpu.SemaphoreType.DMA((9,)),
            pltpu.SemaphoreType.DMA((3,)),
            pltpu.SemaphoreType.DMA,
        ]
        + home_sems
        + home_sems
        + move_semaphores(tasks, chips),
        compiler_params=pltpu.CompilerParams(
            collective_id=5, has_side_effects=True, vmem_limit_bytes=PASS_VMEM
        ),
        cost_estimate=pl.CostEstimate(
            flops=2 * tasks * block * width * (3 * inner + 2 * units + inner),
            bytes_accessed=tasks * block * width * 20,
            transcendentals=0,
        ),
        name="backward_pass",
    )(gin, xin, xarrive, states, early, qkv, dg, ctx, lse, std, wq, wi, wo, wd, gains, *tables, pq, pk)


CHUNK = 256
PIECE = 32
SKEW = 2


def reduce_kernel(
    plan, act, ctx, dproj, dhid, gy, std, late, gains, biases, sums, small,
    out, small_out, late_home, from_left, from_right,
    rhs, raw, lhs, own, inbox, outbox, stage, small_in,
    rhs_sem, raw_sem, right_sem, left_sem, final_sem, load_sem, sent, stage_left, stage_right, out_sem,
    small_sent, small_got, late_sent, late_got,
):
    bounds, tasks, count, piece, skew, ring = plan
    sources = (dproj, dhid, act, ctx)
    total_chunks = bounds[-1]
    per_chunk = CHUNK // piece
    pieces = total_chunks * per_chunk
    width = gy.shape[-1]
    tile = width // per_chunk
    block = raw.shape[2]
    z = lax.axis_index("ctx")
    last = count - 1
    root = count // 2
    turn_at = max(root, last - root)
    low, high, middle = z < root, z > root, z == root

    barrier = pltpu.get_barrier_semaphore()
    for shift in range(1, count):
        pl.semaphore_signal(
            barrier,
            inc=1,
            device_id={"ctx": lax.rem(z + shift, count)},
            device_id_type=pl.DeviceIdType.MESH,
        )

    def small_copy(source, target):
        return pltpu.make_async_remote_copy(
            src_ref=small,
            dst_ref=small_in.at[source],
            send_sem=small_sent.at[target],
            recv_sem=small_got.at[source],
            device_id={"ctx": target},
            device_id_type=pl.DeviceIdType.MESH,
        )

    late_blocks = count // 2
    late_rows = late.shape[0] // late_blocks

    def late_copy(k):
        return pltpu.make_async_remote_copy(
            src_ref=late.at[pl.ds(k * late_rows, late_rows)],
            dst_ref=late_home,
            send_sem=late_sent.at[k],
            recv_sem=late_got,
            device_id={"ctx": k},
            device_id_type=pl.DeviceIdType.MESH,
        )

    def rhs_copy(k):
        return pltpu.make_async_copy((std, gy)[k].at[pl.ds(0, tasks)], rhs.at[k], rhs_sem.at[k])

    def each_source(chunk, act_on):
        for g, source in enumerate(sources):

            @pl.when((chunk >= bounds[g]) & (chunk < bounds[g + 1]))
            def _(g=g, source=source):
                column = pl.multiple_of((chunk - bounds[g]) * CHUNK, CHUNK)
                act_on(
                    pltpu.make_async_copy(
                        source.at[pl.ds(0, tasks), :, pl.ds(column, CHUNK)],
                        raw.at[chunk % 2],
                        raw_sem.at[chunk % 2],
                    )
                )

    def take(chunk):
        each_source(chunk, lambda copy: copy.wait())
        for k in range(tasks):
            lhs[:, k * block : (k + 1) * block] = raw[chunk % 2, k].T
        each_source(chunk + 1, lambda copy: copy.start())

    def multiply(chunk, part):
        second = jnp.where(chunk >= bounds[2], 1, 0)
        group = second + jnp.where(chunk >= bounds[1], 1, 0)
        columns = pl.ds(pl.multiple_of(part * tile, tile), tile)
        value = dot(lhs[:, :block], rhs[second, 0, :, columns])
        for k in range(1, tasks):
            value = value + dot(lhs[:, k * block : (k + 1) * block], rhs[second, k, :, columns])
        row = pl.multiple_of(chunk * CHUNK, CHUNK)
        value = value * gains[group, :, columns] + sums[pl.ds(row, CHUNK), :] * biases[group, :, columns]
        own[chunk % ring, :, columns] = value.astype(bf16)

    def rows_of(index):
        return pl.ds(pl.multiple_of(index * piece, piece), piece)

    def own_piece(index):
        inner = pl.multiple_of((index % per_chunk) * piece, piece)
        return own[(index // per_chunk) % ring, pl.ds(inner, piece), :]

    def remote(source, target_rows, send_sem, recv_sem, target):
        return pltpu.make_async_remote_copy(
            src_ref=source,
            dst_ref=target_rows,
            send_sem=send_sem,
            recv_sem=recv_sem,
            device_id={"ctx": target},
            device_id_type=pl.DeviceIdType.MESH,
        )

    def inward(index, right):
        landing, arrived, target = (from_left, right_sem, z + 1) if right else (from_right, left_sem, z - 1)
        return remote(
            outbox.at[index % 2], landing.at[rows_of(index)], sent.at[index % 2], arrived.at[index], target
        )

    def announce(index, right):
        return remote(
            stage.at[index % 2],
            out.at[rows_of(index)],
            (stage_right if right else stage_left).at[index % 2],
            final_sem.at[index],
            z + 1 if right else z - 1,
        )

    def onward(index, right):
        return remote(
            out.at[rows_of(index)],
            out.at[rows_of(index)],
            sent.at[2 + index % 2],
            final_sem.at[index],
            z + 1 if right else z - 1,
        )

    def load(index, right):
        landing = from_left if right else from_right
        return pltpu.make_async_copy(
            landing.at[rows_of(index)], inbox.at[0 if right else 1], load_sem.at[0 if right else 1]
        )

    def valid(index):
        return (index >= 0) & (index < pieces)

    def side(step, right):
        mine = low if right else high
        hops = z if right else last - z
        inner = step - hops * skew
        comes = hops > 0

        @pl.when(mine & valid(inner) & comes)
        def _():
            inward(inner, right).wait_recv()
            load(inner, right).start()

        @pl.when(mine & valid(inner))
        def _():
            @pl.when(inner >= 2)
            def _():
                inward(inner - 2, right).wait_send()

            @pl.when(comes)
            def _():
                load(inner, right).wait()
                value = own_piece(inner).astype(f32) + inbox[0 if right else 1].astype(f32)
                outbox[inner % 2] = value.astype(bf16)

            @pl.when(jnp.logical_not(comes))
            def _():
                outbox[inner % 2] = own_piece(inner)

            inward(inner, right).start()

        away = root - z if right else z - root
        outer = step - (turn_at + away) * skew

        @pl.when(mine & valid(outer))
        def _():
            onward(outer, not right).wait_recv()

            @pl.when(comes)
            def _():
                @pl.when(outer >= 2)
                def _():
                    onward(outer - 2, not right).wait_send()

                onward(outer, not right).start()

    def out_copy(index):
        return pltpu.make_async_copy(stage.at[index % 2], out.at[rows_of(index)], out_sem.at[index % 2])

    def stage_done(index):
        out_copy(index).wait()
        announce(index, False).wait_send()
        if root < last:
            announce(index, True).wait_send()

    def centre(step):
        index = step - turn_at * skew

        @pl.when(middle & valid(index))
        def _():
            inward(index, True).wait_recv()
            load(index, True).start()
            if root < last:
                inward(index, False).wait_recv()
                load(index, False).start()

            @pl.when(index >= 2)
            def _():
                stage_done(index - 2)

            load(index, True).wait()
            value = own_piece(index).astype(f32) + inbox[0].astype(f32)
            if root < last:
                load(index, False).wait()
                value = value + inbox[1].astype(f32)
            stage[index % 2] = value.astype(bf16)
            announce(index, False).start()
            if root < last:
                announce(index, True).start()
            out_copy(index).start()

    rhs_copy(0).start()
    each_source(0, lambda copy: copy.start())
    rhs_copy(1).start()
    take(0)
    rhs_copy(0).wait()

    @pl.loop(0, per_chunk)
    def _(part):
        multiply(0, part)

    pl.semaphore_wait(barrier, count - 1)
    small_in[z] = small[...]
    for shift in range(1, count):
        small_copy(z, lax.rem(z + shift, count)).start()
    @pl.when(middle)
    def _():
        for k in range(late_blocks):
            late_copy(k).start()

    @pl.loop(0, pieces + (turn_at + max(root, last - root)) * skew)
    def _(step):
        side(step, True)
        side(step, False)
        centre(step)
        chunk, part = step // per_chunk + 1, step % per_chunk

        @pl.when(chunk < total_chunks)
        def _():
            @pl.when(part == 0)
            def _():
                take(chunk)

                @pl.when(chunk == bounds[2])
                def _():
                    rhs_copy(1).wait()

            multiply(chunk, part)

    for shift in range(1, count):
        other = lax.rem(z + shift, count)
        small_copy(z, other).wait_send()
        small_copy(other, other).wait_recv()
    @pl.when(middle)
    def _():
        for k in range(late_blocks):
            late_copy(k).wait_send()

    @pl.when(low)
    def _():
        late_copy(0).wait_recv()

    value = small_in[0]
    for k in range(1, count):
        value = value + small_in[k]
    small_out[...] = value
    for back in (2, 1):
        for right in (True, False):

            @pl.when(low if right else high)
            def _(right=right, back=back):
                inward(pieces - back, right).wait_send()

                @pl.when((z > 0) & (z < last))
                def _():
                    onward(pieces - back, not right).wait_send()

        @pl.when(middle)
        def _(back=back):
            stage_done(pieces - back)


def reduce_gradients(act, ctx, dproj, dhid, gy, std, late, gains, biases, sums, small, tasks):
    count = lax.axis_size("ctx")
    block, width = gy.shape[1:]
    bounds = [0]
    for source in (dproj, dhid, act, ctx):
        bounds.append(bounds[-1] + source.shape[2] // CHUNK)
    total = bounds[-1] * CHUNK
    pieces = total // PIECE
    ring = count // 2 * SKEW // (CHUNK // PIECE) + 3
    plan = (tuple(bounds), tasks, count, PIECE, SKEW, ring)
    anywhere = pl.BlockSpec(memory_space=pl.ANY)
    vmem = pl.BlockSpec(memory_space=pltpu.VMEM)
    result = jax.ShapeDtypeStruct((total, width), bf16)
    late_shape = jax.ShapeDtypeStruct((2 * late.shape[0] // count, width), bf16)
    out, small_out, late_home, _, _ = pl.pallas_call(
        partial(reduce_kernel, plan),
        out_shape=[result, jax.ShapeDtypeStruct(small.shape, f32), late_shape, result, result],
        in_specs=[anywhere] * 7 + [vmem] * 4,
        out_specs=[anywhere, vmem, anywhere, anywhere, anywhere],
        scratch_shapes=[
            pltpu.VMEM((2, tasks, block, width), bf16),
            pltpu.VMEM((2, tasks, block, CHUNK), bf16),
            pltpu.VMEM((CHUNK, tasks * block), bf16),
            pltpu.VMEM((ring, CHUNK, width), bf16),
            pltpu.VMEM((2, PIECE, width), bf16),
            pltpu.VMEM((2, PIECE, width), bf16),
            pltpu.VMEM((2, PIECE, width), bf16),
            pltpu.VMEM((count,) + small.shape, f32),
            pltpu.SemaphoreType.DMA((2,)),
            pltpu.SemaphoreType.DMA((2,)),
            pltpu.SemaphoreType.DMA((pieces,)),
            pltpu.SemaphoreType.DMA((pieces,)),
            pltpu.SemaphoreType.DMA((pieces,)),
            pltpu.SemaphoreType.DMA((2,)),
            pltpu.SemaphoreType.DMA((4,)),
            pltpu.SemaphoreType.DMA((2,)),
            pltpu.SemaphoreType.DMA((2,)),
            pltpu.SemaphoreType.DMA((2,)),
            pltpu.SemaphoreType.DMA((count,)),
            pltpu.SemaphoreType.DMA((count,)),
            pltpu.SemaphoreType.DMA((count // 2,)),
            pltpu.SemaphoreType.DMA,
        ],
        compiler_params=pltpu.CompilerParams(
            collective_id=7, has_side_effects=True, vmem_limit_bytes=60 * 1024 * 1024
        ),
        cost_estimate=pl.CostEstimate(
            flops=2 * total * width * tasks * block,
            bytes_accessed=8 * total * width,
            transcendentals=0,
        ),
        name="reduce_gradients",
    )(act, ctx, dproj, dhid, gy, std, late, gains, biases, sums, small)
    return out, small_out, late_home


def turned_kernel(part, out):
    out[...] = part[...].astype(f32).T


def turned(total, start, count):
    width = total.shape[1]
    wide = 2 * CHUNK if start % (2 * CHUNK) == 0 and count % (2 * CHUNK) == 0 else CHUNK
    return pl.pallas_call(
        turned_kernel,
        out_shape=jax.ShapeDtypeStruct((width, count), f32),
        grid=(count // wide,),
        in_specs=[pl.BlockSpec((wide, width), lambda i: (start // wide + i, 0))],
        out_specs=pl.BlockSpec((width, wide), lambda i: (0, i)),
        compiler_params=pltpu.CompilerParams(vmem_limit_bytes=32 * 1024 * 1024),
        name="turned",
    )(total)


def turned_heads_kernel(heads, part, out):
    size = part.shape[0] // heads
    for h in range(heads):
        out[:, h, :] = part[h * size : (h + 1) * size, :].astype(f32).T


def turned_heads(total, start, count, heads):
    width = total.shape[1]
    return pl.pallas_call(
        partial(turned_heads_kernel, heads),
        out_shape=jax.ShapeDtypeStruct((width, heads, count // heads), f32),
        grid=(width // CHUNK,),
        in_specs=[pl.BlockSpec((count, CHUNK), lambda i: (start // count, i))],
        out_specs=pl.BlockSpec((CHUNK, heads, count // heads), lambda i: (i, 0, 0)),
        compiler_params=pltpu.CompilerParams(vmem_limit_bytes=32 * 1024 * 1024),
        name="turned_heads",
    )(total)


def body(
    inputs,
    out_grads,
    norm1_gain,
    norm1_bias,
    norm2_gain,
    norm2_bias,
    w_qkv,
    b_qkv,
    w_out,
    b_out,
    input_projection,
    input_bias_vector,
    down_projection,
    b_down,
):
    ctx_count = lax.axis_size("ctx")
    tensor = lax.axis_size("tensor")
    micro, _, rows, seqs, width = inputs.shape
    heads = w_qkv.shape[2]
    head_cols = w_qkv.shape[3]
    first = lax.axis_index("section") == 0
    per_device = micro * seqs // ctx_count
    blocks = ctx_count // 2
    tasks = 2 * per_device

    chosen = lax.cond(
        first,
        lambda: inputs[:, 0].transpose(0, 2, 1, 3),
        lambda: out_grads[:, 0].transpose(0, 2, 1, 3),
    )
    chosen = chosen.reshape(per_device, ctx_count, rows, width)

    wq = w_qkv[0].reshape(width, heads * head_cols)
    wi = input_projection[0]
    wo = w_out[0].reshape(-1, width)
    wd = down_projection[0]
    gain_one, bias_one, gain_two, bias_two = norm1_gain[0], norm1_bias[0], norm2_gain[0], norm2_bias[0]
    norms = jnp.stack([gain_one, bias_one, gain_two, bias_two], axis=1)
    out_bias = (b_out[0] + b_down[0])[None]

    relative, tables = position_tables(blocks, rows, tensor)
    places_q, places_k = jnp.asarray(relative[:, None]), jnp.asarray(relative[None, :])

    chips = tensor // 2
    std_all, qkv, act_all, dg_all, ctx_all, lse_all, chosen_rows, states, arrive, early = forward_pass(
        chosen,
        wq,
        wi,
        wo,
        wd,
        b_qkv[0].reshape(1, -1),
        input_bias_vector,
        norms,
        out_bias,
        tables,
        places_q,
        places_k,
        chips,
        heads,
    )
    gains = jnp.stack([gain_one, gain_two])[:, None]
    gy_all, dproj_all, dh_all, dx_home, states_home, last_rows, _, vectors, side_q, side_h = backward_pass(
        chosen_rows,
        chosen_rows,
        arrive,
        states,
        early,
        qkv,
        dg_all,
        ctx_all,
        lse_all,
        std_all,
        wq,
        wi,
        wo,
        wd,
        gains,
        tables,
        places_q,
        places_k,
        chips,
        heads,
    )
    vectors = vectors[:5]

    d_b_qkv, d_b_in = side_q[0], side_h[0]
    units, inner = wd.shape[0], wo.shape[0]
    sums = jnp.concatenate([d_b_qkv, d_b_in, jnp.zeros((units + inner,), f32)])[:, None]
    gains = jnp.stack([gain_one, gain_two, jnp.ones_like(gain_one)])[:, None]
    biases = jnp.stack([bias_one, bias_two, jnp.zeros_like(bias_one)])[:, None]
    mask = 1
    while mask < tensor:
        vectors = vectors + lax.ppermute(vectors, "tensor", [(k, k ^ mask) for k in range(tensor)])
        mask *= 2
    sides = jnp.concatenate([d_b_qkv, d_b_in])
    side_rows = -(-sides.shape[0] // width)
    small = jnp.zeros((-(-(5 + side_rows) // 8) * 8, width), f32)
    small = small.at[:5].set(vectors)
    small = small.at[5 : 5 + side_rows].set(
        jnp.pad(sides, (0, side_rows * width - sides.shape[0])).reshape(side_rows, width)
    )
    summed, small, late_home = reduce_gradients(
        act_all, ctx_all, dproj_all, dh_all, gy_all, std_all, last_rows, gains, biases, sums, small, tasks
    )
    columns = wq.shape[1]
    vectors = small[:5]
    sides = small[5 : 5 + side_rows].reshape(-1)
    d_b_qkv, d_b_in = sides[: d_b_qkv.shape[0]], sides[d_b_qkv.shape[0] : sides.shape[0]]
    d_b_in = d_b_in[: wi.shape[1]]
    d_w_qkv = turned_heads(summed, 0, columns, heads)
    d_w_in = turned(summed, columns, units)
    d_w_down = summed[columns + units : columns + 2 * units].astype(f32)
    d_w_out = summed[columns + 2 * units :].astype(f32)

    def homeward(pieces):
        return pieces.reshape(micro, seqs, rows, width).transpose(0, 2, 1, 3)[None, :, None]

    states = homeward(states_home)
    at = (per_device - 1) * ctx_count + blocks
    late_home = jnp.where(lax.axis_index("ctx") < blocks, late_home, dx_home[at])
    input_grads = homeward(lax.dynamic_update_index_in_dim(dx_home, late_home, at, 0)).astype(f32)
    return (
        states,
        input_grads,
        vectors[0][None],
        vectors[1][None],
        vectors[2][None],
        vectors[3][None],
        d_w_qkv.reshape(w_qkv.shape),
        d_b_qkv.reshape(b_qkv.shape),
        d_w_out.reshape(w_out.shape),
        vectors[4][None],
        d_w_in[None],
        d_b_in[None],
        d_w_down[None],
        vectors[4][None],
    )


def solution(mesh):
    return jax.shard_map(
        body,
        mesh=mesh,
        in_specs=(
            P(None, "ctx", "tensor", None, None),
            P(None, "ctx", "tensor", None, None),
            P("section", None),
            P("section", None),
            P("section", None),
            P("section", None),
            P("section", None, "tensor", None),
            P("section", "tensor", None),
            P("section", "tensor", None, None),
            P("section", None),
            P("section", None, "tensor"),
            P("section", "tensor"),
            P("section", "tensor", None),
            P("section", None),
        ),
        out_specs=(
            P("section", None, "ctx", "tensor", None, None),
            P("section", None, "ctx", "tensor", None, None),
            P("section", None),
            P("section", None),
            P("section", None),
            P("section", None),
            P("section", None, "tensor", None),
            P("section", "tensor", None),
            P("section", "tensor", None, None),
            P("section", None),
            P("section", None, "tensor"),
            P("section", "tensor"),
            P("section", "tensor", None),
            P("section", None),
        ),
        check_vma=False,
    )
```

```python
from functools import partial

import jax
import jax.numpy as jnp
import numpy as np
from jax import lax
from jax.experimental import pallas as pl
from jax.experimental.pallas import tpu as pltpu
from jax.sharding import PartitionSpec as P

ROT = 64
LAG = 3
LANES = 128
epsilon = 1e-05
masked_score = -1e30
f32 = jnp.float32
bf16 = jnp.bfloat16
NT = (((1,), (1,)), ((), ()))
TN = (((0,), (0,)), ((), ()))
NN = (((1,), (0,)), ((), ()))
PASS_VMEM = 62 * 1024 * 1024


def dot(a, b, dims=NN):
    return lax.dot_general(a, b, dims, preferred_element_type=f32)


def standardize(rows):
    values = rows.astype(f32)
    average = jnp.mean(values, axis=-1, keepdims=True)
    centred = values - average
    inverse = lax.rsqrt(jnp.mean(centred * centred, axis=-1, keepdims=True) + epsilon)
    return centred * inverse, inverse


def position_tables(blocks, rows, tensor):
    frequency = (1.0 / 10000.0 ** (np.arange(0, ROT, 2) / ROT)).astype(np.float32)
    core, chip, c, i = np.meshgrid(
        np.arange(2), np.arange(tensor // 2), np.arange(blocks), np.arange(rows), indexing="ij"
    )
    relative = (c * (rows * tensor) + (chip * 2 + core) * rows + i).reshape(-1).astype(np.int32)
    tables = []
    for part in range(2):
        places = (relative + part * blocks * rows * tensor).astype(np.float32)
        angles = (places[:, None] * frequency[None, :]).astype(np.float64)
        cosine, sine = np.cos(angles), np.sin(angles)
        none = np.zeros_like(sine)
        rest = np.zeros((relative.shape[0], LANES - ROT))
        tables.append(
            (
                np.concatenate([cosine, cosine, rest + 1.0], axis=-1),
                np.concatenate([-sine, none, rest], axis=-1),
                np.concatenate([none, sine, rest], axis=-1),
            )
        )
    return relative, [jnp.asarray(np.stack(pair).astype(np.float32)) for pair in zip(*tables)]


def turn(values, cosine, ahead, behind, sign):
    half = ROT // 2
    lead = values[:, :LANES]
    turned = pltpu.roll(lead, LANES - half, 1) * ahead + pltpu.roll(lead, half, 1) * behind
    return jnp.concatenate([lead * cosine + sign * turned, values[:, LANES:]], axis=1)


class Moves:
    def __init__(self, plan, land, arrive, core_land, chip_land, theirs, low, handed, sems):
        self.tasks, self.chips, self.rows = plan
        self.land, self.arrive, self.core_land, self.chip_land = land, arrive, core_land, chip_land
        self.theirs, self.low, self.handed = theirs, low, handed
        self.slots = land.shape[0]
        (
            self.got_chip, self.got_core, self.got_theirs, self.got_low, self.got_hand,
            self.put_chip, self.put_core, self.put_theirs, self.put_low, self.put_hand,
        ) = sems
        self.section = lax.axis_index("section")
        self.index = lax.axis_index("tensor")
        self.total = 2 * self.chips
        self.chip, self.core = self.index // 2, self.index % 2
        self.mate = self.chip * 2 + 1 - self.core

    def mate_on(self, shift):
        return lax.rem(self.index + 2 * shift, self.total)

    def part(self, member):
        at = (member % 2) * self.chips + member // 2
        return pl.ds(pl.multiple_of(at * self.rows, self.rows), self.rows)

    def share(self, core):
        size = self.chips * self.rows
        return pl.ds(pl.multiple_of(core * size, size), size)

    def of_chip(self, chip):
        return pl.ds(pl.multiple_of(chip * self.rows, self.rows), self.rows)

    def remote(self, source, target, sent, arrived, **device):
        return pltpu.make_async_remote_copy(
            src_ref=source,
            dst_ref=target,
            send_sem=sent,
            recv_sem=arrived,
            device_id=device,
            device_id_type=pl.DeviceIdType.MESH,
        )

    def greet(self, line):
        barrier = pltpu.get_barrier_semaphore()
        peers = [{"section": 1 - self.section}, {"tensor": self.mate}]
        peers += [{"ctx": other} for other in line.others()]
        peers += [{"tensor": self.mate_on(shift)} for shift in range(1, self.chips)]
        for peer in peers:
            pl.semaphore_signal(barrier, inc=1, device_id=peer, device_id_type=pl.DeviceIdType.MESH)
        pl.semaphore_wait(barrier, len(peers))

    def gather_chip(self, task, shift, member=None):
        rows = self.land.at[task % self.slots, self.part(self.index if member is None else member)]
        return self.remote(
            rows,
            rows,
            self.put_chip.at[shift - 1],
            self.got_chip.at[task, shift - 1],
            tensor=self.mate_on(shift),
        )

    def gather_chip_in(self, task, shift):
        return self.gather_chip(task, shift, lax.rem(self.index + self.total - 2 * shift, self.total))

    def gather_core(self, task, shift, member=None):
        if member is None:
            member = lax.rem(self.index + self.total - 2 * shift, self.total)
        rows = self.land.at[task % self.slots, self.part(member)]
        return self.remote(
            rows,
            rows,
            self.put_core.at[shift],
            self.got_core.at[task, shift],
            tensor=self.mate,
        )

    def gather_core_in(self, task, shift):
        return self.gather_core(task, shift, lax.rem(self.mate + self.total - 2 * shift, self.total))

    def give_theirs(self, task):
        return self.remote(
            self.theirs, self.core_land.at[task % 2], self.put_theirs, self.got_theirs.at[task], tensor=self.mate
        )

    def give_low(self, task, shift):
        return self.remote(
            self.low.at[self.of_chip(lax.rem(self.chip + shift, self.chips))],
            self.chip_land.at[task % 2, shift - 1],
            self.put_low.at[shift - 1],
            self.got_low.at[task, shift - 1],
            tensor=self.mate_on(shift),
        )

    def hand(self, task):
        return self.remote(
            self.handed.at[task % 2],
            self.arrive.at[task],
            self.put_hand.at[task % 2],
            self.got_hand.at[task],
            section=1 - self.section,
        )


class Line:
    def __init__(self, rows):
        self.rows = rows
        self.count = lax.axis_size("ctx")
        self.blocks = self.count // 2
        self.z = lax.axis_index("ctx")

    def others(self):
        return [lax.rem(self.z + shift, self.count) for shift in range(1, self.count)]

    def remote(self, source, target, sent, arrived, device):
        return pltpu.make_async_remote_copy(
            src_ref=source,
            dst_ref=target,
            send_sem=sent,
            recv_sem=arrived,
            device_id={"ctx": device},
            device_id_type=pl.DeviceIdType.MESH,
        )

    def block(self, at):
        return pl.ds(pl.multiple_of(at * self.rows, self.rows), self.rows)

    def set_in(self, chosen, landed, put, got, kept):
        self.chosen, self.landed, self.put_in, self.got_in, self.kept_in = chosen, landed, put, got, kept

    def bring(self, j, shift, source=None):
        source = self.z if source is None else source
        half = source // self.blocks
        return self.remote(
            self.chosen.at[j, lax.rem(self.z + shift, self.count)],
            self.landed.at[2 * j + half, self.block(source - half * self.blocks)],
            self.put_in.at[j, shift - 1],
            self.got_in.at[j, source],
            lax.rem(self.z + shift, self.count),
        )

    def bring_own(self, j):
        half = self.z // self.blocks
        return pltpu.make_async_copy(
            self.chosen.at[j, self.z],
            self.landed.at[2 * j + half, self.block(self.z - half * self.blocks)],
            self.kept_in.at[j],
        )

    def bring_start(self, j):
        for shift in range(1, self.count):
            self.bring(j, shift).start()
        self.bring_own(j).start()

    def bring_wait(self, task):
        j, half = task // 2, task % 2
        for k in range(self.blocks):
            source = half * self.blocks + k

            @pl.when(source != self.z)
            def _():
                self.bring(j, 1, source).wait_recv()

            @pl.when(source == self.z)
            def _():
                self.bring_own(j).wait()

    def bring_done(self, count):
        for j in range(count):
            for shift in range(1, self.count):
                self.bring(j, shift).wait_send()


class Home:
    def __init__(self, line, source, home, put, got, kept):
        self.line, self.source, self.home = line, source, home
        self.put, self.got, self.kept = put, got, kept

    def take(self, task, k, sender=None):
        line = self.line
        sender = line.z if sender is None else sender
        return line.remote(
            self.source(task).at[pl.ds(k * line.rows, line.rows)],
            self.home.at[(task // 2) * line.count + sender],
            self.put.at[task, k],
            self.got.at[task // 2, sender],
            (task % 2) * line.blocks + k,
        )

    def keep(self, task, k):
        line = self.line
        return pltpu.make_async_copy(
            self.source(task).at[pl.ds(k * line.rows, line.rows)],
            self.home.at[(task // 2) * line.count + line.z],
            self.kept.at[task],
        )

    def each(self, task, begin):
        line = self.line
        for k in range(line.blocks):
            there = (task % 2) * line.blocks + k

            @pl.when(there != line.z)
            def _():
                copy = self.take(task, k)
                copy.start() if begin else copy.wait_send()

            @pl.when(there == line.z)
            def _():
                copy = self.keep(task, k)
                copy.start() if begin else copy.wait()

    def wait(self, tasks):
        for j in range(tasks // 2):
            for other in self.line.others():
                self.take(2 * j, 0, other).wait_recv()


def line_semaphores(tasks, count):
    dma = pltpu.SemaphoreType.DMA
    half = tasks // 2
    return [dma((half, count - 1)), dma((half, count)), dma((half,))], [
        dma((tasks, count // 2)),
        dma((half, count)),
        dma((tasks,)),
    ]


class Early:
    def __init__(self, moves, source, gathered, got_chip, got_core, put_chip, put_core, kept):
        self.moves, self.source, self.gathered = moves, source, gathered
        self.got_chip, self.got_core, self.put_chip, self.put_core = got_chip, got_core, put_chip, put_core
        self.kept = kept

    def at(self, task, member):
        return self.gathered.at[task, self.moves.part(member)]

    def behind(self, start, shift):
        return lax.rem(start + self.moves.total - 2 * shift, self.moves.total)

    def chip(self, task, shift, member=None):
        member = self.moves.index if member is None else member
        return self.moves.remote(
            self.source.at[task],
            self.at(task, member),
            self.put_chip.at[task, shift - 1],
            self.got_chip.at[task, shift - 1],
            tensor=self.moves.mate_on(shift),
        )

    def core(self, task, shift, member=None):
        member = self.behind(self.moves.index, shift) if member is None else member
        rows = self.at(task, member)
        return self.moves.remote(
            self.source.at[task] if shift == 0 else rows,
            rows,
            self.put_core.at[task, shift],
            self.got_core.at[task, shift],
            tensor=self.moves.mate,
        )

    def keep(self, task):
        return pltpu.make_async_copy(
            self.source.at[task], self.at(task, self.moves.index), self.kept.at[task]
        )

    def start(self, task):
        for shift in range(1, self.moves.chips):
            self.chip(task, shift).start()
        self.core(task, 0).start()
        self.keep(task).start()

    def hand_on(self, task):
        for shift in range(1, self.moves.chips):
            self.chip(task, shift, self.behind(self.moves.index, shift)).wait_recv()
            self.core(task, shift).start()

    def finish(self, task):
        self.keep(task).wait()
        for shift in range(1, self.moves.chips):
            self.chip(task, shift).wait_send()
        for shift in range(self.moves.chips):
            self.core(task, shift).wait_send()
            self.core(task, shift, self.behind(self.moves.mate, shift)).wait_recv()


def early_semaphores(tasks, chips):
    dma = pltpu.SemaphoreType.DMA
    return [dma((tasks, chips - 1)), dma((tasks, chips)), dma((tasks, chips - 1)), dma((tasks, chips)), dma((tasks,))]


def opposite(task):
    return task + 1 - 2 * (task % 2)


def reduce_first(moves, task, mine):
    moves.give_theirs(task).wait_recv()

    @pl.when(task >= 1)
    def _():
        for shift in range(1, moves.chips):
            moves.give_low(task - 1, shift).wait_send()

    value = mine[...] + moves.core_land[task % 2].astype(f32)
    mine[...] = value
    moves.low[...] = value.astype(bf16)
    for shift in range(1, moves.chips):
        moves.give_low(task, shift).start()


def reduce_second(moves, task, mine):
    value = mine[moves.of_chip(moves.chip), :]
    for shift in range(1, moves.chips):
        moves.give_low(task, shift).wait_recv()
        value = value + moves.chip_land[task % 2, shift - 1].astype(f32)
    return value


def gather_start(moves, task, value):
    moves.land[task % moves.slots, moves.part(moves.index), :] = value
    for shift in range(1, moves.chips):
        moves.gather_chip(task, shift).start()
    moves.gather_core(task, 0).start()


def gather_free(moves, task):
    for shift in range(1, moves.chips):
        moves.gather_chip(task, shift).wait_send()
    for shift in range(moves.chips):
        moves.gather_core(task, shift).wait_send()


def gather_pass(moves, task):
    for shift in range(1, moves.chips):
        moves.gather_chip_in(task, shift).wait_recv()
        moves.gather_core(task, shift).start()


def gather_wait(moves, task):
    for shift in range(moves.chips):
        moves.gather_core_in(task, shift).wait_recv()


def drain(moves, task):
    for shift in range(1, moves.chips):
        moves.give_low(task, shift).wait_send()
    moves.give_theirs(task).wait_send()


def when(condition):
    return pl.when(condition)


def forward_kernel(
    plan, chosen, wq_all, wi_all, wo_all, wd_all, bq_in, bi_in, norms, out_bias, cosine, ahead, behind, pq, pk,
    std_all, qkv_all, act_all, dg_all, ctx_all, lse_all, xin, states, arrive, early_all,
    wq, wi, wo, wd, bq, bi, land, qkv, act, dg, ctx, lse, kept, theirs, mine, core_land, low, chip_land, handed,
    weight_sem, load_sem, store_sem, state_sem, put_in, got_in, kept_in,
    early_a, early_b, early_c, early_d, early_e, *sems,
):
    tasks, chips, rows, heads = plan
    line = Line(chosen.shape[2])
    line.set_in(chosen, xin, put_in, got_in, kept_in)
    size = wq.shape[1] // (3 * heads)
    moves = Moves((tasks, chips, rows), land, arrive, core_land, chip_land, theirs, low, handed, sems)
    first = moves.section == 0
    base = jnp.where(first, 0, LAG)
    early = Early(moves, xin, early_all, early_a, early_b, early_c, early_d, early_e)
    early_count = min(tasks, 2 * (LAG - 1))

    weights = [
        pltpu.make_async_copy(a, b, weight_sem.at[k])
        for k, (a, b) in enumerate(((wq_all, wq), (wi_all, wi), (wo_all, wo), (wd_all, wd)))
    ]
    moves.greet(line)
    line.bring_start(0)
    for copy in weights:
        copy.start()

    @when(jnp.logical_not(first))
    def _():
        for j in range(1, tasks // 2):
            line.bring_start(j)

    def valid(task):
        return (task >= 0) & (task < tasks)

    def keep_state(task):
        return pltpu.make_async_copy(handed.at[task % 2], states.at[task], state_sem.at[task % 2])

    def fold(weight, bias_in, bias, gain_column):
        bias[...] = bias_in[...]
        step = 256

        @pl.loop(0, weight.shape[0] // step)
        def _(k):
            at = pl.ds(pl.multiple_of(k * step, step), step)
            value = weight[at, :].astype(f32)
            gain = norms[at, gain_column : gain_column + 1]
            shift = norms[at, gain_column + 1 : gain_column + 2]
            bias[...] += jnp.sum(value * shift, axis=0, keepdims=True)
            weight[at, :] = (value * gain).astype(bf16)

    def store(k, task):
        return pltpu.make_async_copy(
            (qkv.at[task % 2], act, dg, ctx, lse, land.at[task % 3])[k],
            (qkv_all, act_all, dg_all, ctx_all, lse_all, std_all)[k].at[task],
            store_sem.at[k],
        )

    def project(task):
        half = task % 2
        table = (cosine[half], ahead[half], behind[half])
        for h in range(heads):
            for k in range(3):
                columns = slice((3 * h + k) * size, (3 * h + k + 1) * size)
                z = dot(land[task % 3], wq[:, columns]) + bq[:, columns]
                if k < 2:
                    z = turn(z, *table, 1.0)
                qkv[half, :, columns] = z.astype(bf16)

    def attend(task, second):
        half = 1 if second else 0
        scale = size**-0.5
        for h in range(heads):
            at = [slice((3 * h + k) * size, (3 * h + k + 1) * size) for k in range(3)]
            q = qkv[half, :, at[0]]
            s = dot(q, qkv[half, :, at[1]], NT) * scale
            s = jnp.where(pq[...] >= pk[...], s, masked_score)
            peak = jnp.max(s, axis=-1, keepdims=True)
            if second:
                sp = dot(q, qkv[0, :, at[1]], NT) * scale
                peak = jnp.maximum(peak, jnp.max(sp, axis=-1, keepdims=True))
            p = jnp.exp(s - peak)
            total = jnp.sum(p, axis=-1, keepdims=True)
            if second:
                pp = jnp.exp(sp - peak)
                total = total + jnp.sum(pp, axis=-1, keepdims=True)
            share = 1.0 / total
            value = dot((p * share).astype(bf16), qkv[half, :, at[2]])
            if second:
                value = value + dot((pp * share).astype(bf16), qkv[0, :, at[2]])
            ctx[:, h * size : (h + 1) * size] = value.astype(bf16)
            lse[:, h * LANES : (h + 1) * LANES] = jnp.broadcast_to(
                peak + jnp.log(total), (q.shape[0], LANES)
            )

    def expand(task):
        for at in range(0, wi.shape[1], 256):
            columns = slice(at, at + 256)
            h = dot(land[task % 3], wi[:, columns]) + bi[:, columns]
            phi = 0.5 + 0.5 * lax.erf(h * (0.5**0.5))
            density = jnp.exp(h * h * -0.5) * 0.3989422804014327
            act[:, columns] = (h * phi).astype(bf16)
            dg[:, columns] = (phi + h * density).astype(bf16)

    def branch_rows(core, result):
        at = moves.share(core)
        for column in range(0, wo.shape[1], 512):
            columns = slice(column, column + 512)
            value = dot(ctx[at, :], wo[:, columns]) + dot(act[at, :], wd[:, columns])
            result[:, columns] = value.astype(result.dtype)

    weights[0].wait()
    fold(wq, bq_in, bq, 0)
    weights[1].wait()
    fold(wi, bi_in, bi, 2)
    weights[2].wait()
    weights[3].wait()

    @pl.loop(0, tasks + LAG + 2)
    def _(step):
        g = step - base
        c = g - 1
        r = g - 2

        def load_rows(task, held):
            return pltpu.make_async_copy(held.at[task], kept.at[task % 3], load_sem)

        @when(first & (step % 2 == 0) & (step // 2 + 1 < tasks // 2))
        def _():
            line.bring_start(step // 2 + 1)

        @when(first & (step < tasks))
        def _():
            line.bring_wait(step)

        for k in range(2):
            late = 2 * (step - 1) + k

            @when(jnp.logical_not(first) & (late >= 0) & (late < early_count))
            def _(late=late):
                early.hand_on(opposite(late))

        for k in range(2):
            fresh = 2 * step + k

            @when(jnp.logical_not(first) & (fresh < early_count))
            def _(fresh=fresh):
                line.bring_wait(opposite(fresh))
                early.start(opposite(fresh))

        @when(valid(g) & first)
        def _():
            load_rows(g, xin).start()

        @when(valid(c))
        def _():
            gather_wait(moves, c)

            @when(c >= 1)
            def _():
                for k in range(6):
                    store(k, c - 1).wait()

            store(5, c).start()
            project(c)
            store(0, c).start()

        @when(valid(g) & jnp.logical_not(first))
        def _():
            moves.hand(g).wait_recv()
            load_rows(g, arrive).start()

        @when(valid(c))
        def _():
            @when(c % 2 == 0)
            def _():
                attend(c, False)

            @when(c % 2 == 1)
            def _():
                attend(c, True)

            store(3, c).start()
            store(4, c).start()

        @when(valid(g))
        def _():
            load_rows(g, xin).wait()

            @when(g >= 1)
            def _():
                gather_free(moves, g - 1)

            gather_start(moves, g, standardize(kept[g % 3])[0].astype(bf16))

        @when(valid(c))
        def _():
            expand(c)
            store(1, c).start()
            store(2, c).start()

        @when(valid(r))
        def _():
            value = reduce_second(moves, r, mine)

            @when(r >= 2)
            def _():
                keep_state(r - 2).wait()

                @when(first)
                def _():
                    moves.hand(r - 2).wait_send()

            handed[r % 2] = (kept[r % 3].astype(f32) + value + out_bias[...]).astype(bf16)

            @when(first)
            def _():
                moves.hand(r).start()

            keep_state(r).start()

        @when(valid(c))
        def _():
            @when(c >= 1)
            def _():
                moves.give_theirs(c - 1).wait_send()

            branch_rows(1 - moves.core, theirs)
            moves.give_theirs(c).start()

            branch_rows(moves.core, mine)
            reduce_first(moves, c, mine)

        @when(valid(g))
        def _():
            gather_pass(moves, g)

    gather_free(moves, tasks - 1)
    drain(moves, tasks - 1)
    for k in range(6):
        store(k, tasks - 1).wait()

    @when(jnp.logical_not(first))
    def _():
        for task in range(early_count):
            early.finish(opposite(task))
        for task in range(early_count, tasks):
            line.bring_wait(opposite(task))

    line.bring_done(tasks // 2)
    for task in range(tasks - 2, tasks):
        keep_state(task).wait()

        @when(first)
        def _(task=task):
            moves.hand(task).wait_send()


def move_semaphores(tasks, chips):
    dma = pltpu.SemaphoreType.DMA
    return [
        dma((tasks, chips - 1)),
        dma((tasks, chips)),
        dma((tasks,)),
        dma((tasks, chips - 1)),
        dma((tasks,)),
        dma((chips - 1,)),
        dma((chips,)),
        dma,
        dma((chips - 1,)),
        dma((2,)),
    ]


def forward_pass(chosen, wq, wi, wo, wd, bq, bi, norms, out_bias, tables, pq, pk, chips, heads):
    per_device, count, part_rows, width = chosen.shape
    tasks, rows = 2 * per_device, count // 2 * part_rows
    in_sems = line_semaphores(tasks, count)[0]
    block = pq.shape[0]
    units, inner = wd.shape[0], wo.shape[0]
    anywhere = pl.BlockSpec(memory_space=pl.ANY)
    vmem = pl.BlockSpec(memory_space=pltpu.VMEM)
    shape = jax.ShapeDtypeStruct
    return pl.pallas_call(
        partial(forward_kernel, (tasks, chips, rows, heads)),
        out_shape=[
            shape((tasks, block, width), bf16),
            shape((tasks, block, 3 * inner), bf16),
            shape((tasks, block, units), bf16),
            shape((tasks, block, units), bf16),
            shape((tasks, block, inner), bf16),
            shape((tasks, block, heads * LANES), f32),
            shape((tasks, rows, width), bf16),
            shape((tasks, rows, width), bf16),
            shape((tasks, rows, width), bf16),
            shape((tasks, block, width), bf16),
        ],
        in_specs=[anywhere] * 5 + [vmem] * 9,
        out_specs=[anywhere] * 10,
        scratch_shapes=[
            pltpu.VMEM(wq.shape, bf16),
            pltpu.VMEM(wi.shape, bf16),
            pltpu.VMEM(wo.shape, bf16),
            pltpu.VMEM(wd.shape, bf16),
            pltpu.VMEM(bq.shape, f32),
            pltpu.VMEM(bi.shape, f32),
            pltpu.VMEM((3, block, width), bf16),
            pltpu.VMEM((2, block, 3 * inner), bf16),
            pltpu.VMEM((block, units), bf16),
            pltpu.VMEM((block, units), bf16),
            pltpu.VMEM((block, inner), bf16),
            pltpu.VMEM((block, heads * LANES), f32),
            pltpu.VMEM((3, rows, width), bf16),
            pltpu.VMEM((chips * rows, width), bf16),
            pltpu.VMEM((chips * rows, width), f32),
            pltpu.VMEM((2, chips * rows, width), bf16),
            pltpu.VMEM((chips * rows, width), bf16),
            pltpu.VMEM((2, chips - 1, rows, width), bf16),
            pltpu.VMEM((2, rows, width), bf16),
            pltpu.SemaphoreType.DMA((4,)),
            pltpu.SemaphoreType.DMA,
            pltpu.SemaphoreType.DMA((6,)),
            pltpu.SemaphoreType.DMA((2,)),
        ]
        + in_sems
        + early_semaphores(tasks, chips)
        + move_semaphores(tasks, chips),
        compiler_params=pltpu.CompilerParams(
            collective_id=3, has_side_effects=True, vmem_limit_bytes=PASS_VMEM
        ),
        cost_estimate=pl.CostEstimate(
            flops=2 * tasks * block * width * (3 * inner + 2 * units + inner),
            bytes_accessed=tasks * block * width * 16,
            transcendentals=0,
        ),
        name="forward_pass",
    )(chosen, wq, wi, wo, wd, bq, bi, norms, out_bias, *tables, pq, pk)


def backward_kernel(
    plan, gin, xin, xarrive, states, early_all, qkv_all, dg_all, ctx_all, lse_all, std_all, wq_all, wi_all, wo_all, wd_all,
    gains, cosine, ahead, behind, pq, pk,
    gy_all, dproj_all, dh_all, home, state_home, last_rows, arrive, vectors, side_q, side_h,
    wq, wi, wo, wd, land, dg, dh, qkv, before, ctx, lse, std, dctx, dproj, dk_held, dv_held,
    kept, theirs, mine, core_land, low, chip_land, handed, xrows,
    weight_sem, load_sem, store_sem, last_sem,
    put_home, got_home, kept_home, put_state, got_state, kept_state, *sems,
):
    tasks, chips, rows, heads = plan
    line = Line(home.shape[1])
    grads_home = Home(line, lambda task: handed.at[place(task) % 2], home, put_home, got_home, kept_home)
    states_home = Home(line, lambda task: states.at[task], state_home, put_state, got_state, kept_state)
    size = wq.shape[1] // (3 * heads)
    scale = size**-0.5

    place = opposite
    moves = Moves((tasks, chips, rows), land, arrive, core_land, chip_land, theirs, low, handed, sems)
    first = moves.section == 0
    source = moves.section == 1
    base = jnp.where(source, 0, LAG)
    early_count = min(tasks, 2 * (LAG - 1))

    def gathers(task):
        return first | (task >= early_count)

    def load_early(task):
        return pltpu.make_async_copy(early_all.at[place(task)], land.at[task % 3], load_sem.at[8])

    weights = [
        pltpu.make_async_copy(a, b, weight_sem.at[k])
        for k, (a, b) in enumerate(((wo_all, wo), (wd_all, wd), (wq_all, wq), (wi_all, wi)))
    ]
    for copy in weights[:2]:
        copy.start()
    for total in (vectors, side_q, side_h):
        total[...] = jnp.zeros_like(total)
    moves.greet(line)

    def valid(task):
        return (task >= 0) & (task < tasks)

    def store(k, task):
        return pltpu.make_async_copy(
            (dproj, dh, land.at[task % 3])[k],
            (dproj_all, dh_all, gy_all)[k].at[place(task)],
            store_sem.at[k],
        )

    def load(k, task):
        return pltpu.make_async_copy(
            (dg_all, qkv_all, ctx_all, lse_all, std_all)[k].at[place(task)],
            (dg, qkv, ctx, lse, std)[k],
            load_sem.at[k],
        )

    def load_before(task):
        return pltpu.make_async_copy(qkv_all.at[place(task) - 1], before, load_sem.at[5])

    def spread(task):
        dctx[...] = dot(land[task % 3], wo[...], NT).astype(bf16)
        for at in range(0, wd.shape[0], 256):
            part = slice(at, at + 256)
            value = (dot(land[task % 3], wd[part, :], NT) * dg[:, part].astype(f32)).astype(bf16)
            dh[:, part] = value
            side_h[:, part] += jnp.sum(value.astype(f32), axis=0, keepdims=True)

    def attend_back(second):
        half = 1 if second else 0
        table = (cosine[half], ahead[half], behind[half])
        for h in range(heads):
            at = [slice((3 * h + k) * size, (3 * h + k + 1) * size) for k in range(3)]
            mid = slice(h * size, (h + 1) * size)
            q = qkv[:, at[0]]
            d_ctx = dctx[:, mid]
            logsum = lse[:, h * LANES : h * LANES + 1]
            delta = jnp.sum(d_ctx.astype(f32) * ctx[:, mid].astype(f32), axis=-1, keepdims=True)

            def pieces(held, masked):
                k, v = held[:, at[1]], held[:, at[2]]
                s = dot(q, k, NT) * scale
                if masked:
                    s = jnp.where(pq[...] >= pk[...], s, masked_score)
                p = jnp.exp(s - logsum)
                d_chance = dot(d_ctx, v, NT)
                d_scores = (p * (d_chance - delta)).astype(bf16)
                return dot(d_scores, k), dot(d_scores, q, TN), dot(p.astype(bf16), d_ctx, TN)

            dq, dk, dv = pieces(qkv, True)
            if second:
                dq_more, dk_more, dv_more = pieces(before, False)
                dq = dq + dq_more
                dk_held[:, mid] = dk_more
                dv_held[:, mid] = dv_more
            else:
                dk = dk + dk_held[:, mid]
                dv = dv + dv_held[:, mid]
            made = (turn(dq * scale, *table, -1.0), turn(dk * scale, *table, -1.0), dv)
            for k in range(3):
                value = made[k].astype(bf16)
                dproj[:, at[k]] = value
                side_q[:, at[k]] += jnp.sum(value.astype(f32), axis=0, keepdims=True)

    def merge_rows(core, result):
        at = moves.share(core)
        for column in range(0, wq.shape[0], 512):
            columns = slice(column, column + 512)
            one = dot(dproj[at, :], wq[columns, :], NT)
            two = dot(dh[at, :], wi[columns, :], NT)
            standard = std[at, columns].astype(f32)
            vectors[0:1, columns] += jnp.sum(one * standard, axis=0, keepdims=True)
            vectors[2:3, columns] += jnp.sum(two * standard, axis=0, keepdims=True)
            value = one * gains[0, :, columns] + two * gains[1, :, columns]
            result[:, columns] = value.astype(result.dtype)

    def keep_last():
        return pltpu.make_async_copy(handed.at[(tasks - 1) % 2], last_rows, last_sem)

    def side_products():
        for k, (side, weight) in enumerate(((side_q, wq), (side_h, wi))):
            value = side[...]
            high = value.astype(bf16)
            rest = (value - high.astype(f32)).astype(bf16)
            pair = jnp.concatenate([high, rest, jnp.zeros((14, value.shape[1]), bf16)])
            vectors[2 * k + 1 : 2 * k + 2, :] = jnp.sum(dot(pair, weight[...], NT), axis=0, keepdims=True)

    @pl.loop(0, tasks + LAG + 2)
    def _(step):
        g = step - base
        c = g - 1
        r = g - 2

        def load_rows(task, held, number):
            return pltpu.make_async_copy(held.at[number], kept.at[task % 3], load_sem.at[6])

        def load_x(task, held):
            return pltpu.make_async_copy(held.at[place(task)], xrows, load_sem.at[7])

        @when(step < tasks)
        def _():
            states_home.each(step, True)

        @when(valid(g) & source)
        def _():
            load_rows(g, gin, place(g)).start()

        @when(valid(r))
        def _():
            @when(first)
            def _():
                load_x(r, xin).start()

            @when(jnp.logical_not(first))
            def _():
                load_x(r, xarrive).start()


        @when(valid(c))
        def _():
            @when(gathers(c))
            def _():
                gather_wait(moves, c)

            @when(jnp.logical_not(gathers(c)))
            def _():
                load_early(c).wait()

            store(2, c).start()

            @when(c == 0)
            def _():
                weights[0].wait()
                weights[1].wait()

            @when(c >= 1)
            def _():
                for k in range(2):
                    store(k, c - 1).wait()

            load(0, c).wait()
            spread(c)
            store(1, c).start()
            for k in range(1, 5):
                load(k, c).wait()
            store(2, c).wait()

        @when(valid(g))
        def _():
            @when(first)
            def _():
                moves.hand(g).wait_recv()
                load_rows(g, arrive, g).start()

            load_rows(g, gin, g).wait()

            @when((g >= 1) & gathers(g - 1))
            def _():
                gather_free(moves, g - 1)

            @when(gathers(g))
            def _():
                gather_start(moves, g, kept[g % 3])

            @when(jnp.logical_not(gathers(g)))
            def _():
                load_early(g).start()

            vectors[4:5, :] += jnp.sum(kept[g % 3].astype(f32), axis=0, keepdims=True)

        @when(valid(c))
        def _():
            @when(c % 2 == 0)
            def _():
                load_before(c).wait()
                attend_back(True)

            @when(c % 2 == 1)
            def _():
                attend_back(False)

            store(0, c).start()

        @when(valid(r))
        def _():
            @when(r == tasks - 1)
            def _():
                side_products()

            e = reduce_second(moves, r, mine)
            load_x(r, xin).wait()

            @when(r >= 2)
            def _():
                grads_home.each(place(r - 2), False)

                @when(source)
                def _():
                    moves.hand(r - 2).wait_send()

            standard, inverse = standardize(xrows[...])
            d_input = kept[r % 3].astype(f32) + inverse * (
                e
                - jnp.mean(e, axis=-1, keepdims=True)
                - standard * jnp.mean(e * standard, axis=-1, keepdims=True)
            )
            handed[r % 2] = d_input.astype(bf16)

            @when(source)
            def _():
                moves.hand(r).start()

            @when((r < tasks - 1) | (line.z != line.blocks))
            def _():
                grads_home.each(place(r), True)

            @when((r == tasks - 1) & (line.z == line.blocks))
            def _():
                keep_last().start()

        @when(valid(c))
        def _():
            @when(c == 0)
            def _():
                weights[2].wait()
                weights[3].wait()

            @when(c >= 1)
            def _():
                moves.give_theirs(c - 1).wait_send()

            merge_rows(1 - moves.core, theirs)
            moves.give_theirs(c).start()

            merge_rows(moves.core, mine)
            reduce_first(moves, c, mine)

        @when(valid(g) & gathers(g))
        def _():
            gather_pass(moves, g)

        @when(valid(c + 1))
        def _():
            for k in range(5):
                load(k, c + 1).start()

            @when((c + 1) % 2 == 0)
            def _():
                load_before(c + 1).start()

            @when(c + 1 == 0)
            def _():
                for copy in weights[2:]:
                    copy.start()

    @when(gathers(tasks - 1))
    def _():
        gather_free(moves, tasks - 1)

    drain(moves, tasks - 1)
    for k in range(2):
        store(k, tasks - 1).wait()
    grads_home.each(place(tasks - 2), False)

    @when(line.z != line.blocks)
    def _():
        grads_home.each(place(tasks - 1), False)

    @when(line.z == line.blocks)
    def _():
        keep_last().wait()

    for task in range(tasks - 2, tasks):

        @when(source)
        def _(task=task):
            moves.hand(task).wait_send()

    grads_home.wait(tasks - 2)

    for other in line.others():

        @when((line.z >= line.blocks) | (other != line.blocks))
        def _(other=other):
            grads_home.take(tasks - 1, 0, other).wait_recv()

    for task in range(tasks):
        states_home.each(task, False)
    states_home.wait(tasks)


def backward_pass(gin, xin, xarrive, states, early, qkv, dg, ctx, lse, std, wq, wi, wo, wd, gains, tables, pq, pk, chips, heads):
    tasks, rows, width = xin.shape
    count = lax.axis_size("ctx")
    home_sems = line_semaphores(tasks, count)[1]
    block = pq.shape[0]
    units, inner = wd.shape[0], wo.shape[0]
    anywhere = pl.BlockSpec(memory_space=pl.ANY)
    vmem = pl.BlockSpec(memory_space=pltpu.VMEM)
    shape = jax.ShapeDtypeStruct
    return pl.pallas_call(
        partial(backward_kernel, (tasks, chips, rows, heads)),
        out_shape=[
            shape((tasks, block, width), bf16),
            shape((tasks, block, 3 * inner), bf16),
            shape((tasks, block, units), bf16),
            shape((tasks // 2 * count, 2 * rows // count, width), bf16),
            shape((tasks // 2 * count, 2 * rows // count, width), bf16),
            shape((rows, width), bf16),
            shape((tasks, rows, width), bf16),
            shape((8, width), f32),
            shape((1, 3 * inner), f32),
            shape((1, units), f32),
        ],
        in_specs=[anywhere] * 14 + [vmem] * 6,
        out_specs=[anywhere] * 7 + [vmem] * 3,
        scratch_shapes=[
            pltpu.VMEM(wq.shape, bf16),
            pltpu.VMEM(wi.shape, bf16),
            pltpu.VMEM(wo.shape, bf16),
            pltpu.VMEM(wd.shape, bf16),
            pltpu.VMEM((3, block, width), bf16),
            pltpu.VMEM((block, units), bf16),
            pltpu.VMEM((block, units), bf16),
            pltpu.VMEM((block, 3 * inner), bf16),
            pltpu.VMEM((block, 3 * inner), bf16),
            pltpu.VMEM((block, inner), bf16),
            pltpu.VMEM((block, heads * LANES), f32),
            pltpu.VMEM((block, width), bf16),
            pltpu.VMEM((block, inner), bf16),
            pltpu.VMEM((block, 3 * inner), bf16),
            pltpu.VMEM((block, inner), f32),
            pltpu.VMEM((block, inner), f32),
            pltpu.VMEM((3, rows, width), bf16),
            pltpu.VMEM((chips * rows, width), bf16),
            pltpu.VMEM((chips * rows, width), f32),
            pltpu.VMEM((2, chips * rows, width), bf16),
            pltpu.VMEM((chips * rows, width), bf16),
            pltpu.VMEM((2, chips - 1, rows, width), bf16),
            pltpu.VMEM((2, rows, width), bf16),
            pltpu.VMEM((rows, width), bf16),
            pltpu.SemaphoreType.DMA((4,)),
            pltpu.SemaphoreType.DMA((9,)),
            pltpu.SemaphoreType.DMA((3,)),
            pltpu.SemaphoreType.DMA,
        ]
        + home_sems
        + home_sems
        + move_semaphores(tasks, chips),
        compiler_params=pltpu.CompilerParams(
            collective_id=5, has_side_effects=True, vmem_limit_bytes=PASS_VMEM
        ),
        cost_estimate=pl.CostEstimate(
            flops=2 * tasks * block * width * (3 * inner + 2 * units + inner),
            bytes_accessed=tasks * block * width * 20,
            transcendentals=0,
        ),
        name="backward_pass",
    )(gin, xin, xarrive, states, early, qkv, dg, ctx, lse, std, wq, wi, wo, wd, gains, *tables, pq, pk)


CHUNK = 256
PIECE = 32
SKEW = 2


def reduce_kernel(
    plan, act, ctx, dproj, dhid, gy, std, late, gains, biases, sums, small,
    out, small_out, late_home, from_left, from_right,
    rhs, raw, lhs, own, inbox, outbox, stage, small_in,
    rhs_sem, raw_sem, right_sem, left_sem, final_sem, load_sem, sent, stage_left, stage_right, out_sem,
    small_sent, small_got, late_sent, late_got,
):
    bounds, tasks, count, piece, skew, ring = plan
    sources = (dproj, dhid, act, ctx)
    total_chunks = bounds[-1]
    per_chunk = CHUNK // piece
    pieces = total_chunks * per_chunk
    width = gy.shape[-1]
    tile = width // per_chunk
    block = raw.shape[2]
    z = lax.axis_index("ctx")
    last = count - 1
    root = count // 2
    turn_at = max(root, last - root)
    low, high, middle = z < root, z > root, z == root

    barrier = pltpu.get_barrier_semaphore()
    for shift in range(1, count):
        pl.semaphore_signal(
            barrier,
            inc=1,
            device_id={"ctx": lax.rem(z + shift, count)},
            device_id_type=pl.DeviceIdType.MESH,
        )

    def small_copy(source, target):
        return pltpu.make_async_remote_copy(
            src_ref=small,
            dst_ref=small_in.at[source],
            send_sem=small_sent.at[target],
            recv_sem=small_got.at[source],
            device_id={"ctx": target},
            device_id_type=pl.DeviceIdType.MESH,
        )

    late_blocks = count // 2
    late_rows = late.shape[0] // late_blocks

    def late_copy(k):
        return pltpu.make_async_remote_copy(
            src_ref=late.at[pl.ds(k * late_rows, late_rows)],
            dst_ref=late_home,
            send_sem=late_sent.at[k],
            recv_sem=late_got,
            device_id={"ctx": k},
            device_id_type=pl.DeviceIdType.MESH,
        )

    def rhs_copy(k):
        return pltpu.make_async_copy((std, gy)[k].at[pl.ds(0, tasks)], rhs.at[k], rhs_sem.at[k])

    def each_source(chunk, act_on):
        for g, source in enumerate(sources):

            @pl.when((chunk >= bounds[g]) & (chunk < bounds[g + 1]))
            def _(g=g, source=source):
                column = pl.multiple_of((chunk - bounds[g]) * CHUNK, CHUNK)
                act_on(
                    pltpu.make_async_copy(
                        source.at[pl.ds(0, tasks), :, pl.ds(column, CHUNK)],
                        raw.at[chunk % 2],
                        raw_sem.at[chunk % 2],
                    )
                )

    def take(chunk):
        each_source(chunk, lambda copy: copy.wait())
        for k in range(tasks):
            lhs[:, k * block : (k + 1) * block] = raw[chunk % 2, k].T
        each_source(chunk + 1, lambda copy: copy.start())

    def multiply(chunk, part):
        second = jnp.where(chunk >= bounds[2], 1, 0)
        group = second + jnp.where(chunk >= bounds[1], 1, 0)
        columns = pl.ds(pl.multiple_of(part * tile, tile), tile)
        value = dot(lhs[:, :block], rhs[second, 0, :, columns])
        for k in range(1, tasks):
            value = value + dot(lhs[:, k * block : (k + 1) * block], rhs[second, k, :, columns])
        row = pl.multiple_of(chunk * CHUNK, CHUNK)
        value = value * gains[group, :, columns] + sums[pl.ds(row, CHUNK), :] * biases[group, :, columns]
        own[chunk % ring, :, columns] = value.astype(bf16)

    def rows_of(index):
        return pl.ds(pl.multiple_of(index * piece, piece), piece)

    def own_piece(index):
        inner = pl.multiple_of((index % per_chunk) * piece, piece)
        return own[(index // per_chunk) % ring, pl.ds(inner, piece), :]

    def remote(source, target_rows, send_sem, recv_sem, target):
        return pltpu.make_async_remote_copy(
            src_ref=source,
            dst_ref=target_rows,
            send_sem=send_sem,
            recv_sem=recv_sem,
            device_id={"ctx": target},
            device_id_type=pl.DeviceIdType.MESH,
        )

    def inward(index, right):
        landing, arrived, target = (from_left, right_sem, z + 1) if right else (from_right, left_sem, z - 1)
        return remote(
            outbox.at[index % 2], landing.at[rows_of(index)], sent.at[index % 2], arrived.at[index], target
        )

    def announce(index, right):
        return remote(
            stage.at[index % 2],
            out.at[rows_of(index)],
            (stage_right if right else stage_left).at[index % 2],
            final_sem.at[index],
            z + 1 if right else z - 1,
        )

    def onward(index, right):
        return remote(
            out.at[rows_of(index)],
            out.at[rows_of(index)],
            sent.at[2 + index % 2],
            final_sem.at[index],
            z + 1 if right else z - 1,
        )

    def load(index, right):
        landing = from_left if right else from_right
        return pltpu.make_async_copy(
            landing.at[rows_of(index)], inbox.at[0 if right else 1], load_sem.at[0 if right else 1]
        )

    def valid(index):
        return (index >= 0) & (index < pieces)

    def side(step, right):
        mine = low if right else high
        hops = z if right else last - z
        inner = step - hops * skew
        comes = hops > 0

        @pl.when(mine & valid(inner) & comes)
        def _():
            inward(inner, right).wait_recv()
            load(inner, right).start()

        @pl.when(mine & valid(inner))
        def _():
            @pl.when(inner >= 2)
            def _():
                inward(inner - 2, right).wait_send()

            @pl.when(comes)
            def _():
                load(inner, right).wait()
                value = own_piece(inner).astype(f32) + inbox[0 if right else 1].astype(f32)
                outbox[inner % 2] = value.astype(bf16)

            @pl.when(jnp.logical_not(comes))
            def _():
                outbox[inner % 2] = own_piece(inner)

            inward(inner, right).start()

        away = root - z if right else z - root
        outer = step - (turn_at + away) * skew

        @pl.when(mine & valid(outer))
        def _():
            onward(outer, not right).wait_recv()

            @pl.when(comes)
            def _():
                @pl.when(outer >= 2)
                def _():
                    onward(outer - 2, not right).wait_send()

                onward(outer, not right).start()

    def out_copy(index):
        return pltpu.make_async_copy(stage.at[index % 2], out.at[rows_of(index)], out_sem.at[index % 2])

    def stage_done(index):
        out_copy(index).wait()
        announce(index, False).wait_send()
        if root < last:
            announce(index, True).wait_send()

    def centre(step):
        index = step - turn_at * skew

        @pl.when(middle & valid(index))
        def _():
            inward(index, True).wait_recv()
            load(index, True).start()
            if root < last:
                inward(index, False).wait_recv()
                load(index, False).start()

            @pl.when(index >= 2)
            def _():
                stage_done(index - 2)

            load(index, True).wait()
            value = own_piece(index).astype(f32) + inbox[0].astype(f32)
            if root < last:
                load(index, False).wait()
                value = value + inbox[1].astype(f32)
            stage[index % 2] = value.astype(bf16)
            announce(index, False).start()
            if root < last:
                announce(index, True).start()
            out_copy(index).start()

    each_source(0, lambda copy: copy.start())
    rhs_copy(0).start()
    take(0)
    rhs_copy(0).wait()
    rhs_copy(1).start()

    @pl.loop(0, per_chunk)
    def _(part):
        multiply(0, part)

    pl.semaphore_wait(barrier, count - 1)
    small_in[z] = small[...]
    for shift in range(1, count):
        small_copy(z, lax.rem(z + shift, count)).start()
    @pl.when(middle)
    def _():
        for k in range(late_blocks):
            late_copy(k).start()

    @pl.loop(0, pieces + (turn_at + max(root, last - root)) * skew)
    def _(step):
        side(step, True)
        side(step, False)
        centre(step)
        chunk, part = step // per_chunk + 1, step % per_chunk

        @pl.when(chunk < total_chunks)
        def _():
            @pl.when(part == 0)
            def _():
                take(chunk)

                @pl.when(chunk == bounds[2])
                def _():
                    rhs_copy(1).wait()

            multiply(chunk, part)

    for shift in range(1, count):
        other = lax.rem(z + shift, count)
        small_copy(z, other).wait_send()
        small_copy(other, other).wait_recv()
    @pl.when(middle)
    def _():
        for k in range(late_blocks):
            late_copy(k).wait_send()

    @pl.when(low)
    def _():
        late_copy(0).wait_recv()

    value = small_in[0]
    for k in range(1, count):
        value = value + small_in[k]
    small_out[...] = value
    for back in (2, 1):
        for right in (True, False):

            @pl.when(low if right else high)
            def _(right=right, back=back):
                inward(pieces - back, right).wait_send()

                @pl.when((z > 0) & (z < last))
                def _():
                    onward(pieces - back, not right).wait_send()

        @pl.when(middle)
        def _(back=back):
            stage_done(pieces - back)


def reduce_gradients(act, ctx, dproj, dhid, gy, std, late, gains, biases, sums, small, tasks):
    count = lax.axis_size("ctx")
    block, width = gy.shape[1:]
    bounds = [0]
    for source in (dproj, dhid, act, ctx):
        bounds.append(bounds[-1] + source.shape[2] // CHUNK)
    total = bounds[-1] * CHUNK
    pieces = total // PIECE
    ring = count // 2 * SKEW // (CHUNK // PIECE) + 3
    plan = (tuple(bounds), tasks, count, PIECE, SKEW, ring)
    anywhere = pl.BlockSpec(memory_space=pl.ANY)
    vmem = pl.BlockSpec(memory_space=pltpu.VMEM)
    result = jax.ShapeDtypeStruct((total, width), bf16)
    late_shape = jax.ShapeDtypeStruct((2 * late.shape[0] // count, width), bf16)
    out, small_out, late_home, _, _ = pl.pallas_call(
        partial(reduce_kernel, plan),
        out_shape=[result, jax.ShapeDtypeStruct(small.shape, f32), late_shape, result, result],
        in_specs=[anywhere] * 7 + [vmem] * 4,
        out_specs=[anywhere, vmem, anywhere, anywhere, anywhere],
        scratch_shapes=[
            pltpu.VMEM((2, tasks, block, width), bf16),
            pltpu.VMEM((2, tasks, block, CHUNK), bf16),
            pltpu.VMEM((CHUNK, tasks * block), bf16),
            pltpu.VMEM((ring, CHUNK, width), bf16),
            pltpu.VMEM((2, PIECE, width), bf16),
            pltpu.VMEM((2, PIECE, width), bf16),
            pltpu.VMEM((2, PIECE, width), bf16),
            pltpu.VMEM((count,) + small.shape, f32),
            pltpu.SemaphoreType.DMA((2,)),
            pltpu.SemaphoreType.DMA((2,)),
            pltpu.SemaphoreType.DMA((pieces,)),
            pltpu.SemaphoreType.DMA((pieces,)),
            pltpu.SemaphoreType.DMA((pieces,)),
            pltpu.SemaphoreType.DMA((2,)),
            pltpu.SemaphoreType.DMA((4,)),
            pltpu.SemaphoreType.DMA((2,)),
            pltpu.SemaphoreType.DMA((2,)),
            pltpu.SemaphoreType.DMA((2,)),
            pltpu.SemaphoreType.DMA((count,)),
            pltpu.SemaphoreType.DMA((count,)),
            pltpu.SemaphoreType.DMA((count // 2,)),
            pltpu.SemaphoreType.DMA,
        ],
        compiler_params=pltpu.CompilerParams(
            collective_id=7, has_side_effects=True, vmem_limit_bytes=60 * 1024 * 1024
        ),
        cost_estimate=pl.CostEstimate(
            flops=2 * total * width * tasks * block,
            bytes_accessed=8 * total * width,
            transcendentals=0,
        ),
        name="reduce_gradients",
    )(act, ctx, dproj, dhid, gy, std, late, gains, biases, sums, small)
    return out, small_out, late_home


def turned_kernel(part, out):
    out[...] = part[...].astype(f32).T


def turned(total, start, count):
    width = total.shape[1]
    wide = 2 * CHUNK if start % (2 * CHUNK) == 0 and count % (2 * CHUNK) == 0 else CHUNK
    return pl.pallas_call(
        turned_kernel,
        out_shape=jax.ShapeDtypeStruct((width, count), f32),
        grid=(count // wide,),
        in_specs=[pl.BlockSpec((wide, width), lambda i: (start // wide + i, 0))],
        out_specs=pl.BlockSpec((width, wide), lambda i: (0, i)),
        compiler_params=pltpu.CompilerParams(vmem_limit_bytes=32 * 1024 * 1024),
        name="turned",
    )(total)


def turned_heads_kernel(heads, part, out):
    size = part.shape[0] // heads
    for h in range(heads):
        out[:, h, :] = part[h * size : (h + 1) * size, :].astype(f32).T


def turned_heads(total, start, count, heads):
    width = total.shape[1]
    return pl.pallas_call(
        partial(turned_heads_kernel, heads),
        out_shape=jax.ShapeDtypeStruct((width, heads, count // heads), f32),
        grid=(width // CHUNK,),
        in_specs=[pl.BlockSpec((count, CHUNK), lambda i: (start // count, i))],
        out_specs=pl.BlockSpec((CHUNK, heads, count // heads), lambda i: (i, 0, 0)),
        compiler_params=pltpu.CompilerParams(vmem_limit_bytes=32 * 1024 * 1024),
        name="turned_heads",
    )(total)


def body(
    inputs,
    out_grads,
    norm1_gain,
    norm1_bias,
    norm2_gain,
    norm2_bias,
    w_qkv,
    b_qkv,
    w_out,
    b_out,
    input_projection,
    input_bias_vector,
    down_projection,
    b_down,
):
    ctx_count = lax.axis_size("ctx")
    tensor = lax.axis_size("tensor")
    micro, _, rows, seqs, width = inputs.shape
    heads = w_qkv.shape[2]
    head_cols = w_qkv.shape[3]
    first = lax.axis_index("section") == 0
    per_device = micro * seqs // ctx_count
    blocks = ctx_count // 2
    tasks = 2 * per_device

    chosen = lax.cond(
        first,
        lambda: inputs[:, 0].transpose(0, 2, 1, 3),
        lambda: out_grads[:, 0].transpose(0, 2, 1, 3),
    )
    chosen = chosen.reshape(per_device, ctx_count, rows, width)

    wq = w_qkv[0].reshape(width, heads * head_cols)
    wi = input_projection[0]
    wo = w_out[0].reshape(-1, width)
    wd = down_projection[0]
    gain_one, bias_one, gain_two, bias_two = norm1_gain[0], norm1_bias[0], norm2_gain[0], norm2_bias[0]
    norms = jnp.stack([gain_one, bias_one, gain_two, bias_two], axis=1)
    out_bias = (b_out[0] + b_down[0])[None]

    relative, tables = position_tables(blocks, rows, tensor)
    places_q, places_k = jnp.asarray(relative[:, None]), jnp.asarray(relative[None, :])

    chips = tensor // 2
    std_all, qkv, act_all, dg_all, ctx_all, lse_all, chosen_rows, states, arrive, early = forward_pass(
        chosen,
        wq,
        wi,
        wo,
        wd,
        b_qkv[0].reshape(1, -1),
        input_bias_vector,
        norms,
        out_bias,
        tables,
        places_q,
        places_k,
        chips,
        heads,
    )
    gains = jnp.stack([gain_one, gain_two])[:, None]
    gy_all, dproj_all, dh_all, dx_home, states_home, last_rows, _, vectors, side_q, side_h = backward_pass(
        chosen_rows,
        chosen_rows,
        arrive,
        states,
        early,
        qkv,
        dg_all,
        ctx_all,
        lse_all,
        std_all,
        wq,
        wi,
        wo,
        wd,
        gains,
        tables,
        places_q,
        places_k,
        chips,
        heads,
    )
    vectors = vectors[:5]

    d_b_qkv, d_b_in = side_q[0], side_h[0]
    units, inner = wd.shape[0], wo.shape[0]
    sums = jnp.concatenate([d_b_qkv, d_b_in, jnp.zeros((units + inner,), f32)])[:, None]
    gains = jnp.stack([gain_one, gain_two, jnp.ones_like(gain_one)])[:, None]
    biases = jnp.stack([bias_one, bias_two, jnp.zeros_like(bias_one)])[:, None]
    mask = 1
    while mask < tensor:
        vectors = vectors + lax.ppermute(vectors, "tensor", [(k, k ^ mask) for k in range(tensor)])
        mask *= 2
    sides = jnp.concatenate([d_b_qkv, d_b_in])
    side_rows = -(-sides.shape[0] // width)
    small = jnp.zeros((-(-(5 + side_rows) // 8) * 8, width), f32)
    small = small.at[:5].set(vectors)
    small = small.at[5 : 5 + side_rows].set(
        jnp.pad(sides, (0, side_rows * width - sides.shape[0])).reshape(side_rows, width)
    )
    summed, small, late_home = reduce_gradients(
        act_all, ctx_all, dproj_all, dh_all, gy_all, std_all, last_rows, gains, biases, sums, small, tasks
    )
    columns = wq.shape[1]
    vectors = small[:5]
    sides = small[5 : 5 + side_rows].reshape(-1)
    d_b_qkv, d_b_in = sides[: d_b_qkv.shape[0]], sides[d_b_qkv.shape[0] : sides.shape[0]]
    d_b_in = d_b_in[: wi.shape[1]]
    d_w_qkv = turned_heads(summed, 0, columns, heads)
    d_w_in = turned(summed, columns, units)
    d_w_down = summed[columns + units : columns + 2 * units].astype(f32)
    d_w_out = summed[columns + 2 * units :].astype(f32)

    def homeward(pieces):
        return pieces.reshape(micro, seqs, rows, width).transpose(0, 2, 1, 3)[None, :, None]

    states = homeward(states_home)
    at = (per_device - 1) * ctx_count + blocks
    late_home = jnp.where(lax.axis_index("ctx") < blocks, late_home, dx_home[at])
    input_grads = homeward(lax.dynamic_update_index_in_dim(dx_home, late_home, at, 0)).astype(f32)
    return (
        states,
        input_grads,
        vectors[0][None],
        vectors[1][None],
        vectors[2][None],
        vectors[3][None],
        d_w_qkv.reshape(w_qkv.shape),
        d_b_qkv.reshape(b_qkv.shape),
        d_w_out.reshape(w_out.shape),
        vectors[4][None],
        d_w_in[None],
        d_b_in[None],
        d_w_down[None],
        vectors[4][None],
    )


def solution(mesh):
    return jax.shard_map(
        body,
        mesh=mesh,
        in_specs=(
            P(None, "ctx", "tensor", None, None),
            P(None, "ctx", "tensor", None, None),
            P("section", None),
            P("section", None),
            P("section", None),
            P("section", None),
            P("section", None, "tensor", None),
            P("section", "tensor", None),
            P("section", "tensor", None, None),
            P("section", None),
            P("section", None, "tensor"),
            P("section", "tensor"),
            P("section", "tensor", None),
            P("section", None),
        ),
        out_specs=(
            P("section", None, "ctx", "tensor", None, None),
            P("section", None, "ctx", "tensor", None, None),
            P("section", None),
            P("section", None),
            P("section", None),
            P("section", None),
            P("section", None, "tensor", None),
            P("section", "tensor", None),
            P("section", "tensor", None, None),
            P("section", None),
            P("section", None, "tensor"),
            P("section", "tensor"),
            P("section", "tensor", None),
            P("section", None),
        ),
        check_vma=False,
    )
```
